128 devices in a mesh: section: 8 (over x, z_hi), ctx: 4 (over z_lo, core), tp: 4 (over y).
Axes of the slice: x: 4, y: 4, z: 4 (z_hi: 2, z_lo: 2; z = z_hi * 2 + z_lo), core: 2. Of those that a mesh axis runs over, the one named last changes fastest.
Arguments:
- boundary: bfloat16 [4, 16, 160, 768], P('ctx', 'section'), may hold values from -6 to 6
- routes: int32 [4, 16, 160, 2], P('ctx', 'section'), may hold values from 0 to 3, all different within a row; in each aligned block of 160 rows (0 to 159, 160 to 319, ..., all dimensions but the last counted through in order) at most 120 rows name the same one
- lengths: int32 [4], replicated, may hold values from 1 to 160, 577 in all
- ln_gains: bfloat16 [2, 2, 768], P(None, None, ('section', 'ctx')), may hold values from 0.5 to 1.5
- ln_biases: bfloat16 [2, 2, 768], P(None, None, ('section', 'ctx')), may hold values from -1 to 1
- w_qkv: bfloat16 [2, 768, 3, 768], P(None, ('section', 'ctx'), None, 'tp'), may hold values from -0.21875 to 0.21875
- w_out: bfloat16 [2, 768, 768], P(None, 'tp', ('section', 'ctx')), may hold values from -0.625 to 0.625
- w_router: bfloat16 [2, 768, 4], P(None, ('section', 'ctx')), may hold values from -0.15625 to 0.15625
- w_in: bfloat16 [2, 4, 768, 3072], P(None, None, ('section', 'ctx'), 'tp'), may hold values from -0.21875 to 0.21875
- w_exp_out: bfloat16 [2, 4, 3072, 768], P(None, None, 'tp', ('section', 'ctx')), may hold values from -0.3125 to 0.3125
Outputs:
- ends_out: float32 [4, 16, 160, 768], P('ctx', 'section')
- grad_ln_gains: float32 [2, 2, 768], P(None, None, ('section', 'ctx'))
- grad_ln_biases: float32 [2, 2, 768], P(None, None, ('section', 'ctx'))
- grad_w_qkv: float32 [2, 768, 3, 768], P(None, ('section', 'ctx'), None, 'tp')
- grad_w_out: float32 [2, 768, 768], P(None, 'tp', ('section', 'ctx'))
- grad_w_router: float32 [2, 768, 4], P(None, ('section', 'ctx'))
- grad_w_in: float32 [2, 4, 768, 3072], P(None, None, ('section', 'ctx'), 'tp')
- grad_w_exp_out: float32 [2, 4, 3072, 768], P(None, None, 'tp', ('section', 'ctx'))
The draws below stay inside these ranges and needn't reach their ends.
Inputs may be any that keep to these rules, and one draw needn't show every extreme that they name: `routes`: each row names two different experts. In each aligned block of 160 rows (rows taken in the order of the array's dimensions: the rows of one device for one micro-batch) no expert is named more than 120 times. The blocks' lengths sum to 577; the largest equals 160.
All inputs are finite; a program needn't handle non-finite values.
Results may differ from the reference program's by a relative error of at most 0.028.
Values may be sent and summed in bfloat16 or wider, within the bound.
A program may use at most 192 MiB of HBM per device.

```python
import math
import jax
import jax.numpy as jnp
import numpy as np
from jax import lax

D = 768
HEADS = 12
HD = 64
FF = 3072
SEQ = 577
EXPERTS = 4
TOPK = 2
CBLK = 160
IMGS = 1
CAP = 120
IMG_ALL = 16
N_CTX = 4


def block_scale(own_key, extent, cuts, least, high):
    loudness, own = 1.0, jax.random.fold_in(own_key, 6)
    for axis_at, parts in cuts:
        steps = jnp.exp(jax.random.uniform(jax.random.fold_in(own, axis_at), (parts,), jnp.float32, least / len(cuts), high / len(cuts)))
        loudness = loudness * jnp.repeat(steps, extent[axis_at] // parts).reshape([-1 if axis == axis_at else 1 for axis in range(len(extent))])
    return loudness


def length_profile(amount, total, limit, skew):
    portions = [(1 << 20) // math.isqrt(rank ** skew) + 1 for rank in range(2, amount + 1)]
    surplus, holding = total - limit - (amount - 1), [1] * (amount - 1)
    while surplus > 0:
        candidates = [i for i in range(amount - 1) if holding[i] < limit]
        mass, remaining = sum([portions[i] for i in candidates]), surplus
        for i in candidates:
            addition = min(limit - holding[i], max(1, remaining * portions[i] // mass), surplus)
            holding[i] = holding[i] + addition
            surplus = surplus - addition
    return np.array([limit] + holding)


def uneven(key, number_of, total, limit, slope):
    if number_of == 2:
        one = jax.random.randint(key, (), max(1, total - limit), min(limit, total - 1) + 1)
        return jnp.stack([one, total - one])
    sizes = jnp.asarray(length_profile(number_of, total, limit, slope), jnp.int32)
    twos = (number_of - 1) // 2
    donor, taker = sizes[1:1 + 2 * twos:2], sizes[2:2 + 2 * twos:2]
    slack = jnp.minimum(donor - 1, limit - taker)
    moved = jax.random.randint(jax.random.fold_in(key, 1), (twos,), 0, 1 << 20) % (slack + 1)
    sizes = sizes.at[1:1 + 2 * twos:2].set(donor - moved).at[2:2 + 2 * twos:2].set(taker + moved)
    return sizes[jax.random.permutation(jax.random.fold_in(key, 2), number_of)]


def shared_out(own_key, own, number, rows, amount, top, reach, slope):
    order = jax.random.permutation(own_key, amount)
    crowded, ordinary = load_shares(amount, rows * top, reach, slope, True), load_shares(amount, rows * top, reach, slope, False)
    places = jnp.arange(amount)

    def named(sizes, rotation):
        used = int((sizes > 0).sum())
        fixed = max(1, used // 4)
        moved = fixed + (places - fixed + rotation * (used - fixed)) % max(1, amount - fixed)
        return jnp.zeros((amount,), jnp.int32).at[order[jnp.where(places < fixed, places, moved)]].set(jnp.asarray(sizes, jnp.int32))

    sizes = jnp.where(number % 4 == 0, named(crowded, number // 4), named(ordinary, number - number // 4 - 1))
    mixed = jax.random.permutation(jax.random.fold_in(own, 3), amount)
    giver, taker = mixed[0:amount // 2 * 2:2], mixed[1:amount // 2 * 2:2]
    margin = jnp.minimum(sizes[giver] - 1, reach - sizes[taker]) // 2
    margin = jnp.where((giver == order[0]) | (taker == order[0]) | (sizes[taker] == 0), 0, jnp.maximum(margin, 0))
    moved = jax.random.randint(jax.random.fold_in(own, 4), (amount // 2,), 0, 1 << 20) % (margin + 1)
    sizes = sizes.at[giver].add(-moved).at[taker].add(moved)
    labels = jnp.searchsorted(jnp.cumsum(sizes), jnp.arange(rows * top), side="right").astype(jnp.int32)
    table = labels.reshape(top, rows).T
    table = table[jax.random.permutation(jax.random.fold_in(own, 1), rows)]
    rotation = jax.random.randint(jax.random.fold_in(own, 2), (rows, 1), 0, top)
    return jnp.take_along_axis(table, (jnp.arange(top)[None, :] + rotation) % top, axis=1)


def load_shares(number_of, total, reach, lean, full):
    portions = [(1 << 20) // math.isqrt(standing ** lean) + 1 for standing in range(1, number_of + 1)]
    largest = reach if full else min(reach, max(-(-total // number_of), total * portions[0] // sum(portions)))
    least = 1 if total - largest >= number_of - 1 else 0
    holding, rest = [largest] + [least] * (number_of - 1), total - largest - least * (number_of - 1)
    while rest > 0:
        free = [i for i in range(1, number_of) if holding[i] < largest] or [i for i in range(1, number_of) if holding[i] < reach]
        whole, budget = sum([portions[i] for i in free]), rest
        for i in free:
            extra = min(reach - holding[i], max(1, budget * portions[i] // whole), rest)
            holding[i] = holding[i] + extra
            rest = rest - extra
    return np.array(holding)


def centred(stream_key, dims, width, reach, pieces=(), kind=jnp.bfloat16):
    values = width * jax.random.normal(stream_key, dims, jnp.float32)
    if pieces:
        values = values * block_scale(stream_key, dims, pieces, -0.22, 0.18)
    return jnp.clip(values, -reach, reach).astype(kind)


def setup_inputs(seed: int = 0) -> dict:
    key_of = jax.random.split(jax.random.key(seed), 11)
    boundary = centred(key_of[0], (N_CTX, IMG_ALL, CBLK, D), 1.0, 6.0, ((0, 4), (1, 8)))
    routes_keys = jax.random.split(jax.random.fold_in(key_of[1], 1), N_CTX * IMG_ALL * CBLK // (IMGS * CBLK))
    routes_turns = jax.random.permutation(jax.random.fold_in(key_of[1], 3), N_CTX * IMG_ALL * CBLK // (IMGS * CBLK))
    routes = jax.vmap(lambda own, number: shared_out(jax.random.fold_in(key_of[1], 2), own, number, IMGS * CBLK, EXPERTS, TOPK, CAP, 1))(routes_keys, routes_turns).reshape((N_CTX, IMG_ALL, CBLK, TOPK))
    lengths = uneven(key_of[2], N_CTX, SEQ, CBLK, 2).astype(jnp.int32)
    ln_gains = jnp.clip(1.0 + 0.1 * jax.random.normal(key_of[3], (2, 2, D), jnp.float32), 0.5, 1.5).astype(jnp.bfloat16)
    ln_biases = centred(key_of[4], (2, 2, D), 0.2, 1.0, ((2, 32),))
    w_qkv = centred(key_of[5], (2, D, 3, HEADS * HD), D ** -0.5, 0.21875, ((1, 32), (3, 4)))
    w_out = centred(key_of[6], (2, HEADS * HD, D), (D // 8) ** -0.5, 0.625, ((1, 4), (2, 32)))
    w_router = centred(key_of[7], (2, D, EXPERTS), (2 * D) ** -0.5, 0.15625, ((1, 32),))
    w_in = centred(key_of[8], (2, EXPERTS, D, FF), D ** -0.5, 0.21875, ((2, 32), (3, 4)))
    w_exp_out = centred(key_of[9], (2, EXPERTS, FF, D), (FF // 8) ** -0.5, 0.3125, ((2, 4), (3, 32)))
    return dict(boundary=boundary, routes=routes, lengths=lengths, ln_gains=ln_gains, ln_biases=ln_biases, w_qkv=w_qkv, w_out=w_out, w_router=w_router, w_in=w_in, w_exp_out=w_exp_out)


highest = lax.Precision.HIGHEST
eps = 1e-06

@jax.custom_vjp
def low(v):
    return lax.optimization_barrier(v.astype(jnp.bfloat16)).astype(jnp.float32)

@jax.custom_vjp
def low_back(v):
    return v

def low_keep(v):
    return (low(v), None)

def low_pass(kept, grad):
    return (grad,)

def back_keep(v):
    return (v, None)

def back_low(kept, grad):
    return (low(grad),)
low.defvjp(low_keep, low_pass)
low_back.defvjp(back_keep, back_low)

def normalize(values, scales, offset):
    average = lax.optimization_barrier(jnp.mean(values, axis=-1, keepdims=True))
    centered = values - average
    variance = lax.optimization_barrier(jnp.mean(centered * centered, axis=-1, keepdims=True))
    return centered * lax.rsqrt(variance + eps) * scales + offset

def expert_tables(route_rows, expert_count, capacity):
    row_count = route_rows.shape[0]
    chosen = (route_rows[:, :, None] == jnp.arange(expert_count, dtype=jnp.int32)[None, None, :]).astype(jnp.int32)
    flat_hits = chosen.reshape(row_count * 2, expert_count)
    earlier = jnp.cumsum(flat_hits, axis=0) - flat_hits
    places = lax.optimization_barrier(jnp.sum(earlier * flat_hits, axis=1)).reshape(row_count, 2)
    slot_hits = places[:, :, None] == jnp.arange(capacity, dtype=jnp.int32)[None, None, :]
    return (chosen.astype(jnp.float32), slot_hits.astype(jnp.float32))

def attend(image_data, key_live):
    length = image_data.shape[0]
    queries = image_data[:, 0].reshape(length, HEADS, HD)
    keys_split = image_data[:, 1].reshape(length, HEADS, HD)
    values_split = image_data[:, 2].reshape(length, HEADS, HD)
    scores = low_back(HD ** (-0.5) * jnp.einsum('qhe,khe->hqk', queries, keys_split, precision=highest))
    scores = jnp.where(key_live[None, None, :], scores, -1e+30)
    weights = low(jax.nn.softmax(scores, axis=-1))
    mixed_heads = jnp.einsum('hqk,khe->qhe', weights, values_split, precision=highest)
    return mixed_heads.reshape(length, HEADS * HD)

def expert_block(normed_rows, route_rows, w_router, w_in, w_exp_out):
    logits = jnp.dot(normed_rows, w_router, precision=highest)
    router_probs = jax.nn.softmax(logits, axis=-1)
    chosen, slot_hits = expert_tables(route_rows, w_in.shape[0], CAP)
    gate_values = lax.optimization_barrier(jnp.sum(router_probs[:, None, :] * chosen, axis=-1))
    dispatch = jnp.einsum('rke,rkc->ecr', chosen, slot_hits, precision=highest)
    combine = jnp.einsum('rke,rkc,rk->ecr', chosen, slot_hits, gate_values, precision=highest)
    expert_in = jnp.einsum('ecr,rd->ecd', dispatch, normed_rows, precision=highest)
    hidden = low_back(jnp.einsum('ecd,edf->ecf', expert_in, w_in, precision=highest))
    active = low(jax.nn.gelu(hidden))
    expert_part = low_back(jnp.einsum('ecf,efd->ecd', active, w_exp_out, precision=highest))
    return jnp.einsum('ecr,ecd->rd', combine, expert_part, precision=highest)

def block_layer(tokens, scales, offsets, w_qkv, w_out, w_router, w_in, w_exp_out, route_half, key_live):
    ctx_count, images, block_len, width_dim = tokens.shape
    normed = low(normalize(tokens, scales[0], offsets[0]))
    projected = low(low_back(jnp.einsum('cibd,dth->cibth', normed, w_qkv, precision=highest)))
    per_image = jnp.transpose(projected, (1, 0, 2, 3, 4)).reshape(images, ctx_count * block_len, 3, HEADS * HD)

    def attend_one(image_data):
        return attend(image_data, key_live)
    mixed_heads = lax.map(jax.checkpoint(attend_one), per_image)
    mixed_heads = low(low_back(mixed_heads))
    attended = low_back(jnp.einsum('isf,fd->isd', mixed_heads, w_out, precision=highest))
    attended = jnp.transpose(attended.reshape(images, ctx_count, block_len, width_dim), (1, 0, 2, 3))
    middle = tokens + attended
    normed_two = low(normalize(middle, scales[1], offsets[1]))
    block_count = ctx_count * (images // IMGS)
    row_blocks = normed_two.reshape(block_count, IMGS * block_len, width_dim)
    route_blocks = route_half.reshape(block_count, IMGS * block_len, 2)

    def expert_one(pair):
        return expert_block(pair[0], pair[1], w_router, w_in, w_exp_out)
    expert_total = lax.map(jax.checkpoint(expert_one), (row_blocks, route_blocks))
    return middle + expert_total.reshape(ctx_count, images, block_len, width_dim)

def reference(boundary, routes, lengths, ln_gains, ln_biases, w_qkv, w_out, w_router, w_in, w_exp_out):
    half_count = boundary.shape[1] // 2
    live_slots = jnp.arange(CBLK, dtype=jnp.int32)[None, :] < lengths[:, None]
    key_live = live_slots.reshape(-1)
    live_mask = live_slots.astype(jnp.float32)[:, None, :, None]
    entering = boundary[:, :half_count].astype(jnp.float32)
    cotangent = boundary[:, half_count:].astype(jnp.float32) * live_mask
    route_first = routes[:, :half_count]
    route_second = routes[:, half_count:]
    params = tuple((p.astype(jnp.float32) for p in (ln_gains, ln_biases, w_qkv, w_out, w_router, w_in, w_exp_out)))

    def forward(start, gain_all, bias_all, wq_all, wo_all, wr_all, wi_all, we_all):
        middle_out = block_layer(start, gain_all[0], bias_all[0], wq_all[0], wo_all[0], wr_all[0], wi_all[0], we_all[0], route_first, key_live)
        passed = low(low_back(middle_out))
        final_out = block_layer(passed, gain_all[1], bias_all[1], wq_all[1], wo_all[1], wr_all[1], wi_all[1], we_all[1], route_second, key_live)
        return final_out * live_mask
    result, pull_back = jax.vjp(forward, entering, *params)
    grads = pull_back(cotangent)
    ends_out = jnp.concatenate([grads[0] * live_mask, result], axis=1)
    return (ends_out, grads[1], grads[2], grads[3], grads[4], grads[5], grads[6], grads[7])
```

```python
import functools

import jax
import jax.numpy as jnp
from jax import lax
from jax.experimental import pallas as pl
from jax.experimental.pallas import tpu as pltpu
from jax.sharding import Mesh
from jax.sharding import PartitionSpec as P

D = 768
HD = 64
HEADS = 3
ROWS = 160
PAIR = 320
KEYS = 640
FE = 384
EXPERTS = 4
EPS = 1e-06
MESH = pl.DeviceIdType.MESH
CHIPS = ("x", "zh", "zl")
f32, bf16 = jnp.float32, jnp.bfloat16
VMEM = pl.BlockSpec(memory_space=pltpu.VMEM)
SMEM = pl.BlockSpec(memory_space=pltpu.SMEM)
NN = (((1,), (0,)), ((), ()))
NT = (((1,), (1,)), ((), ()))
TN = (((0,), (0,)), ((), ()))


def dot(a, b, dims):
    return lax.dot_general(a, b, dims, preferred_element_type=f32)


def dot_exact(a, b, dims):
    return lax.dot_general(
        a, b, dims, preferred_element_type=f32, precision=lax.Precision.HIGHEST
    )


def enter(peers):
    barrier = pltpu.get_barrier_semaphore()
    for peer in peers:
        pl.semaphore_signal(barrier, inc=1, device_id=peer, device_id_type=MESH)
    pl.semaphore_wait(barrier, len(peers))


def remote(src, dst, send, recv, peer):
    return pltpu.make_async_remote_copy(
        src_ref=src, dst_ref=dst, send_sem=send, recv_sem=recv, device_id=peer, device_id_type=MESH
    )


def comm_params(cid):
    return pltpu.CompilerParams(
        collective_id=cid, has_side_effects=True, vmem_limit_bytes=40 * 2**20
    )


def reduce_kernel(both, part, out, landed, rs_send, rs_recv, ag_send, ag_recv, cx_send, cx_recv):
    core, tp = lax.axis_index("core"), lax.axis_index("tp")
    other = 1 - core
    offsets = [(k // 4, k % 4) for k in range(1, 8 if both else 4)]
    peers = [{"core": (core + dc) % 2, "tp": (tp + dt) % 4} for dc, dt in offsets]
    enter(peers if both else peers + [{"core": other}])
    sends = []
    for k, peer in enumerate(peers):
        block = peer["core"] if both else 0
        copy = remote(
            part.at[block, peer["tp"]], landed.at[k], rs_send.at[k], rs_recv.at[k], peer
        )
        copy.start()
        sends.append(copy)
    total = part[core if both else 0, tp].astype(f32)
    for k, copy in enumerate(sends):
        copy.wait_recv()
        total = total + landed[k].astype(f32)
    out[core, tp] = total.astype(bf16)
    gathers = []
    for k in range(3):
        peer = {"tp": (tp + k + 1) % 4}
        copy = remote(out.at[core, tp], out.at[core, tp], ag_send.at[k], ag_recv.at[k], peer)
        copy.start()
        gathers.append(copy)
    crosses = []
    for k in range(4):
        at = (tp + 4 - k) % 4
        if k > 0:
            gathers[k - 1].wait_recv()
        copy = remote(
            out.at[core, at], out.at[core, at], cx_send.at[k], cx_recv.at[k], {"core": other}
        )
        copy.start()
        crosses.append(copy)
    for copy in crosses:
        copy.wait()
    for copy in sends + gathers:
        copy.wait_send()


def reduce_rows(part, cid):
    blocks, _, rows, cols = part.shape
    both = blocks == 2
    count = 7 if both else 3
    return pl.pallas_call(
        functools.partial(reduce_kernel, both),
        out_shape=jax.ShapeDtypeStruct((2, 4, rows, cols), bf16),
        in_specs=[VMEM],
        out_specs=VMEM,
        scratch_shapes=[pltpu.VMEM((count, rows, cols), bf16)]
        + [pltpu.SemaphoreType.DMA((count,))] * 2
        + [pltpu.SemaphoreType.DMA((3,))] * 2
        + [pltpu.SemaphoreType.DMA((4,))] * 2,
        compiler_params=comm_params(cid),
        name="reduce_rows",
    )(part)


def ctx_peers():
    core, zl = lax.axis_index("core"), lax.axis_index("zl")
    return [
        {"zl": (zl + k // 2) % 2, "core": (core + k % 2) % 2} for k in range(1, 4)
    ], zl * 2 + core


def kv_kernel(kv, out, send, recv):
    peers, me = ctx_peers()
    enter(peers)
    copies = []
    for k, peer in enumerate(peers):
        copy = remote(kv, out.at[me], send.at[k], recv.at[k], peer)
        copy.start()
        copies.append(copy)
    out[me] = kv[...]
    for copy in copies:
        copy.wait()


def gather_kv(kv):
    return pl.pallas_call(
        kv_kernel,
        out_shape=jax.ShapeDtypeStruct((4, ROWS, 2 * HEADS * HD), bf16),
        in_specs=[VMEM],
        out_specs=VMEM,
        scratch_shapes=[pltpu.SemaphoreType.DMA((3,))] * 2,
        compiler_params=comm_params(5),
        name="gather_kv",
    )(kv)


def kv_sum_kernel(part, out, landed, send, recv):
    peers, me = ctx_peers()
    enter(peers)
    copies = []
    for k, peer in enumerate(peers):
        at = peer["zl"] * 2 + peer["core"]
        copy = remote(part.at[at], landed.at[k], send.at[k], recv.at[k], peer)
        copy.start()
        copies.append(copy)
    total = part[me].astype(f32)
    for k, copy in enumerate(copies):
        copy.wait_recv()
        total = total + landed[k].astype(f32)
    out[...] = total.astype(bf16)
    for copy in copies:
        copy.wait_send()


def scatter_kv(part):
    return pl.pallas_call(
        kv_sum_kernel,
        out_shape=jax.ShapeDtypeStruct((ROWS, 2 * HEADS * HD), bf16),
        in_specs=[VMEM],
        out_specs=VMEM,
        scratch_shapes=[pltpu.VMEM((3, ROWS, 2 * HEADS * HD), bf16)]
        + [pltpu.SemaphoreType.DMA((3,))] * 2,
        compiler_params=comm_params(6),
        name="scatter_kv",
    )(part)


def start_kernel(images, weights, out_images, out_weights, send, recv):
    core, x = lax.axis_index("core"), lax.axis_index("x")
    high = x // 2
    partner, other = {"x": (x + 2) % 4}, {"core": 1 - core}
    enter([partner, other])
    swap = remote(
        images.at[1 - high], out_images.at[core, high], send.at[0], recv.at[0], partner
    )
    swap.start()
    cross = remote(weights, out_weights, send.at[1], recv.at[1], other)
    cross.start()
    kept = remote(images.at[high], out_images.at[core, high], send.at[2], recv.at[2], other)
    kept.start()
    out_images[core, high] = images[high]
    swap.wait_recv()
    passed = remote(
        out_images.at[core, 1 - high],
        out_images.at[core, 1 - high],
        send.at[3],
        recv.at[3],
        other,
    )
    passed.start()
    for copy in (cross, kept, passed):
        copy.wait()
    swap.wait_send()


def start_exchange(images, weights):
    return pl.pallas_call(
        start_kernel,
        out_shape=(
            jax.ShapeDtypeStruct((2,) + images.shape, bf16),
            jax.ShapeDtypeStruct(weights.shape, bf16),
        ),
        in_specs=[VMEM, VMEM],
        out_specs=(VMEM, VMEM),
        scratch_shapes=[pltpu.SemaphoreType.DMA((4,))] * 2,
        compiler_params=comm_params(0),
        name="start_exchange",
    )(images, weights)


def chip_peer(k):
    x, zh, zl = (lax.axis_index(a) for a in CHIPS)
    dx, dh, dl = k // 4, (k // 2) % 2, k % 2
    ahead = ((x + dx) % 4, (zh + dh) % 2, (zl + dl) % 2)
    back = ((x + 4 - dx) % 4, (zh + 2 - dh) % 2, (zl + 2 - dl) % 2)
    return dict(zip(CHIPS, ahead)), *(c[0] * 4 + c[1] * 2 + c[2] for c in (ahead, back))


def gather_kernel(own, out, send, recv, cx_send, cx_recv):
    core = lax.axis_index("core")
    other = {"core": 1 - core}
    _, me, _ = chip_peer(0)
    enter([chip_peer(k)[0] for k in range(1, 16)] + [other])
    out[me, core] = own[...]

    def push(k):
        peer, _, _ = chip_peer(k)
        return remote(own, out.at[me, core], send.at[k], recv.at[k], peer)

    def cross(k):
        _, _, at = chip_peer(k)
        return remote(out.at[at, core], out.at[at, core], cx_send.at[k], cx_recv.at[k], other)

    def first(k, carry):
        push(k).start()
        return carry

    def onward(k, carry):
        push(k).wait_recv()
        cross(k).start()
        return carry

    def last(k, carry):
        push(k).wait_send()
        cross(k).wait()
        return carry

    lax.fori_loop(1, 16, first, 0)
    cross(0).start()
    lax.fori_loop(1, 16, onward, 0)
    cross(0).wait()
    lax.fori_loop(1, 16, last, 0)


def gather_small(own):
    return pl.pallas_call(
        gather_kernel,
        out_shape=jax.ShapeDtypeStruct((16, 2) + own.shape, bf16),
        in_specs=[VMEM],
        out_specs=VMEM,
        scratch_shapes=[pltpu.SemaphoreType.DMA((16,))] * 4,
        compiler_params=comm_params(1),
        name="gather_small",
    )(own)


def scatter_kernel(part, out, landed, sums, pieces, cx, send, recv):
    core = lax.axis_index("core")
    other = {"core": 1 - core}
    _, me, _ = chip_peer(0)
    enter([chip_peer(k)[0] for k in range(1, 16)] + [other])
    cross = remote(part.at[1 - core], landed, cx.at[0], cx.at[1], other)
    cross.start()
    cross.wait()

    def push(k):
        peer, at, _ = chip_peer(k)
        return remote(sums.at[at], pieces.at[k], send.at[k], recv.at[k], peer)

    def add(k, carry):
        _, at, _ = chip_peer(k)
        sums[at] = (part[core, at].astype(f32) + landed[at].astype(f32)).astype(bf16)
        push(k).start()
        return carry

    def collect(k, carry):
        push(k).wait_recv()
        out[...] += pieces[k].astype(f32)
        return carry

    def last(k, carry):
        push(k).wait_send()
        return carry

    lax.fori_loop(1, 16, add, 0)
    out[...] = part[core, me].astype(f32) + landed[me].astype(f32)
    lax.fori_loop(1, 16, collect, 0)
    lax.fori_loop(1, 16, last, 0)


def scatter_small(part):
    shape = part.shape[2:]
    return pl.pallas_call(
        scatter_kernel,
        out_shape=jax.ShapeDtypeStruct(shape, f32),
        in_specs=[VMEM],
        out_specs=VMEM,
        scratch_shapes=[pltpu.VMEM((16,) + shape, bf16)] * 3
        + [pltpu.SemaphoreType.DMA((2,))]
        + [pltpu.SemaphoreType.DMA((16,))] * 2,
        compiler_params=comm_params(7),
        name="scatter_small",
    )(part)


def compute_params():
    return pltpu.CompilerParams(vmem_limit_bytes=56 * 2**20)


def block_rows(ref, block):
    top = jnp.concatenate([ref[block, 0, 0:80], ref[block, 1, 0:80]], axis=1)
    low = jnp.concatenate([ref[block, 2, 0:80], ref[block, 3, 0:80]], axis=1)
    return jnp.concatenate([top, low], axis=0).astype(f32)


def pair_rows(ref):
    return jnp.concatenate([block_rows(ref, 0), block_rows(ref, 1)], axis=0)


def chunks(value):
    return [
        value[80 * (j // 2) : 80 * (j // 2) + 80, 384 * (j % 2) : 384 * (j % 2) + 384]
        for j in range(4)
    ]


def norm_parts(rows):
    centered = rows - jnp.mean(rows, axis=-1, keepdims=True)
    scale = lax.rsqrt(jnp.mean(centered * centered, axis=-1, keepdims=True) + EPS)
    return centered * scale, scale


def norm_back(grad, unit, scale, gain):
    inner = grad * gain
    return scale * (
        inner
        - jnp.mean(inner, axis=-1, keepdims=True)
        - unit * jnp.mean(inner * unit, axis=-1, keepdims=True)
    )


def softmax(logits, axis):
    top = jnp.max(logits, axis=axis, keepdims=True)
    powers = jnp.exp(logits - top)
    return powers / jnp.sum(powers, axis=axis, keepdims=True)


def project(rows, small, w_qkv, q, kv):
    unit, _ = norm_parts(rows)
    normed = (unit * small[0:1] + small[2:3]).astype(bf16)
    out = dot(normed, w_qkv[...], NN).astype(bf16)
    q[...] = out[:, : HEADS * HD]
    kv[...] = out[:, HEADS * HD :]


def first_kernel(core, x, small, w_qkv, q, kv):
    rows = x[pl.ds(pl.multiple_of(core[0] * ROWS, ROWS), ROWS)].astype(f32)
    project(rows, small, w_qkv, q, kv)


def next_kernel(core, x, att, moe, small, w_qkv, q, kv, x_next):
    x_next[...] = (x[...].astype(f32) + pair_rows(att) + pair_rows(moe)).astype(bf16)
    rows = x_next[pl.ds(pl.multiple_of(core[0] * ROWS, ROWS), ROWS)].astype(f32)
    project(rows, small, w_qkv, q, kv)


def call(kernel, out_shapes, *args, name):
    return pl.pallas_call(
        kernel,
        out_shape=[jax.ShapeDtypeStruct(s, t) for s, t in out_shapes],
        in_specs=[SMEM if a.dtype == jnp.int32 else VMEM for a in args],
        out_specs=[VMEM] * len(out_shapes),
        compiler_params=compute_params(),
        name=name,
    )(*args)


def head(value, h):
    return value[:, HD * h : HD * h + HD]


def attend_kernel(q, kv, dead, w_out_t, part, mixed):
    width = HEADS * HD
    keys = kv[...].reshape(KEYS, 2 * width)
    queries = q[...]
    outs = []
    for h in range(HEADS):
        scores = HD**-0.5 * dot(head(queries, h), head(keys, h), NT) + dead[...]
        probs = softmax(scores, -1).astype(bf16)
        outs.append(dot(probs, head(keys, HEADS + h), NN))
    mixed[...] = jnp.concatenate(outs, axis=1).astype(bf16)
    value = dot(mixed[...], w_out_t[...], NT).astype(bf16)
    for j, chunk in enumerate(chunks(value)):
        part[0, j] = chunk


def gelu_parts(u):
    c = 0.7978845608028654
    t = jnp.tanh(c * (u + 0.044715 * u * u * u))
    return 0.5 * u * (1.0 + t), t


def gelu_slope(u, t):
    c = 0.7978845608028654
    return 0.5 * (1.0 + t) + 0.5 * u * (1.0 - t * t) * (c * (1.0 + 3 * 0.044715 * u * u))


def expert_weights(weights):
    block = weights[...]
    return block[:, 0].reshape(D, FE), block[:, 1].reshape(D, FE)


def experts_setup(x, att, small, routes, b, gates):
    unit, _ = norm_parts(x[...].astype(f32) + pair_rows(att))
    b[...] = (unit * small[1:2] + small[3:4]).astype(bf16)
    probs = softmax(dot(b[...], small[4:8].astype(bf16), NT), -1)
    ids = lax.broadcasted_iota(jnp.int32, (PAIR, EXPERTS), 1).astype(f32)
    named = (routes[:, 0:1] == ids) | (routes[:, 1:2] == ids)
    gates[...] = jnp.where(named, probs, 0.0)


def gate_of(gates, expert):
    ids = lax.broadcasted_iota(jnp.int32, (PAIR, EXPERTS), 1)
    return jnp.sum(jnp.where(ids == expert, gates[...], 0.0), axis=1, keepdims=True)


def experts_kernel(x, att, small, routes, weights, part, b, gates, total):
    expert = pl.program_id(0)

    @pl.when(expert == 0)
    def _():
        experts_setup(x, att, small, routes, b, gates)
        total[...] = jnp.zeros_like(total)

    w_in, w_out_t = expert_weights(weights)
    u = dot(b[...], w_in, NN)
    active = gelu_parts(u)[0].astype(bf16).astype(f32)
    gated = (gate_of(gates, expert) * active).astype(bf16)
    total[...] += dot(gated, w_out_t, NT)

    @pl.when(expert == EXPERTS - 1)
    def _():
        for block in range(2):
            value = total[ROWS * block : ROWS * block + ROWS].astype(bf16)
            for j, chunk in enumerate(chunks(value)):
                part[block, j] = chunk


def experts_back_kernel(
    with_moe, x, att, small, routes, grad, weights, part, grad_w, b, gates, total, moe, gate_t
):
    expert = pl.program_id(0)

    @pl.when(expert == 0)
    def _():
        experts_setup(x, att, small, routes, b, gates)
        total[...] = jnp.zeros_like(total)
        if with_moe:
            moe[...] = jnp.zeros_like(moe)

    w_in, w_out_t = expert_weights(weights)
    u = dot(b[...], w_in, NN)
    act, t = gelu_parts(u)
    active = act.astype(bf16).astype(f32)
    gate = gate_of(gates, expert)
    gated = (gate * active).astype(bf16)
    if with_moe:
        moe[...] += dot(gated, w_out_t, NT)
    back = dot(grad[...], w_out_t, NN)
    ones = jnp.ones((8, FE), f32)
    gate_t[expert] = dot_exact(ones, back * active, NT)
    grad_u = (gate * back * gelu_slope(u, t)).astype(bf16)
    total[...] += dot(grad_u, w_in, NT)
    grad_w[:, 0] = dot(b[...], grad_u, TN).astype(bf16).reshape(16, 48, FE)
    grad_w[:, 1] = dot(grad[...], gated, TN).astype(bf16).reshape(16, 48, FE)

    @pl.when(expert == EXPERTS - 1)
    def _():
        part[...] = jnp.zeros_like(part)
        for block in range(2):
            value = total[ROWS * block : ROWS * block + ROWS].astype(bf16)
            for j, chunk in enumerate(chunks(value)):
                part[block, j, 0:80] = chunk
            table = jnp.concatenate(
                [gate_t[e, 0:1, ROWS * block : ROWS * block + ROWS] for e in range(EXPERTS)]
                + [jnp.zeros((12, ROWS), f32)],
                axis=0,
            )
            part[block, 0, 80:96, 0:ROWS] = table.astype(bf16)
            if with_moe:
                value = moe[ROWS * block : ROWS * block + ROWS].astype(bf16)
                for j, chunk in enumerate(chunks(value)):
                    part[block, j, 96:176] = chunk


def fixed(shape):
    return pl.BlockSpec(shape, lambda e: (0,) * len(shape))


EXPERT_BLOCK = pl.BlockSpec((16, 2, 48, FE), lambda e: (0, e, 0, 0))


def experts_forward(x, att, small, routes, weights):
    args = (x, att, small, routes)
    return pl.pallas_call(
        experts_kernel,
        grid=(EXPERTS,),
        out_shape=jax.ShapeDtypeStruct((2, 4, 80, 384), bf16),
        in_specs=[fixed(a.shape) for a in args] + [EXPERT_BLOCK],
        out_specs=fixed((2, 4, 80, 384)),
        scratch_shapes=[
            pltpu.VMEM((PAIR, D), bf16),
            pltpu.VMEM((PAIR, EXPERTS), f32),
            pltpu.VMEM((PAIR, D), f32),
        ],
        compiler_params=compute_params(),
        name="experts_forward",
    )(*args, weights)


def experts_backward(x, att, small, routes, grad, weights, with_moe):
    args = (x, att, small, routes, grad)
    rows = 176 if with_moe else 96
    return pl.pallas_call(
        functools.partial(experts_back_kernel, with_moe),
        grid=(EXPERTS,),
        out_shape=[
            jax.ShapeDtypeStruct((2, 4, rows, 384), bf16),
            jax.ShapeDtypeStruct((16, 2 * EXPERTS, 48, FE), bf16),
        ],
        in_specs=[fixed(a.shape) for a in args] + [EXPERT_BLOCK],
        out_specs=[fixed((2, 4, rows, 384)), EXPERT_BLOCK],
        scratch_shapes=[
            pltpu.VMEM((PAIR, D), bf16),
            pltpu.VMEM((PAIR, EXPERTS), f32),
            pltpu.VMEM((PAIR, D), f32),
            pltpu.VMEM((PAIR, D), f32),
            pltpu.VMEM((EXPERTS, 8, PAIR), f32),
        ],
        compiler_params=compute_params(),
        name="experts_backward",
    )(*args, weights)


def attend_back_kernel(
    core, x, att, small, routes_t, grad, back, q, kv, mixed, dead, w_out_t,
    grad_h, grad_q, grad_kv, grad_w_out, grad_small,
):
    unit, scale = norm_parts(x[...].astype(f32) + pair_rows(att))
    b = (unit * small[1:2] + small[3:4]).astype(bf16)
    router = small[4:8]
    probs = softmax(dot(router.astype(bf16), b, NT), 0)
    ids = lax.broadcasted_iota(jnp.int32, (EXPERTS, PAIR), 0).astype(f32)
    named = (routes_t[0:1] == ids) | (routes_t[1:2] == ids)
    tables = [back[block, 0, 80:96, 0:ROWS].astype(f32)[0:EXPERTS] for block in range(2)]
    gate_grads = jnp.where(named, jnp.concatenate(tables, axis=1), 0.0)
    grad_logits = probs * (gate_grads - jnp.sum(probs * gate_grads, axis=0, keepdims=True))
    grad_b = pair_rows(back) + dot_exact(grad_logits, router, TN)
    grad_h[...] = grad[...].astype(f32) + norm_back(grad_b, unit, scale, small[1:2])
    first = core[0] == 0
    lanes = lax.broadcasted_iota(jnp.int32, (EXPERTS, PAIR), 1)
    own_t = (lanes < ROWS) == first
    lines = lax.broadcasted_iota(jnp.int32, (PAIR, 1), 0)
    own = (lines < ROWS) == first
    kept = jnp.where(own, grad_b, 0.0)
    grad_small[0:1] = jnp.sum(kept * unit, axis=0, keepdims=True)
    grad_small[1:2] = jnp.sum(kept, axis=0, keepdims=True)
    grad_small[2:4] = jnp.zeros((2, D), f32)
    grad_small[4:8] = dot_exact(jnp.where(own_t, grad_logits, 0.0), b.astype(f32), NN)
    at = pl.ds(pl.multiple_of(core[0] * ROWS, ROWS), ROWS)
    grad_att = grad_h[at].astype(bf16)
    grad_w_out[...] = dot(grad_att, mixed[...], TN).astype(bf16)
    grad_mixed = dot(grad_att, w_out_t[...], NN).astype(bf16)
    width = HEADS * HD
    keys = kv[...].reshape(KEYS, 2 * width)
    queries = q[...]
    q_parts, k_parts, v_parts = [], [], []
    for h in range(HEADS):
        q_h, k_h, v_h, g_h = head(queries, h), head(keys, h), head(keys, HEADS + h), head(grad_mixed, h)
        weights = softmax(HD**-0.5 * dot(q_h, k_h, NT) + dead[...], -1)
        v_parts.append(dot(weights.astype(bf16), g_h, TN))
        grad_weights = dot(g_h, v_h, NT)
        grad_scores = weights * (
            grad_weights - jnp.sum(weights * grad_weights, axis=-1, keepdims=True)
        )
        grad_scores = grad_scores.astype(bf16)
        q_parts.append(HD**-0.5 * dot(grad_scores, k_h, NN))
        k_parts.append(HD**-0.5 * dot(grad_scores, q_h, TN))
    grad_q[...] = jnp.concatenate(q_parts, axis=1).astype(bf16)
    total = jnp.concatenate(k_parts + v_parts, axis=1).astype(bf16)
    grad_kv[...] = total.reshape(4, ROWS, 2 * width)


def project_back_kernel(core, x, small, grad_q, grad_kv, w_qkv, part, grad_w):
    rows = x[pl.ds(pl.multiple_of(core[0] * ROWS, ROWS), ROWS)].astype(f32)
    unit, _ = norm_parts(rows)
    normed = (unit * small[0:1] + small[2:3]).astype(bf16)
    grads = jnp.concatenate([grad_q[...], grad_kv[...]], axis=1)
    grad_w[...] = dot(normed, grads, TN).astype(bf16)
    value = dot(grads, w_qkv[...], NT).astype(bf16)
    for j, chunk in enumerate(chunks(value)):
        part[0, j] = chunk


def tokens_back_kernel(core, x, small, grad_h, back, grad_x, grad_small):
    unit, scale = norm_parts(x[...].astype(f32))
    grad_a = pair_rows(back)
    grad_x[...] = (grad_h[...] + norm_back(grad_a, unit, scale, small[0:1])).astype(bf16)
    lines = lax.broadcasted_iota(jnp.int32, (PAIR, 1), 0)
    own = (lines < ROWS) == (core[0] == 0)
    kept = jnp.where(own, grad_a, 0.0)
    grad_small[0:1] = jnp.sum(kept * unit, axis=0, keepdims=True)
    grad_small[1:2] = jnp.sum(kept, axis=0, keepdims=True)
    grad_small[2:8] = jnp.zeros((6, D), f32)


def layer_back(core, x, att, small, routes, grad, saved, dead, w_qkv, w_out_t, weights, with_moe, cid):
    q, kv, mixed = saved
    part, grad_experts = experts_backward(x, att, small, routes, grad, weights, with_moe)
    back = reduce_rows(part, cid)
    grad_h, grad_q, grad_kv, grad_w_out, small_two = call(
        attend_back_kernel,
        [
            ((PAIR, D), f32),
            ((ROWS, 192), bf16),
            ((4, ROWS, 384), bf16),
            ((D, 192), bf16),
            ((8, D), f32),
        ],
        core, x, att, small, routes.T, grad, back, q, kv, mixed, dead, w_out_t,
        name="attend_back",
    )
    grad_kv = scatter_kv(grad_kv)
    part, grad_w_qkv = call(
        project_back_kernel,
        [((1, 4, 80, 384), bf16), ((D, 576), bf16)],
        core, x, small, grad_q, grad_kv, w_qkv,
        name="project_back",
    )
    back_one = reduce_rows(part, 2)
    grad_x, small_one = call(
        tokens_back_kernel,
        [((PAIR, D), bf16), ((8, D), f32)],
        core, x, small, grad_h, back_one,
        name="tokens_back",
    )
    grad_small = jnp.stack(
        [small_one[0], small_two[0], small_one[1], small_two[1]], axis=0
    )
    grad_small = jnp.concatenate([grad_small, small_two[4:8]], axis=0)
    grad_attn = jnp.concatenate([grad_w_qkv, grad_w_out], axis=1).reshape(32, 24, D)
    grad_small = grad_small.reshape(8, 32, 24).transpose(1, 0, 2).astype(bf16)
    grad_small = jnp.pad(grad_small, ((0, 0), (0, 0), (0, D - 24)))
    grad_pack = jnp.concatenate([grad_attn, grad_small], axis=1)
    return grad_x, grad_experts, grad_pack, back


def shards(boundary, routes, lengths, ln_gains, ln_biases, w_qkv, w_out, w_router, w_in, w_exp_out):
    core = lax.axis_index("core")
    high = lax.axis_index("x") // 2
    core_ref = core.astype(jnp.int32).reshape(1)

    turned = jnp.pad(
        routes[0].astype(bf16).transpose(0, 2, 1), ((0, 0), (0, 14), (0, D - ROWS))
    )
    images = jnp.concatenate([boundary[0], turned], axis=1)
    stacked = jnp.stack([w_in, w_exp_out.transpose(0, 1, 3, 2)], axis=2).reshape(384, 2, FE)
    own_half = lax.dynamic_index_in_dim(stacked, core, 1, keepdims=False)
    other_half = lax.dynamic_index_in_dim(stacked, 1 - core, 1, keepdims=False)
    got_images, got_half = start_exchange(images, other_half)
    low_half = jnp.where(core == 0, own_half, got_half).reshape(2, 8, 24, FE)
    high_half = jnp.where(core == 0, got_half, own_half).reshape(2, 8, 24, FE)
    chip_shard = jnp.concatenate([low_half, high_half], axis=2).reshape(2, 384, FE)
    experts = [
        lax.all_gather(chip_shard[layer], CHIPS, axis=0).reshape(16, 8, 48, FE)
        for layer in range(2)
    ]

    attn = jnp.concatenate([w_qkv.reshape(2, 24, 576), w_out.transpose(0, 2, 1)], axis=2)
    tiny = jnp.concatenate([ln_gains, ln_biases, w_router.transpose(0, 2, 1)], axis=1)
    tiny = jnp.pad(tiny, ((0, 0), (0, 0), (0, D - 24)))
    pack = jnp.concatenate([attn, tiny], axis=1).reshape(64, D)
    packs = gather_small(pack).reshape(32, 2, 32, D)
    w_qkvs, w_outs, smalls = [], [], []
    for layer in range(2):
        both = packs[:, layer, 0:24].reshape(D, D)
        w_qkvs.append(both[:, :576])
        w_outs.append(both[:, 576:])
        smalls.append(
            packs[:, layer, 24:32, 0:24].transpose(1, 0, 2).reshape(8, D).astype(f32)
        )

    live = jnp.arange(ROWS, dtype=jnp.int32)[None, :] < lengths[:, None]
    dead = jnp.where(live.reshape(1, KEYS), 0.0, -1e30).astype(f32)
    chip_live = lax.dynamic_slice_in_dim(live, 2 * lax.axis_index("zl"), 2, 0)
    own_live = lax.dynamic_index_in_dim(chip_live, core, 0, keepdims=False)

    x0 = got_images[:, 0, 0:ROWS].reshape(PAIR, D)
    cotangent = jnp.where(chip_live[:, :, None], got_images[:, 1, 0:ROWS], 0).reshape(PAIR, D)
    route_cols = [
        got_images[:, kind, ROWS : ROWS + 2, 0:ROWS].transpose(0, 2, 1).reshape(PAIR, 2).astype(f32)
        for kind in range(2)
    ]

    q0, kv0 = call(
        first_kernel, [((ROWS, 192), bf16), ((ROWS, 384), bf16)],
        core_ref, x0, smalls[0], w_qkvs[0], name="first_project",
    )
    kv0 = gather_kv(kv0)
    part, mixed0 = call(
        attend_kernel, [((1, 4, 80, 384), bf16), ((ROWS, 192), bf16)],
        q0, kv0, dead, w_outs[0], name="attend",
    )
    att0 = reduce_rows(part, 2)
    part = experts_forward(x0, att0, smalls[0], route_cols[0], experts[0])
    moe0 = reduce_rows(part, 3)

    q1, kv1, x1 = call(
        next_kernel, [((ROWS, 192), bf16), ((ROWS, 384), bf16), ((PAIR, D), bf16)],
        core_ref, x0, att0, moe0, smalls[1], w_qkvs[1], name="next_project",
    )
    kv1 = gather_kv(kv1)
    part, mixed1 = call(
        attend_kernel, [((1, 4, 80, 384), bf16), ((ROWS, 192), bf16)],
        q1, kv1, dead, w_outs[1], name="attend",
    )
    att1 = reduce_rows(part, 2)

    grad_x1, grad_experts1, grad_pack1, back1 = layer_back(
        core_ref, x1, att1, smalls[1], route_cols[1], cotangent, (q1, kv1, mixed1), dead,
        w_qkvs[1], w_outs[1], experts[1], True, 4,
    )
    grad_x0, grad_experts0, grad_pack0, _ = layer_back(
        core_ref, x0, att0, smalls[0], route_cols[0], grad_x1, (q0, kv0, mixed0), dead,
        w_qkvs[0], w_outs[0], experts[0], False, 8,
    )

    def own_block(value):
        return lax.dynamic_index_in_dim(value, core, 0, keepdims=False)

    def unchunk(value):
        return value.reshape(2, 2, 80, 384).transpose(0, 2, 1, 3).reshape(ROWS, D).astype(f32)

    y1 = (
        own_block(x1.reshape(2, ROWS, D)).astype(f32)
        + unchunk(own_block(att1))
        + unchunk(own_block(back1)[:, 96:176])
    )
    mine = jnp.stack([own_block(grad_x0.reshape(2, ROWS, D)).astype(f32), y1])
    mine = jnp.where(own_live[None, :, None], mine, 0.0)
    kept = lax.dynamic_index_in_dim(mine, high, 0, keepdims=False)
    sent = lax.dynamic_index_in_dim(mine, 1 - high, 0, keepdims=False).astype(bf16)
    landed = lax.ppermute(sent, "x", [(i, (i + 2) % 4) for i in range(4)]).astype(f32)
    ends = jnp.where(high == 0, jnp.stack([kept, landed]), jnp.stack([landed, kept]))

    sums = [
        lax.psum_scatter(g.reshape(16, 384, FE), CHIPS, scatter_dimension=0)
        for g in (grad_experts0, grad_experts1)
    ]
    sums = jnp.stack(sums).reshape(16, 2, 24, FE)
    own_sum = lax.dynamic_index_in_dim(sums, core, 1, keepdims=False)
    other_sum = lax.dynamic_index_in_dim(sums, 1 - core, 1, keepdims=False).reshape(384, FE)
    got_sum = lax.ppermute(other_sum, "core", [(0, 1), (1, 0)]).reshape(16, 24, FE)
    first = jnp.where(core == 0, own_sum, got_sum)
    second = jnp.where(core == 0, got_sum, own_sum)
    full = jnp.concatenate([first, second], axis=2).reshape(2, EXPERTS, 2, 24, D).astype(f32)
    grad_w_in = full[:, :, 0]
    grad_w_exp_out = full[:, :, 1].transpose(0, 1, 3, 2)

    packs = jnp.stack([grad_pack0, grad_pack1], axis=1).reshape(16, 2, 64, D)
    own = scatter_small(packs.transpose(1, 0, 2, 3)).reshape(2, 32, D)
    grad_w_qkv = own[:, 0:24, :576].reshape(2, 24, 3, 192)
    grad_w_out = own[:, 0:24, 576:].transpose(0, 2, 1)
    tiny = own[:, 24:32, 0:24]
    return (
        ends[None],
        tiny[:, 0:2],
        tiny[:, 2:4],
        grad_w_qkv,
        grad_w_out,
        tiny[:, 4:8].transpose(0, 2, 1),
        grad_w_in,
        grad_w_exp_out,
    )


def solution(mesh):
    fine = Mesh(mesh.devices.reshape(4, 2, 2, 2, 4), CHIPS + ("core", "tp"))
    section, ctx = ("x", "zh"), ("zl", "core")
    every = section + ctx
    return jax.shard_map(
        shards,
        mesh=fine,
        in_specs=(
            P(ctx, section, None, None),
            P(ctx, section, None, None),
            P(),
            P(None, None, every),
            P(None, None, every),
            P(None, every, None, "tp"),
            P(None, "tp", every),
            P(None, every, None),
            P(None, None, every, "tp"),
            P(None, None, "tp", every),
        ),
        out_specs=(
            P(ctx, section, None, None),
            P(None, None, every),
            P(None, None, every),
            P(None, every, None, "tp"),
            P(None, "tp", every),
            P(None, every, None),
            P(None, None, every, "tp"),
            P(None, None, "tp", every),
        ),
        check_vma=False,
    )
```

```python
import functools

import jax
import jax.numpy as jnp
from jax import lax
from jax.experimental import pallas as pl
from jax.experimental.pallas import tpu as pltpu
from jax.sharding import Mesh
from jax.sharding import PartitionSpec as P

D = 768
HD = 64
HEADS = 3
ROWS = 160
PAIR = 320
KEYS = 640
FE = 384
EXPERTS = 4
EPS = 1e-06
WIDTH = HEADS * HD
MESH = pl.DeviceIdType.MESH
CHIPS = ("x", "zh", "zl")
f32, bf16 = jnp.float32, jnp.bfloat16
VMEM = pl.BlockSpec(memory_space=pltpu.VMEM)
SMEM = pl.BlockSpec(memory_space=pltpu.SMEM)
NN = (((1,), (0,)), ((), ()))
NT = (((1,), (1,)), ((), ()))
TN = (((0,), (0,)), ((), ()))


def dot(a, b, dims):
    return lax.dot_general(a, b, dims, preferred_element_type=f32)


def dot_exact(a, b, dims):
    return lax.dot_general(
        a, b, dims, preferred_element_type=f32, precision=lax.Precision.HIGHEST
    )


def params(cid, mib):
    return pltpu.CompilerParams(
        collective_id=cid, has_side_effects=True, vmem_limit_bytes=mib * 2**20
    )


def arrive(peers):
    barrier = pltpu.get_barrier_semaphore()
    for peer in peers:
        pl.semaphore_signal(barrier, inc=1, device_id=peer, device_id_type=MESH)


def all_here(count):
    pl.semaphore_wait(pltpu.get_barrier_semaphore(), count)


def dma_sems(*counts):
    return [pltpu.SemaphoreType.DMA((count,)) for count in counts for _ in range(2)]


def remote(src, dst, send, recv, peer):
    return pltpu.make_async_remote_copy(
        src_ref=src, dst_ref=dst, send_sem=send, recv_sem=recv, device_id=peer, device_id_type=MESH
    )


def sum_peers(both):
    core, tp = lax.axis_index("core"), lax.axis_index("tp")
    offsets = [(k // 4, k % 4) for k in range(1, 8 if both else 4)]
    return [{"core": (core + dc) % 2, "tp": (tp + dt) % 4} for dc, dt in offsets]


def sum_terms(both, part, landed, send, recv):
    return [
        remote(part.at[peer["core"] if both else 0, peer["tp"]], landed.at[k], send.at[k], recv.at[k], peer)
        for k, peer in enumerate(sum_peers(both))
    ]


def sum_results(out, send, recv):
    core, tp = lax.axis_index("core"), lax.axis_index("tp")
    return [
        remote(out.at[core, tp], out.at[core, tp], send.at[k], recv.at[k], {"tp": (tp + k + 1) % 4})
        for k in range(3)
    ]


def sum_cross(out, send, recv):
    core, tp = lax.axis_index("core"), lax.axis_index("tp")
    return [
        remote(out.at[core, at], out.at[core, at], send.at[k], recv.at[k], {"core": 1 - core})
        for k, at in enumerate([(tp + 4 - k) % 4 for k in range(4)])
    ]


def sum_start(both, part, out, landed, rs, rr, gs, gr, cs, cr):
    for copy in sum_terms(both, part, landed, rs, rr):
        copy.start()


def sum_middle(both, part, out, landed, rs, rr, gs, gr, cs, cr):
    core, tp = lax.axis_index("core"), lax.axis_index("tp")
    total = part[core if both else 0, tp].astype(f32)
    for k, copy in enumerate(sum_terms(both, part, landed, rs, rr)):
        copy.wait_recv()
        total = total + landed[k].astype(f32)
    out[core, tp] = total.astype(bf16)
    for copy in sum_results(out, gs, gr):
        copy.start()


def sum_end(both, part, out, landed, rs, rr, gs, gr, cs, cr):
    gathers, crosses = sum_results(out, gs, gr), sum_cross(out, cs, cr)
    for k in range(4):
        if k > 0:
            gathers[k - 1].wait_recv()
        crosses[k].start()
    for copy in crosses:
        copy.wait()
    for copy in sum_terms(both, part, landed, rs, rr) + gathers:
        copy.wait_send()


def sum_scratch(both, rows):
    count = 7 if both else 3
    return [
        pltpu.VMEM((2 if both else 1, 4, rows, 384), bf16),
        pltpu.VMEM((count, rows, 384), bf16),
    ] + dma_sems(count, 3, 4)


def ctx_peers():
    core, zl = lax.axis_index("core"), lax.axis_index("zl")
    return [
        {"zl": (zl + k // 2) % 2, "core": (core + k % 2) % 2} for k in range(1, 4)
    ], zl * 2 + core


def chip_peer(k):
    x, zh, zl = (lax.axis_index(a) for a in CHIPS)
    dx, dh, dl = k // 4, (k // 2) % 2, k % 2
    ahead = ((x + dx) % 4, (zh + dh) % 2, (zl + dl) % 2)
    back = ((x + 4 - dx) % 4, (zh + 2 - dh) % 2, (zl + 2 - dl) % 2)
    return dict(zip(CHIPS, ahead)), *(c[0] * 4 + c[1] * 2 + c[2] for c in (ahead, back))


def cross_kernel(own, out, send, recv):
    other = {"core": 1 - lax.axis_index("core")}
    arrive([other])
    all_here(1)
    copy = remote(own, out, send.at[0], recv.at[0], other)
    copy.start()
    copy.wait()


def cross(own, cid):
    return pl.pallas_call(
        cross_kernel,
        out_shape=jax.ShapeDtypeStruct(own.shape, own.dtype),
        in_specs=[VMEM],
        out_specs=VMEM,
        scratch_shapes=dma_sems(1),
        compiler_params=params(cid, 8),
        name="cross",
    )(own)


def start_kernel(images, own, out_images, out, im_send, im_recv, send, recv, cx_send, cx_recv):
    core, x = lax.axis_index("core"), lax.axis_index("x")
    high = x // 2
    other = {"core": 1 - core}
    _, me, _ = chip_peer(0)
    arrive([chip_peer(k)[0] for k in range(1, 16)] + [other])
    out[me, core] = own[...]
    out_images[core, high] = images[high]
    all_here(16)

    def push(k):
        peer, _, _ = chip_peer(k)
        return remote(own, out.at[me, core], send.at[k], recv.at[k], peer)

    def pass_on(k):
        _, _, at = chip_peer(k)
        return remote(out.at[at, core], out.at[at, core], cx_send.at[k], cx_recv.at[k], other)

    swap = remote(
        images.at[1 - high], out_images.at[core, high], im_send.at[0], im_recv.at[0], {"x": (x + 2) % 4}
    )
    kept = remote(images.at[high], out_images.at[core, high], im_send.at[1], im_recv.at[1], other)
    swap.start()

    def first(k, carry):
        push(k).start()
        return carry

    def onward(k, carry):
        push(k).wait_recv()
        pass_on(k).start()
        return carry

    def last(k, carry):
        push(k).wait_send()
        pass_on(k).wait()
        return carry

    lax.fori_loop(1, 16, first, 0)
    kept.start()
    pass_on(0).start()
    swap.wait_recv()
    passed = remote(
        out_images.at[core, 1 - high], out_images.at[core, 1 - high], im_send.at[2], im_recv.at[2], other
    )
    passed.start()
    lax.fori_loop(1, 16, onward, 0)
    pass_on(0).wait()
    lax.fori_loop(1, 16, last, 0)
    for copy in (kept, passed):
        copy.wait()
    swap.wait_send()


def start_exchange(images, own):
    return pl.pallas_call(
        start_kernel,
        out_shape=(
            jax.ShapeDtypeStruct((2,) + images.shape, bf16),
            jax.ShapeDtypeStruct((16, 2) + own.shape, bf16),
        ),
        in_specs=[VMEM, VMEM],
        out_specs=(VMEM, VMEM),
        scratch_shapes=dma_sems(3, 16, 16),
        compiler_params=params(1, 56),
        name="start_exchange",
    )(images, own)


def end_kernel(
    part, image, half, out, out_image, out_half, landed, sums, pieces, cx_s, cx_r, send, recv
):
    core, x = lax.axis_index("core"), lax.axis_index("x")
    other = {"core": 1 - core}
    _, me, _ = chip_peer(0)
    arrive([chip_peer(k)[0] for k in range(1, 16)] + [other])
    all_here(16)
    crossing = remote(part.at[1 - core], landed, cx_s.at[0], cx_r.at[0], other)
    crossing.start()
    swap = remote(image, out_image, cx_s.at[1], cx_r.at[1], {"x": (x + 2) % 4})
    swap.start()
    halves = remote(half, out_half, cx_s.at[2], cx_r.at[2], other)
    halves.start()
    crossing.wait()

    def push(k):
        peer, at, _ = chip_peer(k)
        return remote(sums.at[at], pieces.at[k], send.at[k], recv.at[k], peer)

    def add(k, carry):
        _, at, _ = chip_peer(k)
        sums[at] = (part[core, at].astype(f32) + landed[at].astype(f32)).astype(bf16)
        push(k).start()
        return carry

    def collect(k, carry):
        push(k).wait_recv()
        out[...] += pieces[k].astype(f32)
        return carry

    def last(k, carry):
        push(k).wait_send()
        return carry

    lax.fori_loop(1, 16, add, 0)
    out[...] = part[core, me].astype(f32) + landed[me].astype(f32)
    lax.fori_loop(1, 16, collect, 0)
    lax.fori_loop(1, 16, last, 0)
    swap.wait()
    halves.wait()


def end_exchange(part, image, half):
    shape = part.shape[2:]
    return pl.pallas_call(
        end_kernel,
        out_shape=(
            jax.ShapeDtypeStruct(shape, f32),
            jax.ShapeDtypeStruct(image.shape, bf16),
            jax.ShapeDtypeStruct(half.shape, bf16),
        ),
        in_specs=[VMEM] * 3,
        out_specs=(VMEM,) * 3,
        scratch_shapes=[pltpu.VMEM((16,) + shape, bf16)] * 3 + dma_sems(3, 16),
        compiler_params=params(2, 56),
        name="end_exchange",
    )(part, image, half)


def block_rows(ref, block):
    top = jnp.concatenate([ref[block, 0, 0:80], ref[block, 1, 0:80]], axis=1)
    low = jnp.concatenate([ref[block, 2, 0:80], ref[block, 3, 0:80]], axis=1)
    return jnp.concatenate([top, low], axis=0).astype(f32)


def pair_rows(ref):
    return jnp.concatenate([block_rows(ref, 0), block_rows(ref, 1)], axis=0)


def put_chunks(ref, block, value, first=0):
    for j in range(4):
        r, c = 80 * (j // 2), 384 * (j % 2)
        ref[block, j, first : first + 80] = value[r : r + 80, c : c + 384]


def norm_parts(rows):
    centered = rows - jnp.mean(rows, axis=-1, keepdims=True)
    scale = lax.rsqrt(jnp.mean(centered * centered, axis=-1, keepdims=True) + EPS)
    return centered * scale, scale


def norm_back(grad, unit, scale, gain):
    inner = grad * gain
    return scale * (
        inner
        - jnp.mean(inner, axis=-1, keepdims=True)
        - unit * jnp.mean(inner * unit, axis=-1, keepdims=True)
    )


def softmax(logits, axis):
    top = jnp.max(logits, axis=axis, keepdims=True)
    powers = jnp.exp(logits - top)
    return powers / jnp.sum(powers, axis=axis, keepdims=True)


def own_rows(core):
    return pl.ds(pl.multiple_of(core * ROWS, ROWS), ROWS)


def head(value, h):
    return value[:, HD * h : HD * h + HD]


def gelu_parts(u):
    c = 0.7978845608028654
    t = jnp.tanh(c * (u + 0.044715 * u * u * u))
    return 0.5 * u * (1.0 + t), t


def gelu_slope(u, t):
    c = 0.7978845608028654
    return 0.5 * (1.0 + t) + 0.5 * u * (1.0 - t * t) * (c * (1.0 + 3 * 0.044715 * u * u))


def attend_forward_kernel(follows, *refs):
    if follows:
        x, att_before, moe_before, small, w_kv, w_qo, dead, q, kv, mixed, att, x_next, *scratch = refs
    else:
        x, small, w_kv, w_qo, dead, q, kv, mixed, att, *scratch = refs
    part, landed, *sems, kv_send, kv_recv = scratch
    sums = (False, part, att, landed, *sems)
    core = lax.axis_index("core")
    peers, me = ctx_peers()
    arrive(peers + sum_peers(False))
    if follows:
        x_next[...] = (x[...].astype(f32) + pair_rows(att_before) + pair_rows(moe_before)).astype(bf16)
        x = x_next
    unit, _ = norm_parts(x[own_rows(core)].astype(f32))
    normed = (unit * small[0:1] + small[2:3]).astype(bf16)
    kv[me] = dot(normed, w_kv[...], NN).astype(bf16)
    all_here(6)
    copies = [
        remote(kv.at[me], kv.at[me], kv_send.at[k], kv_recv.at[k], peer)
        for k, peer in enumerate(peers)
    ]
    for copy in copies:
        copy.start()
    queries = dot(normed, w_qo[:, :WIDTH], NN).astype(bf16)
    q[...] = queries
    for copy in copies:
        copy.wait_recv()
    keys = kv[...].reshape(KEYS, 2 * WIDTH)
    outs = []
    for h in range(HEADS):
        scores = HD**-0.5 * dot(head(queries, h), head(keys, h), NT) + dead[...]
        probs = softmax(scores, -1).astype(bf16)
        outs.append(dot(probs, head(keys, HEADS + h), NN))
    heads = jnp.concatenate(outs, axis=1).astype(bf16)
    mixed[...] = heads
    put_chunks(part, 0, dot(heads, w_qo[:, WIDTH:], NT).astype(bf16))
    sum_start(*sums)
    sum_middle(*sums)
    sum_end(*sums)
    for copy in copies:
        copy.wait_send()


def attend_forward(x, before, small, w_kv, w_qo, dead, cid):
    args = (x, *before, small, w_kv, w_qo, dead)
    shapes = [(ROWS, WIDTH), (4, ROWS, 2 * WIDTH), (ROWS, WIDTH), (2, 4, 80, 384)]
    if before:
        shapes.append((PAIR, D))
    return pl.pallas_call(
        functools.partial(attend_forward_kernel, bool(before)),
        out_shape=[jax.ShapeDtypeStruct(s, bf16) for s in shapes],
        in_specs=[VMEM] * len(args),
        out_specs=[VMEM] * len(shapes),
        scratch_shapes=sum_scratch(False, 80) + dma_sems(3),
        compiler_params=params(cid, 56),
        name="attend_forward",
    )(*args)


def expert_weights(weights):
    block = weights[...]
    return block[:, 0:48].reshape(D, FE), block[:, 48:96].reshape(D, FE)


def experts_setup(x, att, small, routes, b, gates):
    unit, _ = norm_parts(x[...].astype(f32) + pair_rows(att))
    b[...] = (unit * small[1:2] + small[3:4]).astype(bf16)
    probs = softmax(dot(b[...], small[4:8].astype(bf16), NT), -1)
    ids = lax.broadcasted_iota(jnp.int32, (PAIR, EXPERTS), 1).astype(f32)
    named = (routes[:, 0:1] == ids) | (routes[:, 1:2] == ids)
    gates[...] = jnp.where(named, probs, 0.0)


def gate_of(gates, expert):
    ids = lax.broadcasted_iota(jnp.int32, (PAIR, EXPERTS), 1)
    return jnp.sum(jnp.where(ids == expert, gates[...], 0.0), axis=1, keepdims=True)


def experts_forward_kernel(
    x, att, small, routes, weights, result, b, gates, total, out, part, landed, *sems
):
    expert = pl.program_id(0)
    sums = (True, part, out, landed, *sems)

    @pl.when(expert == 0)
    def _():
        arrive(sum_peers(True))
        experts_setup(x, att, small, routes, b, gates)
        total[...] = jnp.zeros_like(total)

    w_in, w_out_t = expert_weights(weights)
    u = dot(b[...], w_in, NN)
    active = gelu_parts(u)[0].astype(bf16).astype(f32)
    gated = (gate_of(gates, expert) * active).astype(bf16)
    total[...] += dot(gated, w_out_t, NT)

    @pl.when(expert == EXPERTS - 1)
    def _():
        for block in range(2):
            put_chunks(part, block, total[ROWS * block : ROWS * block + ROWS].astype(bf16))
        all_here(7)
        sum_start(*sums)
        sum_middle(*sums)
        sum_end(*sums)
        result[...] = out[...]


def fixed(shape):
    return pl.BlockSpec(shape, lambda e: (0,) * len(shape))


def experts_forward(x, att, small, routes, weights, cid):
    args = (x, att, small, routes)
    return pl.pallas_call(
        experts_forward_kernel,
        grid=(EXPERTS,),
        out_shape=jax.ShapeDtypeStruct((2, 4, 80, 384), bf16),
        in_specs=[fixed(a.shape) for a in args] + [pl.BlockSpec((16, 96, FE), lambda e: (0, e, 0))],
        out_specs=fixed((2, 4, 80, 384)),
        scratch_shapes=[
            pltpu.VMEM((PAIR, D), bf16),
            pltpu.VMEM((PAIR, EXPERTS), f32),
            pltpu.VMEM((PAIR, D), f32),
            pltpu.VMEM((2, 4, 80, 384), bf16),
        ]
        + sum_scratch(True, 80),
        compiler_params=params(cid, 56),
        name="experts_forward",
    )(*args, weights)


def experts_backward_kernel(
    steps, x, att, small, routes, grad, extra, weights, result, moe_part, grad_w,
    b, gates, total, moe, gate_t, gated_all, grad_u_all, out, part, landed, *sems,
):
    step = pl.program_id(0)
    sums = (True, part, out, landed, *sems)
    with_moe = moe_part is not None

    @pl.when(step == 0)
    def _():
        arrive(sum_peers(True))
        experts_setup(x, att, small, routes, b, gates)
        total[...] = jnp.zeros_like(total)
        if with_moe:
            moe[...] = jnp.zeros_like(moe)

    @pl.when(step < EXPERTS)
    def _():
        w_in, w_out_t = expert_weights(weights)
        u = dot(b[...], w_in, NN)
        act, t = gelu_parts(u)
        active = act.astype(bf16).astype(f32)
        gate = gate_of(gates, step)
        gated = (gate * active).astype(bf16)
        gated_all[step] = gated
        if with_moe:
            moe[...] += dot(gated, w_out_t, NT)
        back = dot(grad[...], w_out_t, NN)
        gate_t[step] = dot_exact(jnp.ones((8, FE), f32), back * active, NT)
        grad_u = (gate * back * gelu_slope(u, t)).astype(bf16)
        grad_u_all[step] = grad_u
        total[...] += dot(grad_u, w_in, NT)

    @pl.when(step == EXPERTS - 1)
    def _():
        part[...] = jnp.zeros_like(part)
        for block in range(2):
            lines = slice(ROWS * block, ROWS * block + ROWS)
            put_chunks(part, block, total[lines].astype(bf16))
            table = jnp.concatenate(
                [gate_t[e, 0:1, lines] for e in range(EXPERTS)] + [jnp.zeros((12, ROWS), f32)], axis=0
            )
            part[block, 0, 80:96, 0:ROWS] = table.astype(bf16)
            if with_moe:
                put_chunks(moe_part, block, moe[lines].astype(bf16))
        all_here(7)
        sum_start(*sums)

    @pl.when((step >= EXPERTS) & (step < 2 * EXPERTS))
    def _():
        at = step - EXPERTS
        grad_w[:, 0:48] = dot(b[...], grad_u_all[at], TN).astype(bf16).reshape(16, 48, FE)
        grad_w[:, 48:96] = dot(grad[...], gated_all[at], TN).astype(bf16).reshape(16, 48, FE)

    @pl.when(step == EXPERTS + 1)
    def _():
        sum_middle(*sums)

    if steps > 2 * EXPERTS:

        @pl.when(step == 2 * EXPERTS)
        def _():
            grad_w[:, 0:48] = extra[0].reshape(16, 48, FE)
            grad_w[:, 48:96] = extra[1].reshape(16, 48, FE)

    @pl.when(step == steps - 1)
    def _():
        sum_end(*sums)
        result[...] = out[...]


def experts_backward(x, att, small, routes, grad, extra, weights, first, cid):
    args = (x, att, small, routes, grad)
    steps = 2 * EXPERTS
    shapes = [(2, 4, 96, 384)]
    blocks = [fixed((2, 4, 96, 384))]
    if extra is None:
        shapes.append((2, 4, 80, 384))
        blocks.append(fixed((2, 4, 80, 384)))

        def kernel(*refs):
            experts_backward_kernel(steps, *refs[:5], None, *refs[5:])
    else:
        args, steps = args + (extra,), steps + 1

        def kernel(*refs):
            experts_backward_kernel(steps, *refs[:8], None, *refs[8:])

    grads = steps - EXPERTS
    return pl.pallas_call(
        kernel,
        grid=(steps,),
        out_shape=[jax.ShapeDtypeStruct(s, bf16) for s in shapes + [(16, 96 * grads, FE)]],
        in_specs=[fixed(a.shape) for a in args]
        + [pl.BlockSpec((16, 96, FE), lambda s: (0, first + jnp.minimum(s, EXPERTS - 1), 0))],
        out_specs=blocks + [pl.BlockSpec((16, 96, FE), lambda s: (0, jnp.maximum(s - EXPERTS, 0), 0))],
        scratch_shapes=[
            pltpu.VMEM((PAIR, D), bf16),
            pltpu.VMEM((PAIR, EXPERTS), f32),
            pltpu.VMEM((PAIR, D), f32),
            pltpu.VMEM((PAIR, D), f32),
            pltpu.VMEM((EXPERTS, 8, PAIR), f32),
            pltpu.VMEM((EXPERTS, PAIR, FE), bf16),
            pltpu.VMEM((EXPERTS, PAIR, FE), bf16),
            pltpu.VMEM((2, 4, 96, 384), bf16),
        ]
        + sum_scratch(True, 96),
        compiler_params=params(cid, 56),
        name="experts_backward",
    )(*args, weights)


def attend_backward_kernel(with_moe, *refs):
    x, att, small, routes_t, grad, back, q, kv, mixed, dead, w_kv, w_qo, *refs = refs
    if with_moe:
        moe_part, *refs = refs
    grad_x, grad_small, grad_w, *refs = refs
    if with_moe:
        moe, *refs = refs
    grad_h, both_units, parts, kv_landed, back_one, part, landed, *sems = refs
    if with_moe:
        *sems, moe_landed, ms, mr, ns, nr = sems
    *sems, kv_send, kv_recv = sems
    sums = (False, part, back_one, landed, *sems)
    core, tp = lax.axis_index("core"), lax.axis_index("tp")
    peers, me = ctx_peers()
    arrive(peers + sum_peers(False) + (sum_peers(True)[4:] if with_moe else []))
    unit, scale = norm_parts(x[...].astype(f32) + pair_rows(att))
    b = (unit * small[1:2] + small[3:4]).astype(bf16)
    router = small[4:8]
    probs = softmax(dot(router.astype(bf16), b, NT), 0)
    ids = lax.broadcasted_iota(jnp.int32, (EXPERTS, PAIR), 0).astype(f32)
    named = (routes_t[0:1] == ids) | (routes_t[1:2] == ids)
    tables = [back[block, 0, 80:96, 0:ROWS].astype(f32)[0:EXPERTS] for block in range(2)]
    gate_grads = jnp.where(named, jnp.concatenate(tables, axis=1), 0.0)
    grad_logits = probs * (gate_grads - jnp.sum(probs * gate_grads, axis=0, keepdims=True))
    grad_b = pair_rows(back) + dot_exact(grad_logits, router, TN)
    grad_h[...] = grad[...].astype(f32) + norm_back(grad_b, unit, scale, small[1:2])
    grad_att = grad_h[own_rows(core)].astype(bf16)
    grad_mixed = dot(grad_att, w_qo[:, WIDTH:], NN).astype(bf16)
    keys = kv[...].reshape(KEYS, 2 * WIDTH)
    queries = q[...]
    q_parts, k_parts, v_parts = [], [], []
    for h in range(HEADS):
        q_h, g_h = head(queries, h), head(grad_mixed, h)
        k_h, v_h = head(keys, h), head(keys, HEADS + h)
        weights = softmax(HD**-0.5 * dot(q_h, k_h, NT) + dead[...], -1)
        v_parts.append(dot(weights.astype(bf16), g_h, TN))
        grad_weights = dot(g_h, v_h, NT)
        grad_scores = weights * (
            grad_weights - jnp.sum(weights * grad_weights, axis=-1, keepdims=True)
        )
        grad_scores = grad_scores.astype(bf16)
        q_parts.append(HD**-0.5 * dot(grad_scores, k_h, NN))
        k_parts.append(HD**-0.5 * dot(grad_scores, q_h, TN))
    total = jnp.concatenate(k_parts + v_parts, axis=1).astype(bf16)
    parts[...] = total.reshape(4, ROWS, 2 * WIDTH)
    all_here(9 if with_moe else 6)
    copies = [
        remote(parts.at[peer["zl"] * 2 + peer["core"]], kv_landed.at[k], kv_send.at[k], kv_recv.at[k], peer)
        for k, peer in enumerate(peers)
    ]
    for copy in copies:
        copy.start()
    if with_moe:
        moe_terms = sum_terms(True, moe_part, moe_landed, ms, mr)
        for copy in moe_terms:
            copy.start()
    grad_q = jnp.concatenate(q_parts, axis=1).astype(bf16)
    grad_w[1, :, WIDTH:] = dot(grad_att, mixed[...], TN).astype(bf16)
    lanes = lax.broadcasted_iota(jnp.int32, (EXPERTS, PAIR), 1)
    own_lanes = (lanes < ROWS) == (core == 0)
    own = (lax.broadcasted_iota(jnp.int32, (PAIR, 1), 0) < ROWS) == (core == 0)
    kept = jnp.where(own, grad_b, 0.0)
    grad_small[1:2] = jnp.sum(kept * unit, axis=0, keepdims=True)
    grad_small[3:4] = jnp.sum(kept, axis=0, keepdims=True)
    grad_small[4:8] = dot_exact(jnp.where(own_lanes, grad_logits, 0.0), b.astype(f32), NN)
    unit_one, scale_one = norm_parts(x[...].astype(f32))
    both_units[...] = unit_one
    normed = (both_units[own_rows(core)] * small[0:1] + small[2:3]).astype(bf16)
    grad_kv = parts[me].astype(f32)
    for k, copy in enumerate(copies):
        copy.wait_recv()
        grad_kv = grad_kv + kv_landed[k].astype(f32)
    grad_kv = grad_kv.astype(bf16)
    value = dot(grad_kv, w_kv[...], NT) + dot(grad_q, w_qo[:, :WIDTH], NT)
    put_chunks(part, 0, value.astype(bf16))
    sum_start(*sums)
    grad_w[0] = dot(normed, grad_kv, TN).astype(bf16)
    grad_w[1, :, :WIDTH] = dot(normed, grad_q, TN).astype(bf16)
    sum_middle(*sums)
    if with_moe:
        total = moe_part[core, tp].astype(f32)
        for k, copy in enumerate(moe_terms):
            copy.wait_recv()
            total = total + moe_landed[k].astype(f32)
        moe[tp] = total.astype(bf16)
        moe_results = [
            remote(moe.at[tp], moe.at[tp], ns.at[k], nr.at[k], {"tp": (tp + k + 1) % 4}) for k in range(3)
        ]
        for copy in moe_results:
            copy.start()
    sum_end(*sums)
    grad_a = pair_rows(back_one)
    grad_x[...] = (grad_h[...] + norm_back(grad_a, unit_one, scale_one, small[0:1])).astype(bf16)
    kept = jnp.where(own, grad_a, 0.0)
    grad_small[0:1] = jnp.sum(kept * unit_one, axis=0, keepdims=True)
    grad_small[2:3] = jnp.sum(kept, axis=0, keepdims=True)
    for copy in copies:
        copy.wait_send()
    if with_moe:
        for copy in moe_terms:
            copy.wait_send()
        for copy in moe_results:
            copy.wait()


def attend_backward(args, moe_part, cid):
    with_moe = moe_part is not None
    shapes = [((PAIR, D), bf16), ((8, D), f32), ((2, D, 2 * WIDTH), bf16)]
    scratch = [
        pltpu.VMEM((PAIR, D), f32),
        pltpu.VMEM((PAIR, D), f32),
        pltpu.VMEM((4, ROWS, 2 * WIDTH), bf16),
        pltpu.VMEM((3, ROWS, 2 * WIDTH), bf16),
        pltpu.VMEM((2, 4, 80, 384), bf16),
    ]
    scratch += sum_scratch(False, 80) + dma_sems(3)
    if with_moe:
        args = args + (moe_part,)
        shapes.append(((4, 80, 384), bf16))
        scratch += [pltpu.VMEM((7, 80, 384), bf16)] + dma_sems(7, 3)
    return pl.pallas_call(
        functools.partial(attend_backward_kernel, with_moe),
        out_shape=[jax.ShapeDtypeStruct(*s) for s in shapes],
        in_specs=[VMEM] * len(args),
        out_specs=[VMEM] * len(shapes),
        scratch_shapes=scratch,
        compiler_params=params(cid, 56),
        name="attend_backward",
    )(*args)


def shards(boundary, routes, lengths, ln_gains, ln_biases, w_qkv, w_out, w_router, w_in, w_exp_out):
    core = lax.axis_index("core")
    high = lax.axis_index("x") // 2

    def pick(value, at, axis):
        return lax.dynamic_index_in_dim(value, at, axis, keepdims=False)

    halves = jnp.stack(
        [
            w_qkv[:, :, 1:].reshape(2, 24, 384),
            jnp.concatenate([w_qkv[:, :, 0], w_out.transpose(0, 2, 1)], axis=2),
        ],
        axis=1,
    )

    stacked = jnp.stack([w_in, w_exp_out.transpose(0, 1, 3, 2)], axis=2).reshape(384, 2, FE)
    attn_one = halves[1].reshape(48, 384)
    own_half = jnp.concatenate([pick(stacked, core, 1), attn_one])
    got_half = cross(jnp.concatenate([pick(stacked, 1 - core, 1), attn_one]), 0)
    low_half = jnp.where(core == 0, own_half, got_half).reshape(18, 24, FE)
    high_half = jnp.where(core == 0, got_half, own_half).reshape(18, 24, FE)
    chip = jnp.concatenate([low_half, high_half], axis=1).reshape(864, FE)
    every = lax.all_gather(chip, CHIPS, axis=0)
    experts = [every, every]

    turned = jnp.pad(
        routes[0].astype(bf16).transpose(0, 2, 1), ((0, 0), (0, 14), (0, D - ROWS))
    )
    images = jnp.concatenate([boundary[0], turned], axis=1)
    tiny = jnp.concatenate([ln_gains, ln_biases, w_router.transpose(0, 2, 1)], axis=1)
    tiny = jnp.pad(tiny.transpose(1, 0, 2).reshape(8, 48), ((0, 0), (0, D - 48)))
    pack = jnp.concatenate([jnp.concatenate([halves[0, 0], halves[0, 1]], axis=1), tiny])
    got_images, packs = start_exchange(images, pack)
    packs = packs.reshape(32, 32, D)
    w_kvs, w_qos = [packs[:, 0:24, 0:384].reshape(D, 384)], [packs[:, 0:24, 384:].reshape(D, 384)]
    w_kvs.append(every[:, 768:816].reshape(D, 384))
    w_qos.append(every[:, 816:864].reshape(D, 384))
    tiny = packs[:, 24:32, 0:48].reshape(32, 8, 2, 24).transpose(2, 1, 0, 3).reshape(2, 8, D)
    smalls = [tiny[0].astype(f32), tiny[1].astype(f32)]

    live = jnp.arange(ROWS, dtype=jnp.int32)[None, :] < lengths[:, None]
    dead = jnp.where(live.reshape(1, KEYS), 0.0, -1e30).astype(f32)
    chip_live = lax.dynamic_slice_in_dim(live, 2 * lax.axis_index("zl"), 2, 0)
    own_live = pick(chip_live, core, 0)

    x0 = got_images[:, 0, 0:ROWS].reshape(PAIR, D)
    cotangent = jnp.where(chip_live[:, :, None], got_images[:, 1, 0:ROWS], 0).reshape(PAIR, D)
    route_rows = [
        got_images[:, kind, ROWS : ROWS + 2, 0:ROWS].transpose(1, 0, 2).reshape(2, PAIR).astype(f32)
        for kind in range(2)
    ]
    route_cols = [rows.T for rows in route_rows]

    q0, kv0, mixed0, att0 = attend_forward(x0, (), smalls[0], w_kvs[0], w_qos[0], dead, 3)
    moe0 = experts_forward(x0, att0, smalls[0], route_cols[0], experts[0], 4)
    q1, kv1, mixed1, att1, x1 = attend_forward(
        x0, (att0, moe0), smalls[1], w_kvs[1], w_qos[1], dead, 5
    )
    back, moe_part, grad_experts1 = experts_backward(
        x1, att1, smalls[1], route_cols[1], cotangent, None, experts[1], EXPERTS, 6
    )
    sums1 = lax.psum_scatter(grad_experts1, CHIPS, scatter_dimension=0).reshape(8, 48, FE)
    grad_x1, grad_small1, grad_attn1, moe1 = attend_backward(
        (x1, att1, smalls[1], route_rows[1], cotangent, back, q1, kv1, mixed1, dead, w_kvs[1], w_qos[1]),
        moe_part,
        7,
    )
    back, grad_experts0 = experts_backward(
        x0, att0, smalls[0], route_cols[0], grad_x1, grad_attn1, experts[0], 0, 8
    )
    sums0 = lax.psum_scatter(grad_experts0, CHIPS, scatter_dimension=0).reshape(10, 48, FE)
    grad_x0, grad_small0, grad_attn0 = attend_backward(
        (x0, att0, smalls[0], route_rows[0], grad_x1, back, q0, kv0, mixed0, dead, w_kvs[0], w_qos[0]),
        None,
        9,
    )

    def own_block(value):
        return pick(value, core, 0)

    def unchunk(value):
        return value.reshape(2, 2, 80, 384).transpose(0, 2, 1, 3).reshape(ROWS, D).astype(f32)

    y1 = own_block(x1.reshape(2, ROWS, D)).astype(f32) + unchunk(own_block(att1)) + unchunk(moe1)
    mine = jnp.stack([own_block(grad_x0.reshape(2, ROWS, D)).astype(f32), y1])
    mine = jnp.where(own_live[None, :, None], mine, 0.0)
    kept, sent = pick(mine, high, 0), pick(mine, 1 - high, 0).astype(bf16)

    tiny = jnp.stack([grad_small0, grad_small1], axis=1).astype(bf16).reshape(8, 2, 16, 2, 24)
    tiny = tiny.transpose(3, 2, 0, 1, 4).reshape(2, 16, 8, 48)
    tiny = jnp.pad(tiny, ((0, 0), (0, 0), (0, 0), (0, D - 48)))
    packs = grad_attn0.reshape(2, 16, 2, 24, 384).transpose(2, 1, 3, 0, 4).reshape(2, 16, 24, D)
    packs = jnp.concatenate([packs, tiny], axis=2)

    def by_core(sums, at):
        return lax.dynamic_slice_in_dim(sums, 24 * at, 24, 1)

    own, landed, got1 = end_exchange(packs, sent, by_core(sums1, 1 - core).reshape(192, FE))
    landed = landed.astype(f32)
    ends = jnp.where(high == 0, jnp.stack([kept, landed]), jnp.stack([landed, kept]))
    got0 = cross(by_core(sums0, 1 - core).reshape(240, FE), 10).reshape(10, 24, FE)
    own0 = by_core(sums0, core)
    attn1 = own0[8:10].astype(f32) + got0[8:10].astype(f32)

    def both_halves(own_sum, got_sum):
        first = jnp.where(core == 0, own_sum, got_sum)
        second = jnp.where(core == 0, got_sum, own_sum)
        return jnp.concatenate([first, second], axis=2).reshape(EXPERTS, 2, 24, D).astype(f32)

    full = jnp.stack(
        [both_halves(own0[0:8], got0[0:8]), both_halves(by_core(sums1, core), got1.reshape(8, 24, FE))]
    )
    attn0 = own[0:24].reshape(24, 2, 384).transpose(1, 0, 2)
    attn = jnp.stack([attn0, attn1])
    grad_w_qkv = jnp.concatenate([attn[:, 1, :, None, :WIDTH], attn[:, 0].reshape(2, 24, 2, WIDTH)], axis=2)
    grad_w_out = attn[:, 1, :, WIDTH:].transpose(0, 2, 1)
    tiny = own[24:32, 0:48].reshape(8, 2, 24).transpose(1, 0, 2)
    return (
        ends[None],
        tiny[:, 0:2],
        tiny[:, 2:4],
        grad_w_qkv,
        grad_w_out,
        tiny[:, 4:8].transpose(0, 2, 1),
        full[:, :, 0],
        full[:, :, 1].transpose(0, 1, 3, 2),
    )


def solution(mesh):
    fine = Mesh(mesh.devices.reshape(4, 2, 2, 2, 4), CHIPS + ("core", "tp"))
    section, ctx = ("x", "zh"), ("zl", "core")
    every = section + ctx
    return jax.shard_map(
        shards,
        mesh=fine,
        in_specs=(
            P(ctx, section, None, None),
            P(ctx, section, None, None),
            P(),
            P(None, None, every),
            P(None, None, every),
            P(None, every, None, "tp"),
            P(None, "tp", every),
            P(None, every, None),
            P(None, None, every, "tp"),
            P(None, None, "tp", every),
        ),
        out_specs=(
            P(ctx, section, None, None),
            P(None, None, every),
            P(None, None, every),
            P(None, every, None, "tp"),
            P(None, "tp", every),
            P(None, every, None),
            P(None, None, every, "tp"),
            P(None, None, "tp", every),
        ),
        check_vma=False,
    )
```

```python
import functools

import jax
import jax.numpy as jnp
from jax import lax
from jax.experimental import pallas as pl
from jax.experimental.pallas import tpu as pltpu
from jax.sharding import Mesh
from jax.sharding import PartitionSpec as P

D = 768
HD = 64
HEADS = 3
ROWS = 160
PAIR = 320
KEYS = 640
FE = 384
EXPERTS = 4
EPS = 1e-06
WIDTH = HEADS * HD
MESH = pl.DeviceIdType.MESH
CHIPS = ("x", "zh", "zl")
f32, bf16 = jnp.float32, jnp.bfloat16
VMEM = pl.BlockSpec(memory_space=pltpu.VMEM)
SMEM = pl.BlockSpec(memory_space=pltpu.SMEM)
NN = (((1,), (0,)), ((), ()))
NT = (((1,), (1,)), ((), ()))
TN = (((0,), (0,)), ((), ()))


def dot(a, b, dims):
    return lax.dot_general(a, b, dims, preferred_element_type=f32)


def dot_exact(a, b, dims):
    return lax.dot_general(
        a, b, dims, preferred_element_type=f32, precision=lax.Precision.HIGHEST
    )


def params(cid, mib):
    return pltpu.CompilerParams(
        collective_id=cid, has_side_effects=True, vmem_limit_bytes=mib * 2**20
    )


def arrive(peers):
    barrier = pltpu.get_barrier_semaphore()
    for peer in peers:
        pl.semaphore_signal(barrier, inc=1, device_id=peer, device_id_type=MESH)


def all_here(count):
    pl.semaphore_wait(pltpu.get_barrier_semaphore(), count)


def dma_sems(*counts):
    return [pltpu.SemaphoreType.DMA((count,)) for count in counts for _ in range(2)]


def remote(src, dst, send, recv, peer):
    return pltpu.make_async_remote_copy(
        src_ref=src, dst_ref=dst, send_sem=send, recv_sem=recv, device_id=peer, device_id_type=MESH
    )


def tp_peers():
    return [{"tp": (lax.axis_index("tp") + k) % 4} for k in (1, 2, 3)]


def sum_cores(part, crossed, send, recv):
    core = lax.axis_index("core")
    return remote(part.at[1 - core], crossed, send.at[0], recv.at[0], {"core": 1 - core})


def sum_terms(both, part, landed, send, recv):
    block = lax.axis_index("core") if both else 0
    return [
        remote(part.at[block, peer["tp"]], landed.at[k], send.at[k], recv.at[k], peer)
        for k, peer in enumerate(tp_peers())
    ]


def sum_results(out, send, recv):
    core, tp = lax.axis_index("core"), lax.axis_index("tp")
    return [
        remote(out.at[core, tp], out.at[core, tp], send.at[k], recv.at[k], peer)
        for k, peer in enumerate(tp_peers())
    ]


def sum_cross(out, send, recv):
    core, tp = lax.axis_index("core"), lax.axis_index("tp")
    return [
        remote(out.at[core, at], out.at[core, at], send.at[k], recv.at[k], {"core": 1 - core})
        for k, at in enumerate([(tp + 4 - k) % 4 for k in range(4)])
    ]


def sum_start(both, out, part, landed, rs, rr, gs, gr, cs, cr, crossed=None, ps=None, pr=None):
    if both:
        core = lax.axis_index("core")
        pre = sum_cores(part, crossed, ps, pr)
        pre.start()
        pre.wait_recv()
        for j in range(4):
            part[core, j] = (part[core, j].astype(f32) + crossed[j].astype(f32)).astype(bf16)
    for copy in sum_terms(both, part, landed, rs, rr):
        copy.start()


def sum_middle(both, out, part, landed, rs, rr, gs, gr, cs, cr, *pre):
    core, tp = lax.axis_index("core"), lax.axis_index("tp")
    total = part[core if both else 0, tp].astype(f32)
    for k, copy in enumerate(sum_terms(both, part, landed, rs, rr)):
        copy.wait_recv()
        total = total + landed[k].astype(f32)
    out[core, tp] = total.astype(bf16)
    for copy in sum_results(out, gs, gr):
        copy.start()


def sum_end(both, out, part, landed, rs, rr, gs, gr, cs, cr, *pre):
    gathers, crosses = sum_results(out, gs, gr), sum_cross(out, cs, cr)
    for k in range(4):
        if k > 0:
            gathers[k - 1].wait_recv()
        crosses[k].start()
    for copy in crosses:
        copy.wait()
    for copy in sum_terms(both, part, landed, rs, rr) + gathers:
        copy.wait_send()
    if both:
        sum_cores(part, *pre).wait_send()


def sum_scratch(both, rows):
    scratch = [
        pltpu.VMEM((2 if both else 1, 4, rows, 384), bf16),
        pltpu.VMEM((3, rows, 384), bf16),
    ] + dma_sems(3, 3, 4)
    if both:
        scratch += [pltpu.VMEM((4, rows, 384), bf16)] + dma_sems(1)
    return scratch


def chip_peers():
    core, zl = lax.axis_index("core"), lax.axis_index("zl")
    return {"core": 1 - core}, {"zl": 1 - zl}, zl * 2 + core


def chip_peer(k):
    x, zh, zl = (lax.axis_index(a) for a in CHIPS)
    dx, dh, dl = k // 4, (k // 2) % 2, k % 2
    ahead = ((x + dx) % 4, (zh + dh) % 2, (zl + dl) % 2)
    back = ((x + 4 - dx) % 4, (zh + 2 - dh) % 2, (zl + 2 - dl) % 2)
    return dict(zip(CHIPS, ahead)), *(c[0] * 4 + c[1] * 2 + c[2] for c in (ahead, back))


def cross_kernel(own, out, send, recv):
    other = {"core": 1 - lax.axis_index("core")}
    arrive([other])
    all_here(1)
    copy = remote(own, out, send.at[0], recv.at[0], other)
    copy.start()
    copy.wait()


def cross(own, cid):
    return pl.pallas_call(
        cross_kernel,
        out_shape=jax.ShapeDtypeStruct(own.shape, own.dtype),
        in_specs=[VMEM],
        out_specs=VMEM,
        scratch_shapes=dma_sems(1),
        compiler_params=params(cid, 8),
        name="cross",
    )(own)


def places():
    return lax.axis_index("x"), lax.axis_index("zh") * 2 + lax.axis_index("zl")


def axis_peer(along_x, k):
    x, z = places()
    if along_x:
        return {"x": (x + k) % 4}, (x + k) % 4
    to = (z + k) % 4
    return {"zh": to // 2, "zl": to % 2}, to


def half(rows, route):
    return pl.ds(route * (rows // 2), rows // 2)


def line(whole, route, second, rows):
    return whole.at[:, second, rows] if route == 0 else whole.at[second, :, rows]


def axis_peers(*ks):
    return [axis_peer(along_x, k)[0] for along_x in (True, False) for k in ks]


def start_kernel(
    images, urgent, later, out_images, all_urgent, all_later, own_sem, im_s, im_r, u1_s, u1_r, u2_s, u2_r, l_s, l_r
):
    core = lax.axis_index("core")
    at_x, at_z = places()
    high = at_x // 2
    other = {"core": 1 - core}
    arrive(axis_peers(1, 2, 3) + [other])
    all_urgent[at_x, at_z] = urgent[...]
    out_images[core, high] = images[high]
    own = pltpu.make_async_copy(later, all_later.at[at_x, at_z], own_sem)
    own.start()
    all_here(7)
    firsts, seconds, laters = [], [], []
    for route in range(2):
        b = (at_z, at_x)[route]
        rows, late = half(urgent.shape[0], route), half(later.shape[0], route)
        for k in range(1, 4):
            peer, _ = axis_peer(route == 0, k)
            n = 3 * route + k - 1
            firsts.append(
                remote(urgent.at[rows], all_urgent.at[at_x, at_z, rows], u1_s.at[n], u1_r.at[n], peer)
            )
            laters.append(
                remote(later.at[late], all_later.at[at_x, at_z, late], l_s.at[n], l_r.at[n], peer)
            )
            slabs = line(all_urgent, route, b, rows)
            seconds.append(remote(slabs, slabs, u2_s.at[n], u2_r.at[n], axis_peer(route == 1, k)[0]))
    swap = remote(images.at[1 - high], out_images.at[core, high], im_s.at[0], im_r.at[0], {"x": (at_x + 2) % 4})
    kept = remote(images.at[high], out_images.at[core, high], im_s.at[1], im_r.at[1], other)
    passed = remote(
        out_images.at[core, 1 - high], out_images.at[core, 1 - high], im_s.at[2], im_r.at[2], other
    )
    for copy in firsts + [swap, kept]:
        copy.start()
    for copy in firsts:
        copy.wait_recv()
    for copy in seconds + laters:
        copy.start()
    swap.wait_recv()
    passed.start()
    for copy in seconds + laters + [kept, passed]:
        copy.wait()
    for copy in firsts + [swap]:
        copy.wait_send()
    own.wait()


def start_exchange(images, urgent, later):
    return pl.pallas_call(
        start_kernel,
        out_shape=[
            jax.ShapeDtypeStruct(s, bf16)
            for s in ((2,) + images.shape, (4, 4) + urgent.shape, (4, 4) + later.shape)
        ],
        in_specs=[VMEM] * 3,
        out_specs=[VMEM, VMEM, pl.BlockSpec(memory_space=pl.ANY)],
        scratch_shapes=[pltpu.SemaphoreType.DMA] + dma_sems(3, 6, 6, 6),
        compiler_params=params(1, 56),
        name="start_exchange",
    )(images, urgent, later)


def spread_near(whole, send, recv):
    copies = []
    for route in range(2):
        slabs = line(whole, route, places()[1 - route], half(whole.shape[2], route))
        for n, k in enumerate((1, 3)):
            at, peer = 2 * route + n, axis_peer(route == 1, k)[0]
            copies.append(remote(slabs, slabs, send.at[at], recv.at[at], peer))
    return copies


def spread_far(whole, send, recv):
    copies = []
    size = whole.shape[2] // 2
    cut = size // 32 * 16 + size % 32
    for route in range(2):
        b = places()[1 - route]
        for n, k in enumerate((1, 3)):
            rows = pl.ds(route * size + n * cut, size - cut if n else cut)
            slabs = line(whole, route, (b + 4 - k) % 4, rows)
            at, peer = 4 + 2 * route + n, axis_peer(route == 1, k)[0]
            copies.append(remote(slabs, slabs, send.at[at], recv.at[at], peer))
    return copies


def part_rows(rows, route, n):
    size = rows // 2
    cut = size // 32 * 16 + size % 32
    return pl.ds(route * size + n * cut, size - cut if n else cut)


def toward_far(whole, passing, route, send, recv):
    copies, b = [], places()[1 - route]
    for n, k in enumerate((1, 3)):
        rows = part_rows(whole.shape[2], route, n)
        target = passing.at[route, n, :, 0 : rows.size]
        at, peer = 2 * route + n, axis_peer(route == 1, k)[0]
        copies.append(remote(line(whole, route, (b + 2) % 4, rows), target, send.at[at], recv.at[at], peer))
    return copies


def toward_near(whole, passing, landed, route, send, recv):
    copies, b = [], places()[1 - route]
    for n, k in enumerate((1, 3)):
        rows, others = (part_rows(whole.shape[2], route, m) for m in (n, 1 - n))
        at, peer = 4 * route + 2 * n, axis_peer(route == 1, k)[0]
        copies += [
            remote(passing.at[route, n, :, 0 : rows.size], landed.at[n, :, rows], send.at[at], recv.at[at], peer),
            remote(
                line(whole, route, (b + k) % 4, others), landed.at[n, :, others],
                send.at[at + 1], recv.at[at + 1], peer,
            ),
        ]
    return copies


def add_passing(whole, passing, route):
    x, z = places()
    b = (z, x)[route]
    for n, k in enumerate((1, 3)):
        rows, to = part_rows(whole.shape[2], route, n), (b + k) % 4

        def add(j, carry, n=n, rows=rows, to=to):
            own = whole[j, to, rows] if route == 0 else whole[to, j, rows]
            total = passing[route, n, j, 0 : rows.size].astype(f32) + own.astype(f32)
            passing[route, n, j, 0 : rows.size] = total.astype(bf16)
            return carry

        lax.fori_loop(0, 4, add, 0)


def last_copies(some, slabs, send, recv):
    copies = []
    for route in range(2):
        rows = half(some.shape[1], route)
        for k in range(1, 4):
            peer, at = axis_peer(route == 0, k)
            n = 3 * route + k - 1
            copies.append(remote(some.at[at, rows], slabs.at[k - 1, rows], send.at[n], recv.at[n], peer))
    return copies


def add_slabs(some, slabs, out):
    x, z = places()
    steps = out.shape[0] // 48

    def add(i, carry):
        rows, route = pl.ds(pl.multiple_of(i * 48, 48), 48), i // (steps // 2)
        total = some[x * (1 - route) + z * route, rows].astype(f32)
        for k in range(3):
            total = total + slabs[k, rows].astype(f32)
        out[rows] = total.astype(bf16)
        return carry

    lax.fori_loop(0, steps, add, 0)


def end_kernel(
    part, image, half, some, out, out_image, out_half, own_sum, other_sum,
    landed, sums, pieces, total, slabs, cx_s, cx_r, sl_s, sl_r, send, recv,
):
    core, x = lax.axis_index("core"), lax.axis_index("x")
    other = {"core": 1 - core}
    _, me, _ = chip_peer(0)
    arrive([chip_peer(k)[0] for k in range(1, 16)] + [other])
    all_here(16)
    crossing = remote(part.at[1 - core], landed, cx_s.at[0], cx_r.at[0], other)
    crossing.start()
    lasts = last_copies(some, slabs, sl_s, sl_r)
    for copy in lasts:
        copy.start()
    crossing.wait()

    def push(k):
        peer, at, _ = chip_peer(k)
        return remote(sums.at[at], pieces.at[k], send.at[k], recv.at[k], peer)

    def add(k, carry):
        _, at, _ = chip_peer(k)
        sums[at] = (part[core, at].astype(f32) + landed[at].astype(f32)).astype(bf16)
        push(k).start()
        return carry

    def collect(k, carry):
        push(k).wait_recv()
        total[...] += pieces[k].astype(f32)
        return carry

    def last(k, carry):
        push(k).wait_send()
        return carry

    lax.fori_loop(1, 16, add, 0)
    swap = remote(image, out_image, cx_s.at[1], cx_r.at[1], {"x": (x + 2) % 4})
    swap.start()
    halves = remote(half, out_half, cx_s.at[2], cx_r.at[2], other)
    halves.start()
    total[...] = part[core, me].astype(f32) + landed[me].astype(f32)
    lax.fori_loop(1, 16, collect, 0)
    out[core] = total[...]
    given = remote(out.at[core], out.at[core], cx_s.at[4], cx_r.at[4], other)
    given.start()
    for copy in lasts:
        copy.wait()
    add_slabs(some, slabs, own_sum)
    final = remote(own_sum, other_sum, cx_s.at[3], cx_r.at[3], other)
    final.start()
    lax.fori_loop(1, 16, last, 0)
    for copy in (given, final, swap, halves):
        copy.wait()


def end_exchange(part, image, half, some):
    shape, slab = part.shape[2:], some.shape[1:]
    return pl.pallas_call(
        end_kernel,
        out_shape=[jax.ShapeDtypeStruct((2,) + shape, f32)]
        + [jax.ShapeDtypeStruct(s, bf16) for s in (image.shape, half.shape, slab, slab)],
        in_specs=[VMEM] * 4,
        out_specs=[VMEM] * 5,
        scratch_shapes=[pltpu.VMEM((16,) + shape, bf16)] * 3
        + [pltpu.VMEM(shape, f32), pltpu.VMEM((3,) + slab, bf16)]
        + dma_sems(5, 6, 16),
        compiler_params=params(2, 56),
        name="end_exchange",
    )(part, image, half, some)


def block_rows(ref, block):
    top = jnp.concatenate([ref[block, 0, 0:80], ref[block, 1, 0:80]], axis=1)
    low = jnp.concatenate([ref[block, 2, 0:80], ref[block, 3, 0:80]], axis=1)
    return jnp.concatenate([top, low], axis=0).astype(f32)


def pair_rows(ref):
    return jnp.concatenate([block_rows(ref, 0), block_rows(ref, 1)], axis=0)


def put_chunks(ref, block, value, first=0):
    for j in range(4):
        r, c = 80 * (j // 2), 384 * (j % 2)
        ref[block, j, first : first + 80] = value[r : r + 80, c : c + 384]


def norm_parts(rows):
    centered = rows - jnp.mean(rows, axis=-1, keepdims=True)
    scale = lax.rsqrt(jnp.mean(centered * centered, axis=-1, keepdims=True) + EPS)
    return centered * scale, scale


def norm_back(grad, unit, scale, gain):
    inner = grad * gain
    return scale * (
        inner
        - jnp.mean(inner, axis=-1, keepdims=True)
        - unit * jnp.mean(inner * unit, axis=-1, keepdims=True)
    )


def softmax(logits, axis):
    top = jnp.max(logits, axis=axis, keepdims=True)
    powers = jnp.exp(logits - top)
    return powers / jnp.sum(powers, axis=axis, keepdims=True)


def own_rows(core):
    return pl.ds(pl.multiple_of(core * ROWS, ROWS), ROWS)


def head(value, h):
    return value[:, HD * h : HD * h + HD]


def gelu_parts(u):
    c = 0.7978845608028654
    t = jnp.tanh(c * (u + 0.044715 * u * u * u))
    return 0.5 * u * (1.0 + t), t


def gelu_slope(u, t):
    c = 0.7978845608028654
    return 0.5 * (1.0 + t) + 0.5 * u * (1.0 - t * t) * (c * (1.0 + 3 * 0.044715 * u * u))


def attn_weights(weights):
    w_kv = weights[:, 0:48].reshape(D, 2 * WIDTH)
    w_q = weights[:, 48:96, :WIDTH].reshape(D, WIDTH)
    return w_kv, w_q, weights[:, 48:96, WIDTH:].reshape(D, WIDTH)


def attend_forward_kernel(follows, *refs):
    if follows:
        x, att_before, moe_before, small, weights, dead, q, kv, mixed, att, x_next, *scratch = refs
    else:
        x, small, weights, dead, _, q, kv, mixed, att, whole, *scratch = refs
        *scratch, sp_send, sp_recv = scratch
    part, landed, *sems, kv_send, kv_recv = scratch
    sums = (False, att, part, landed, *sems)
    core = lax.axis_index("core")
    other, across, me = chip_peers()
    arrive([other, across] + tp_peers())
    if not follows:
        arrive(axis_peers(1, 3))
    if follows:
        x_next[...] = (x[...].astype(f32) + pair_rows(att_before) + pair_rows(moe_before)).astype(bf16)
        x = x_next
    unit, _ = norm_parts(x[own_rows(core)].astype(f32))
    normed = (unit * small[0:1] + small[2:3]).astype(bf16)
    w_kv, w_q, w_out_t = attn_weights(weights)
    kv[me] = dot(normed, w_kv, NN).astype(bf16)
    all_here(5 if follows else 9)
    far = (me + 2) % 4
    copies = [
        remote(kv.at[at], kv.at[at], kv_send.at[k], kv_recv.at[k], peer)
        for k, (at, peer) in enumerate(((me, across), (me, other), (far, other)))
    ]
    copies[0].start()
    copies[1].start()
    if not follows:
        nears = spread_near(whole, sp_send, sp_recv)
        fars = spread_far(whole, sp_send, sp_recv)
        for copy in nears:
            copy.start()
    queries = dot(normed, w_q, NN).astype(bf16)
    q[...] = queries
    copies[0].wait_recv()
    copies[2].start()
    copies[1].wait_recv()
    copies[2].wait_recv()
    keys = kv[...].reshape(KEYS, 2 * WIDTH)
    outs = []
    for h in range(HEADS):
        scores = HD**-0.5 * dot(head(queries, h), head(keys, h), NT) + dead[...]
        probs = softmax(scores, -1).astype(bf16)
        outs.append(dot(probs, head(keys, HEADS + h), NN))
    heads = jnp.concatenate(outs, axis=1).astype(bf16)
    mixed[...] = heads
    put_chunks(part, 0, dot(heads, w_out_t, NT).astype(bf16))
    sum_start(*sums)
    sum_middle(*sums)
    if not follows:
        for copy in nears:
            copy.wait_recv()
        for copy in fars:
            copy.start()
    sum_end(*sums)
    for copy in copies:
        copy.wait_send()
    if not follows:
        for copy in fars:
            copy.wait()
        for copy in nears:
            copy.wait_send()


def attend_forward(x, before, small, weights, dead, some, cid):
    args = (x, *before, small, weights, dead)
    shapes = [(ROWS, WIDTH), (4, ROWS, 2 * WIDTH), (ROWS, WIDTH), (2, 4, 80, 384)]
    in_specs, out_specs = [VMEM] * len(args), [VMEM] * 5
    scratch = sum_scratch(False, 80) + dma_sems(3)
    if before:
        shapes.append((PAIR, D))
    else:
        args += (some,)
        shapes.append(some.shape)
        in_specs.append(pl.BlockSpec(memory_space=pl.ANY))
        out_specs[4] = pl.BlockSpec(memory_space=pl.ANY)
        scratch += dma_sems(8)
    return pl.pallas_call(
        functools.partial(attend_forward_kernel, bool(before)),
        out_shape=[jax.ShapeDtypeStruct(s, bf16) for s in shapes],
        in_specs=in_specs,
        out_specs=out_specs,
        scratch_shapes=scratch,
        input_output_aliases={} if before else {len(args) - 1: 4},
        compiler_params=params(cid, 56),
        name="attend_forward",
    )(*args)


def expert_weights(weights):
    block = weights[...]
    return block[:, 0:48].reshape(D, FE), block[:, 48:96].reshape(D, FE)


def experts_setup(x, att, small, routes, b, gates):
    unit, _ = norm_parts(x[...].astype(f32) + pair_rows(att))
    b[...] = (unit * small[1:2] + small[3:4]).astype(bf16)
    probs = softmax(dot(b[...], small[4:8].astype(bf16), NT), -1)
    ids = lax.broadcasted_iota(jnp.int32, (PAIR, EXPERTS), 1).astype(f32)
    named = (routes[:, 0:1] == ids) | (routes[:, 1:2] == ids)
    gates[...] = jnp.where(named, probs, 0.0)


def gate_of(gates, expert):
    ids = lax.broadcasted_iota(jnp.int32, (PAIR, EXPERTS), 1)
    return jnp.sum(jnp.where(ids == expert, gates[...], 0.0), axis=1, keepdims=True)


def experts_forward_kernel(
    x, att, small, routes, weights, result, b, gates, total, out, part, landed, *sems
):
    expert = pl.program_id(0)
    sums = (True, out, part, landed, *sems)

    @pl.when(expert == 0)
    def _():
        arrive(tp_peers() + [{"core": 1 - lax.axis_index("core")}])
        experts_setup(x, att, small, routes, b, gates)
        total[...] = jnp.zeros_like(total)

    w_in, w_out_t = expert_weights(weights)
    u = dot(b[...], w_in, NN)
    active = gelu_parts(u)[0].astype(bf16).astype(f32)
    gated = (gate_of(gates, expert) * active).astype(bf16)
    total[...] += dot(gated, w_out_t, NT)

    @pl.when(expert == EXPERTS - 1)
    def _():
        for block in range(2):
            put_chunks(part, block, total[ROWS * block : ROWS * block + ROWS].astype(bf16))
        all_here(4)
        sum_start(*sums)
        sum_middle(*sums)
        sum_end(*sums)
        result[...] = out[...]


def fixed(shape):
    return pl.BlockSpec(shape, lambda e: (0,) * len(shape))


def experts_forward(x, att, small, routes, weights, cid):
    args = (x, att, small, routes)
    return pl.pallas_call(
        experts_forward_kernel,
        grid=(EXPERTS,),
        out_shape=jax.ShapeDtypeStruct((2, 4, 80, 384), bf16),
        in_specs=[fixed(a.shape) for a in args] + [pl.BlockSpec((16, 96, FE), lambda e: (0, e, 0))],
        out_specs=fixed((2, 4, 80, 384)),
        scratch_shapes=[
            pltpu.VMEM((PAIR, D), bf16),
            pltpu.VMEM((PAIR, EXPERTS), f32),
            pltpu.VMEM((PAIR, D), f32),
            pltpu.VMEM((2, 4, 80, 384), bf16),
        ]
        + sum_scratch(True, 80),
        compiler_params=params(cid, 56),
        name="experts_forward",
    )(*args, weights)


def experts_backward_kernel(
    steps, x, att, small, routes, grad, extra, some, weights, result, moe_part, own_sum, grad_w,
    b, gates, total, moe, gate_t, gated_all, grad_u_all, out, part, landed, *sems,
):
    step = pl.program_id(0)
    sums = (True, out, part, landed, *sems)
    with_moe = moe_part is not None
    if not with_moe:
        *sems, slabs, slab_send, slab_recv = sems
        sums, lasts = (True, out, part, landed, *sems), last_copies(some, slabs, slab_send, slab_recv)

    @pl.when(step == 0)
    def _():
        arrive(tp_peers() + [{"core": 1 - lax.axis_index("core")}])
        if not with_moe:
            arrive(axis_peers(1, 2, 3))
        experts_setup(x, att, small, routes, b, gates)
        total[...] = jnp.zeros_like(total)
        if with_moe:
            moe[...] = jnp.zeros_like(moe)

    @pl.when(step < EXPERTS)
    def _():
        w_in, w_out_t = expert_weights(weights)
        u = dot(b[...], w_in, NN)
        act, t = gelu_parts(u)
        active = act.astype(bf16).astype(f32)
        gate = gate_of(gates, step)
        gated = (gate * active).astype(bf16)
        gated_all[step] = gated
        if with_moe:
            moe[...] += dot(gated, w_out_t, NT)
        back = dot(grad[...], w_out_t, NN)
        gate_t[step] = dot_exact(jnp.ones((8, FE), f32), back * active, NT)
        grad_u = (gate * back * gelu_slope(u, t)).astype(bf16)
        grad_u_all[step] = grad_u
        total[...] += dot(grad_u, w_in, NT)

    @pl.when(step == EXPERTS - 1)
    def _():
        part[...] = jnp.zeros_like(part)
        for block in range(2):
            lines = slice(ROWS * block, ROWS * block + ROWS)
            put_chunks(part, block, total[lines].astype(bf16))
            table = jnp.concatenate(
                [gate_t[e, 0:1, lines] for e in range(EXPERTS)] + [jnp.zeros((12, ROWS), f32)], axis=0
            )
            part[block, 0, 80:96, 0:ROWS] = table.astype(bf16)
            if with_moe:
                put_chunks(moe_part, block, moe[lines].astype(bf16))
        all_here(4 if with_moe else 10)
        sum_start(*sums)
        if not with_moe:
            for copy in lasts:
                copy.start()

    @pl.when((step >= EXPERTS) & (step < 2 * EXPERTS))
    def _():
        at = step - EXPERTS
        grad_w[:, 0:48] = dot(b[...], grad_u_all[at], TN).astype(bf16).reshape(16, 48, FE)
        grad_w[:, 48:96] = dot(grad[...], gated_all[at], TN).astype(bf16).reshape(16, 48, FE)

    @pl.when(step == EXPERTS + 1)
    def _():
        sum_middle(*sums)

    if steps > 2 * EXPERTS:

        @pl.when(step == 2 * EXPERTS)
        def _():
            grad_w[:, 0:48] = extra[0].reshape(16, 48, FE)
            grad_w[:, 48:96] = extra[1].reshape(16, 48, FE)

    @pl.when(step == steps - 1)
    def _():
        sum_end(*sums)
        result[...] = out[...]
        if not with_moe:
            for copy in lasts:
                copy.wait()
            add_slabs(some, slabs, own_sum)


def experts_backward(x, att, small, routes, grad, extra, some, weights, cid):
    args = (x, att, small, routes, grad)
    steps = 2 * EXPERTS
    shapes = [(2, 4, 96, 384)]
    blocks = [fixed((2, 4, 96, 384))]
    scratch = []
    if extra is None:
        shapes.append((2, 4, 80, 384))
        blocks.append(fixed((2, 4, 80, 384)))

        def kernel(*refs):
            experts_backward_kernel(steps, *refs[:5], None, None, *refs[5:8], None, *refs[8:])
    else:
        args, steps = args + (extra, some), steps + 1
        slab = some.shape[1:]
        shapes.append(slab)
        blocks.append(fixed(slab))
        scratch = [pltpu.VMEM((3,) + slab, bf16)] + dma_sems(6)

        def kernel(*refs):
            experts_backward_kernel(steps, *refs[:9], None, *refs[9:])

    grads = steps - EXPERTS
    return pl.pallas_call(
        kernel,
        grid=(steps,),
        out_shape=[jax.ShapeDtypeStruct(s, bf16) for s in shapes + [(16, 96 * grads, FE)]],
        in_specs=[fixed(a.shape) for a in args]
        + [pl.BlockSpec((16, 96, FE), lambda s: (0, jnp.minimum(s, EXPERTS - 1), 0))],
        out_specs=blocks + [pl.BlockSpec((16, 96, FE), lambda s: (0, jnp.maximum(s - EXPERTS, 0), 0))],
        scratch_shapes=[
            pltpu.VMEM((PAIR, D), bf16),
            pltpu.VMEM((PAIR, EXPERTS), f32),
            pltpu.VMEM((PAIR, D), f32),
            pltpu.VMEM((PAIR, D), f32),
            pltpu.VMEM((EXPERTS, 8, PAIR), f32),
            pltpu.VMEM((EXPERTS, PAIR, FE), bf16),
            pltpu.VMEM((EXPERTS, PAIR, FE), bf16),
            pltpu.VMEM((2, 4, 96, 384), bf16),
        ]
        + sum_scratch(True, 96)
        + scratch,
        compiler_params=params(cid, 56),
        name="experts_backward",
    )(*args, weights)


def attend_backward_kernel(with_moe, *refs):
    x, att, small, routes_t, grad, back, q, kv, mixed, dead, weights, whole, *refs = refs
    if with_moe:
        moe_part, *refs = refs
    grad_x, grad_small, grad_w, some, *refs = refs
    if with_moe:
        moe, *refs = refs
    grad_h, both_units, parts, kv_landed, back_one, part, landed, *sems = refs
    if with_moe:
        *sems, moe_landed, ms, mr, ns, nr, moe_crossed, ps, pr = sems
        moe_sums = (moe_part, moe_crossed, ps, pr)
    *sems, slabs, passing, fs, fr, ns2, nr2, kv_out, kv_send, kv_recv = sems
    fars = [toward_far(whole, passing, route, fs, fr) for route in range(2)]
    nears = [toward_near(whole, passing, slabs, route, ns2, nr2) for route in range(2)]
    sums = (False, back_one, part, landed, *sems)
    core, tp = lax.axis_index("core"), lax.axis_index("tp")
    other, across, me = chip_peers()
    far = (me + 2) % 4
    arrive([other, across] + tp_peers() + axis_peers(1, 3))
    all_here(9)
    for copy in fars[1] + fars[0]:
        copy.start()
    unit, scale = norm_parts(x[...].astype(f32) + pair_rows(att))
    b = (unit * small[1:2] + small[3:4]).astype(bf16)
    router = small[4:8]
    chances = softmax(dot(router.astype(bf16), b, NT), 0)
    ids = lax.broadcasted_iota(jnp.int32, (EXPERTS, PAIR), 0).astype(f32)
    named = (routes_t[0:1] == ids) | (routes_t[1:2] == ids)
    tables = [back[block, 0, 80:96, 0:ROWS].astype(f32)[0:EXPERTS] for block in range(2)]
    gate_grads = jnp.where(named, jnp.concatenate(tables, axis=1), 0.0)
    grad_logits = chances * (gate_grads - jnp.sum(chances * gate_grads, axis=0, keepdims=True))
    grad_b = pair_rows(back) + dot_exact(grad_logits, router, TN)
    grad_h[...] = grad[...].astype(f32) + norm_back(grad_b, unit, scale, small[1:2])
    grad_att = grad_h[own_rows(core)].astype(bf16)
    w_kv, w_q, w_out_t = attn_weights(weights)
    grad_mixed = dot(grad_att, w_out_t, NN).astype(bf16)
    keys = kv[...].reshape(KEYS, 2 * WIDTH)
    queries = q[...]
    q_parts, k_parts, v_parts = [], [], []
    for h in range(HEADS):
        q_h, g_h = head(queries, h), head(grad_mixed, h)
        k_h, v_h = head(keys, h), head(keys, HEADS + h)
        probs = softmax(HD**-0.5 * dot(q_h, k_h, NT) + dead[...], -1)
        v_parts.append(dot(probs.astype(bf16), g_h, TN))
        grad_weights = dot(g_h, v_h, NT)
        grad_scores = probs * (
            grad_weights - jnp.sum(probs * grad_weights, axis=-1, keepdims=True)
        )
        grad_scores = grad_scores.astype(bf16)
        q_parts.append(HD**-0.5 * dot(grad_scores, k_h, NN))
        k_parts.append(HD**-0.5 * dot(grad_scores, q_h, TN))
    total = jnp.concatenate(k_parts + v_parts, axis=1).astype(bf16)
    parts[...] = total.reshape(4, ROWS, 2 * WIDTH)
    crosses = [
        remote(parts.at[(at + 1 - 2 * core) % 4], kv_landed.at[k], kv_send.at[k], kv_recv.at[k], other)
        for k, at in enumerate((me, far))
    ]
    onward = remote(kv_out, kv_landed.at[2], kv_send.at[2], kv_recv.at[2], across)
    crosses[1].start()
    crosses[0].start()
    if with_moe:
        pre = sum_cores(*moe_sums)
        pre.start()
    crosses[1].wait_recv()
    kv_out[...] = (parts[far].astype(f32) + kv_landed[1].astype(f32)).astype(bf16)
    onward.start()
    if with_moe:
        pre.wait_recv()
        for j in range(4):
            moe_sum = moe_part[core, j].astype(f32) + moe_crossed[j].astype(f32)
            moe_crossed[j] = moe_sum.astype(bf16)
        moe_terms = [
            remote(moe_crossed.at[peer["tp"]], moe_landed.at[k], ms.at[k], mr.at[k], peer)
            for k, peer in enumerate(tp_peers())
        ]
        for copy in moe_terms:
            copy.start()
    for route in (1, 0):
        for copy in fars[route]:
            copy.wait_recv()
        add_passing(whole, passing, route)
        for copy in nears[route]:
            copy.start()
    grad_q = jnp.concatenate(q_parts, axis=1).astype(bf16)
    grad_w[1, :, WIDTH:] = dot(grad_att, mixed[...], TN).astype(bf16)
    lanes = lax.broadcasted_iota(jnp.int32, (EXPERTS, PAIR), 1)
    own_lanes = (lanes < ROWS) == (core == 0)
    own = (lax.broadcasted_iota(jnp.int32, (PAIR, 1), 0) < ROWS) == (core == 0)
    kept = jnp.where(own, grad_b, 0.0)
    grad_small[1:2] = jnp.sum(kept * unit, axis=0, keepdims=True)
    grad_small[3:4] = jnp.sum(kept, axis=0, keepdims=True)
    grad_small[4:8] = dot_exact(jnp.where(own_lanes, grad_logits, 0.0), b.astype(f32), NN)
    unit_one, scale_one = norm_parts(x[...].astype(f32))
    both_units[...] = unit_one
    normed = (both_units[own_rows(core)] * small[0:1] + small[2:3]).astype(bf16)
    crosses[0].wait_recv()
    onward.wait_recv()
    grad_kv = parts[me].astype(f32) + kv_landed[0].astype(f32) + kv_landed[2].astype(f32)
    grad_kv = grad_kv.astype(bf16)
    value = dot(grad_kv, w_kv, NT) + dot(grad_q, w_q, NT)
    put_chunks(part, 0, value.astype(bf16))
    sum_start(*sums)
    grad_w[0] = dot(normed, grad_kv, TN).astype(bf16)
    grad_w[1, :, :WIDTH] = dot(normed, grad_q, TN).astype(bf16)
    sum_middle(*sums)
    if with_moe:
        total = moe_crossed[tp].astype(f32)
        for k, copy in enumerate(moe_terms):
            copy.wait_recv()
            total = total + moe_landed[k].astype(f32)
        moe[tp] = total.astype(bf16)
        moe_results = [
            remote(moe.at[tp], moe.at[tp], ns.at[k], nr.at[k], {"tp": (tp + k + 1) % 4}) for k in range(3)
        ]
        for copy in moe_results:
            copy.start()
    sum_end(*sums)
    grad_a = pair_rows(back_one)
    grad_x[...] = (grad_h[...] + norm_back(grad_a, unit_one, scale_one, small[0:1])).astype(bf16)
    kept = jnp.where(own, grad_a, 0.0)
    grad_small[0:1] = jnp.sum(kept * unit_one, axis=0, keepdims=True)
    grad_small[2:3] = jnp.sum(kept, axis=0, keepdims=True)
    for copy in crosses + [onward]:
        copy.wait_send()
    if with_moe:
        pre.wait_send()
        for copy in moe_terms:
            copy.wait_send()
        for copy in moe_results:
            copy.wait()
    for route in range(2):
        for copy in fars[route]:
            copy.wait_send()
        for copy in nears[route]:
            copy.wait()
    at_x, at_z = places()
    steps = some.shape[1] // 48

    def add(i, carry):
        j, at = i % 4, i // 4
        rows, route = pl.ds(pl.multiple_of(at * 48, 48), 48), at // (steps // 2)
        own = whole[j * (1 - route) + at_x * route, at_z * (1 - route) + j * route, rows]
        total = own.astype(f32) + slabs[0, j, rows].astype(f32) + slabs[1, j, rows].astype(f32)
        some[j, rows] = total.astype(bf16)
        return carry

    lax.fori_loop(0, 4 * steps, add, 0)


def attend_backward(args, moe_part, cid):
    with_moe = moe_part is not None
    shapes = [((PAIR, D), bf16), ((8, D), f32), ((2, D, 2 * WIDTH), bf16)]
    scratch = [
        pltpu.VMEM((PAIR, D), f32),
        pltpu.VMEM((PAIR, D), f32),
        pltpu.VMEM((4, ROWS, 2 * WIDTH), bf16),
        pltpu.VMEM((3, ROWS, 2 * WIDTH), bf16),
        pltpu.VMEM((2, 4, 80, 384), bf16),
    ]
    slab = args[-1].shape[2:]
    shapes.append(((4,) + slab, bf16))
    scratch += sum_scratch(False, 80)
    scratch += [pltpu.VMEM((2, 4) + slab, bf16), pltpu.VMEM((2, 2, 4, 128, FE), bf16)]
    scratch += dma_sems(4, 8) + [pltpu.VMEM((ROWS, 2 * WIDTH), bf16)] + dma_sems(3)
    in_specs = [VMEM] * len(args)
    if with_moe:
        args, in_specs = args + (moe_part,), in_specs + [VMEM]
        shapes.append(((4, 80, 384), bf16))
        scratch += [pltpu.VMEM((3, 80, 384), bf16)] + dma_sems(3, 3)
        scratch += [pltpu.VMEM((4, 80, 384), bf16)] + dma_sems(1)
    return pl.pallas_call(
        functools.partial(attend_backward_kernel, with_moe),
        out_shape=[jax.ShapeDtypeStruct(*s) for s in shapes],
        in_specs=in_specs,
        out_specs=[VMEM] * len(shapes),
        scratch_shapes=scratch,
        compiler_params=params(cid, 56),
        name="attend_backward",
    )(*args)


def shards(boundary, routes, lengths, ln_gains, ln_biases, w_qkv, w_out, w_router, w_in, w_exp_out):
    core = lax.axis_index("core")
    high = lax.axis_index("x") // 2

    def pick(value, at, axis):
        return lax.dynamic_index_in_dim(value, at, axis, keepdims=False)

    halves = jnp.stack(
        [
            w_qkv[:, :, 1:].reshape(2, 24, 384),
            jnp.concatenate([w_qkv[:, :, 0], w_out.transpose(0, 2, 1)], axis=2),
        ],
        axis=1,
    )

    stacked = jnp.stack([w_in, w_exp_out.transpose(0, 1, 3, 2)], axis=2).reshape(384, 2, FE)
    tiny = jnp.concatenate([ln_gains, ln_biases, w_router.transpose(0, 2, 1)], axis=1)
    tiny = jnp.pad(tiny.transpose(1, 0, 2).reshape(8, 48), ((0, 8), (0, 384 - 48)))
    attn_one, attn_zero = halves[1].reshape(48, 384), halves[0].reshape(48, 384)
    own_half = jnp.concatenate([pick(stacked, core, 1), attn_one, attn_zero, tiny])
    got_half = cross(jnp.concatenate([pick(stacked, 1 - core, 1), attn_one, attn_zero, tiny]), 0)
    low_half = jnp.where(core == 0, own_half, got_half)
    high_half = jnp.where(core == 0, got_half, own_half)
    chip = jnp.concatenate(
        [low_half[:480].reshape(20, 24, FE), high_half[:480].reshape(20, 24, FE)], axis=1
    )
    later = jnp.concatenate([chip[0:8], chip[16:18]]).reshape(480, FE)
    urgent = jnp.concatenate([chip[18:20].reshape(96, FE), low_half[480:496], high_half[480:496]])

    turned = jnp.pad(
        routes[0].astype(bf16).transpose(0, 2, 1), ((0, 0), (0, 14), (0, D - ROWS))
    )
    images = jnp.concatenate([boundary[0], turned], axis=1)
    got_images, packs, some = start_exchange(images, urgent, later)
    packs = packs.reshape(16, 128, 384)
    tiny = packs[:, 96:128].reshape(32, 16, 384)[:, 0:8, 0:48].reshape(32, 8, 2, 24).transpose(2, 1, 0, 3).reshape(2, 8, D)
    smalls = [tiny[0].astype(f32), tiny[1].astype(f32)]

    live = jnp.arange(ROWS, dtype=jnp.int32)[None, :] < lengths[:, None]
    dead = jnp.where(live.reshape(1, KEYS), 0.0, -1e30).astype(f32)
    chip_live = lax.dynamic_slice_in_dim(live, 2 * lax.axis_index("zl"), 2, 0)
    own_live = pick(chip_live, core, 0)

    x0 = got_images[:, 0, 0:ROWS].reshape(PAIR, D)
    cotangent = jnp.where(chip_live[:, :, None], got_images[:, 1, 0:ROWS], 0).reshape(PAIR, D)
    route_rows = [
        got_images[:, kind, ROWS : ROWS + 2, 0:ROWS].transpose(1, 0, 2).reshape(2, PAIR).astype(f32)
        for kind in range(2)
    ]
    route_cols = [rows.T for rows in route_rows]

    attn_w0 = packs[:, 0:96]
    q0, kv0, mixed0, att0, experts_zero = attend_forward(x0, (), smalls[0], attn_w0, dead, some, 3)
    experts_zero = experts_zero.reshape(16, 480, 384)
    attn_w1 = experts_zero[:, 384:480]
    shard, att0 = lax.optimization_barrier((chip[8:16].reshape(384, FE), att0))
    experts_one = lax.all_gather(shard, CHIPS, axis=0)
    moe0 = experts_forward(x0, att0, smalls[0], route_cols[0], experts_zero, 4)
    q1, kv1, mixed1, att1, x1 = attend_forward(
        x0, (att0, moe0), smalls[1], attn_w1, dead, None, 5
    )
    back, moe_part, grad_experts1 = experts_backward(
        x1, att1, smalls[1], route_cols[1], cotangent, None, None, experts_one, 6
    )
    grad_x1, grad_small1, grad_attn1, some, moe1 = attend_backward(
        (x1, att1, smalls[1], route_rows[1], cotangent, back, q1, kv1, mixed1, dead, attn_w1, grad_experts1.reshape(4, 4, 384, FE)),
        moe_part,
        7,
    )
    back, sums1, grad_experts0 = experts_backward(
        x0, att0, smalls[0], route_cols[0], grad_x1, grad_attn1, some, experts_zero, 8
    )
    grad_x0, grad_small0, grad_attn0, some = attend_backward(
        (x0, att0, smalls[0], route_rows[0], grad_x1, back, q0, kv0, mixed0, dead, attn_w0, grad_experts0.reshape(4, 4, 480, FE)),
        None,
        9,
    )

    def own_block(value):
        return pick(value, core, 0)

    def unchunk(value):
        return value.reshape(2, 2, 80, 384).transpose(0, 2, 1, 3).reshape(ROWS, D).astype(f32)

    y1 = own_block(x1.reshape(2, ROWS, D)).astype(f32) + unchunk(own_block(att1)) + unchunk(moe1)
    mine = jnp.stack([own_block(grad_x0.reshape(2, ROWS, D)).astype(f32), y1])
    mine = jnp.where(own_live[None, :, None], mine, 0.0)
    kept, sent = pick(mine, high, 0), pick(mine, 1 - high, 0).astype(bf16)

    tiny = jnp.stack([grad_small0, grad_small1]).astype(bf16).reshape(2, 8, 16, 2, 24)
    tiny = tiny.transpose(0, 2, 3, 1, 4).reshape(2, 16, 16, 24)
    tiny = jnp.pad(tiny, ((0, 0), (0, 0), (0, 0), (0, 384 - 24)))
    packs = jnp.concatenate([grad_attn0.reshape(2, 16, 48, 384), tiny], axis=2)
    own, landed, got1, own0, got0 = end_exchange(packs, sent, sums1, some)
    landed = landed.astype(f32)
    ends = jnp.where(high == 0, jnp.stack([kept, landed]), jnp.stack([landed, kept]))

    def own_lines(sums):
        return lax.dynamic_slice_in_dim(sums.reshape(-1, 48, FE), 24 * core, 24, 1).astype(f32)

    own0, got0, own1, got1 = (own_lines(sums) for sums in (own0, got0, sums1, got1))
    attn1 = own0[8:10] + got0[8:10]

    def both_halves(own_sum, got_sum):
        first = jnp.where(core == 0, own_sum, got_sum)
        second = jnp.where(core == 0, got_sum, own_sum)
        return jnp.concatenate([first, second], axis=2).reshape(EXPERTS, 2, 24, D)

    full = jnp.stack([both_halves(own0[0:8], got0[0:8]), both_halves(own1, got1)])
    attn0 = lax.dynamic_slice_in_dim(own, 24 * core, 24, 1)
    attn = jnp.stack([attn0, attn1])
    grad_w_qkv = jnp.concatenate([attn[:, 1, :, None, :WIDTH], attn[:, 0].reshape(2, 24, 2, WIDTH)], axis=2)
    grad_w_out = attn[:, 1, :, WIDTH:].transpose(0, 2, 1)
    tiny = lax.dynamic_slice_in_dim(own[:, 48:64, 0:24], 8 * core, 8, 1)
    return (
        ends[None],
        tiny[:, 0:2],
        tiny[:, 2:4],
        grad_w_qkv,
        grad_w_out,
        tiny[:, 4:8].transpose(0, 2, 1),
        full[:, :, 0],
        full[:, :, 1].transpose(0, 1, 3, 2),
    )


def solution(mesh):
    fine = Mesh(mesh.devices.reshape(4, 2, 2, 2, 4), CHIPS + ("core", "tp"))
    section, ctx = ("x", "zh"), ("zl", "core")
    every = section + ctx
    return jax.shard_map(
        shards,
        mesh=fine,
        in_specs=(
            P(ctx, section, None, None),
            P(ctx, section, None, None),
            P(),
            P(None, None, every),
            P(None, None, every),
            P(None, every, None, "tp"),
            P(None, "tp", every),
            P(None, every, None),
            P(None, None, every, "tp"),
            P(None, None, "tp", every),
        ),
        out_specs=(
            P(ctx, section, None, None),
            P(None, None, every),
            P(None, None, every),
            P(None, every, None, "tp"),
            P(None, "tp", every),
            P(None, every, None),
            P(None, None, every, "tp"),
            P(None, None, "tp", every),
        ),
        check_vma=False,
    )
```

```python
import functools

import jax
import jax.numpy as jnp
from jax import lax
from jax.experimental import pallas as pl
from jax.experimental.pallas import tpu as pltpu
from jax.sharding import Mesh
from jax.sharding import PartitionSpec as P

D = 768
HD = 64
HEADS = 3
ROWS = 160
PAIR = 320
KEYS = 640
FE = 384
EXPERTS = 4
EPS = 1e-06
WIDTH = HEADS * HD
MESH = pl.DeviceIdType.MESH
CHIPS = ("x", "zh", "zl")
f32, bf16 = jnp.float32, jnp.bfloat16
VMEM = pl.BlockSpec(memory_space=pltpu.VMEM)
SMEM = pl.BlockSpec(memory_space=pltpu.SMEM)
NN = (((1,), (0,)), ((), ()))
NT = (((1,), (1,)), ((), ()))
TN = (((0,), (0,)), ((), ()))


def dot(a, b, dims):
    return lax.dot_general(a, b, dims, preferred_element_type=f32)


def dot_split(a, b, dims):
    high = a.astype(bf16)
    return dot(high, b, dims) + dot((a - high.astype(f32)).astype(bf16), b, dims)


def params(cid, mib):
    return pltpu.CompilerParams(
        collective_id=cid, has_side_effects=True, vmem_limit_bytes=mib * 2**20
    )


ANY = pl.BlockSpec(memory_space=pl.ANY)


def arrive(peers):
    barrier = pltpu.get_barrier_semaphore()
    for peer in peers:
        pl.semaphore_signal(barrier, inc=1, device_id=peer, device_id_type=MESH)


def all_here(count):
    pl.semaphore_wait(pltpu.get_barrier_semaphore(), count)


def dma_sems(*counts):
    return [pltpu.SemaphoreType.DMA((count,)) for count in counts for _ in range(2)]


def remote(src, dst, send, recv, peer):
    return pltpu.make_async_remote_copy(
        src_ref=src, dst_ref=dst, send_sem=send, recv_sem=recv, device_id=peer, device_id_type=MESH
    )


def tp_peers():
    return [{"tp": (lax.axis_index("tp") + k) % 4} for k in (1, 2, 3)]


def pieces_of(rows):
    return (pl.ds(0, 48), pl.ds(48, rows - 48))


def sum_cores(part, crossed, send, recv):
    core = lax.axis_index("core")
    return [
        remote(part.at[1 - core, :, rows], crossed.at[:, rows], send.at[p], recv.at[p], {"core": 1 - core})
        for p, rows in enumerate(pieces_of(part.shape[2]))
    ]


def sum_terms(both, part, landed, send, recv):
    block = lax.axis_index("core") if both else 0
    return [
        [
            remote(
                part.at[block, peer["tp"], rows], landed.at[k, rows],
                send.at[3 * p + k], recv.at[3 * p + k], peer,
            )
            for k, peer in enumerate(tp_peers())
        ]
        for p, rows in enumerate(pieces_of(part.shape[2]))
    ]


def sum_results(out, send, recv):
    core, tp = lax.axis_index("core"), lax.axis_index("tp")
    return [
        [
            remote(out.at[core, tp, rows], out.at[core, tp, rows], send.at[3 * p + k], recv.at[3 * p + k], peer)
            for k, peer in enumerate(tp_peers())
        ]
        for p, rows in enumerate(pieces_of(out.shape[2]))
    ]


def sum_cross(out, send, recv):
    core, tp = lax.axis_index("core"), lax.axis_index("tp")
    return [
        [
            remote(
                out.at[core, at, rows], out.at[core, at, rows],
                send.at[4 * p + k], recv.at[4 * p + k], {"core": 1 - core},
            )
            for k, at in enumerate([(tp + 4 - k) % 4 for k in range(4)])
        ]
        for p, rows in enumerate(pieces_of(out.shape[2]))
    ]


def sum_start(both, out, part, landed, rs, rr, gs, gr, cs, cr, crossed=None, ps=None, pr=None):
    terms = sum_terms(both, part, landed, rs, rr)
    if both:
        core = lax.axis_index("core")
        pres = sum_cores(part, crossed, ps, pr)
        for pre in pres:
            pre.start()
    for p, rows in enumerate(pieces_of(part.shape[2])):
        if both:
            pres[p].wait_recv()
            for j in range(4):
                total = part[core, j, rows].astype(f32) + crossed[j, rows].astype(f32)
                part[core, j, rows] = total.astype(bf16)
        for copy in terms[p]:
            copy.start()


def sum_middle(both, out, part, landed, rs, rr, gs, gr, cs, cr, *pre):
    core, tp = lax.axis_index("core"), lax.axis_index("tp")
    terms, results, crosses = sum_terms(both, part, landed, rs, rr), sum_results(out, gs, gr), sum_cross(out, cs, cr)
    for p, rows in enumerate(pieces_of(part.shape[2])):
        total = part[core if both else 0, tp, rows].astype(f32)
        for k, copy in enumerate(terms[p]):
            copy.wait_recv()
            total = total + landed[k, rows].astype(f32)
        out[core, tp, rows] = total.astype(bf16)
        for copy in results[p]:
            copy.start()
        crosses[p][0].start()


def sum_end(both, out, part, landed, rs, rr, gs, gr, cs, cr, *pre):
    terms, results, crosses = sum_terms(both, part, landed, rs, rr), sum_results(out, gs, gr), sum_cross(out, cs, cr)
    for p in range(2):
        for k in range(3):
            results[p][k].wait_recv()
            crosses[p][k + 1].start()
    for p in range(2):
        for copy in crosses[p]:
            copy.wait()
        for copy in terms[p] + results[p]:
            copy.wait_send()
    if both:
        for copy in sum_cores(part, *pre):
            copy.wait_send()


def sum_scratch(both, rows):
    scratch = [
        pltpu.VMEM((2 if both else 1, 4, rows, 384), bf16),
        pltpu.VMEM((3, rows, 384), bf16),
    ] + dma_sems(6, 6, 8)
    if both:
        scratch += [pltpu.VMEM((4, rows, 384), bf16)] + dma_sems(2)
    return scratch


def chip_peers():
    core, zl = lax.axis_index("core"), lax.axis_index("zl")
    return {"core": 1 - core}, {"zl": 1 - zl}, zl * 2 + core


def cross_kernel(own, out, send, recv):
    other = {"core": 1 - lax.axis_index("core")}
    arrive([other])
    all_here(1)
    copy = remote(own, out, send.at[0], recv.at[0], other)
    copy.start()
    copy.wait()


def cross(own, cid):
    return pl.pallas_call(
        cross_kernel,
        out_shape=jax.ShapeDtypeStruct(own.shape, own.dtype),
        in_specs=[VMEM],
        out_specs=VMEM,
        scratch_shapes=dma_sems(1),
        compiler_params=params(cid, 8),
        name="cross",
    )(own)


def places():
    return lax.axis_index("x"), lax.axis_index("zh") * 2 + lax.axis_index("zl")


def axis_peer(along_x, k):
    x, z = places()
    if along_x:
        return {"x": (x + k) % 4}, (x + k) % 4
    to = (z + k) % 4
    return {"zh": to // 2, "zl": to % 2}, to


def half(rows, route):
    return pl.ds(route * (rows // 2), rows // 2)


def line(whole, route, second, rows):
    return whole.at[:, second, rows] if route == 0 else whole.at[second, :, rows]


def axis_peers(*ks):
    return [axis_peer(along_x, k)[0] for along_x in (True, False) for k in ks]


def start_kernel(
    images, urgent, later, out_images, all_urgent, all_later, own_sem, im_s, im_r, u1_s, u1_r, u2_s, u2_r, l_s, l_r
):
    core = lax.axis_index("core")
    at_x, at_z = places()
    high = at_x // 2
    other = {"core": 1 - core}
    arrive(axis_peers(1, 2, 3) + [other])
    all_urgent[at_x, at_z] = urgent[...]
    out_images[core, high] = images[high]
    own = pltpu.make_async_copy(later, all_later.at[at_x, at_z], own_sem)
    own.start()
    all_here(7)
    firsts, seconds, laters = [], [], []
    for route in range(2):
        b = (at_z, at_x)[route]
        rows, late = half(urgent.shape[0], route), half(later.shape[0], route)
        for k in range(1, 4):
            peer, _ = axis_peer(route == 0, k)
            n = 3 * route + k - 1
            firsts.append(
                remote(urgent.at[rows], all_urgent.at[at_x, at_z, rows], u1_s.at[n], u1_r.at[n], peer)
            )
            laters.append(
                remote(later.at[late], all_later.at[at_x, at_z, late], l_s.at[n], l_r.at[n], peer)
            )
            slabs = line(all_urgent, route, b, rows)
            seconds.append(remote(slabs, slabs, u2_s.at[n], u2_r.at[n], axis_peer(route == 1, k)[0]))
    swap = remote(images.at[1 - high], out_images.at[core, high], im_s.at[0], im_r.at[0], {"x": (at_x + 2) % 4})
    kept = remote(images.at[high], out_images.at[core, high], im_s.at[1], im_r.at[1], other)
    passed = remote(
        out_images.at[core, 1 - high], out_images.at[core, 1 - high], im_s.at[2], im_r.at[2], other
    )
    for copy in firsts + [swap, kept] + laters:
        copy.start()
    for copy in firsts:
        copy.wait_recv()
    for copy in seconds:
        copy.start()
    swap.wait_recv()
    passed.start()
    for copy in seconds + laters + [kept, passed]:
        copy.wait()
    for copy in firsts + [swap]:
        copy.wait_send()
    own.wait()


def start_exchange(images, urgent, later):
    return pl.pallas_call(
        start_kernel,
        out_shape=[
            jax.ShapeDtypeStruct(s, bf16)
            for s in ((2,) + images.shape, (4, 4) + urgent.shape, (4, 4) + later.shape)
        ],
        in_specs=[VMEM] * 3,
        out_specs=[VMEM, VMEM, ANY],
        scratch_shapes=[pltpu.SemaphoreType.DMA] + dma_sems(3, 6, 6, 6),
        compiler_params=params(1, 56),
        name="start_exchange",
    )(images, urgent, later)


def spread_near(whole, send, recv):
    copies = []
    for route in range(2):
        slabs = line(whole, route, places()[1 - route], half(whole.shape[2], route))
        for n, k in enumerate((1, 3)):
            at, peer = 2 * route + n, axis_peer(route == 1, k)[0]
            copies.append(remote(slabs, slabs, send.at[at], recv.at[at], peer))
    return copies


def spread_far(whole, send, recv):
    copies = []
    size = whole.shape[2] // 2
    cut = size // 32 * 16 + size % 32
    for route in range(2):
        b = places()[1 - route]
        for n, k in enumerate((1, 3)):
            rows = pl.ds(route * size + n * cut, size - cut if n else cut)
            slabs = line(whole, route, (b + 4 - k) % 4, rows)
            at, peer = 4 + 2 * route + n, axis_peer(route == 1, k)[0]
            copies.append(remote(slabs, slabs, send.at[at], recv.at[at], peer))
    return copies


def part_rows(rows, route, n):
    size = rows // 2
    cut = size // 32 * 16 + size % 32
    return pl.ds(route * size + n * cut, size - cut if n else cut)


def toward_far(whole, passing, route, send, recv):
    copies, b = [], places()[1 - route]
    for n, k in enumerate((1, 3)):
        rows = part_rows(whole.shape[2], route, n)
        target = passing.at[route, n, :, 0 : rows.size]
        at, peer = 2 * route + n, axis_peer(route == 1, k)[0]
        copies.append(remote(line(whole, route, (b + 2) % 4, rows), target, send.at[at], recv.at[at], peer))
    return copies


def toward_near(whole, passing, landed, route, send, recv):
    copies, b = [], places()[1 - route]
    for n, k in enumerate((1, 3)):
        rows, others = (part_rows(whole.shape[2], route, m) for m in (n, 1 - n))
        at, peer = 4 * route + 2 * n, axis_peer(route == 1, k)[0]
        copies += [
            remote(passing.at[route, n, :, 0 : rows.size], landed.at[n, :, rows], send.at[at], recv.at[at], peer),
            remote(
                line(whole, route, (b + k) % 4, others), landed.at[n, :, others],
                send.at[at + 1], recv.at[at + 1], peer,
            ),
        ]
    return copies


def add_passing(whole, passing, route):
    x, z = places()
    b = (z, x)[route]
    for n, k in enumerate((1, 3)):
        rows, to = part_rows(whole.shape[2], route, n), (b + k) % 4

        def add(j, carry, n=n, rows=rows, to=to):
            own = whole[j, to, rows] if route == 0 else whole[to, j, rows]
            total = passing[route, n, j, 0 : rows.size].astype(f32) + own.astype(f32)
            passing[route, n, j, 0 : rows.size] = total.astype(bf16)
            return carry

        lax.fori_loop(0, 4, add, 0)


def last_copies(some, slabs, send, recv):
    copies = []
    for route in range(2):
        rows = half(some.shape[1], route)
        for k in range(1, 4):
            peer, at = axis_peer(route == 0, k)
            n = 3 * route + k - 1
            copies.append(remote(some.at[at, rows], slabs.at[k - 1, rows], send.at[n], recv.at[n], peer))
    return copies


def add_slabs(some, slabs, out):
    x, z = places()
    steps = some.shape[1] // 48

    def add(i, carry):
        rows, route = pl.ds(pl.multiple_of(i * 48, 48), 48), i // (steps // 2)
        total = some[x * (1 - route) + z * route, rows].astype(f32)
        for k in range(3):
            total = total + slabs[k, rows].astype(f32)
        out[rows] = total.astype(bf16)
        return carry

    lax.fori_loop(0, steps, add, 0)


def end_kernel(
    part, image, half_sum, some, some_attn, out, out_image, out_half, own_sum, other_sum,
    landed, sums, pieces, mids, lands, slabs, attn_slabs, cx_s, cx_r, sl_s, sl_r, at_s, at_r, p1_s, p1_r, p2_s, p2_r,
):
    core, x = lax.axis_index("core"), lax.axis_index("x")
    other = {"core": 1 - core}
    arrive(axis_peers(1, 2, 3) + [other])
    all_here(7)
    crossing = remote(part.at[1 - core], landed, cx_s.at[0], cx_r.at[0], other)
    crossing.start()
    lasts = last_copies(some, slabs, sl_s, sl_r)
    firsts, seconds = [], []
    for route in range(2):
        rows = half(64, route)
        for k in range(1, 4):
            peer, at = axis_peer(route == 0, k)
            n = 3 * route + k - 1
            lasts.append(
                remote(some_attn.at[route, at], attn_slabs.at[route, k - 1], at_s.at[n], at_r.at[n], peer)
            )
            seconds.append(remote(mids.at[at, rows], lands.at[k - 1, rows], p2_s.at[n], p2_r.at[n], peer))
            peer, at = axis_peer(route == 1, k)
            firsts.append(
                remote(line(sums, route, at, rows), pieces.at[k - 1, :, rows], p1_s.at[n], p1_r.at[n], peer)
            )
    swap = remote(image, out_image, cx_s.at[1], cx_r.at[1], {"x": (x + 2) % 4})
    halves = remote(half_sum, out_half, cx_s.at[2], cx_r.at[2], other)
    for copy in lasts + [halves]:
        copy.start()
    crossing.wait()

    def add(i, carry):
        total = part[core, i // 4, i % 4].astype(f32) + landed[i // 4, i % 4].astype(f32)
        sums[i // 4, i % 4] = total.astype(bf16)
        return carry

    lax.fori_loop(0, 16, add, 0)
    for copy in firsts + [swap]:
        copy.start()
    for copy in firsts:
        copy.wait_recv()
    at_x, at_z = places()
    for route in range(2):
        rows = half(64, route)

        def gather(j, carry, route=route, rows=rows):
            total = (sums[j, at_z, rows] if route == 0 else sums[at_x, j, rows]).astype(f32)
            for k in range(3):
                total = total + pieces[k, j, rows].astype(f32)
            mids[j, rows] = total.astype(bf16)
            return carry

        lax.fori_loop(0, 4, gather, 0)
    for copy in seconds:
        copy.start()
    for copy in lasts:
        copy.wait()
    add_slabs(some, slabs, own_sum)
    for route in range(2):
        attn = some_attn[route, places()[route]].astype(f32)
        for k in range(3):
            attn = attn + attn_slabs[route, k].astype(f32)
        first = 384 + 48 * route
        own_sum[first : first + 48] = attn.astype(bf16)
    final = remote(own_sum, other_sum, cx_s.at[3], cx_r.at[3], other)
    final.start()
    for copy in seconds:
        copy.wait()
    for route in range(2):
        rows = half(64, route)
        total = mids[places()[route], rows].astype(f32)
        for k in range(3):
            total = total + lands[k, rows].astype(f32)
        out[core, rows] = total
    given = remote(out.at[core], out.at[core], cx_s.at[4], cx_r.at[4], other)
    given.start()
    for copy in firsts:
        copy.wait_send()
    for copy in (given, final, swap, halves):
        copy.wait()


def end_exchange(part, image, half_sum, some, some_attn):
    slab = (480, FE)
    scratch = [(4, 4, 64, FE)] * 2 + [(3, 4, 64, FE), (4, 64, FE), (3, 64, FE)]
    scratch += [(3,) + some.shape[1:], (2, 3, 48, FE)]
    return pl.pallas_call(
        end_kernel,
        out_shape=[jax.ShapeDtypeStruct((2, 64, FE), f32)]
        + [jax.ShapeDtypeStruct(s, bf16) for s in (image.shape, half_sum.shape, slab, slab)],
        in_specs=[VMEM] * 5,
        out_specs=[VMEM] * 5,
        scratch_shapes=[pltpu.VMEM(s, bf16) for s in scratch] + dma_sems(5, 6, 6, 6, 6),
        compiler_params=params(2, 56),
        name="end_exchange",
    )(part, image, half_sum, some, some_attn)


def block_rows(ref, block):
    top = jnp.concatenate([ref[block, 0, 0:80], ref[block, 1, 0:80]], axis=1)
    low = jnp.concatenate([ref[block, 2, 0:80], ref[block, 3, 0:80]], axis=1)
    return jnp.concatenate([top, low], axis=0).astype(f32)


def pair_rows(ref):
    return jnp.concatenate([block_rows(ref, 0), block_rows(ref, 1)], axis=0)


def put_chunks(ref, block, value, first=0):
    for j in range(4):
        r, c = 80 * (j // 2), 384 * (j % 2)
        ref[block, j, first : first + 80] = value[r : r + 80, c : c + 384]


def norm_parts(rows):
    centered = rows - jnp.mean(rows, axis=-1, keepdims=True)
    scale = lax.rsqrt(jnp.mean(centered * centered, axis=-1, keepdims=True) + EPS)
    return centered * scale, scale


def norm_back(grad, unit, scale, gain):
    inner = grad * gain
    return scale * (
        inner
        - jnp.mean(inner, axis=-1, keepdims=True)
        - unit * jnp.mean(inner * unit, axis=-1, keepdims=True)
    )


def softmax(logits, axis):
    top = jnp.max(logits, axis=axis, keepdims=True)
    powers = jnp.exp(logits - top)
    return powers / jnp.sum(powers, axis=axis, keepdims=True)


def own_rows(core):
    return pl.ds(pl.multiple_of(core * ROWS, ROWS), ROWS)


def head(value, h):
    return value[:, HD * h : HD * h + HD]


def gelu_parts(u):
    c = 0.7978845608028654
    t = jnp.tanh(c * (u + 0.044715 * u * u * u))
    return 0.5 * u * (1.0 + t), t


def gelu_slope(u, t):
    c = 0.7978845608028654
    return 0.5 * (1.0 + t) + 0.5 * u * (1.0 - t * t) * (c * (1.0 + 3 * 0.044715 * u * u))


def attn_weights(weights):
    w_kv = weights[:, 0:48].reshape(D, 2 * WIDTH)
    w_q = weights[:, 48:96, :WIDTH].reshape(D, WIDTH)
    return w_kv, w_q, weights[:, 48:96, WIDTH:].reshape(D, WIDTH)


def attend_forward_kernel(follows, *refs):
    if follows:
        x, att_before, moe_before, small, weights, dead, q, kv, mixed, att, x_next, *scratch = refs
    else:
        x, small, weights, dead, ahead, _, q, kv, mixed, att, whole, all_ahead, *scratch = refs
        *scratch, sp_send, sp_recv, ah_send, ah_recv, own_sem = scratch
    part, landed, *sems, kv_send, kv_recv = scratch
    sums = (False, att, part, landed, *sems)
    core = lax.axis_index("core")
    other, across, me = chip_peers()
    arrive([other, across] + tp_peers())
    if not follows:
        arrive(axis_peers(1, 2, 3))
    if follows:
        x_next[...] = (x[...].astype(f32) + pair_rows(att_before) + pair_rows(moe_before)).astype(bf16)
        x = x_next
    unit, _ = norm_parts(x[own_rows(core)].astype(f32))
    normed = (unit * small[0:1] + small[2:3]).astype(bf16)
    w_kv, w_q, w_out_t = attn_weights(weights)
    kv[me] = dot(normed, w_kv, NN).astype(bf16)
    all_here(5 if follows else 11)
    far = (me + 2) % 4
    copies = [
        remote(kv.at[at], kv.at[at], kv_send.at[k], kv_recv.at[k], peer)
        for k, (at, peer) in enumerate(((me, across), (me, other), (far, other)))
    ]
    copies[0].start()
    copies[1].start()
    if not follows:
        nears = spread_near(whole, sp_send, sp_recv)
        fars = spread_far(whole, sp_send, sp_recv)
        at_x, at_z = places()
        aheads = [pltpu.make_async_copy(ahead, all_ahead.at[at_x, at_z], own_sem)]
        for route in range(2):
            rows = half(ahead.shape[0], route)
            for k in range(1, 4):
                n, peer = 3 * route + k - 1, axis_peer(route == 0, k)[0]
                aheads.append(
                    remote(ahead.at[rows], all_ahead.at[at_x, at_z, rows], ah_send.at[n], ah_recv.at[n], peer)
                )
        for copy in nears + aheads:
            copy.start()
    queries = dot(normed, w_q, NN).astype(bf16)
    q[...] = queries
    copies[0].wait_recv()
    copies[2].start()
    copies[1].wait_recv()
    copies[2].wait_recv()
    keys = kv[...].reshape(KEYS, 2 * WIDTH)
    outs = []
    for h in range(HEADS):
        scores = HD**-0.5 * dot(head(queries, h), head(keys, h), NT) + dead[...]
        probs = softmax(scores, -1).astype(bf16)
        outs.append(dot(probs, head(keys, HEADS + h), NN))
    heads = jnp.concatenate(outs, axis=1).astype(bf16)
    mixed[...] = heads
    put_chunks(part, 0, dot(heads, w_out_t, NT).astype(bf16))
    sum_start(*sums)
    sum_middle(*sums)
    if not follows:
        for copy in nears:
            copy.wait_recv()
        for copy in fars:
            copy.start()
    sum_end(*sums)
    for copy in copies:
        copy.wait_send()
    if not follows:
        for copy in fars + aheads:
            copy.wait()
        for copy in nears:
            copy.wait_send()


def attend_forward(x, before, small, weights, dead, some, ahead, cid):
    args = (x, *before, small, weights, dead)
    shapes = [(ROWS, WIDTH), (4, ROWS, 2 * WIDTH), (ROWS, WIDTH), (2, 4, 80, 384)]
    in_specs, out_specs = [VMEM] * len(args), [VMEM] * 5
    scratch = sum_scratch(False, 80) + dma_sems(3)
    if before:
        shapes.append((PAIR, D))
    else:
        args += (ahead, some)
        shapes += [some.shape, (4, 4) + ahead.shape]
        in_specs += [VMEM, ANY]
        out_specs[4:] = [ANY, ANY]
        scratch += dma_sems(8, 6) + [pltpu.SemaphoreType.DMA]
    return pl.pallas_call(
        functools.partial(attend_forward_kernel, bool(before)),
        out_shape=[jax.ShapeDtypeStruct(s, bf16) for s in shapes],
        in_specs=in_specs,
        out_specs=out_specs,
        scratch_shapes=scratch,
        input_output_aliases={} if before else {len(args) - 1: 4},
        compiler_params=params(cid, 56),
        name="attend_forward",
    )(*args)


def expert_weights(weights):
    block = weights[...]
    return block[:, 0:48].reshape(D, FE), block[:, 48:96].reshape(D, FE)


def experts_setup(x, att, small, routes, b, gates):
    unit, _ = norm_parts(x[...].astype(f32) + pair_rows(att))
    b[...] = (unit * small[1:2] + small[3:4]).astype(bf16)
    probs = softmax(dot(b[...], small[4:8].astype(bf16), NT), -1)
    ids = lax.broadcasted_iota(jnp.int32, (PAIR, EXPERTS), 1).astype(f32)
    named = (routes[:, 0:1] == ids) | (routes[:, 1:2] == ids)
    gates[...] = jnp.where(named, probs, 0.0)


def gate_of(gates, expert):
    ids = lax.broadcasted_iota(jnp.int32, (PAIR, EXPERTS), 1)
    return jnp.sum(jnp.where(ids == expert, gates[...], 0.0), axis=1, keepdims=True)


def experts_forward_kernel(
    x, att, small, routes, _, weights, result, ahead, b, gates, total, ah_send, ah_recv, out, part, landed, *sems
):
    expert = pl.program_id(0)
    sums = (True, out, part, landed, *sems)
    aheads = []
    for route in range(2):
        slabs = line(ahead, route, places()[1 - route], half(ahead.shape[2], route))
        for k in range(1, 4):
            n, peer = 3 * route + k - 1, axis_peer(route == 1, k)[0]
            aheads.append(remote(slabs, slabs, ah_send.at[n], ah_recv.at[n], peer))

    @pl.when(expert == 0)
    def _():
        arrive(tp_peers() + [{"core": 1 - lax.axis_index("core")}] + axis_peers(1, 2, 3))
        experts_setup(x, att, small, routes, b, gates)
        total[...] = jnp.zeros_like(total)
        all_here(10)
        for copy in aheads:
            copy.start()

    w_in, w_out_t = expert_weights(weights)
    u = dot(b[...], w_in, NN)
    active = gelu_parts(u)[0].astype(bf16).astype(f32)
    gated = (gate_of(gates, expert) * active).astype(bf16)
    total[...] += dot(gated, w_out_t, NT)

    @pl.when(expert == EXPERTS - 1)
    def _():
        for block in range(2):
            put_chunks(part, block, total[ROWS * block : ROWS * block + ROWS].astype(bf16))
        sum_start(*sums)
        sum_middle(*sums)
        sum_end(*sums)
        result[...] = out[...]
        for copy in aheads:
            copy.wait()


def fixed(shape):
    return pl.BlockSpec(shape, lambda e: (0,) * len(shape))


def experts_forward(x, att, small, routes, ahead, weights, cid):
    args = (x, att, small, routes)
    return pl.pallas_call(
        experts_forward_kernel,
        grid=(EXPERTS,),
        out_shape=[jax.ShapeDtypeStruct((2, 4, 80, 384), bf16), jax.ShapeDtypeStruct(ahead.shape, bf16)],
        in_specs=[fixed(a.shape) for a in args] + [ANY, pl.BlockSpec((16, 96, FE), lambda e: (0, e, 0))],
        out_specs=[fixed((2, 4, 80, 384)), ANY],
        scratch_shapes=[
            pltpu.VMEM((PAIR, D), bf16),
            pltpu.VMEM((PAIR, EXPERTS), f32),
            pltpu.VMEM((PAIR, D), f32),
        ]
        + dma_sems(6)
        + [pltpu.VMEM((2, 4, 80, 384), bf16)]
        + sum_scratch(True, 80),
        input_output_aliases={4: 1},
        compiler_params=params(cid, 56),
        name="experts_forward",
    )(*args, ahead, weights)


def experts_backward_kernel(
    x, att, small, routes, grad, extra, some, weights, result, moe_part, own_sum, some_attn, grad_w,
    b, gates, total, moe, gate_grads, gated_all, grad_u_all, out, part, landed, *sems,
):
    step = pl.program_id(0)
    sums = (True, out, part, landed, *sems)
    with_moe = moe_part is not None
    if not with_moe:
        *sems, slabs, slab_send, slab_recv, attn_slabs, at_send, at_recv = sems
        sums, lasts = (True, out, part, landed, *sems), last_copies(some, slabs, slab_send, slab_recv)
        for route in range(2):
            for k in range(1, 4):
                n, (peer, to) = 3 * route + k - 1, axis_peer(route == 1, k)
                slab = extra.at[0, :, to] if route == 0 else extra.at[1, to]
                lasts.append(remote(slab, attn_slabs.at[route, k - 1], at_send.at[n], at_recv.at[n], peer))

    @pl.when(step == 0)
    def _():
        arrive(tp_peers() + [{"core": 1 - lax.axis_index("core")}])
        if not with_moe:
            arrive(axis_peers(1, 2, 3))
        experts_setup(x, att, small, routes, b, gates)
        total[...] = jnp.zeros_like(total)
        gate_grads[...] = jnp.zeros_like(gate_grads)
        if with_moe:
            moe[...] = jnp.zeros_like(moe)
        all_here(4 if with_moe else 10)
        if not with_moe:
            for copy in lasts:
                copy.start()

    @pl.when(step < EXPERTS)
    def _():
        w_in, w_out_t = expert_weights(weights)
        u = dot(b[...], w_in, NN)
        act, t = gelu_parts(u)
        active = act.astype(bf16).astype(f32)
        gate = gate_of(gates, step)
        gated = (gate * active).astype(bf16)
        gated_all[step] = gated
        if with_moe:
            moe[...] += dot(gated, w_out_t, NT)
        back = dot(grad[...], w_out_t, NN)
        ids = lax.broadcasted_iota(jnp.int32, (PAIR, 128), 1)
        gate_grad = jnp.sum(back * active, axis=1, keepdims=True)
        gate_grads[...] = jnp.where(ids == step, gate_grad, gate_grads[...])
        grad_u = (gate * back * gelu_slope(u, t)).astype(bf16)
        grad_u_all[step] = grad_u
        total[...] += dot(grad_u, w_in, NT)

    @pl.when(step == EXPERTS - 1)
    def _():
        part[...] = jnp.zeros_like(part)
        pick = lax.broadcasted_iota(jnp.int32, (16, 128), 0) == lax.broadcasted_iota(jnp.int32, (16, 128), 1)
        pick = (pick & (lax.broadcasted_iota(jnp.int32, (16, 128), 0) < EXPERTS)).astype(f32).astype(bf16)
        for block in range(2):
            lines = slice(ROWS * block, ROWS * block + ROWS)
            put_chunks(part, block, total[lines].astype(bf16))
            part[block, 0, 80:96, 0:ROWS] = dot(pick, gate_grads[lines].astype(bf16), NT).astype(bf16)
            if with_moe:
                put_chunks(moe_part, block, moe[lines].astype(bf16))
        sum_start(*sums)

    @pl.when(step >= EXPERTS)
    def _():
        at = step - EXPERTS
        grad_w[:, 0:48] = dot(b[...], grad_u_all[at], TN).astype(bf16).reshape(16, 48, FE)
        grad_w[:, 48:96] = dot(grad[...], gated_all[at], TN).astype(bf16).reshape(16, 48, FE)

    @pl.when(step == EXPERTS + 1)
    def _():
        sum_middle(*sums)

    if not with_moe:

        @pl.when(step == 2 * EXPERTS - 2)
        def _():
            for copy in lasts:
                copy.wait()
            add_slabs(some, slabs, own_sum)
            at_x, at_z = places()
            for route in range(2):

                def add(j, carry, route=route):
                    attn = (extra[0, j, at_z] if route == 0 else extra[1, at_x, j]).astype(f32)
                    for k in range(3):
                        attn = attn + attn_slabs[route, k, j].astype(f32)
                    some_attn[route, j] = attn.astype(bf16)
                    return carry

                lax.fori_loop(0, 4, add, 0)

    @pl.when(step == 2 * EXPERTS - 1)
    def _():
        sum_end(*sums)
        result[...] = out[...]


def experts_backward(x, att, small, routes, grad, extra, some, weights, cid):
    args = (x, att, small, routes, grad)
    shapes = [(2, 4, 96, 384)]
    scratch = []
    if extra is None:
        shapes.append((2, 4, 80, 384))

        def kernel(*refs):
            experts_backward_kernel(*refs[:5], None, None, *refs[5:8], None, None, *refs[8:])
    else:
        args += (extra, some)
        slab = some.shape[1:]
        shapes += [slab, (2, 4, 48, FE)]
        scratch = [pltpu.VMEM((3,) + slab, bf16)] + dma_sems(6)
        scratch += [pltpu.VMEM((2, 3, 4, 48, FE), bf16)] + dma_sems(6)

        def kernel(*refs):
            experts_backward_kernel(*refs[:9], None, *refs[9:])

    blocks = [fixed(shape) for shape in shapes]
    return pl.pallas_call(
        kernel,
        grid=(2 * EXPERTS,),
        out_shape=[jax.ShapeDtypeStruct(s, bf16) for s in shapes + [(16, 96 * EXPERTS, FE)]],
        in_specs=[fixed(a.shape) for a in args]
        + [pl.BlockSpec((16, 96, FE), lambda s: (0, jnp.minimum(s, EXPERTS - 1), 0))],
        out_specs=blocks + [pl.BlockSpec((16, 96, FE), lambda s: (0, jnp.maximum(s - EXPERTS, 0), 0))],
        scratch_shapes=[
            pltpu.VMEM((PAIR, D), bf16),
            pltpu.VMEM((PAIR, EXPERTS), f32),
            pltpu.VMEM((PAIR, D), f32),
            pltpu.VMEM((PAIR, D), f32),
            pltpu.VMEM((PAIR, 128), f32),
            pltpu.VMEM((EXPERTS, PAIR, FE), bf16),
            pltpu.VMEM((EXPERTS, PAIR, FE), bf16),
            pltpu.VMEM((2, 4, 96, 384), bf16),
        ]
        + sum_scratch(True, 96)
        + scratch,
        compiler_params=params(cid, 56),
        name="experts_backward",
    )(*args, weights)


def attend_backward_kernel(with_moe, *refs):
    x, att, small, routes_t, grad, back, q, kv, mixed, dead, weights, whole, *refs = refs
    if with_moe:
        moe_part, *refs = refs
    grad_x, grad_small, grad_w, some, *refs = refs
    if with_moe:
        moe, *refs = refs
    grad_h, both_units, parts, kv_landed, back_one, part, landed, *sems = refs
    if with_moe:
        *sems, moe_landed, ms, mr, ns, nr, moe_crossed, ps, pr = sems
        moe_sums = (moe_part, moe_crossed, ps, pr)
    *sems, slabs, passing, fs, fr, ns2, nr2, kv_out, kv_send, kv_recv = sems
    fars = [toward_far(whole, passing, route, fs, fr) for route in range(2)]
    nears = [toward_near(whole, passing, slabs, route, ns2, nr2) for route in range(2)]
    sums = (False, back_one, part, landed, *sems)
    core, tp = lax.axis_index("core"), lax.axis_index("tp")
    other, across, me = chip_peers()
    far = (me + 2) % 4
    arrive([other, across] + tp_peers() + axis_peers(1, 3))
    all_here(9)
    for copy in fars[1] + fars[0]:
        copy.start()
    unit, scale = norm_parts(x[...].astype(f32) + pair_rows(att))
    b = (unit * small[1:2] + small[3:4]).astype(bf16)
    router = small[4:8]
    chances = softmax(dot(router.astype(bf16), b, NT), 0)
    ids = lax.broadcasted_iota(jnp.int32, (EXPERTS, PAIR), 0).astype(f32)
    named = (routes_t[0:1] == ids) | (routes_t[1:2] == ids)
    tables = [back[block, 0, 80:96, 0:ROWS].astype(f32)[0:EXPERTS] for block in range(2)]
    gate_grads = jnp.where(named, jnp.concatenate(tables, axis=1), 0.0)
    grad_logits = chances * (gate_grads - jnp.sum(chances * gate_grads, axis=0, keepdims=True))
    grad_b = pair_rows(back) + dot_split(grad_logits, router.astype(bf16), TN)
    grad_h[...] = grad[...].astype(f32) + norm_back(grad_b, unit, scale, small[1:2])
    grad_att = grad_h[own_rows(core)].astype(bf16)
    w_kv, w_q, w_out_t = attn_weights(weights)
    grad_mixed = dot(grad_att, w_out_t, NN).astype(bf16)
    keys = kv[...].reshape(KEYS, 2 * WIDTH)
    queries = q[...]
    q_parts, k_parts, v_parts = [], [], []
    for h in range(HEADS):
        q_h, g_h = head(queries, h), head(grad_mixed, h)
        k_h, v_h = head(keys, h), head(keys, HEADS + h)
        probs = softmax(HD**-0.5 * dot(q_h, k_h, NT) + dead[...], -1)
        v_parts.append(dot(probs.astype(bf16), g_h, TN))
        grad_weights = dot(g_h, v_h, NT)
        grad_scores = probs * (
            grad_weights - jnp.sum(probs * grad_weights, axis=-1, keepdims=True)
        )
        grad_scores = grad_scores.astype(bf16)
        q_parts.append(HD**-0.5 * dot(grad_scores, k_h, NN))
        k_parts.append(HD**-0.5 * dot(grad_scores, q_h, TN))
    total = jnp.concatenate(k_parts + v_parts, axis=1).astype(bf16)
    parts[...] = total.reshape(4, ROWS, 2 * WIDTH)
    crosses = [
        remote(parts.at[(at + 1 - 2 * core) % 4], kv_landed.at[k], kv_send.at[k], kv_recv.at[k], other)
        for k, at in enumerate((me, far))
    ]
    onward = remote(kv_out, kv_landed.at[2], kv_send.at[2], kv_recv.at[2], across)
    crosses[1].start()
    crosses[0].start()
    if with_moe:
        pres = sum_cores(*moe_sums)
        for copy in pres:
            copy.start()
    crosses[1].wait_recv()
    kv_out[...] = (parts[far].astype(f32) + kv_landed[1].astype(f32)).astype(bf16)
    onward.start()
    if with_moe:
        for copy in pres:
            copy.wait_recv()
        for j in range(4):
            moe_sum = moe_part[core, j].astype(f32) + moe_crossed[j].astype(f32)
            moe_crossed[j] = moe_sum.astype(bf16)
        moe_terms = [
            remote(moe_crossed.at[peer["tp"]], moe_landed.at[k], ms.at[k], mr.at[k], peer)
            for k, peer in enumerate(tp_peers())
        ]
        for copy in moe_terms:
            copy.start()
    for route in (1, 0):
        for copy in fars[route]:
            copy.wait_recv()
        add_passing(whole, passing, route)
        for copy in nears[route]:
            copy.start()
    grad_q = jnp.concatenate(q_parts, axis=1).astype(bf16)
    grad_w[1, :, WIDTH:] = dot(grad_att, mixed[...], TN).astype(bf16)
    lanes = lax.broadcasted_iota(jnp.int32, (EXPERTS, PAIR), 1)
    own_lanes = (lanes < ROWS) == (core == 0)
    own = (lax.broadcasted_iota(jnp.int32, (PAIR, 1), 0) < ROWS) == (core == 0)
    kept = jnp.where(own, grad_b, 0.0)
    grad_small[1:2] = jnp.sum(kept * unit, axis=0, keepdims=True)
    grad_small[3:4] = jnp.sum(kept, axis=0, keepdims=True)
    grad_small[4:8] = dot_split(jnp.where(own_lanes, grad_logits, 0.0), b, NN)
    unit_one, scale_one = norm_parts(x[...].astype(f32))
    both_units[...] = unit_one
    normed = (both_units[own_rows(core)] * small[0:1] + small[2:3]).astype(bf16)
    crosses[0].wait_recv()
    onward.wait_recv()
    grad_kv = parts[me].astype(f32) + kv_landed[0].astype(f32) + kv_landed[2].astype(f32)
    grad_kv = grad_kv.astype(bf16)
    value = dot(grad_kv, w_kv, NT) + dot(grad_q, w_q, NT)
    put_chunks(part, 0, value.astype(bf16))
    sum_start(*sums)
    grad_w[0] = dot(normed, grad_kv, TN).astype(bf16)
    grad_w[1, :, :WIDTH] = dot(normed, grad_q, TN).astype(bf16)
    sum_middle(*sums)
    if with_moe:
        total = moe_crossed[tp].astype(f32)
        for k, copy in enumerate(moe_terms):
            copy.wait_recv()
            total = total + moe_landed[k].astype(f32)
        moe[tp] = total.astype(bf16)
        moe_results = [
            remote(moe.at[tp], moe.at[tp], ns.at[k], nr.at[k], {"tp": (tp + k + 1) % 4}) for k in range(3)
        ]
        for copy in moe_results:
            copy.start()
    sum_end(*sums)
    grad_a = pair_rows(back_one)
    grad_x[...] = (grad_h[...] + norm_back(grad_a, unit_one, scale_one, small[0:1])).astype(bf16)
    kept = jnp.where(own, grad_a, 0.0)
    grad_small[0:1] = jnp.sum(kept * unit_one, axis=0, keepdims=True)
    grad_small[2:3] = jnp.sum(kept, axis=0, keepdims=True)
    for copy in crosses + [onward]:
        copy.wait_send()
    if with_moe:
        for copy in pres:
            copy.wait_send()
        for copy in moe_terms:
            copy.wait_send()
        for copy in moe_results:
            copy.wait()
    for route in range(2):
        for copy in fars[route]:
            copy.wait_send()
        for copy in nears[route]:
            copy.wait()
    at_x, at_z = places()
    steps = some.shape[1] // 48

    def add(i, carry):
        j, at = i % 4, i // 4
        rows, route = pl.ds(pl.multiple_of(at * 48, 48), 48), at // (steps // 2)
        own = whole[j * (1 - route) + at_x * route, at_z * (1 - route) + j * route, rows]
        total = own.astype(f32) + slabs[0, j, rows].astype(f32) + slabs[1, j, rows].astype(f32)
        some[j, rows] = total.astype(bf16)
        return carry

    lax.fori_loop(0, 4 * steps, add, 0)


def attend_backward(args, moe_part, cid):
    with_moe = moe_part is not None
    shapes = [((PAIR, D), bf16), ((8, D), f32), ((2, D, 2 * WIDTH), bf16)]
    scratch = [
        pltpu.VMEM((PAIR, D), f32),
        pltpu.VMEM((PAIR, D), f32),
        pltpu.VMEM((4, ROWS, 2 * WIDTH), bf16),
        pltpu.VMEM((3, ROWS, 2 * WIDTH), bf16),
        pltpu.VMEM((2, 4, 80, 384), bf16),
    ]
    slab = args[-1].shape[2:]
    shapes.append(((4,) + slab, bf16))
    scratch += sum_scratch(False, 80)
    scratch += [pltpu.VMEM((2, 4) + slab, bf16), pltpu.VMEM((2, 2, 4, 128, FE), bf16)]
    scratch += dma_sems(4, 8) + [pltpu.VMEM((ROWS, 2 * WIDTH), bf16)] + dma_sems(3)
    in_specs = [VMEM] * len(args)
    if with_moe:
        args, in_specs = args + (moe_part,), in_specs + [VMEM]
        shapes.append(((4, 80, 384), bf16))
        scratch += [pltpu.VMEM((3, 80, 384), bf16)] + dma_sems(3, 3)
        scratch += [pltpu.VMEM((4, 80, 384), bf16)] + dma_sems(2)
    return pl.pallas_call(
        functools.partial(attend_backward_kernel, with_moe),
        out_shape=[jax.ShapeDtypeStruct(*s) for s in shapes],
        in_specs=in_specs,
        out_specs=[VMEM] * len(shapes),
        scratch_shapes=scratch,
        compiler_params=params(cid, 56),
        name="attend_backward",
    )(*args)


def shards(boundary, routes, lengths, ln_gains, ln_biases, w_qkv, w_out, w_router, w_in, w_exp_out):
    core = lax.axis_index("core")
    high = lax.axis_index("x") // 2

    def pick(value, at, axis):
        return lax.dynamic_index_in_dim(value, at, axis, keepdims=False)

    halves = jnp.stack(
        [
            w_qkv[:, :, 1:].reshape(2, 24, 384),
            jnp.concatenate([w_qkv[:, :, 0], w_out.transpose(0, 2, 1)], axis=2),
        ],
        axis=1,
    )

    stacked = jnp.stack([w_in, w_exp_out.transpose(0, 1, 3, 2)], axis=2).reshape(384, 2, FE)
    tiny = jnp.concatenate([ln_gains, ln_biases, w_router.transpose(0, 2, 1)], axis=1)
    tiny = jnp.pad(tiny.transpose(1, 0, 2).reshape(8, 48), ((0, 8), (0, 384 - 48)))
    attn_one, attn_zero = halves[1].reshape(48, 384), halves[0].reshape(48, 384)
    own_half = jnp.concatenate([pick(stacked, core, 1), attn_one, attn_zero, tiny])
    got_half = cross(jnp.concatenate([pick(stacked, 1 - core, 1), attn_one, attn_zero, tiny]), 0)
    low_half = jnp.where(core == 0, own_half, got_half)
    high_half = jnp.where(core == 0, got_half, own_half)
    chip = jnp.concatenate(
        [low_half[:480].reshape(20, 24, FE), high_half[:480].reshape(20, 24, FE)], axis=1
    )
    later, ahead = chip[0:8].reshape(384, FE), chip[16:18].reshape(96, FE)
    urgent = jnp.concatenate([chip[18:20].reshape(96, FE), low_half[480:496], high_half[480:496]])

    turned = jnp.pad(
        routes[0].astype(bf16).transpose(0, 2, 1), ((0, 0), (0, 14), (0, D - ROWS))
    )
    images = jnp.concatenate([boundary[0], turned], axis=1)
    got_images, packs, some = start_exchange(images, urgent, later)
    packs = packs.reshape(16, 128, 384)
    tiny = packs[:, 96:128].reshape(32, 16, 384)[:, 0:8, 0:48].reshape(32, 8, 2, 24).transpose(2, 1, 0, 3).reshape(2, 8, D)
    smalls = [tiny[0].astype(f32), tiny[1].astype(f32)]

    live = jnp.arange(ROWS, dtype=jnp.int32)[None, :] < lengths[:, None]
    dead = jnp.where(live.reshape(1, KEYS), 0.0, -1e30).astype(f32)
    chip_live = lax.dynamic_slice_in_dim(live, 2 * lax.axis_index("zl"), 2, 0)
    own_live = pick(chip_live, core, 0)

    x0 = got_images[:, 0, 0:ROWS].reshape(PAIR, D)
    cotangent = jnp.where(chip_live[:, :, None], got_images[:, 1, 0:ROWS], 0).reshape(PAIR, D)
    route_rows = [
        got_images[:, kind, ROWS : ROWS + 2, 0:ROWS].transpose(1, 0, 2).reshape(2, PAIR).astype(f32)
        for kind in range(2)
    ]
    route_cols = [rows.T for rows in route_rows]

    q0, kv0, mixed0, att0, experts_zero, ahead = attend_forward(x0, (), smalls[0], packs, dead, some, ahead, 3)
    experts_zero = experts_zero.reshape(16, 384, FE)
    shard, att0 = lax.optimization_barrier((chip[8:16].reshape(384, FE), att0))
    experts_one = lax.all_gather(shard, CHIPS, axis=0)
    moe0, attn_w1 = experts_forward(x0, att0, smalls[0], route_cols[0], ahead, experts_zero, 4)
    attn_w1 = attn_w1.reshape(16, 96, FE)
    q1, kv1, mixed1, att1, x1 = attend_forward(
        x0, (att0, moe0), smalls[1], attn_w1, dead, None, None, 5
    )
    back, moe_part, grad_experts1 = experts_backward(
        x1, att1, smalls[1], route_cols[1], cotangent, None, None, experts_one, 6
    )
    grad_x1, grad_small1, grad_attn1, some, moe1 = attend_backward(
        (x1, att1, smalls[1], route_rows[1], cotangent, back, q1, kv1, mixed1, dead, attn_w1, grad_experts1.reshape(4, 4, 384, FE)),
        moe_part,
        7,
    )
    grad_attn1 = grad_attn1.reshape(2, 4, 4, 48, FE)
    back, sums1, some_attn, grad_experts0 = experts_backward(
        x0, att0, smalls[0], route_cols[0], grad_x1, grad_attn1, some, experts_zero, 8
    )
    grad_x0, grad_small0, grad_attn0, some = attend_backward(
        (x0, att0, smalls[0], route_rows[0], grad_x1, back, q0, kv0, mixed0, dead, packs, grad_experts0.reshape(4, 4, 384, FE)),
        None,
        9,
    )

    def own_block(value):
        return pick(value, core, 0)

    def unchunk(value):
        return value.reshape(2, 2, 80, 384).transpose(0, 2, 1, 3).reshape(ROWS, D).astype(f32)

    y1 = own_block(x1.reshape(2, ROWS, D)).astype(f32) + unchunk(own_block(att1)) + unchunk(moe1)
    mine = jnp.stack([own_block(grad_x0.reshape(2, ROWS, D)).astype(f32), y1])
    mine = jnp.where(own_live[None, :, None], mine, 0.0)
    kept, sent = pick(mine, high, 0), pick(mine, 1 - high, 0).astype(bf16)

    tiny = jnp.stack([grad_small0, grad_small1]).astype(bf16).reshape(2, 8, 16, 2, 24)
    tiny = tiny.transpose(0, 2, 3, 1, 4).reshape(2, 16, 16, 24)
    tiny = jnp.pad(tiny, ((0, 0), (0, 0), (0, 0), (0, 384 - 24)))
    packs = jnp.concatenate([grad_attn0.reshape(2, 16, 48, 384), tiny], axis=2).reshape(2, 4, 4, 64, FE)
    own, landed, got1, own0, got0 = end_exchange(packs, sent, sums1, some, some_attn)
    landed = landed.astype(f32)
    ends = jnp.where(high == 0, jnp.stack([kept, landed]), jnp.stack([landed, kept]))

    def own_lines(sums):
        return lax.dynamic_slice_in_dim(sums.reshape(-1, 48, FE), 24 * core, 24, 1).astype(f32)

    own0, got0, own1, got1 = (own_lines(sums) for sums in (own0, got0, sums1, got1))
    attn1 = own0[8:10] + got0[8:10]

    def both_halves(own_sum, got_sum):
        first = jnp.where(core == 0, own_sum, got_sum)
        second = jnp.where(core == 0, got_sum, own_sum)
        return jnp.concatenate([first, second], axis=2).reshape(EXPERTS, 2, 24, D)

    full = jnp.stack([both_halves(own0[0:8], got0[0:8]), both_halves(own1, got1)])
    attn0 = lax.dynamic_slice_in_dim(own, 24 * core, 24, 1)
    attn = jnp.stack([attn0, attn1])
    grad_w_qkv = jnp.concatenate([attn[:, 1, :, None, :WIDTH], attn[:, 0].reshape(2, 24, 2, WIDTH)], axis=2)
    grad_w_out = attn[:, 1, :, WIDTH:].transpose(0, 2, 1)
    tiny = lax.dynamic_slice_in_dim(own[:, 48:64, 0:24], 8 * core, 8, 1)
    return (
        ends[None],
        tiny[:, 0:2],
        tiny[:, 2:4],
        grad_w_qkv,
        grad_w_out,
        tiny[:, 4:8].transpose(0, 2, 1),
        full[:, :, 0],
        full[:, :, 1].transpose(0, 1, 3, 2),
    )


def solution(mesh):
    fine = Mesh(mesh.devices.reshape(4, 2, 2, 2, 4), CHIPS + ("core", "tp"))
    section, ctx = ("x", "zh"), ("zl", "core")
    every = section + ctx
    return jax.shard_map(
        shards,
        mesh=fine,
        in_specs=(
            P(ctx, section, None, None),
            P(ctx, section, None, None),
            P(),
            P(None, None, every),
            P(None, None, every),
            P(None, every, None, "tp"),
            P(None, "tp", every),
            P(None, every, None),
            P(None, None, every, "tp"),
            P(None, None, "tp", every),
        ),
        out_specs=(
            P(ctx, section, None, None),
            P(None, None, every),
            P(None, None, every),
            P(None, every, None, "tp"),
            P(None, "tp", every),
            P(None, every, None),
            P(None, None, every, "tp"),
            P(None, None, "tp", every),
        ),
        check_vma=False,
    )
```

```python
import functools

import jax
import jax.numpy as jnp
from jax import lax
from jax.experimental import pallas as pl
from jax.experimental.pallas import tpu as pltpu
from jax.sharding import Mesh
from jax.sharding import PartitionSpec as P

D = 768
HD = 64
HEADS = 3
ROWS = 160
PAIR = 320
KEYS = 640
FE = 384
EXPERTS = 4
EPS = 1e-06
WIDTH = HEADS * HD
MESH = pl.DeviceIdType.MESH
CHIPS = ("x", "zh", "zl")
f32, bf16 = jnp.float32, jnp.bfloat16
VMEM = pl.BlockSpec(memory_space=pltpu.VMEM)
SMEM = pl.BlockSpec(memory_space=pltpu.SMEM)
NN = (((1,), (0,)), ((), ()))
NT = (((1,), (1,)), ((), ()))
TN = (((0,), (0,)), ((), ()))


def dot(a, b, dims):
    return lax.dot_general(a, b, dims, preferred_element_type=f32)


def dot_split(a, b, dims):
    high = a.astype(bf16)
    return dot(high, b, dims) + dot((a - high.astype(f32)).astype(bf16), b, dims)


def params(cid, mib):
    return pltpu.CompilerParams(
        collective_id=cid, has_side_effects=True, vmem_limit_bytes=mib * 2**20
    )


ANY = pl.BlockSpec(memory_space=pl.ANY)


def arrive(peers):
    barrier = pltpu.get_barrier_semaphore()
    for peer in peers:
        pl.semaphore_signal(barrier, inc=1, device_id=peer, device_id_type=MESH)


def all_here(count):
    pl.semaphore_wait(pltpu.get_barrier_semaphore(), count)


def dma_sems(*counts):
    return [pltpu.SemaphoreType.DMA((count,)) for count in counts for _ in range(2)]


def remote(src, dst, send, recv, peer):
    return pltpu.make_async_remote_copy(
        src_ref=src, dst_ref=dst, send_sem=send, recv_sem=recv, device_id=peer, device_id_type=MESH
    )


def tp_peers():
    return [{"tp": (lax.axis_index("tp") + k) % 4} for k in (1, 2, 3)]


def pieces_of(rows):
    return (pl.ds(0, 48), pl.ds(48, rows - 48))


def sum_cores(part, crossed, send, recv):
    core = lax.axis_index("core")
    return [
        remote(part.at[1 - core, :, rows], crossed.at[:, rows], send.at[p], recv.at[p], {"core": 1 - core})
        for p, rows in enumerate(pieces_of(part.shape[2]))
    ]


def sum_terms(both, part, landed, send, recv):
    block = lax.axis_index("core") if both else 0
    return [
        [
            remote(
                part.at[block, peer["tp"], rows], landed.at[k, rows],
                send.at[3 * p + k], recv.at[3 * p + k], peer,
            )
            for k, peer in enumerate(tp_peers())
        ]
        for p, rows in enumerate(pieces_of(part.shape[2]))
    ]


def sum_results(out, send, recv):
    core, tp = lax.axis_index("core"), lax.axis_index("tp")
    return [
        [
            remote(out.at[core, tp, rows], out.at[core, tp, rows], send.at[3 * p + k], recv.at[3 * p + k], peer)
            for k, peer in enumerate(tp_peers())
        ]
        for p, rows in enumerate(pieces_of(out.shape[2]))
    ]


def sum_cross(out, send, recv):
    core, tp = lax.axis_index("core"), lax.axis_index("tp")
    return [
        [
            remote(
                out.at[core, at, rows], out.at[core, at, rows],
                send.at[4 * p + k], recv.at[4 * p + k], {"core": 1 - core},
            )
            for k, at in enumerate([(tp + 4 - k) % 4 for k in range(4)])
        ]
        for p, rows in enumerate(pieces_of(out.shape[2]))
    ]


def sum_start(both, out, part, landed, rs, rr, gs, gr, cs, cr, crossed=None, ps=None, pr=None):
    terms = sum_terms(both, part, landed, rs, rr)
    if both:
        core = lax.axis_index("core")
        pres = sum_cores(part, crossed, ps, pr)
        for pre in pres:
            pre.start()
    for p, rows in enumerate(pieces_of(part.shape[2])):
        if both:
            pres[p].wait_recv()
            for j in range(4):
                total = part[core, j, rows].astype(f32) + crossed[j, rows].astype(f32)
                part[core, j, rows] = total.astype(bf16)
        for copy in terms[p]:
            copy.start()


def sum_middle(both, out, part, landed, rs, rr, gs, gr, cs, cr, *pre):
    core, tp = lax.axis_index("core"), lax.axis_index("tp")
    terms, results, crosses = sum_terms(both, part, landed, rs, rr), sum_results(out, gs, gr), sum_cross(out, cs, cr)
    for p, rows in enumerate(pieces_of(part.shape[2])):
        total = part[core if both else 0, tp, rows].astype(f32)
        for k, copy in enumerate(terms[p]):
            copy.wait_recv()
            total = total + landed[k, rows].astype(f32)
        out[core, tp, rows] = total.astype(bf16)
        for copy in results[p]:
            copy.start()
        crosses[p][0].start()


def sum_end(both, out, part, landed, rs, rr, gs, gr, cs, cr, *pre):
    terms, results, crosses = sum_terms(both, part, landed, rs, rr), sum_results(out, gs, gr), sum_cross(out, cs, cr)
    for p in range(2):
        for k in range(3):
            results[p][k].wait_recv()
            crosses[p][k + 1].start()
    for p in range(2):
        for copy in crosses[p]:
            copy.wait()
        for copy in terms[p] + results[p]:
            copy.wait_send()
    if both:
        for copy in sum_cores(part, *pre):
            copy.wait_send()


def sum_scratch(both, rows):
    scratch = [
        pltpu.VMEM((2 if both else 1, 4, rows, 384), bf16),
        pltpu.VMEM((3, rows, 384), bf16),
    ] + dma_sems(6, 6, 8)
    if both:
        scratch += [pltpu.VMEM((4, rows, 384), bf16)] + dma_sems(2)
    return scratch


def chip_peers():
    core, zl = lax.axis_index("core"), lax.axis_index("zl")
    return {"core": 1 - core}, {"zl": 1 - zl}, zl * 2 + core


def cross_kernel(own, out, send, recv):
    other = {"core": 1 - lax.axis_index("core")}
    arrive([other])
    all_here(1)
    copy = remote(own, out, send.at[0], recv.at[0], other)
    copy.start()
    copy.wait()


def cross(own, cid):
    return pl.pallas_call(
        cross_kernel,
        out_shape=jax.ShapeDtypeStruct(own.shape, own.dtype),
        in_specs=[VMEM],
        out_specs=VMEM,
        scratch_shapes=dma_sems(1),
        compiler_params=params(cid, 8),
        name="cross",
    )(own)


def places():
    return lax.axis_index("x"), lax.axis_index("zh") * 2 + lax.axis_index("zl")


def axis_peer(along_x, k):
    x, z = places()
    if along_x:
        return {"x": (x + k) % 4}, (x + k) % 4
    to = (z + k) % 4
    return {"zh": to // 2, "zl": to % 2}, to


def half(rows, route):
    return pl.ds(route * (rows // 2), rows // 2)


def uneven(rows, route):
    first = {128: 80, 64: 48}[rows]
    return pl.ds(first, rows - first) if route else pl.ds(0, first)


def line(whole, route, second, rows):
    return whole.at[:, second, rows] if route == 0 else whole.at[second, :, rows]


def axis_peers(*ks):
    return [axis_peer(along_x, k)[0] for along_x in (True, False) for k in ks]


def start_kernel(
    images, urgent, later, out_images, all_urgent, all_later, own_sem, im_s, im_r, u1_s, u1_r, u2_s, u2_r, l_s, l_r
):
    core = lax.axis_index("core")
    at_x, at_z = places()
    high = at_x // 2
    other = {"core": 1 - core}
    arrive(axis_peers(1, 2, 3) + [other])
    all_urgent[at_x, at_z] = urgent[...]
    out_images[core, high] = images[high]
    own = pltpu.make_async_copy(later, all_later.at[at_x, at_z], own_sem)
    own.start()
    all_here(7)
    firsts, seconds, laters = [], [], []
    for route in range(2):
        b = (at_z, at_x)[route]
        rows, late = uneven(urgent.shape[0], route), half(later.shape[0], route)
        for k in range(1, 4):
            peer, _ = axis_peer(route == 0, k)
            n = 3 * route + k - 1
            firsts.append(
                remote(urgent.at[rows], all_urgent.at[at_x, at_z, rows], u1_s.at[n], u1_r.at[n], peer)
            )
            laters.append(
                remote(later.at[late], all_later.at[at_x, at_z, late], l_s.at[n], l_r.at[n], peer)
            )
            slabs = line(all_urgent, route, b, rows)
            seconds.append(remote(slabs, slabs, u2_s.at[n], u2_r.at[n], axis_peer(route == 1, k)[0]))
    swap = remote(images.at[1 - high], out_images.at[core, high], im_s.at[0], im_r.at[0], {"x": (at_x + 2) % 4})
    kept = remote(images.at[high], out_images.at[core, high], im_s.at[1], im_r.at[1], other)
    passed = remote(
        out_images.at[core, 1 - high], out_images.at[core, 1 - high], im_s.at[2], im_r.at[2], other
    )
    for copy in firsts + [swap, kept] + laters:
        copy.start()
    for copy in firsts:
        copy.wait_recv()
    for copy in seconds:
        copy.start()
    swap.wait_recv()
    passed.start()
    for copy in seconds + laters + [kept, passed]:
        copy.wait()
    for copy in firsts + [swap]:
        copy.wait_send()
    own.wait()


def start_exchange(images, urgent, later):
    return pl.pallas_call(
        start_kernel,
        out_shape=[
            jax.ShapeDtypeStruct(s, bf16)
            for s in ((2,) + images.shape, (4, 4) + urgent.shape, (4, 4) + later.shape)
        ],
        in_specs=[VMEM] * 3,
        out_specs=[VMEM, VMEM, ANY],
        scratch_shapes=[pltpu.SemaphoreType.DMA] + dma_sems(3, 6, 6, 6),
        compiler_params=params(1, 56),
        name="start_exchange",
    )(images, urgent, later)


def spread_near(whole, send, recv):
    copies = []
    for route in range(2):
        slabs = line(whole, route, places()[1 - route], half(whole.shape[2], route))
        for n, k in enumerate((1, 3)):
            at, peer = 2 * route + n, axis_peer(route == 1, k)[0]
            copies.append(remote(slabs, slabs, send.at[at], recv.at[at], peer))
    return copies


def spread_far(whole, send, recv):
    copies = []
    size = whole.shape[2] // 2
    cut = size // 32 * 16 + size % 32
    for route in range(2):
        b = places()[1 - route]
        for n, k in enumerate((1, 3)):
            rows = pl.ds(route * size + n * cut, size - cut if n else cut)
            slabs = line(whole, route, (b + 4 - k) % 4, rows)
            at, peer = 4 + 2 * route + n, axis_peer(route == 1, k)[0]
            copies.append(remote(slabs, slabs, send.at[at], recv.at[at], peer))
    return copies


def part_rows(rows, route, n):
    size = rows // 2
    cut = size // 32 * 16 + size % 32
    return pl.ds(route * size + n * cut, size - cut if n else cut)


def toward_far(whole, passing, route, send, recv):
    copies, b = [], places()[1 - route]
    for n, k in enumerate((1, 3)):
        rows = part_rows(whole.shape[2], route, n)
        target = passing.at[route, n, :, 0 : rows.size]
        at, peer = 2 * route + n, axis_peer(route == 1, k)[0]
        copies.append(remote(line(whole, route, (b + 2) % 4, rows), target, send.at[at], recv.at[at], peer))
    return copies


def toward_near(whole, passing, landed, route, send, recv):
    copies, b = [], places()[1 - route]
    for n, k in enumerate((1, 3)):
        rows, others = (part_rows(whole.shape[2], route, m) for m in (n, 1 - n))
        at, peer = 4 * route + 2 * n, axis_peer(route == 1, k)[0]
        copies += [
            remote(passing.at[route, n, :, 0 : rows.size], landed.at[n, :, rows], send.at[at], recv.at[at], peer),
            remote(
                line(whole, route, (b + k) % 4, others), landed.at[n, :, others],
                send.at[at + 1], recv.at[at + 1], peer,
            ),
        ]
    return copies


def add_passing(whole, passing, route):
    x, z = places()
    b = (z, x)[route]
    for n, k in enumerate((1, 3)):
        rows, to = part_rows(whole.shape[2], route, n), (b + k) % 4

        def add(j, carry, n=n, rows=rows, to=to):
            own = whole[j, to, rows] if route == 0 else whole[to, j, rows]
            total = passing[route, n, j, 0 : rows.size].astype(f32) + own.astype(f32)
            passing[route, n, j, 0 : rows.size] = total.astype(bf16)
            return carry

        lax.fori_loop(0, 4, add, 0)


def last_copies(some, slabs, send, recv):
    copies = []
    for route in range(2):
        rows = half(some.shape[1], route)
        for k in range(1, 4):
            peer, at = axis_peer(route == 0, k)
            n = 3 * route + k - 1
            copies.append(remote(some.at[at, rows], slabs.at[k - 1, rows], send.at[n], recv.at[n], peer))
    return copies


def add_slabs(some, slabs, out):
    x, z = places()
    steps = some.shape[1] // 48

    def add(i, carry):
        rows, route = pl.ds(pl.multiple_of(i * 48, 48), 48), i // (steps // 2)
        total = some[x * (1 - route) + z * route, rows].astype(f32)
        for k in range(3):
            total = total + slabs[k, rows].astype(f32)
        out[rows] = total.astype(bf16)
        return carry

    lax.fori_loop(0, steps, add, 0)


def end_kernel(
    part, image, half_sum, some, some_attn, tiny, out_image, grad_in, grad_out, grad_attn,
    out, out_half, own_sum, other_sum, landed, sums, pieces, mids, lands, slabs, attn_slabs, cx_s, cx_r, sl_s, sl_r, at_s, at_r, p1_s, p1_r, p2_s, p2_r,
):
    def own_lines(rows):
        rows = rows.astype(f32)
        return jnp.where(core == 0, rows[0:24], rows[24:48])

    def put_experts(layer, own, got):
        for at in range(2 * EXPERTS):
            rows = slice(48 * at, 48 * at + 48)
            mine, others = own_lines(own[rows]), own_lines(got[rows])
            ref = grad_out if at % 2 else grad_in
            ref[layer, at // 2, :, 0:FE] = jnp.where(core == 0, mine, others)
            ref[layer, at // 2, :, FE:] = jnp.where(core == 0, others, mine)

    core, x = lax.axis_index("core"), lax.axis_index("x")
    other = {"core": 1 - core}
    arrive(axis_peers(1, 2, 3) + [other])
    all_here(7)
    crossing = remote(part.at[1 - core], landed, cx_s.at[0], cx_r.at[0], other)
    crossing.start()
    lasts = last_copies(some, slabs, sl_s, sl_r)
    firsts, seconds = [], []
    for route in range(2):
        rows = uneven(64, route)
        for k in range(1, 4):
            peer, at = axis_peer(route == 0, k)
            n = 3 * route + k - 1
            lasts.append(
                remote(some_attn.at[route, at], attn_slabs.at[route, k - 1], at_s.at[n], at_r.at[n], peer)
            )
            seconds.append(remote(mids.at[at, rows], lands.at[k - 1, rows], p2_s.at[n], p2_r.at[n], peer))
            peer, at = axis_peer(route == 1, k)
            firsts.append(
                remote(line(sums, route, at, rows), pieces.at[k - 1, :, rows], p1_s.at[n], p1_r.at[n], peer)
            )
    swap = remote(image, out_image, cx_s.at[1], cx_r.at[1], {"x": (x + 2) % 4})
    halves = remote(half_sum, out_half, cx_s.at[2], cx_r.at[2], other)
    for copy in lasts + [halves]:
        copy.start()
    crossing.wait()

    def add(i, carry):
        total = part[core, i // 4, i % 4].astype(f32) + landed[i // 4, i % 4].astype(f32)
        sums[i // 4, i % 4] = total.astype(bf16)
        return carry

    lax.fori_loop(0, 16, add, 0)
    for copy in firsts + [swap]:
        copy.start()
    halves.wait_recv()
    put_experts(1, half_sum, out_half)
    for copy in firsts:
        copy.wait_recv()
    at_x, at_z = places()
    for route in range(2):
        rows = uneven(64, route)

        def gather(j, carry, route=route, rows=rows):
            total = (sums[j, at_z, rows] if route == 0 else sums[at_x, j, rows]).astype(f32)
            for k in range(3):
                total = total + pieces[k, j, rows].astype(f32)
            mids[j, rows] = total.astype(bf16)
            return carry

        lax.fori_loop(0, 4, gather, 0)
    for copy in seconds:
        copy.start()
    for copy in lasts:
        copy.wait()
    add_slabs(some, slabs, own_sum)
    for route in range(2):
        attn = some_attn[route, places()[route]].astype(f32)
        for k in range(3):
            attn = attn + attn_slabs[route, k].astype(f32)
        first = 384 + 48 * route
        own_sum[first : first + 48] = attn.astype(bf16)
    final = remote(own_sum, other_sum, cx_s.at[3], cx_r.at[3], other)
    final.start()
    for copy in seconds:
        copy.wait()
    for route in range(2):
        rows = uneven(64, route)
        total = mids[places()[route], rows].astype(f32)
        for k in range(3):
            total = total + lands[k, rows].astype(f32)
        out[core, rows] = total
    given = remote(out.at[core], out.at[core], cx_s.at[4], cx_r.at[4], other)
    given.start()
    final.wait()
    put_experts(0, own_sum, other_sum)
    given.wait()
    for route in range(2):
        first = 384 + 48 * route
        rows = slice(first, first + 48)
        grad_attn[0, route] = own_lines(out[route, 0:48])
        grad_attn[1, route] = own_lines(own_sum[rows]) + own_lines(other_sum[rows])
        tiny[route] = jnp.where(core == 0, out[route, 48:56], out[route, 56:64])
    for copy in firsts + [halves]:
        copy.wait_send()
    swap.wait()


def end_exchange(part, image, half_sum, some, some_attn):
    slab = (480, FE)
    scratch = [half_sum.shape, slab, slab] + [(4, 4, 64, FE)] * 2 + [(3, 4, 64, FE), (4, 64, FE), (3, 64, FE)]
    scratch += [(3,) + some.shape[1:], (2, 3, 48, FE)]
    return pl.pallas_call(
        end_kernel,
        out_shape=[
            jax.ShapeDtypeStruct((2, 8, FE), f32),
            jax.ShapeDtypeStruct(image.shape, bf16),
            jax.ShapeDtypeStruct((2, EXPERTS, 24, D), f32),
            jax.ShapeDtypeStruct((2, EXPERTS, 24, D), f32),
            jax.ShapeDtypeStruct((2, 2, 24, FE), f32),
        ],
        in_specs=[VMEM] * 5,
        out_specs=[VMEM] * 5,
        scratch_shapes=[pltpu.VMEM((2, 64, FE), f32)]
        + [pltpu.VMEM(s, bf16) for s in scratch]
        + dma_sems(5, 6, 6, 6, 6),
        compiler_params=params(2, 56),
        name="end_exchange",
    )(part, image, half_sum, some, some_attn)


def block_rows(ref, block):
    top = jnp.concatenate([ref[block, 0, 0:80], ref[block, 1, 0:80]], axis=1)
    low = jnp.concatenate([ref[block, 2, 0:80], ref[block, 3, 0:80]], axis=1)
    return jnp.concatenate([top, low], axis=0).astype(f32)


def pair_rows(ref):
    return jnp.concatenate([block_rows(ref, 0), block_rows(ref, 1)], axis=0)


def put_chunks(ref, block, value, first=0):
    for j in range(4):
        r, c = 80 * (j // 2), 384 * (j % 2)
        ref[block, j, first : first + 80] = value[r : r + 80, c : c + 384]


def norm_parts(rows):
    centered = rows - jnp.mean(rows, axis=-1, keepdims=True)
    scale = lax.rsqrt(jnp.mean(centered * centered, axis=-1, keepdims=True) + EPS)
    return centered * scale, scale


def norm_back(grad, unit, scale, gain):
    inner = grad * gain
    return scale * (
        inner
        - jnp.mean(inner, axis=-1, keepdims=True)
        - unit * jnp.mean(inner * unit, axis=-1, keepdims=True)
    )


def softmax(logits, axis):
    top = jnp.max(logits, axis=axis, keepdims=True)
    powers = jnp.exp(logits - top)
    return powers / jnp.sum(powers, axis=axis, keepdims=True)


def own_rows(core):
    return pl.ds(pl.multiple_of(core * ROWS, ROWS), ROWS)


def head(value, h):
    return value[:, HD * h : HD * h + HD]


def gelu_parts(u):
    c = 0.7978845608028654
    t = jnp.tanh(c * (u + 0.044715 * u * u * u))
    return 0.5 * u * (1.0 + t), t


def gelu_slope(u, t):
    c = 0.7978845608028654
    return 0.5 * (1.0 + t) + 0.5 * u * (1.0 - t * t) * (c * (1.0 + 3 * 0.044715 * u * u))


def attn_weights(weights):
    w_kv = weights[:, 0:48].reshape(D, 2 * WIDTH)
    w_q = weights[:, 48:96, :WIDTH].reshape(D, WIDTH)
    return w_kv, w_q, weights[:, 48:96, WIDTH:].reshape(D, WIDTH)


def attend_forward_kernel(follows, *refs):
    if follows:
        x, att_before, moe_before, small, weights, dead, q, kv, mixed, att, x_next, *scratch = refs
    else:
        x, small, weights, dead, ahead, _, q, kv, mixed, att, whole, all_ahead, *scratch = refs
        *scratch, sp_send, sp_recv, ah_send, ah_recv, own_sem = scratch
    part, landed, *sems, kv_send, kv_recv = scratch
    sums = (False, att, part, landed, *sems)
    core = lax.axis_index("core")
    other, across, me = chip_peers()
    arrive([other, across] + tp_peers())
    if not follows:
        arrive(axis_peers(1, 2, 3))
    if follows:
        x_next[...] = (x[...].astype(f32) + pair_rows(att_before) + pair_rows(moe_before)).astype(bf16)
        x = x_next
    unit, _ = norm_parts(x[own_rows(core)].astype(f32))
    normed = (unit * small[0:1] + small[2:3]).astype(bf16)
    w_kv, w_q, w_out_t = attn_weights(weights)
    kv[me] = dot(normed, w_kv, NN).astype(bf16)
    all_here(5 if follows else 11)
    far = (me + 2) % 4
    copies = [
        remote(kv.at[at], kv.at[at], kv_send.at[k], kv_recv.at[k], peer)
        for k, (at, peer) in enumerate(((me, across), (me, other), (far, other)))
    ]
    copies[0].start()
    copies[1].start()
    if not follows:
        nears = spread_near(whole, sp_send, sp_recv)
        fars = spread_far(whole, sp_send, sp_recv)
        at_x, at_z = places()
        aheads = [pltpu.make_async_copy(ahead, all_ahead.at[at_x, at_z], own_sem)]
        for route in range(2):
            rows = half(ahead.shape[0], route)
            for k in range(1, 4):
                n, peer = 3 * route + k - 1, axis_peer(route == 0, k)[0]
                aheads.append(
                    remote(ahead.at[rows], all_ahead.at[at_x, at_z, rows], ah_send.at[n], ah_recv.at[n], peer)
                )
        for copy in nears + aheads:
            copy.start()
    queries = dot(normed, w_q, NN).astype(bf16)
    q[...] = queries
    copies[0].wait_recv()
    copies[2].start()
    copies[1].wait_recv()
    copies[2].wait_recv()
    keys = kv[...].reshape(KEYS, 2 * WIDTH)
    outs = []
    for h in range(HEADS):
        scores = HD**-0.5 * dot(head(queries, h), head(keys, h), NT) + dead[...]
        probs = softmax(scores, -1).astype(bf16)
        outs.append(dot(probs, head(keys, HEADS + h), NN))
    heads = jnp.concatenate(outs, axis=1).astype(bf16)
    mixed[...] = heads
    put_chunks(part, 0, dot(heads, w_out_t, NT).astype(bf16))
    sum_start(*sums)
    sum_middle(*sums)
    if not follows:
        for copy in nears:
            copy.wait_recv()
        for copy in fars:
            copy.start()
    sum_end(*sums)
    for copy in copies:
        copy.wait_send()
    if not follows:
        for copy in fars + aheads:
            copy.wait()
        for copy in nears:
            copy.wait_send()


def attend_forward(x, before, small, weights, dead, some, ahead, cid):
    args = (x, *before, small, weights, dead)
    shapes = [(ROWS, WIDTH), (4, ROWS, 2 * WIDTH), (ROWS, WIDTH), (2, 4, 80, 384)]
    in_specs, out_specs = [VMEM] * len(args), [VMEM] * 5
    scratch = sum_scratch(False, 80) + dma_sems(3)
    if before:
        shapes.append((PAIR, D))
    else:
        args += (ahead, some)
        shapes += [some.shape, (4, 4) + ahead.shape]
        in_specs += [VMEM, ANY]
        out_specs[4:] = [ANY, ANY]
        scratch += dma_sems(8, 6) + [pltpu.SemaphoreType.DMA]
    return pl.pallas_call(
        functools.partial(attend_forward_kernel, bool(before)),
        out_shape=[jax.ShapeDtypeStruct(s, bf16) for s in shapes],
        in_specs=in_specs,
        out_specs=out_specs,
        scratch_shapes=scratch,
        input_output_aliases={} if before else {len(args) - 1: 4},
        compiler_params=params(cid, 56),
        name="attend_forward",
    )(*args)


def expert_weights(weights):
    block = weights[...]
    return block[:, 0:48].reshape(D, FE), block[:, 48:96].reshape(D, FE)


def experts_setup(x, att, small, routes, b, gates):
    unit, _ = norm_parts(x[...].astype(f32) + pair_rows(att))
    b[...] = (unit * small[1:2] + small[3:4]).astype(bf16)
    put_gates(b, small, routes, gates)


def put_gates(b, small, routes, gates):
    probs = softmax(dot(b[...], small[4:8].astype(bf16), NT), -1)
    ids = lax.broadcasted_iota(jnp.int32, (PAIR, EXPERTS), 1).astype(f32)
    ones = lax.broadcasted_iota(jnp.int32, (16, 16), 0) == lax.broadcasted_iota(jnp.int32, (16, 16), 1)
    lines = dot(routes[...], ones.astype(f32).astype(bf16), TN)
    named = (lines[:, 0:1] == ids) | (lines[:, 1:2] == ids)
    gates[...] = jnp.where(named, probs, 0.0)


def gate_of(gates, expert):
    ids = lax.broadcasted_iota(jnp.int32, (PAIR, EXPERTS), 1)
    return jnp.sum(jnp.where(ids == expert, gates[...], 0.0), axis=1, keepdims=True)


def experts_forward_kernel(
    x, att, small, routes, _, weights, result, ahead, b, gates, total, ah_send, ah_recv, out, part, landed, *sems
):
    expert = pl.program_id(0)
    sums = (True, out, part, landed, *sems)
    aheads = []
    for route in range(2):
        slabs = line(ahead, route, places()[1 - route], half(ahead.shape[2], route))
        for k in range(1, 4):
            n, peer = 3 * route + k - 1, axis_peer(route == 1, k)[0]
            aheads.append(remote(slabs, slabs, ah_send.at[n], ah_recv.at[n], peer))

    @pl.when(expert == 0)
    def _():
        arrive(tp_peers() + [{"core": 1 - lax.axis_index("core")}] + axis_peers(1, 2, 3))
        experts_setup(x, att, small, routes, b, gates)
        total[...] = jnp.zeros_like(total)
        all_here(10)
        for copy in aheads:
            copy.start()

    w_in, w_out_t = expert_weights(weights)
    u = dot(b[...], w_in, NN)
    active = gelu_parts(u)[0].astype(bf16).astype(f32)
    gated = (gate_of(gates, expert) * active).astype(bf16)
    total[...] += dot(gated, w_out_t, NT)

    @pl.when(expert == EXPERTS - 1)
    def _():
        for block in range(2):
            put_chunks(part, block, total[ROWS * block : ROWS * block + ROWS].astype(bf16))
        sum_start(*sums)
        sum_middle(*sums)
        sum_end(*sums)
        result[...] = out[...]
        for copy in aheads:
            copy.wait()


def fixed(shape):
    return pl.BlockSpec(shape, lambda e: (0,) * len(shape))


def experts_forward(x, att, small, routes, ahead, weights, cid):
    args = (x, att, small, routes)
    return pl.pallas_call(
        experts_forward_kernel,
        grid=(EXPERTS,),
        out_shape=[jax.ShapeDtypeStruct((2, 4, 80, 384), bf16), jax.ShapeDtypeStruct(ahead.shape, bf16)],
        in_specs=[fixed(a.shape) for a in args] + [ANY, pl.BlockSpec((16, 96, FE), lambda e: (0, e, 0))],
        out_specs=[fixed((2, 4, 80, 384)), ANY],
        scratch_shapes=[
            pltpu.VMEM((PAIR, D), bf16),
            pltpu.VMEM((PAIR, EXPERTS), f32),
            pltpu.VMEM((PAIR, D), f32),
        ]
        + dma_sems(6)
        + [pltpu.VMEM((2, 4, 80, 384), bf16)]
        + sum_scratch(True, 80),
        input_output_aliases={4: 1},
        compiler_params=params(cid, 56),
        name="experts_forward",
    )(*args, ahead, weights)


def layer_backward_kernel(with_moe, *refs):
    x, att, small, routes, grad, q, kv, mixed, dead, attn_w, *refs = refs
    if not with_moe:
        extra, some_before, *refs = refs
    weights, grad_x, grad_small, grad_w, some, *refs = refs
    if with_moe:
        moe_result, *refs = refs
    else:
        own_sum, some_attn, *refs = refs
    b, gates, unit_two, scale_two, total, gate_grads, gated_all, grad_u_all, *refs = refs
    whole, slabs, passing, all_probs, grad_h, unit_one, parts, kv_landed, kv_out, back, back_one, *refs = refs
    fs, fr, ns, nr, kv_send, kv_recv, *refs = refs
    sums_two, sums_one, refs = (True, back, *refs[:11]), (False, back_one, *refs[11:19]), refs[19:]
    part_two, part_one = sums_two[2], sums_one[2]
    if with_moe:
        moe, moe_part, moe_out, moe_landed, ms, mr, mg, mh, moe_crossed, ps, pr = refs
        moe_sums = (moe_part, moe_crossed, ps, pr)
    else:
        last_slabs, ls, lr, attn_slabs, as_, ar = refs
        lasts = last_copies(some_before, last_slabs, ls, lr)
        for route in range(2):
            for k in range(1, 4):
                n, (peer, to) = 3 * route + k - 1, axis_peer(route == 1, k)
                slab = extra.at[0, :, to] if route == 0 else extra.at[1, to]
                lasts.append(remote(slab, attn_slabs.at[route, k - 1], as_.at[n], ar.at[n], peer))
    fars = [toward_far(whole, passing, route, fs, fr) for route in range(2)]
    nears = [toward_near(whole, passing, slabs, route, ns, nr) for route in range(2)]
    core, tp = lax.axis_index("core"), lax.axis_index("tp")
    at_x, at_z = places()
    other, across, me = chip_peers()
    far = (me + 2) % 4
    step = pl.program_id(0)

    @pl.when(step == 0)
    def _():
        arrive([other, across] + tp_peers() + axis_peers(1, 2, 3))
        unit, scale = norm_parts(x[...].astype(f32) + pair_rows(att))
        unit_two[...] = unit
        scale_two[...] = scale
        b[...] = (unit * small[1:2] + small[3:4]).astype(bf16)
        put_gates(b, small, routes, gates)
        total[...] = jnp.zeros_like(total)
        gate_grads[...] = jnp.zeros_like(gate_grads)
        if with_moe:
            moe[...] = jnp.zeros_like(moe)
        all_here(11)
        if not with_moe:
            for copy in lasts:
                copy.start()

    @pl.when(step < EXPERTS)
    def _():
        w_in, w_out_t = expert_weights(weights)
        u = dot(b[...], w_in, NN)
        act, t = gelu_parts(u)
        active = act.astype(bf16).astype(f32)
        gate = gate_of(gates, step)
        gated = (gate * active).astype(bf16)
        gated_all[step] = gated
        if with_moe:
            moe[...] += dot(gated, w_out_t, NT)
        grad_active = dot(grad[...], w_out_t, NN)
        ids = lax.broadcasted_iota(jnp.int32, (PAIR, 128), 1)
        gate_grad = jnp.sum(grad_active * active, axis=1, keepdims=True)
        gate_grads[...] = jnp.where(ids == step, gate_grad, gate_grads[...])
        grad_u = (gate * grad_active * gelu_slope(u, t)).astype(bf16)
        grad_u_all[step] = grad_u
        total[...] += dot(grad_u, w_in, NT)

    @pl.when(step == EXPERTS - 1)
    def _():
        part_two[...] = jnp.zeros_like(part_two)
        lines, lanes = (lax.broadcasted_iota(jnp.int32, (16, 128), axis) for axis in range(2))
        ones = ((lines == lanes) & (lines < EXPERTS)).astype(f32).astype(bf16)
        for block in range(2):
            rows = slice(ROWS * block, ROWS * block + ROWS)
            put_chunks(part_two, block, total[rows].astype(bf16))
            part_two[block, 0, 80:96, 0:ROWS] = dot(ones, gate_grads[rows].astype(bf16), NT).astype(bf16)
            if with_moe:
                put_chunks(moe_part, block, moe[rows].astype(bf16))
        sum_start(*sums_two)

    @pl.when(step >= EXPERTS)
    def _():
        at = step - EXPERTS
        first = pl.multiple_of(96 * at, 96)
        grad_in = dot(b[...], grad_u_all[at], TN).astype(bf16)
        whole[:, :, pl.ds(first, 48)] = grad_in.reshape(4, 4, 48, FE)
        grad_out = dot(grad[...], gated_all[at], TN).astype(bf16)
        whole[:, :, pl.ds(first + 48, 48)] = grad_out.reshape(4, 4, 48, FE)

    @pl.when(step == EXPERTS + 1)
    def _():
        sum_middle(*sums_two)

    @pl.when(step == 2 * EXPERTS - 2)
    def _():
        keys = kv[...].reshape(KEYS, 2 * WIDTH)
        for h in range(HEADS):
            all_probs[h] = softmax(HD**-0.5 * dot(head(q[...], h), head(keys, h), NT) + dead[...], -1)
        if not with_moe:
            for copy in lasts:
                copy.wait()
            add_slabs(some_before, last_slabs, own_sum)
            for route in range(2):

                def add(j, carry, route=route):
                    attn = (extra[0, j, at_z] if route == 0 else extra[1, at_x, j]).astype(f32)
                    for k in range(3):
                        attn = attn + attn_slabs[route, k, j].astype(f32)
                    some_attn[route, j] = attn.astype(bf16)
                    return carry

                lax.fori_loop(0, 4, add, 0)

    @pl.when(step == 2 * EXPERTS - 1)
    def _():
        for copy in fars[1] + fars[0]:
            copy.start()
        sum_end(*sums_two)
        router = small[4:8]
        chances = softmax(dot(router.astype(bf16), b[...], NT), 0)
        ids = lax.broadcasted_iota(jnp.int32, (EXPERTS, PAIR), 0).astype(f32)
        lines = routes[...].astype(f32)
        named = (lines[0:1] == ids) | (lines[1:2] == ids)
        tables = [back[block, 0, 80:96, 0:ROWS].astype(f32)[0:EXPERTS] for block in range(2)]
        gate_rows = jnp.where(named, jnp.concatenate(tables, axis=1), 0.0)
        grad_logits = chances * (gate_rows - jnp.sum(chances * gate_rows, axis=0, keepdims=True))
        grad_b = pair_rows(back) + dot_split(grad_logits, router.astype(bf16), TN)
        grad_h[...] = grad[...].astype(f32) + norm_back(grad_b, unit_two[...], scale_two[...], small[1:2])
        grad_att = grad_h[own_rows(core)].astype(bf16)
        w_kv, w_q, w_out_t = attn_weights(attn_w)
        grad_mixed = dot(grad_att, w_out_t, NN).astype(bf16)
        keys = kv[...].reshape(KEYS, 2 * WIDTH)
        queries = q[...]
        q_parts, k_parts, v_parts = [], [], []
        for h in range(HEADS):
            q_h, g_h = head(queries, h), head(grad_mixed, h)
            k_h, v_h = head(keys, h), head(keys, HEADS + h)
            probs = all_probs[h]
            v_parts.append(dot(probs.astype(bf16), g_h, TN))
            grad_weights = dot(g_h, v_h, NT)
            grad_scores = probs * (grad_weights - jnp.sum(probs * grad_weights, axis=-1, keepdims=True))
            grad_scores = grad_scores.astype(bf16)
            q_parts.append(HD**-0.5 * dot(grad_scores, k_h, NN))
            k_parts.append(HD**-0.5 * dot(grad_scores, q_h, TN))
        grad_keys = jnp.concatenate(k_parts + v_parts, axis=1).astype(bf16)
        parts[...] = grad_keys.reshape(4, ROWS, 2 * WIDTH)
        crosses = [
            remote(parts.at[(at + 1 - 2 * core) % 4], kv_landed.at[k], kv_send.at[k], kv_recv.at[k], other)
            for k, at in enumerate((me, far))
        ]
        onward = remote(kv_out, kv_landed.at[2], kv_send.at[2], kv_recv.at[2], across)
        crosses[1].start()
        crosses[0].start()
        if with_moe:
            pres = sum_cores(*moe_sums)
            for copy in pres:
                copy.start()
        crosses[1].wait_recv()
        kv_out[...] = (parts[far].astype(f32) + kv_landed[1].astype(f32)).astype(bf16)
        onward.start()
        if with_moe:
            for copy in pres:
                copy.wait_recv()
            for j in range(4):
                moe_sum = moe_part[core, j].astype(f32) + moe_crossed[j].astype(f32)
                moe_crossed[j] = moe_sum.astype(bf16)
            moe_terms = [
                remote(moe_crossed.at[peer["tp"]], moe_landed.at[k], ms.at[k], mr.at[k], peer)
                for k, peer in enumerate(tp_peers())
            ]
            for copy in moe_terms:
                copy.start()
        for route in (1, 0):
            for copy in fars[route]:
                copy.wait_recv()
            add_passing(whole, passing, route)
            for copy in nears[route]:
                copy.start()
        grad_q = jnp.concatenate(q_parts, axis=1).astype(bf16)
        grad_w[1, :, WIDTH:] = dot(grad_att, mixed[...], TN).astype(bf16)
        lanes = lax.broadcasted_iota(jnp.int32, (EXPERTS, PAIR), 1)
        own_lanes = (lanes < ROWS) == (core == 0)
        own = (lax.broadcasted_iota(jnp.int32, (PAIR, 1), 0) < ROWS) == (core == 0)
        kept = jnp.where(own, grad_b, 0.0)
        grad_small[1:2] = jnp.sum(kept * unit_two[...], axis=0, keepdims=True)
        grad_small[3:4] = jnp.sum(kept, axis=0, keepdims=True)
        grad_small[4:8] = dot_split(jnp.where(own_lanes, grad_logits, 0.0), b[...], NN)
        unit, scale_one = norm_parts(x[...].astype(f32))
        unit_one[...] = unit
        normed = (unit_one[own_rows(core)] * small[0:1] + small[2:3]).astype(bf16)
        crosses[0].wait_recv()
        onward.wait_recv()
        grad_kv = parts[me].astype(f32) + kv_landed[0].astype(f32) + kv_landed[2].astype(f32)
        grad_kv = grad_kv.astype(bf16)
        value = dot(grad_kv, w_kv, NT) + dot(grad_q, w_q, NT)
        put_chunks(part_one, 0, value.astype(bf16))
        sum_start(*sums_one)
        grad_w[0] = dot(normed, grad_kv, TN).astype(bf16)
        grad_w[1, :, :WIDTH] = dot(normed, grad_q, TN).astype(bf16)
        sum_middle(*sums_one)
        if with_moe:
            moe_total = moe_crossed[tp].astype(f32)
            for k, copy in enumerate(moe_terms):
                copy.wait_recv()
                moe_total = moe_total + moe_landed[k].astype(f32)
            moe_out[tp] = moe_total.astype(bf16)
            moe_results = [
                remote(moe_out.at[tp], moe_out.at[tp], mg.at[k], mh.at[k], peer)
                for k, peer in enumerate(tp_peers())
            ]
            for copy in moe_results:
                copy.start()
        for route in range(2):
            for copy in fars[route]:
                copy.wait_send()
            for copy in nears[route]:
                copy.wait()
        steps = some.shape[1] // 48

        def add(i, carry):
            j, at = i % 4, i // 4
            rows, route = pl.ds(pl.multiple_of(at * 48, 48), 48), at // (steps // 2)
            mine = whole[j * (1 - route) + at_x * route, at_z * (1 - route) + j * route, rows]
            total = mine.astype(f32) + slabs[0, j, rows].astype(f32) + slabs[1, j, rows].astype(f32)
            some[j, rows] = total.astype(bf16)
            return carry

        lax.fori_loop(0, 4 * steps, add, 0)
        sum_end(*sums_one)
        grad_a = pair_rows(back_one)
        grad_x[...] = (grad_h[...] + norm_back(grad_a, unit_one[...], scale_one, small[0:1])).astype(bf16)
        kept = jnp.where(own, grad_a, 0.0)
        grad_small[0:1] = jnp.sum(kept * unit_one[...], axis=0, keepdims=True)
        grad_small[2:3] = jnp.sum(kept, axis=0, keepdims=True)
        for copy in crosses + [onward]:
            copy.wait_send()
        if with_moe:
            for copy in pres + moe_terms:
                copy.wait_send()
            for copy in moe_results:
                copy.wait()
            moe_result[...] = moe_out[...]


def layer_backward(args, others, weights, cid):
    with_moe = not others
    slab = (384, FE)
    shapes = [((PAIR, D), bf16), ((8, D), f32), ((2, D, 2 * WIDTH), bf16), ((4,) + slab, bf16)]
    scratch = [
        ((PAIR, D), bf16),
        ((PAIR, EXPERTS), f32),
        ((PAIR, D), f32),
        ((PAIR, 1), f32),
        ((PAIR, D), f32),
        ((PAIR, 128), f32),
        ((EXPERTS, PAIR, FE), bf16),
        ((EXPERTS, PAIR, FE), bf16),
        ((4, 4) + slab, bf16),
        ((2, 4) + slab, bf16),
        ((2, 2, 4, 96, FE), bf16),
        ((HEADS, ROWS, KEYS), f32),
        ((PAIR, D), f32),
        ((PAIR, D), f32),
        ((4, ROWS, 2 * WIDTH), bf16),
        ((3, ROWS, 2 * WIDTH), bf16),
        ((ROWS, 2 * WIDTH), bf16),
        ((2, 4, 96, 384), bf16),
        ((2, 4, 80, 384), bf16),
    ]
    scratch = [pltpu.VMEM(*s) for s in scratch] + dma_sems(4, 8, 3)
    scratch += sum_scratch(True, 96) + sum_scratch(False, 80)
    if with_moe:
        shapes.append(((4, 80, 384), bf16))
        scratch += [pltpu.VMEM((PAIR, D), f32), pltpu.VMEM((2, 4, 80, 384), bf16)]
        scratch += [pltpu.VMEM((4, 80, 384), bf16), pltpu.VMEM((3, 80, 384), bf16)] + dma_sems(3, 3)
        scratch += [pltpu.VMEM((4, 80, 384), bf16)] + dma_sems(2)
    else:
        shapes += [(slab, bf16), ((2, 4, 48, FE), bf16)]
        scratch += [pltpu.VMEM((3,) + slab, bf16)] + dma_sems(6)
        scratch += [pltpu.VMEM((2, 3, 4, 48, FE), bf16)] + dma_sems(6)
    args = args + others
    return pl.pallas_call(
        functools.partial(layer_backward_kernel, with_moe),
        grid=(2 * EXPERTS,),
        out_shape=[jax.ShapeDtypeStruct(*s) for s in shapes],
        in_specs=[fixed(a.shape) for a in args]
        + [pl.BlockSpec((16, 96, FE), lambda s: (0, jnp.minimum(s, EXPERTS - 1), 0))],
        out_specs=[fixed(s) for s, _ in shapes],
        scratch_shapes=scratch,
        compiler_params=params(cid, 60),
        name="layer_backward",
    )(*args, weights)


def shards(boundary, routes, lengths, ln_gains, ln_biases, w_qkv, w_out, w_router, w_in, w_exp_out):
    core = lax.axis_index("core")
    high = lax.axis_index("x") // 2

    def pick(value, at, axis):
        return lax.dynamic_index_in_dim(value, at, axis, keepdims=False)

    halves = jnp.stack(
        [
            w_qkv[:, :, 1:].reshape(2, 24, 384),
            jnp.concatenate([w_qkv[:, :, 0], w_out.transpose(0, 2, 1)], axis=2),
        ],
        axis=1,
    )

    stacked = jnp.stack([w_in, w_exp_out.transpose(0, 1, 3, 2)], axis=2).reshape(384, 2, FE)
    tiny = jnp.concatenate([ln_gains, ln_biases, w_router.transpose(0, 2, 1)], axis=1)
    tiny = jnp.pad(tiny.transpose(1, 0, 2).reshape(8, 48), ((0, 8), (0, 384 - 48)))
    attn_one, attn_zero = halves[1].reshape(48, 384), halves[0].reshape(48, 384)
    own_half = jnp.concatenate([pick(stacked, core, 1), attn_one, attn_zero, tiny])
    got_half = cross(jnp.concatenate([pick(stacked, 1 - core, 1), attn_one, attn_zero, tiny]), 0)
    low_half = jnp.where(core == 0, own_half, got_half)
    high_half = jnp.where(core == 0, got_half, own_half)
    chip = jnp.concatenate(
        [low_half[:480].reshape(20, 24, FE), high_half[:480].reshape(20, 24, FE)], axis=1
    )
    later, ahead = chip[0:8].reshape(384, FE), chip[16:18].reshape(96, FE)
    urgent = jnp.concatenate([chip[18:20].reshape(96, FE), low_half[480:496], high_half[480:496]])

    turned = jnp.pad(
        routes[0].astype(bf16).transpose(0, 2, 1), ((0, 0), (0, 14), (0, D - ROWS))
    )
    images = jnp.concatenate([boundary[0], turned], axis=1)
    got_images, packs, some = start_exchange(images, urgent, later)
    packs = packs.reshape(16, 128, 384)
    tiny = packs[:, 96:128].reshape(32, 16, 384)[:, 0:8, 0:48].reshape(32, 8, 2, 24).transpose(2, 1, 0, 3).reshape(2, 8, D)
    smalls = [tiny[0].astype(f32), tiny[1].astype(f32)]

    live = jnp.arange(ROWS, dtype=jnp.int32)[None, :] < lengths[:, None]
    dead = jnp.where(live.reshape(1, KEYS), 0.0, -1e30).astype(f32)
    chip_live = lax.dynamic_slice_in_dim(live, 2 * lax.axis_index("zl"), 2, 0)
    own_live = pick(chip_live, core, 0)

    x0 = got_images[:, 0, 0:ROWS].reshape(PAIR, D)
    cotangent = jnp.where(chip_live[:, :, None], got_images[:, 1, 0:ROWS], 0).reshape(PAIR, D)
    route_rows = [
        got_images[:, kind, ROWS:, 0:ROWS].transpose(1, 0, 2).reshape(16, PAIR) for kind in range(2)
    ]

    q0, kv0, mixed0, att0, experts_zero, ahead = attend_forward(x0, (), smalls[0], packs, dead, some, ahead, 3)
    experts_zero = experts_zero.reshape(16, 384, FE)
    shard, att0 = lax.optimization_barrier((chip[8:16].reshape(384, FE), att0))
    experts_one = lax.all_gather(shard, CHIPS, axis=0)
    moe0, attn_w1 = experts_forward(x0, att0, smalls[0], route_rows[0], ahead, experts_zero, 4)
    attn_w1 = attn_w1.reshape(16, 96, FE)
    q1, kv1, mixed1, att1, x1 = attend_forward(
        x0, (att0, moe0), smalls[1], attn_w1, dead, None, None, 5
    )
    grad_x1, grad_small1, grad_attn1, some, moe1 = layer_backward(
        (x1, att1, smalls[1], route_rows[1], cotangent, q1, kv1, mixed1, dead, attn_w1), (), experts_one, 6
    )
    grad_x0, grad_small0, grad_attn0, some, sums1, some_attn = layer_backward(
        (x0, att0, smalls[0], route_rows[0], grad_x1, q0, kv0, mixed0, dead, packs),
        (grad_attn1.reshape(2, 4, 4, 48, FE), some),
        experts_zero,
        7,
    )

    def own_block(value):
        return pick(value, core, 0)

    def unchunk(value):
        return value.reshape(2, 2, 80, 384).transpose(0, 2, 1, 3).reshape(ROWS, D).astype(f32)

    y1 = own_block(x1.reshape(2, ROWS, D)).astype(f32) + unchunk(own_block(att1)) + unchunk(moe1)
    mine = jnp.stack([own_block(grad_x0.reshape(2, ROWS, D)).astype(f32), y1])
    mine = jnp.where(own_live[None, :, None], mine, 0.0)
    kept, sent = pick(mine, high, 0), pick(mine, 1 - high, 0).astype(bf16)

    tiny = jnp.stack([grad_small0, grad_small1]).astype(bf16).reshape(2, 8, 16, 2, 24)
    tiny = tiny.transpose(0, 2, 3, 1, 4).reshape(2, 16, 16, 24)
    tiny = jnp.pad(tiny, ((0, 0), (0, 0), (0, 0), (0, 384 - 24)))
    packs = jnp.concatenate([grad_attn0.reshape(2, 16, 48, 384), tiny], axis=2).reshape(2, 4, 4, 64, FE)
    tiny, landed, grad_w_in, grad_w_exp_out, attn = end_exchange(packs, sent, sums1, some, some_attn)
    landed = landed.astype(f32)
    ends = jnp.where(high == 0, jnp.stack([kept, landed]), jnp.stack([landed, kept]))
    grad_w_qkv = jnp.concatenate([attn[:, 1, :, None, :WIDTH], attn[:, 0].reshape(2, 24, 2, WIDTH)], axis=2)
    grad_w_out = attn[:, 1, :, WIDTH:].transpose(0, 2, 1)
    tiny = tiny[:, :, 0:24]
    return (
        ends[None],
        tiny[:, 0:2],
        tiny[:, 2:4],
        grad_w_qkv,
        grad_w_out,
        tiny[:, 4:8].transpose(0, 2, 1),
        grad_w_in,
        grad_w_exp_out.transpose(0, 1, 3, 2),
    )


def solution(mesh):
    fine = Mesh(mesh.devices.reshape(4, 2, 2, 2, 4), CHIPS + ("core", "tp"))
    section, ctx = ("x", "zh"), ("zl", "core")
    every = section + ctx
    return jax.shard_map(
        shards,
        mesh=fine,
        in_specs=(
            P(ctx, section, None, None),
            P(ctx, section, None, None),
            P(),
            P(None, None, every),
            P(None, None, every),
            P(None, every, None, "tp"),
            P(None, "tp", every),
            P(None, every, None),
            P(None, None, every, "tp"),
            P(None, None, "tp", every),
        ),
        out_specs=(
            P(ctx, section, None, None),
            P(None, None, every),
            P(None, None, every),
            P(None, every, None, "tp"),
            P(None, "tp", every),
            P(None, every, None),
            P(None, None, every, "tp"),
            P(None, None, "tp", every),
        ),
        check_vma=False,
    )
```

```python
import functools

import jax
import jax.numpy as jnp
from jax import lax
from jax.experimental import pallas as pl
from jax.experimental.pallas import tpu as pltpu
from jax.sharding import Mesh
from jax.sharding import PartitionSpec as P

D = 768
HD = 64
HEADS = 3
ROWS = 160
PAIR = 320
KEYS = 640
FE = 384
EXPERTS = 4
EPS = 1e-06
WIDTH = HEADS * HD
MESH = pl.DeviceIdType.MESH
CHIPS = ("x", "zh", "zl")
f32, bf16 = jnp.float32, jnp.bfloat16
VMEM = pl.BlockSpec(memory_space=pltpu.VMEM)
SMEM = pl.BlockSpec(memory_space=pltpu.SMEM)
NN = (((1,), (0,)), ((), ()))
NT = (((1,), (1,)), ((), ()))
TN = (((0,), (0,)), ((), ()))


def dot(a, b, dims):
    return lax.dot_general(a, b, dims, preferred_element_type=f32)


def dot_split(a, b, dims):
    high = a.astype(bf16)
    return dot(high, b, dims) + dot((a - high.astype(f32)).astype(bf16), b, dims)


def params(cid, mib):
    return pltpu.CompilerParams(
        collective_id=cid, has_side_effects=True, vmem_limit_bytes=mib * 2**20
    )


ANY = pl.BlockSpec(memory_space=pl.ANY)


def arrive(peers):
    barrier = pltpu.get_barrier_semaphore()
    for peer in peers:
        pl.semaphore_signal(barrier, inc=1, device_id=peer, device_id_type=MESH)


def all_here(count):
    pl.semaphore_wait(pltpu.get_barrier_semaphore(), count)


def dma_sems(*counts):
    return [pltpu.SemaphoreType.DMA((count,)) for count in counts for _ in range(2)]


def remote(src, dst, send, recv, peer):
    return pltpu.make_async_remote_copy(
        src_ref=src, dst_ref=dst, send_sem=send, recv_sem=recv, device_id=peer, device_id_type=MESH
    )


def tp_peers():
    return [{"tp": (lax.axis_index("tp") + k) % 4} for k in (1, 2, 3)]


def pieces_of(rows):
    return (pl.ds(0, 48), pl.ds(48, rows - 48))


def sum_cores(part, crossed, send, recv):
    core = lax.axis_index("core")
    return [
        remote(part.at[1 - core, :, rows], crossed.at[:, rows], send.at[p], recv.at[p], {"core": 1 - core})
        for p, rows in enumerate(pieces_of(part.shape[2]))
    ]


def sum_terms(both, part, landed, send, recv):
    block = lax.axis_index("core") if both else 0
    return [
        [
            remote(
                part.at[block, peer["tp"], rows], landed.at[k, rows],
                send.at[3 * p + k], recv.at[3 * p + k], peer,
            )
            for k, peer in enumerate(tp_peers())
        ]
        for p, rows in enumerate(pieces_of(part.shape[2]))
    ]


def sum_results(out, send, recv):
    core, tp = lax.axis_index("core"), lax.axis_index("tp")
    return [
        [
            remote(out.at[core, tp, rows], out.at[core, tp, rows], send.at[3 * p + k], recv.at[3 * p + k], peer)
            for k, peer in enumerate(tp_peers())
        ]
        for p, rows in enumerate(pieces_of(out.shape[2]))
    ]


def sum_cross(out, send, recv):
    core, tp = lax.axis_index("core"), lax.axis_index("tp")
    return [
        [
            remote(
                out.at[core, at, rows], out.at[core, at, rows],
                send.at[4 * p + k], recv.at[4 * p + k], {"core": 1 - core},
            )
            for k, at in enumerate([(tp + 4 - k) % 4 for k in range(4)])
        ]
        for p, rows in enumerate(pieces_of(out.shape[2]))
    ]


def sum_start(both, out, part, landed, rs, rr, gs, gr, cs, cr, crossed=None, ps=None, pr=None):
    terms = sum_terms(both, part, landed, rs, rr)
    if both:
        core = lax.axis_index("core")
        pres = sum_cores(part, crossed, ps, pr)
        for pre in pres:
            pre.start()
    for p, rows in enumerate(pieces_of(part.shape[2])):
        if both:
            pres[p].wait_recv()
            for j in range(4):
                total = part[core, j, rows].astype(f32) + crossed[j, rows].astype(f32)
                part[core, j, rows] = total.astype(bf16)
        for copy in terms[p]:
            copy.start()


def sum_middle(both, out, part, landed, rs, rr, gs, gr, cs, cr, *pre):
    core, tp = lax.axis_index("core"), lax.axis_index("tp")
    terms, results, crosses = sum_terms(both, part, landed, rs, rr), sum_results(out, gs, gr), sum_cross(out, cs, cr)
    for p, rows in enumerate(pieces_of(part.shape[2])):
        total = part[core if both else 0, tp, rows].astype(f32)
        for k, copy in enumerate(terms[p]):
            copy.wait_recv()
            total = total + landed[k, rows].astype(f32)
        out[core, tp, rows] = total.astype(bf16)
        for copy in results[p]:
            copy.start()
        crosses[p][0].start()


def sum_end(both, out, part, landed, rs, rr, gs, gr, cs, cr, *pre):
    terms, results, crosses = sum_terms(both, part, landed, rs, rr), sum_results(out, gs, gr), sum_cross(out, cs, cr)
    for p in range(2):
        for k in range(3):
            results[p][k].wait_recv()
            crosses[p][k + 1].start()
    for p in range(2):
        for copy in crosses[p]:
            copy.wait()
        for copy in terms[p] + results[p]:
            copy.wait_send()
    if both:
        for copy in sum_cores(part, *pre):
            copy.wait_send()


def sum_scratch(both, rows):
    scratch = [
        pltpu.VMEM((2 if both else 1, 4, rows, 384), bf16),
        pltpu.VMEM((3, rows, 384), bf16),
    ] + dma_sems(6, 6, 8)
    if both:
        scratch += [pltpu.VMEM((4, rows, 384), bf16)] + dma_sems(2)
    return scratch


def chip_peers():
    core, zl = lax.axis_index("core"), lax.axis_index("zl")
    return {"core": 1 - core}, {"zl": 1 - zl}, zl * 2 + core


def cross_kernel(own, out, send, recv):
    other = {"core": 1 - lax.axis_index("core")}
    arrive([other])
    all_here(1)
    copy = remote(own, out, send.at[0], recv.at[0], other)
    copy.start()
    copy.wait()


def cross(own, cid):
    return pl.pallas_call(
        cross_kernel,
        out_shape=jax.ShapeDtypeStruct(own.shape, own.dtype),
        in_specs=[VMEM],
        out_specs=VMEM,
        scratch_shapes=dma_sems(1),
        compiler_params=params(cid, 8),
        name="cross",
    )(own)


def places():
    return lax.axis_index("x"), lax.axis_index("zh") * 2 + lax.axis_index("zl")


def axis_peer(along_x, k):
    x, z = places()
    if along_x:
        return {"x": (x + k) % 4}, (x + k) % 4
    to = (z + k) % 4
    return {"zh": to // 2, "zl": to % 2}, to


def half(rows, route):
    return pl.ds(route * (rows // 2), rows // 2)


def uneven(rows, route):
    first = {128: 80, 64: 48}[rows]
    return pl.ds(first, rows - first) if route else pl.ds(0, first)


def line(whole, route, second, rows):
    return whole.at[:, second, rows] if route == 0 else whole.at[second, :, rows]


def axis_peers(*ks):
    return [axis_peer(along_x, k)[0] for along_x in (True, False) for k in ks]


def start_kernel(
    images, urgent, later, out_images, all_urgent, all_later, own_sem, im_s, im_r, u1_s, u1_r, u2_s, u2_r, l_s, l_r
):
    core = lax.axis_index("core")
    at_x, at_z = places()
    high = at_x // 2
    other = {"core": 1 - core}
    arrive(axis_peers(1, 2, 3) + [other])
    all_urgent[at_x, at_z] = urgent[...]
    out_images[core, high] = images[high]
    own = pltpu.make_async_copy(later, all_later.at[at_x, at_z], own_sem)
    own.start()
    all_here(7)
    firsts, seconds, laters = [], [], []
    for route in range(2):
        b = (at_z, at_x)[route]
        rows, late = uneven(urgent.shape[0], route), half(later.shape[0], route)
        for k in range(1, 4):
            peer, _ = axis_peer(route == 0, k)
            n = 3 * route + k - 1
            firsts.append(
                remote(urgent.at[rows], all_urgent.at[at_x, at_z, rows], u1_s.at[n], u1_r.at[n], peer)
            )
            laters.append(
                remote(later.at[late], all_later.at[at_x, at_z, late], l_s.at[n], l_r.at[n], peer)
            )
            slabs = line(all_urgent, route, b, rows)
            seconds.append(remote(slabs, slabs, u2_s.at[n], u2_r.at[n], axis_peer(route == 1, k)[0]))
    swap = remote(images.at[1 - high], out_images.at[core, high], im_s.at[0], im_r.at[0], {"x": (at_x + 2) % 4})
    kept = remote(images.at[high], out_images.at[core, high], im_s.at[1], im_r.at[1], other)
    passed = remote(
        out_images.at[core, 1 - high], out_images.at[core, 1 - high], im_s.at[2], im_r.at[2], other
    )
    for copy in firsts + [swap, kept] + laters:
        copy.start()
    for copy in firsts:
        copy.wait_recv()
    for copy in seconds:
        copy.start()
    swap.wait_recv()
    passed.start()
    for copy in seconds + laters + [kept, passed]:
        copy.wait()
    for copy in firsts + [swap]:
        copy.wait_send()
    own.wait()


def start_exchange(images, urgent, later):
    return pl.pallas_call(
        start_kernel,
        out_shape=[
            jax.ShapeDtypeStruct(s, bf16)
            for s in ((2,) + images.shape, (4, 4) + urgent.shape, (4, 4) + later.shape)
        ],
        in_specs=[VMEM] * 3,
        out_specs=[VMEM, VMEM, ANY],
        scratch_shapes=[pltpu.SemaphoreType.DMA] + dma_sems(3, 6, 6, 6),
        compiler_params=params(1, 56),
        name="start_exchange",
    )(images, urgent, later)


def spread_near(whole, send, recv):
    copies = []
    for route in range(2):
        slabs = line(whole, route, places()[1 - route], half(whole.shape[2], route))
        for n, k in enumerate((1, 3)):
            at, peer = 2 * route + n, axis_peer(route == 1, k)[0]
            copies.append(remote(slabs, slabs, send.at[at], recv.at[at], peer))
    return copies


def spread_far(whole, send, recv):
    copies = []
    size = whole.shape[2] // 2
    cut = size // 32 * 16 + size % 32
    for route in range(2):
        b = places()[1 - route]
        for n, k in enumerate((1, 3)):
            rows = pl.ds(route * size + n * cut, size - cut if n else cut)
            slabs = line(whole, route, (b + 4 - k) % 4, rows)
            at, peer = 4 + 2 * route + n, axis_peer(route == 1, k)[0]
            copies.append(remote(slabs, slabs, send.at[at], recv.at[at], peer))
    return copies


def part_rows(rows, route, n):
    size = rows // 2
    cut = size // 32 * 16 + size % 32
    return pl.ds(route * size + n * cut, size - cut if n else cut)


def toward_far(whole, passing, route, send, recv):
    copies, b = [], places()[1 - route]
    for n, k in enumerate((1, 3)):
        rows = part_rows(whole.shape[2], route, n)
        target = passing.at[route, n, :, 0 : rows.size]
        at, peer = 2 * route + n, axis_peer(route == 1, k)[0]
        copies.append(remote(line(whole, route, (b + 2) % 4, rows), target, send.at[at], recv.at[at], peer))
    return copies


def toward_near(whole, passing, landed, route, send, recv):
    copies, b = [], places()[1 - route]
    for n, k in enumerate((1, 3)):
        rows, others = (part_rows(whole.shape[2], route, m) for m in (n, 1 - n))
        at, peer = 4 * route + 2 * n, axis_peer(route == 1, k)[0]
        copies += [
            remote(passing.at[route, n, :, 0 : rows.size], landed.at[n, :, rows], send.at[at], recv.at[at], peer),
            remote(
                line(whole, route, (b + k) % 4, others), landed.at[n, :, others],
                send.at[at + 1], recv.at[at + 1], peer,
            ),
        ]
    return copies


def add_passing(whole, passing, route):
    x, z = places()
    b = (z, x)[route]
    for n, k in enumerate((1, 3)):
        rows, to = part_rows(whole.shape[2], route, n), (b + k) % 4

        def add(j, carry, n=n, rows=rows, to=to):
            own = whole[j, to, rows] if route == 0 else whole[to, j, rows]
            total = passing[route, n, j, 0 : rows.size].astype(f32) + own.astype(f32)
            passing[route, n, j, 0 : rows.size] = total.astype(bf16)
            return carry

        lax.fori_loop(0, 4, add, 0)


def last_copies(some, slabs, send, recv):
    copies = []
    for route in range(2):
        rows = half(some.shape[1], route)
        for k in range(1, 4):
            peer, at = axis_peer(route == 0, k)
            n = 3 * route + k - 1
            copies.append(remote(some.at[at, rows], slabs.at[k - 1, rows], send.at[n], recv.at[n], peer))
    return copies


def add_slabs(some, slabs, out):
    x, z = places()
    steps = some.shape[1] // 48

    def add(i, carry):
        rows, route = pl.ds(pl.multiple_of(i * 48, 48), 48), i // (steps // 2)
        total = some[x * (1 - route) + z * route, rows].astype(f32)
        for k in range(3):
            total = total + slabs[k, rows].astype(f32)
        out[rows] = total.astype(bf16)
        return carry

    lax.fori_loop(0, steps, add, 0)


def end_kernel(
    part, image, half_sum, some, some_attn, tiny, out_image, grad_in, grad_out, grad_attn,
    out, out_half, own_sum, other_sum, landed, sums, pieces, mids, lands, slabs, attn_slabs, cx_s, cx_r, sl_s, sl_r, at_s, at_r, p1_s, p1_r, p2_s, p2_r,
):
    def own_lines(rows):
        rows = rows.astype(f32)
        return jnp.where(core == 0, rows[0:24], rows[24:48])

    def put_experts(layer, own, got):
        for at in range(2 * EXPERTS):
            rows = slice(48 * at, 48 * at + 48)
            mine, others = own_lines(own[rows]), own_lines(got[rows])
            ref = grad_out if at % 2 else grad_in
            ref[layer, at // 2, :, 0:FE] = jnp.where(core == 0, mine, others)
            ref[layer, at // 2, :, FE:] = jnp.where(core == 0, others, mine)

    core, x = lax.axis_index("core"), lax.axis_index("x")
    other = {"core": 1 - core}
    arrive(axis_peers(1, 2, 3) + [other])
    all_here(7)
    crossing = remote(part.at[1 - core], landed, cx_s.at[0], cx_r.at[0], other)
    crossing.start()
    lasts = last_copies(some, slabs, sl_s, sl_r)
    firsts, seconds = [], []
    for route in range(2):
        rows = uneven(64, route)
        for k in range(1, 4):
            peer, at = axis_peer(route == 0, k)
            n = 3 * route + k - 1
            lasts.append(
                remote(some_attn.at[route, at], attn_slabs.at[route, k - 1], at_s.at[n], at_r.at[n], peer)
            )
            seconds.append(remote(mids.at[at, rows], lands.at[k - 1, rows], p2_s.at[n], p2_r.at[n], peer))
            peer, at = axis_peer(route == 1, k)
            firsts.append(
                remote(line(sums, route, at, rows), pieces.at[k - 1, :, rows], p1_s.at[n], p1_r.at[n], peer)
            )
    swap = remote(image, out_image, cx_s.at[1], cx_r.at[1], {"x": (x + 2) % 4})
    halves = remote(half_sum, out_half, cx_s.at[2], cx_r.at[2], other)
    for copy in lasts + [halves]:
        copy.start()
    crossing.wait()

    def add(i, carry):
        total = part[core, i // 4, i % 4].astype(f32) + landed[i // 4, i % 4].astype(f32)
        sums[i // 4, i % 4] = total.astype(bf16)
        return carry

    lax.fori_loop(0, 16, add, 0)
    for copy in firsts + [swap]:
        copy.start()
    halves.wait_recv()
    put_experts(1, half_sum, out_half)
    for copy in firsts:
        copy.wait_recv()
    at_x, at_z = places()
    for route in range(2):
        rows = uneven(64, route)

        def gather(j, carry, route=route, rows=rows):
            total = (sums[j, at_z, rows] if route == 0 else sums[at_x, j, rows]).astype(f32)
            for k in range(3):
                total = total + pieces[k, j, rows].astype(f32)
            mids[j, rows] = total.astype(bf16)
            return carry

        lax.fori_loop(0, 4, gather, 0)
    for copy in seconds:
        copy.start()
    for copy in lasts:
        copy.wait()
    add_slabs(some, slabs, own_sum)
    for route in range(2):
        attn = some_attn[route, places()[route]].astype(f32)
        for k in range(3):
            attn = attn + attn_slabs[route, k].astype(f32)
        first = 384 + 48 * route
        own_sum[first : first + 48] = attn.astype(bf16)
    final = remote(own_sum, other_sum, cx_s.at[3], cx_r.at[3], other)
    final.start()
    for copy in seconds:
        copy.wait()
    for route in range(2):
        rows = uneven(64, route)
        total = mids[places()[route], rows].astype(f32)
        for k in range(3):
            total = total + lands[k, rows].astype(f32)
        out[core, rows] = total
    given = remote(out.at[core], out.at[core], cx_s.at[4], cx_r.at[4], other)
    given.start()
    final.wait()
    put_experts(0, own_sum, other_sum)
    given.wait()
    for route in range(2):
        first = 384 + 48 * route
        rows = slice(first, first + 48)
        grad_attn[0, route] = own_lines(out[route, 0:48])
        grad_attn[1, route] = own_lines(own_sum[rows]) + own_lines(other_sum[rows])
        tiny[route] = jnp.where(core == 0, out[route, 48:56], out[route, 56:64])
    for copy in firsts + [halves]:
        copy.wait_send()
    swap.wait()


def end_exchange(part, image, half_sum, some, some_attn):
    slab = (480, FE)
    scratch = [half_sum.shape, slab, slab] + [(4, 4, 64, FE)] * 2 + [(3, 4, 64, FE), (4, 64, FE), (3, 64, FE)]
    scratch += [(3,) + some.shape[1:], (2, 3, 48, FE)]
    return pl.pallas_call(
        end_kernel,
        out_shape=[
            jax.ShapeDtypeStruct((2, 8, FE), f32),
            jax.ShapeDtypeStruct(image.shape, bf16),
            jax.ShapeDtypeStruct((2, EXPERTS, 24, D), f32),
            jax.ShapeDtypeStruct((2, EXPERTS, 24, D), f32),
            jax.ShapeDtypeStruct((2, 2, 24, FE), f32),
        ],
        in_specs=[VMEM] * 5,
        out_specs=[VMEM] * 5,
        scratch_shapes=[pltpu.VMEM((2, 64, FE), f32)]
        + [pltpu.VMEM(s, bf16) for s in scratch]
        + dma_sems(5, 6, 6, 6, 6),
        compiler_params=params(2, 56),
        name="end_exchange",
    )(part, image, half_sum, some, some_attn)


def block_rows(ref, block):
    top = jnp.concatenate([ref[block, 0, 0:80], ref[block, 1, 0:80]], axis=1)
    low = jnp.concatenate([ref[block, 2, 0:80], ref[block, 3, 0:80]], axis=1)
    return jnp.concatenate([top, low], axis=0).astype(f32)


def pair_rows(ref):
    return jnp.concatenate([block_rows(ref, 0), block_rows(ref, 1)], axis=0)


def put_chunks(ref, block, value, first=0):
    for j in range(4):
        r, c = 80 * (j // 2), 384 * (j % 2)
        ref[block, j, first : first + 80] = value[r : r + 80, c : c + 384]


def norm_parts(rows):
    centered = rows - jnp.mean(rows, axis=-1, keepdims=True)
    scale = lax.rsqrt(jnp.mean(centered * centered, axis=-1, keepdims=True) + EPS)
    return centered * scale, scale


def norm_back(grad, unit, scale, gain):
    inner = grad * gain
    return scale * (
        inner
        - jnp.mean(inner, axis=-1, keepdims=True)
        - unit * jnp.mean(inner * unit, axis=-1, keepdims=True)
    )


def softmax(logits, axis):
    top = jnp.max(logits, axis=axis, keepdims=True)
    powers = jnp.exp(logits - top)
    return powers / jnp.sum(powers, axis=axis, keepdims=True)


def own_rows(core):
    return pl.ds(pl.multiple_of(core * ROWS, ROWS), ROWS)


def head(value, h):
    return value[:, HD * h : HD * h + HD]


def gelu_parts(u):
    c = 0.7978845608028654
    t = jnp.tanh(c * (u + 0.044715 * u * u * u))
    return 0.5 * u * (1.0 + t), t


def gelu_slope(u, t):
    c = 0.7978845608028654
    return 0.5 * (1.0 + t) + 0.5 * u * (1.0 - t * t) * (c * (1.0 + 3 * 0.044715 * u * u))


def attn_weights(weights):
    chips = (slice(None),) * (len(weights.shape) - 2)
    w_kv = weights[(*chips, slice(0, 48))].reshape(D, 2 * WIDTH)
    w_q = weights[(*chips, slice(48, 96), slice(0, WIDTH))].reshape(D, WIDTH)
    return w_kv, w_q, weights[(*chips, slice(48, 96), slice(WIDTH, None))].reshape(D, WIDTH)


def attend_forward_kernel(follows, *refs):
    if follows:
        x, att_before, moe_before, small, weights, dead, q, kv, mixed, att, x_next, *scratch = refs
    else:
        x, small, weights, dead, ahead, _, q, kv, mixed, att, whole, all_ahead, *scratch = refs
        *scratch, sp_send, sp_recv, ah_send, ah_recv, own_sem = scratch
    part, landed, *sems, kv_send, kv_recv = scratch
    sums = (False, att, part, landed, *sems)
    core = lax.axis_index("core")
    other, across, me = chip_peers()
    arrive([other, across] + tp_peers())
    if not follows:
        arrive(axis_peers(1, 2, 3))
    if follows:
        x_next[...] = (x[...].astype(f32) + pair_rows(att_before) + pair_rows(moe_before)).astype(bf16)
        x = x_next
    unit, _ = norm_parts(x[own_rows(core)].astype(f32))
    normed = (unit * small[0:1] + small[2:3]).astype(bf16)
    w_kv, w_q, w_out_t = attn_weights(weights)
    kv[me] = dot(normed, w_kv, NN).astype(bf16)
    all_here(5 if follows else 11)
    far = (me + 2) % 4
    copies = [
        remote(kv.at[at], kv.at[at], kv_send.at[k], kv_recv.at[k], peer)
        for k, (at, peer) in enumerate(((me, across), (me, other), (far, other)))
    ]
    copies[0].start()
    copies[1].start()
    if not follows:
        nears = spread_near(whole, sp_send, sp_recv)
        fars = spread_far(whole, sp_send, sp_recv)
        at_x, at_z = places()
        aheads = [pltpu.make_async_copy(ahead, all_ahead.at[at_x, at_z], own_sem)]
        for route in range(2):
            rows = half(ahead.shape[0], route)
            for k in range(1, 4):
                n, peer = 3 * route + k - 1, axis_peer(route == 0, k)[0]
                aheads.append(
                    remote(ahead.at[rows], all_ahead.at[at_x, at_z, rows], ah_send.at[n], ah_recv.at[n], peer)
                )
        for copy in nears + aheads:
            copy.start()
    queries = dot(normed, w_q, NN).astype(bf16)
    q[...] = queries
    copies[0].wait_recv()
    copies[2].start()
    copies[1].wait_recv()
    copies[2].wait_recv()
    keys = kv[...].reshape(KEYS, 2 * WIDTH)
    outs = []
    for h in range(HEADS):
        scores = HD**-0.5 * dot(head(queries, h), head(keys, h), NT) + dead[...]
        probs = softmax(scores, -1).astype(bf16)
        outs.append(dot(probs, head(keys, HEADS + h), NN))
    heads = jnp.concatenate(outs, axis=1).astype(bf16)
    mixed[...] = heads
    put_chunks(part, 0, dot(heads, w_out_t, NT).astype(bf16))
    sum_start(*sums)
    sum_middle(*sums)
    if not follows:
        for copy in nears:
            copy.wait_recv()
        for copy in fars:
            copy.start()
    sum_end(*sums)
    for copy in copies:
        copy.wait_send()
    if not follows:
        for copy in fars + aheads:
            copy.wait()
        for copy in nears:
            copy.wait_send()


def attend_forward(x, before, small, weights, dead, some, ahead, cid):
    args = (x, *before, small, weights, dead)
    shapes = [(ROWS, WIDTH), (4, ROWS, 2 * WIDTH), (ROWS, WIDTH), (2, 4, 80, 384)]
    in_specs, out_specs = [VMEM] * len(args), [VMEM] * 5
    scratch = sum_scratch(False, 80) + dma_sems(3)
    if before:
        shapes.append((PAIR, D))
    else:
        args += (ahead, some)
        shapes += [some.shape, (4, 4) + ahead.shape]
        in_specs += [VMEM, ANY]
        out_specs[4:] = [ANY, ANY]
        scratch += dma_sems(8, 6) + [pltpu.SemaphoreType.DMA]
    return pl.pallas_call(
        functools.partial(attend_forward_kernel, bool(before)),
        out_shape=[jax.ShapeDtypeStruct(s, bf16) for s in shapes],
        in_specs=in_specs,
        out_specs=out_specs,
        scratch_shapes=scratch,
        input_output_aliases={} if before else {len(args) - 1: 4},
        compiler_params=params(cid, 56),
        name="attend_forward",
    )(*args)


def expert_weights(weights):
    block = weights[...]
    return block[:, 0:48].reshape(D, FE), block[:, 48:96].reshape(D, FE)


def experts_setup(x, att, small, routes, b, gates):
    unit, _ = norm_parts(x[...].astype(f32) + pair_rows(att))
    b[...] = (unit * small[1:2] + small[3:4]).astype(bf16)
    put_gates(b, small, routes, gates)


def put_gates(b, small, routes, gates):
    probs = softmax(dot(b[...], small[4:8].astype(bf16), NT), -1)
    ids = lax.broadcasted_iota(jnp.int32, (PAIR, EXPERTS), 1).astype(f32)
    ones = lax.broadcasted_iota(jnp.int32, (16, 16), 0) == lax.broadcasted_iota(jnp.int32, (16, 16), 1)
    lines = dot(routes[...], ones.astype(f32).astype(bf16), TN)
    named = (lines[:, 0:1] == ids) | (lines[:, 1:2] == ids)
    gates[...] = jnp.where(named, probs, 0.0)


def gate_of(gates, expert):
    ids = lax.broadcasted_iota(jnp.int32, (PAIR, EXPERTS), 1)
    return jnp.sum(jnp.where(ids == expert, gates[...], 0.0), axis=1, keepdims=True)


def fixed(shape):
    return pl.BlockSpec(shape, lambda e: (0,) * len(shape))


def middle_kernel(
    x, att, small, routes, small_next, dead, ahead, later, weights,
    q, kv_result, mixed, att_result, x_next, attn_result, whole,
    b, gates, total, moe, attn_w, kv, att_next,
    ah_send, ah_recv, l_send, l_recv, sp_send, sp_recv, kv_send, kv_recv, own_sem, *sems,
):
    expert = pl.program_id(0)
    sums, sums_next = (True, moe, *sems[:11]), (False, att_next, *sems[11:])
    part, part_next = sums[2], sums_next[2]
    core = lax.axis_index("core")
    at_x, at_z = places()
    other, across, me = chip_peers()
    far = (me + 2) % 4
    aheads, laters = [], []
    for route in range(2):
        second, rows, late = (at_z, at_x)[route], half(ahead.shape[2], route), half(later.shape[0], route)
        for k in range(1, 4):
            n = 3 * route + k - 1
            aheads.append(
                remote(
                    line(ahead, route, second, rows), line(attn_w, route, second, rows),
                    ah_send.at[n], ah_recv.at[n], axis_peer(route == 1, k)[0],
                )
            )
            laters.append(
                remote(
                    later.at[late], whole.at[at_x, at_z, late],
                    l_send.at[n], l_recv.at[n], axis_peer(route == 0, k)[0],
                )
            )
    own = pltpu.make_async_copy(later, whole.at[at_x, at_z], own_sem)
    nears, fars = spread_near(whole, sp_send, sp_recv), spread_far(whole, sp_send, sp_recv)

    @pl.when(expert == 0)
    def _():
        arrive([other, across] + tp_peers() + axis_peers(1, 2, 3))
        experts_setup(x, att, small, routes, b, gates)
        total[...] = jnp.zeros_like(total)
        for j in range(4):
            rows = half(ahead.shape[2], 0)
            attn_w[j, at_z, rows] = ahead[j, at_z, rows]
            rows = half(ahead.shape[2], 1)
            attn_w[at_x, j, rows] = ahead[at_x, j, rows]
        all_here(11)
        for copy in aheads + laters + [own]:
            copy.start()

    w_in, w_out_t = expert_weights(weights)
    u = dot(b[...], w_in, NN)
    active = gelu_parts(u)[0].astype(bf16).astype(f32)
    gated = (gate_of(gates, expert) * active).astype(bf16)
    total[...] += dot(gated, w_out_t, NT)

    @pl.when(expert == EXPERTS - 1)
    def _():
        for block in range(2):
            put_chunks(part, block, total[ROWS * block : ROWS * block + ROWS].astype(bf16))
        sum_start(*sums)
        for copy in laters:
            copy.wait_recv()
        own.wait()
        for copy in nears:
            copy.start()
        sum_middle(*sums)
        sum_end(*sums)
        x_next[...] = (x[...].astype(f32) + pair_rows(att) + pair_rows(moe)).astype(bf16)
        unit, _ = norm_parts(x_next[own_rows(core)].astype(f32))
        normed = (unit * small_next[0:1] + small_next[2:3]).astype(bf16)
        for copy in aheads:
            copy.wait_recv()
        w_kv, w_q, w_out = attn_weights(attn_w)
        kv[me] = dot(normed, w_kv, NN).astype(bf16)
        copies = [
            remote(kv.at[at], kv.at[at], kv_send.at[k], kv_recv.at[k], peer)
            for k, (at, peer) in enumerate(((me, across), (me, other), (far, other)))
        ]
        copies[0].start()
        copies[1].start()
        queries = dot(normed, w_q, NN).astype(bf16)
        q[...] = queries
        attn_result[...] = attn_w[...]
        copies[0].wait_recv()
        copies[2].start()
        copies[1].wait_recv()
        copies[2].wait_recv()
        keys = kv[...].reshape(KEYS, 2 * WIDTH)
        outs = []
        for h in range(HEADS):
            scores = HD**-0.5 * dot(head(queries, h), head(keys, h), NT) + dead[...]
            probs = softmax(scores, -1).astype(bf16)
            outs.append(dot(probs, head(keys, HEADS + h), NN))
        heads = jnp.concatenate(outs, axis=1).astype(bf16)
        mixed[...] = heads
        put_chunks(part_next, 0, dot(heads, w_out, NT).astype(bf16))
        sum_start(*sums_next)
        for copy in nears:
            copy.wait_recv()
        for copy in fars:
            copy.start()
        kv_result[...] = kv[...]
        sum_middle(*sums_next)
        sum_end(*sums_next)
        att_result[...] = att_next[...]
        for copy in copies + nears + laters + aheads:
            copy.wait_send()
        for copy in fars:
            copy.wait()


def middle(x, att, small, routes, small_next, dead, ahead, later, weights, cid):
    args = (x, att, small, routes, small_next, dead, ahead, later)
    shapes = [(ROWS, WIDTH), (4, ROWS, 2 * WIDTH), (ROWS, WIDTH), (2, 4, 80, 384), (PAIR, D), ahead.shape]
    return pl.pallas_call(
        middle_kernel,
        grid=(EXPERTS,),
        out_shape=[jax.ShapeDtypeStruct(s, bf16) for s in shapes + [(4, 4) + later.shape]],
        in_specs=[fixed(a.shape) for a in args] + [pl.BlockSpec((16, 96, FE), lambda e: (0, e, 0))],
        out_specs=[fixed(s) for s in shapes] + [ANY],
        scratch_shapes=[
            pltpu.VMEM((PAIR, D), bf16),
            pltpu.VMEM((PAIR, EXPERTS), f32),
            pltpu.VMEM((PAIR, D), f32),
            pltpu.VMEM((2, 4, 80, 384), bf16),
            pltpu.VMEM(ahead.shape, bf16),
            pltpu.VMEM((4, ROWS, 2 * WIDTH), bf16),
            pltpu.VMEM((2, 4, 80, 384), bf16),
        ]
        + dma_sems(6, 6, 8, 3)
        + [pltpu.SemaphoreType.DMA]
        + sum_scratch(True, 80)
        + sum_scratch(False, 80),
        compiler_params=params(cid, 56),
        name="middle",
    )(*args, weights)


def layer_backward_kernel(with_moe, *refs):
    x, att, small, routes, grad, q, kv, mixed, dead, attn_w, *refs = refs
    if not with_moe:
        extra, some_before, *refs = refs
    weights, grad_x, grad_small, grad_w, some, *refs = refs
    if with_moe:
        moe_result, *refs = refs
    else:
        own_sum, some_attn, *refs = refs
    b, gates, unit_two, scale_two, total, gate_grads, gated_all, grad_u_all, *refs = refs
    whole, slabs, passing, all_probs, grad_h, unit_one, parts, kv_landed, kv_out, back, back_one, *refs = refs
    fs, fr, ns, nr, kv_send, kv_recv, *refs = refs
    sums_two, sums_one, refs = (True, back, *refs[:11]), (False, back_one, *refs[11:19]), refs[19:]
    part_two, part_one = sums_two[2], sums_one[2]
    if with_moe:
        moe, moe_part, moe_out, moe_landed, ms, mr, mg, mh, moe_crossed, ps, pr = refs
        moe_sums = (moe_part, moe_crossed, ps, pr)
    else:
        last_slabs, ls, lr, attn_slabs, as_, ar = refs
        lasts = last_copies(some_before, last_slabs, ls, lr)
        for route in range(2):
            for k in range(1, 4):
                n, (peer, to) = 3 * route + k - 1, axis_peer(route == 1, k)
                slab = extra.at[0, :, to] if route == 0 else extra.at[1, to]
                lasts.append(remote(slab, attn_slabs.at[route, k - 1], as_.at[n], ar.at[n], peer))
    fars = [toward_far(whole, passing, route, fs, fr) for route in range(2)]
    nears = [toward_near(whole, passing, slabs, route, ns, nr) for route in range(2)]
    core, tp = lax.axis_index("core"), lax.axis_index("tp")
    at_x, at_z = places()
    other, across, me = chip_peers()
    far = (me + 2) % 4
    step = pl.program_id(0)

    @pl.when(step == 0)
    def _():
        arrive([other, across] + tp_peers() + axis_peers(1, 2, 3))
        unit, scale = norm_parts(x[...].astype(f32) + pair_rows(att))
        unit_two[...] = unit
        scale_two[...] = scale
        b[...] = (unit * small[1:2] + small[3:4]).astype(bf16)
        put_gates(b, small, routes, gates)
        total[...] = jnp.zeros_like(total)
        gate_grads[...] = jnp.zeros_like(gate_grads)
        if with_moe:
            moe[...] = jnp.zeros_like(moe)
        all_here(11)
        if not with_moe:
            for copy in lasts:
                copy.start()

    @pl.when(step < EXPERTS)
    def _():
        w_in, w_out_t = expert_weights(weights)
        u = dot(b[...], w_in, NN)
        act, t = gelu_parts(u)
        active = act.astype(bf16).astype(f32)
        gate = gate_of(gates, step)
        gated = (gate * active).astype(bf16)
        gated_all[step] = gated
        if with_moe:
            moe[...] += dot(gated, w_out_t, NT)
        grad_active = dot(grad[...], w_out_t, NN)
        ids = lax.broadcasted_iota(jnp.int32, (PAIR, 128), 1)
        gate_grad = jnp.sum(grad_active * active, axis=1, keepdims=True)
        gate_grads[...] = jnp.where(ids == step, gate_grad, gate_grads[...])
        grad_u = (gate * grad_active * gelu_slope(u, t)).astype(bf16)
        grad_u_all[step] = grad_u
        total[...] += dot(grad_u, w_in, NT)

    @pl.when(step == EXPERTS - 1)
    def _():
        part_two[...] = jnp.zeros_like(part_two)
        lines, lanes = (lax.broadcasted_iota(jnp.int32, (16, 128), axis) for axis in range(2))
        ones = ((lines == lanes) & (lines < EXPERTS)).astype(f32).astype(bf16)
        for block in range(2):
            rows = slice(ROWS * block, ROWS * block + ROWS)
            put_chunks(part_two, block, total[rows].astype(bf16))
            part_two[block, 0, 80:96, 0:ROWS] = dot(ones, gate_grads[rows].astype(bf16), NT).astype(bf16)
            if with_moe:
                put_chunks(moe_part, block, moe[rows].astype(bf16))
        sum_start(*sums_two)

    @pl.when(step >= EXPERTS)
    def _():
        at = step - EXPERTS
        first = pl.multiple_of(96 * at, 96)
        grad_in = dot(b[...], grad_u_all[at], TN).astype(bf16)
        whole[:, :, pl.ds(first, 48)] = grad_in.reshape(4, 4, 48, FE)
        grad_out = dot(grad[...], gated_all[at], TN).astype(bf16)
        whole[:, :, pl.ds(first + 48, 48)] = grad_out.reshape(4, 4, 48, FE)

    @pl.when(step == EXPERTS + 1)
    def _():
        sum_middle(*sums_two)

    @pl.when(step == 2 * EXPERTS - 2)
    def _():
        keys = kv[...].reshape(KEYS, 2 * WIDTH)
        for h in range(HEADS):
            all_probs[h] = softmax(HD**-0.5 * dot(head(q[...], h), head(keys, h), NT) + dead[...], -1)
        if not with_moe:
            for copy in lasts:
                copy.wait()
            add_slabs(some_before, last_slabs, own_sum)
            for route in range(2):

                def add(j, carry, route=route):
                    attn = (extra[0, j, at_z] if route == 0 else extra[1, at_x, j]).astype(f32)
                    for k in range(3):
                        attn = attn + attn_slabs[route, k, j].astype(f32)
                    some_attn[route, j] = attn.astype(bf16)
                    return carry

                lax.fori_loop(0, 4, add, 0)

    @pl.when(step == 2 * EXPERTS - 1)
    def _():
        for copy in fars[1] + fars[0]:
            copy.start()
        sum_end(*sums_two)
        router = small[4:8]
        chances = softmax(dot(router.astype(bf16), b[...], NT), 0)
        ids = lax.broadcasted_iota(jnp.int32, (EXPERTS, PAIR), 0).astype(f32)
        lines = routes[...].astype(f32)
        named = (lines[0:1] == ids) | (lines[1:2] == ids)
        tables = [back[block, 0, 80:96, 0:ROWS].astype(f32)[0:EXPERTS] for block in range(2)]
        gate_rows = jnp.where(named, jnp.concatenate(tables, axis=1), 0.0)
        grad_logits = chances * (gate_rows - jnp.sum(chances * gate_rows, axis=0, keepdims=True))
        grad_b = pair_rows(back) + dot_split(grad_logits, router.astype(bf16), TN)
        grad_h[...] = grad[...].astype(f32) + norm_back(grad_b, unit_two[...], scale_two[...], small[1:2])
        grad_att = grad_h[own_rows(core)].astype(bf16)
        w_kv, w_q, w_out_t = attn_weights(attn_w)
        grad_mixed = dot(grad_att, w_out_t, NN).astype(bf16)
        keys = kv[...].reshape(KEYS, 2 * WIDTH)
        queries = q[...]
        q_parts, k_parts, v_parts = [], [], []
        for h in range(HEADS):
            q_h, g_h = head(queries, h), head(grad_mixed, h)
            k_h, v_h = head(keys, h), head(keys, HEADS + h)
            probs = all_probs[h]
            v_parts.append(dot(probs.astype(bf16), g_h, TN))
            grad_weights = dot(g_h, v_h, NT)
            grad_scores = probs * (grad_weights - jnp.sum(probs * grad_weights, axis=-1, keepdims=True))
            grad_scores = grad_scores.astype(bf16)
            q_parts.append(HD**-0.5 * dot(grad_scores, k_h, NN))
            k_parts.append(HD**-0.5 * dot(grad_scores, q_h, TN))
        grad_keys = jnp.concatenate(k_parts + v_parts, axis=1).astype(bf16)
        parts[...] = grad_keys.reshape(4, ROWS, 2 * WIDTH)
        crosses = [
            remote(parts.at[(at + 1 - 2 * core) % 4], kv_landed.at[k], kv_send.at[k], kv_recv.at[k], other)
            for k, at in enumerate((me, far))
        ]
        onward = remote(kv_out, kv_landed.at[2], kv_send.at[2], kv_recv.at[2], across)
        crosses[1].start()
        crosses[0].start()
        if with_moe:
            pres = sum_cores(*moe_sums)
            for copy in pres:
                copy.start()
        crosses[1].wait_recv()
        kv_out[...] = (parts[far].astype(f32) + kv_landed[1].astype(f32)).astype(bf16)
        onward.start()
        if with_moe:
            for copy in pres:
                copy.wait_recv()
            for j in range(4):
                moe_sum = moe_part[core, j].astype(f32) + moe_crossed[j].astype(f32)
                moe_crossed[j] = moe_sum.astype(bf16)
            moe_terms = [
                remote(moe_crossed.at[peer["tp"]], moe_landed.at[k], ms.at[k], mr.at[k], peer)
                for k, peer in enumerate(tp_peers())
            ]
            for copy in moe_terms:
                copy.start()
        for route in (1, 0):
            for copy in fars[route]:
                copy.wait_recv()
            add_passing(whole, passing, route)
            for copy in nears[route]:
                copy.start()
        grad_q = jnp.concatenate(q_parts, axis=1).astype(bf16)
        grad_w[1, :, WIDTH:] = dot(grad_att, mixed[...], TN).astype(bf16)
        lanes = lax.broadcasted_iota(jnp.int32, (EXPERTS, PAIR), 1)
        own_lanes = (lanes < ROWS) == (core == 0)
        own = (lax.broadcasted_iota(jnp.int32, (PAIR, 1), 0) < ROWS) == (core == 0)
        kept = jnp.where(own, grad_b, 0.0)
        grad_small[1:2] = jnp.sum(kept * unit_two[...], axis=0, keepdims=True)
        grad_small[3:4] = jnp.sum(kept, axis=0, keepdims=True)
        grad_small[4:8] = dot_split(jnp.where(own_lanes, grad_logits, 0.0), b[...], NN)
        unit, scale_one = norm_parts(x[...].astype(f32))
        unit_one[...] = unit
        normed = (unit_one[own_rows(core)] * small[0:1] + small[2:3]).astype(bf16)
        crosses[0].wait_recv()
        onward.wait_recv()
        grad_kv = parts[me].astype(f32) + kv_landed[0].astype(f32) + kv_landed[2].astype(f32)
        grad_kv = grad_kv.astype(bf16)
        value = dot(grad_kv, w_kv, NT) + dot(grad_q, w_q, NT)
        put_chunks(part_one, 0, value.astype(bf16))
        sum_start(*sums_one)
        grad_w[0] = dot(normed, grad_kv, TN).astype(bf16)
        grad_w[1, :, :WIDTH] = dot(normed, grad_q, TN).astype(bf16)
        sum_middle(*sums_one)
        if with_moe:
            moe_total = moe_crossed[tp].astype(f32)
            for k, copy in enumerate(moe_terms):
                copy.wait_recv()
                moe_total = moe_total + moe_landed[k].astype(f32)
            moe_out[tp] = moe_total.astype(bf16)
            moe_results = [
                remote(moe_out.at[tp], moe_out.at[tp], mg.at[k], mh.at[k], peer)
                for k, peer in enumerate(tp_peers())
            ]
            for copy in moe_results:
                copy.start()
        for route in range(2):
            for copy in fars[route]:
                copy.wait_send()
            for copy in nears[route]:
                copy.wait()
        steps = some.shape[1] // 48

        def add(i, carry):
            j, at = i % 4, i // 4
            rows, route = pl.ds(pl.multiple_of(at * 48, 48), 48), at // (steps // 2)
            mine = whole[j * (1 - route) + at_x * route, at_z * (1 - route) + j * route, rows]
            total = mine.astype(f32) + slabs[0, j, rows].astype(f32) + slabs[1, j, rows].astype(f32)
            some[j, rows] = total.astype(bf16)
            return carry

        lax.fori_loop(0, 4 * steps, add, 0)
        sum_end(*sums_one)
        grad_a = pair_rows(back_one)
        grad_x[...] = (grad_h[...] + norm_back(grad_a, unit_one[...], scale_one, small[0:1])).astype(bf16)
        kept = jnp.where(own, grad_a, 0.0)
        grad_small[0:1] = jnp.sum(kept * unit_one[...], axis=0, keepdims=True)
        grad_small[2:3] = jnp.sum(kept, axis=0, keepdims=True)
        for copy in crosses + [onward]:
            copy.wait_send()
        if with_moe:
            for copy in pres + moe_terms:
                copy.wait_send()
            for copy in moe_results:
                copy.wait()
            moe_result[...] = moe_out[...]


def layer_backward(args, others, weights, cid):
    with_moe = not others
    slab = (384, FE)
    shapes = [((PAIR, D), bf16), ((8, D), f32), ((2, D, 2 * WIDTH), bf16), ((4,) + slab, bf16)]
    scratch = [
        ((PAIR, D), bf16),
        ((PAIR, EXPERTS), f32),
        ((PAIR, D), f32),
        ((PAIR, 1), f32),
        ((PAIR, D), f32),
        ((PAIR, 128), f32),
        ((EXPERTS, PAIR, FE), bf16),
        ((EXPERTS, PAIR, FE), bf16),
        ((4, 4) + slab, bf16),
        ((2, 4) + slab, bf16),
        ((2, 2, 4, 96, FE), bf16),
        ((HEADS, ROWS, KEYS), f32),
        ((PAIR, D), f32),
        ((PAIR, D), f32),
        ((4, ROWS, 2 * WIDTH), bf16),
        ((3, ROWS, 2 * WIDTH), bf16),
        ((ROWS, 2 * WIDTH), bf16),
        ((2, 4, 96, 384), bf16),
        ((2, 4, 80, 384), bf16),
    ]
    scratch = [pltpu.VMEM(*s) for s in scratch] + dma_sems(4, 8, 3)
    scratch += sum_scratch(True, 96) + sum_scratch(False, 80)
    if with_moe:
        shapes.append(((4, 80, 384), bf16))
        scratch += [pltpu.VMEM((PAIR, D), f32), pltpu.VMEM((2, 4, 80, 384), bf16)]
        scratch += [pltpu.VMEM((4, 80, 384), bf16), pltpu.VMEM((3, 80, 384), bf16)] + dma_sems(3, 3)
        scratch += [pltpu.VMEM((4, 80, 384), bf16)] + dma_sems(2)
    else:
        shapes += [(slab, bf16), ((2, 4, 48, FE), bf16)]
        scratch += [pltpu.VMEM((3,) + slab, bf16)] + dma_sems(6)
        scratch += [pltpu.VMEM((2, 3, 4, 48, FE), bf16)] + dma_sems(6)
    args = args + others
    return pl.pallas_call(
        functools.partial(layer_backward_kernel, with_moe),
        grid=(2 * EXPERTS,),
        out_shape=[jax.ShapeDtypeStruct(*s) for s in shapes],
        in_specs=[fixed(a.shape) for a in args]
        + [pl.BlockSpec((16, 96, FE), lambda s: (0, jnp.minimum(s, EXPERTS - 1), 0))],
        out_specs=[fixed(s) for s, _ in shapes],
        scratch_shapes=scratch,
        compiler_params=params(cid, 60),
        name="layer_backward",
    )(*args, weights)


def shards(boundary, routes, lengths, ln_gains, ln_biases, w_qkv, w_out, w_router, w_in, w_exp_out):
    core = lax.axis_index("core")
    high = lax.axis_index("x") // 2

    def pick(value, at, axis):
        return lax.dynamic_index_in_dim(value, at, axis, keepdims=False)

    halves = jnp.stack(
        [
            w_qkv[:, :, 1:].reshape(2, 24, 384),
            jnp.concatenate([w_qkv[:, :, 0], w_out.transpose(0, 2, 1)], axis=2),
        ],
        axis=1,
    )

    stacked = jnp.stack([w_in, w_exp_out.transpose(0, 1, 3, 2)], axis=2).reshape(384, 2, FE)
    tiny = jnp.concatenate([ln_gains, ln_biases, w_router.transpose(0, 2, 1)], axis=1)
    tiny = jnp.pad(tiny.transpose(1, 0, 2).reshape(8, 48), ((0, 8), (0, 384 - 48)))
    attn_one, attn_zero = halves[1].reshape(48, 384), halves[0].reshape(48, 384)
    own_half = jnp.concatenate([pick(stacked, core, 1), attn_one, attn_zero, tiny])
    got_half = cross(jnp.concatenate([pick(stacked, 1 - core, 1), attn_one, attn_zero, tiny]), 0)
    low_half = jnp.where(core == 0, own_half, got_half)
    high_half = jnp.where(core == 0, got_half, own_half)
    chip = jnp.concatenate(
        [low_half[:480].reshape(20, 24, FE), high_half[:480].reshape(20, 24, FE)], axis=1
    )
    later, ahead = chip[0:8].reshape(384, FE), chip[16:18].reshape(96, FE)
    urgent = jnp.concatenate([chip[18:20].reshape(96, FE), low_half[480:496], high_half[480:496]])

    turned = jnp.pad(
        routes[0].astype(bf16).transpose(0, 2, 1), ((0, 0), (0, 14), (0, D - ROWS))
    )
    images = jnp.concatenate([boundary[0], turned], axis=1)
    got_images, packs, some = start_exchange(images, urgent, later)
    packs = packs.reshape(16, 128, 384)
    tiny = packs[:, 96:128].reshape(32, 16, 384)[:, 0:8, 0:48].reshape(32, 8, 2, 24).transpose(2, 1, 0, 3).reshape(2, 8, D)
    smalls = [tiny[0].astype(f32), tiny[1].astype(f32)]

    live = jnp.arange(ROWS, dtype=jnp.int32)[None, :] < lengths[:, None]
    dead = jnp.where(live.reshape(1, KEYS), 0.0, -1e30).astype(f32)
    chip_live = lax.dynamic_slice_in_dim(live, 2 * lax.axis_index("zl"), 2, 0)
    own_live = pick(chip_live, core, 0)

    x0 = got_images[:, 0, 0:ROWS].reshape(PAIR, D)
    cotangent = jnp.where(chip_live[:, :, None], got_images[:, 1, 0:ROWS], 0).reshape(PAIR, D)
    route_rows = [
        got_images[:, kind, ROWS:, 0:ROWS].transpose(1, 0, 2).reshape(16, PAIR) for kind in range(2)
    ]

    q0, kv0, mixed0, att0, experts_zero, ahead = attend_forward(x0, (), smalls[0], packs, dead, some, ahead, 3)
    experts_zero = experts_zero.reshape(16, 384, FE)
    q1, kv1, mixed1, att1, x1, attn_w1, experts_one = middle(
        x0, att0, smalls[0], route_rows[0], smalls[1], dead, ahead, chip[8:16].reshape(384, FE), experts_zero, 4
    )
    experts_one = experts_one.reshape(16, 384, FE)
    grad_x1, grad_small1, grad_attn1, some, moe1 = layer_backward(
        (x1, att1, smalls[1], route_rows[1], cotangent, q1, kv1, mixed1, dead, attn_w1), (), experts_one, 6
    )
    grad_x0, grad_small0, grad_attn0, some, sums1, some_attn = layer_backward(
        (x0, att0, smalls[0], route_rows[0], grad_x1, q0, kv0, mixed0, dead, packs),
        (grad_attn1.reshape(2, 4, 4, 48, FE), some),
        experts_zero,
        7,
    )

    def own_block(value):
        return pick(value, core, 0)

    def unchunk(value):
        return value.reshape(2, 2, 80, 384).transpose(0, 2, 1, 3).reshape(ROWS, D).astype(f32)

    y1 = own_block(x1.reshape(2, ROWS, D)).astype(f32) + unchunk(own_block(att1)) + unchunk(moe1)
    mine = jnp.stack([own_block(grad_x0.reshape(2, ROWS, D)).astype(f32), y1])
    mine = jnp.where(own_live[None, :, None], mine, 0.0)
    kept, sent = pick(mine, high, 0), pick(mine, 1 - high, 0).astype(bf16)

    tiny = jnp.stack([grad_small0, grad_small1]).astype(bf16).reshape(2, 8, 16, 2, 24)
    tiny = tiny.transpose(0, 2, 3, 1, 4).reshape(2, 16, 16, 24)
    tiny = jnp.pad(tiny, ((0, 0), (0, 0), (0, 0), (0, 384 - 24)))
    packs = jnp.concatenate([grad_attn0.reshape(2, 16, 48, 384), tiny], axis=2).reshape(2, 4, 4, 64, FE)
    tiny, landed, grad_w_in, grad_w_exp_out, attn = end_exchange(packs, sent, sums1, some, some_attn)
    landed = landed.astype(f32)
    ends = jnp.where(high == 0, jnp.stack([kept, landed]), jnp.stack([landed, kept]))
    grad_w_qkv = jnp.concatenate([attn[:, 1, :, None, :WIDTH], attn[:, 0].reshape(2, 24, 2, WIDTH)], axis=2)
    grad_w_out = attn[:, 1, :, WIDTH:].transpose(0, 2, 1)
    tiny = tiny[:, :, 0:24]
    return (
        ends[None],
        tiny[:, 0:2],
        tiny[:, 2:4],
        grad_w_qkv,
        grad_w_out,
        tiny[:, 4:8].transpose(0, 2, 1),
        grad_w_in,
        grad_w_exp_out.transpose(0, 1, 3, 2),
    )


def solution(mesh):
    fine = Mesh(mesh.devices.reshape(4, 2, 2, 2, 4), CHIPS + ("core", "tp"))
    section, ctx = ("x", "zh"), ("zl", "core")
    every = section + ctx
    return jax.shard_map(
        shards,
        mesh=fine,
        in_specs=(
            P(ctx, section, None, None),
            P(ctx, section, None, None),
            P(),
            P(None, None, every),
            P(None, None, every),
            P(None, every, None, "tp"),
            P(None, "tp", every),
            P(None, every, None),
            P(None, None, every, "tp"),
            P(None, None, "tp", every),
        ),
        out_specs=(
            P(ctx, section, None, None),
            P(None, None, every),
            P(None, None, every),
            P(None, every, None, "tp"),
            P(None, "tp", every),
            P(None, every, None),
            P(None, None, every, "tp"),
            P(None, None, "tp", every),
        ),
        check_vma=False,
    )
```

```python
import functools

import jax
import jax.numpy as jnp
from jax import lax
from jax.experimental import pallas as pl
from jax.experimental.pallas import tpu as pltpu
from jax.sharding import Mesh
from jax.sharding import PartitionSpec as P

D = 768
HD = 64
HEADS = 3
ROWS = 160
PAIR = 320
KEYS = 640
FE = 384
EXPERTS = 4
EPS = 1e-06
WIDTH = HEADS * HD
MESH = pl.DeviceIdType.MESH
CHIPS = ("x", "zh", "zl")
f32, bf16 = jnp.float32, jnp.bfloat16
VMEM = pl.BlockSpec(memory_space=pltpu.VMEM)
SMEM = pl.BlockSpec(memory_space=pltpu.SMEM)
NN = (((1,), (0,)), ((), ()))
NT = (((1,), (1,)), ((), ()))
TN = (((0,), (0,)), ((), ()))


def dot(a, b, dims):
    return lax.dot_general(a, b, dims, preferred_element_type=f32)


def dot_split(a, b, dims):
    high = a.astype(bf16)
    return dot(high, b, dims) + dot((a - high.astype(f32)).astype(bf16), b, dims)


def params(cid, mib):
    return pltpu.CompilerParams(
        collective_id=cid, has_side_effects=True, vmem_limit_bytes=mib * 2**20
    )


ANY = pl.BlockSpec(memory_space=pl.ANY)


def arrive(peers):
    barrier = pltpu.get_barrier_semaphore()
    for peer in peers:
        pl.semaphore_signal(barrier, inc=1, device_id=peer, device_id_type=MESH)


def all_here(count):
    pl.semaphore_wait(pltpu.get_barrier_semaphore(), count)


def dma_sems(*counts):
    return [pltpu.SemaphoreType.DMA((count,)) for count in counts for _ in range(2)]


def remote(src, dst, send, recv, peer):
    return pltpu.make_async_remote_copy(
        src_ref=src, dst_ref=dst, send_sem=send, recv_sem=recv, device_id=peer, device_id_type=MESH
    )


def tp_peers():
    return [{"tp": (lax.axis_index("tp") + k) % 4} for k in (1, 2, 3)]


def pieces_of(rows):
    return (pl.ds(0, 48), pl.ds(48, rows - 48))


def sum_cores(part, crossed, send, recv):
    core = lax.axis_index("core")
    return [
        remote(part.at[1 - core, :, rows], crossed.at[:, rows], send.at[p], recv.at[p], {"core": 1 - core})
        for p, rows in enumerate(pieces_of(part.shape[2]))
    ]


def sum_terms(both, part, landed, send, recv):
    block = lax.axis_index("core") if both else 0
    return [
        [
            remote(
                part.at[block, peer["tp"], rows], landed.at[k, rows],
                send.at[3 * p + k], recv.at[3 * p + k], peer,
            )
            for k, peer in enumerate(tp_peers())
        ]
        for p, rows in enumerate(pieces_of(part.shape[2]))
    ]


def sum_results(out, send, recv):
    core, tp = lax.axis_index("core"), lax.axis_index("tp")
    return [
        [
            remote(out.at[core, tp, rows], out.at[core, tp, rows], send.at[3 * p + k], recv.at[3 * p + k], peer)
            for k, peer in enumerate(tp_peers())
        ]
        for p, rows in enumerate(pieces_of(out.shape[2]))
    ]


def sum_cross(out, send, recv):
    core, tp = lax.axis_index("core"), lax.axis_index("tp")
    return [
        [
            remote(
                out.at[core, at, rows], out.at[core, at, rows],
                send.at[4 * p + k], recv.at[4 * p + k], {"core": 1 - core},
            )
            for k, at in enumerate([(tp + 4 - k) % 4 for k in range(4)])
        ]
        for p, rows in enumerate(pieces_of(out.shape[2]))
    ]


def sum_start(both, out, part, landed, rs, rr, gs, gr, cs, cr, crossed=None, ps=None, pr=None):
    terms = sum_terms(both, part, landed, rs, rr)
    if both:
        core = lax.axis_index("core")
        pres = sum_cores(part, crossed, ps, pr)
        for pre in pres:
            pre.start()
    for p, rows in enumerate(pieces_of(part.shape[2])):
        if both:
            pres[p].wait_recv()
            for j in range(4):
                total = part[core, j, rows].astype(f32) + crossed[j, rows].astype(f32)
                part[core, j, rows] = total.astype(bf16)
        for copy in terms[p]:
            copy.start()


def sum_middle(both, out, part, landed, rs, rr, gs, gr, cs, cr, *pre):
    core, tp = lax.axis_index("core"), lax.axis_index("tp")
    terms, results, crosses = sum_terms(both, part, landed, rs, rr), sum_results(out, gs, gr), sum_cross(out, cs, cr)
    for p, rows in enumerate(pieces_of(part.shape[2])):
        total = part[core if both else 0, tp, rows].astype(f32)
        for k, copy in enumerate(terms[p]):
            copy.wait_recv()
            total = total + landed[k, rows].astype(f32)
        out[core, tp, rows] = total.astype(bf16)
        for copy in results[p]:
            copy.start()
        crosses[p][0].start()


def sum_end(both, out, part, landed, rs, rr, gs, gr, cs, cr, *pre):
    terms, results, crosses = sum_terms(both, part, landed, rs, rr), sum_results(out, gs, gr), sum_cross(out, cs, cr)
    for p in range(2):
        for k in range(3):
            results[p][k].wait_recv()
            crosses[p][k + 1].start()
    for p in range(2):
        for copy in crosses[p]:
            copy.wait()
        for copy in terms[p] + results[p]:
            copy.wait_send()
    if both:
        for copy in sum_cores(part, *pre):
            copy.wait_send()


def sum_scratch(both, rows):
    scratch = [
        pltpu.VMEM((2 if both else 1, 4, rows, 384), bf16),
        pltpu.VMEM((3, rows, 384), bf16),
    ] + dma_sems(6, 6, 8)
    if both:
        scratch += [pltpu.VMEM((4, rows, 384), bf16)] + dma_sems(2)
    return scratch


def chip_peers():
    core, zl = lax.axis_index("core"), lax.axis_index("zl")
    return {"core": 1 - core}, {"zl": 1 - zl}, zl * 2 + core


def cross_kernel(own, out, send, recv):
    other = {"core": 1 - lax.axis_index("core")}
    arrive([other])
    all_here(1)
    copy = remote(own, out, send.at[0], recv.at[0], other)
    copy.start()
    copy.wait()


def cross(own, cid):
    return pl.pallas_call(
        cross_kernel,
        out_shape=jax.ShapeDtypeStruct(own.shape, own.dtype),
        in_specs=[VMEM],
        out_specs=VMEM,
        scratch_shapes=dma_sems(1),
        compiler_params=params(cid, 8),
        name="cross",
    )(own)


def places():
    return lax.axis_index("x"), lax.axis_index("zh") * 2 + lax.axis_index("zl")


def axis_peer(along_x, k):
    x, z = places()
    if along_x:
        return {"x": (x + k) % 4}, (x + k) % 4
    to = (z + k) % 4
    return {"zh": to // 2, "zl": to % 2}, to


def half(rows, route):
    return pl.ds(route * (rows // 2), rows // 2)


def uneven(rows, route):
    first = {128: 80, 64: 48}[rows]
    return pl.ds(first, rows - first) if route else pl.ds(0, first)


def line(whole, route, second, rows):
    return whole.at[:, second, rows] if route == 0 else whole.at[second, :, rows]


def axis_peers(*ks):
    return [axis_peer(along_x, k)[0] for along_x in (True, False) for k in ks]


def start_kernel(
    lengths, images, routes, urgent, later, x_out, cot_out, out_routes, dead, all_urgent, all_later,
    got, own_sem, im_s, im_r, u1_s, u1_r, u2_s, u2_r, l_s, l_r,
):
    core = lax.axis_index("core")
    at_x, at_z = places()
    high = at_x // 2
    other = {"core": 1 - core}
    arrive(axis_peers(1, 2, 3) + [other])
    all_urgent[at_x, at_z] = urgent[...]
    got[high, core] = images[high]
    out_routes[high, core] = routes[high]
    lanes = lax.broadcasted_iota(jnp.int32, (1, KEYS), 1)
    live = lanes < lengths[0]
    for block in range(1, 4):
        live = live | ((lanes >= ROWS * block) & (lanes < ROWS * block + lengths[block]))
    dead[...] = jnp.where(live, 0.0, -1e30)
    own = pltpu.make_async_copy(later, all_later.at[at_x, at_z], own_sem)
    own.start()
    all_here(7)
    firsts, seconds, laters = [], [], []
    for route in range(2):
        b = (at_z, at_x)[route]
        rows, late = uneven(urgent.shape[0], route), half(later.shape[0], route)
        for k in range(1, 4):
            peer, _ = axis_peer(route == 0, k)
            n = 3 * route + k - 1
            firsts.append(
                remote(urgent.at[rows], all_urgent.at[at_x, at_z, rows], u1_s.at[n], u1_r.at[n], peer)
            )
            laters.append(
                remote(later.at[late], all_later.at[at_x, at_z, late], l_s.at[n], l_r.at[n], peer)
            )
            slabs = line(all_urgent, route, b, rows)
            seconds.append(remote(slabs, slabs, u2_s.at[n], u2_r.at[n], axis_peer(route == 1, k)[0]))
    swaps, kepts, passes = [], [], []
    for n, (source, target) in enumerate(((images, got), (routes, out_routes))):
        here, there = target.at[high, core], target.at[1 - high, core]
        swaps.append(remote(source.at[1 - high], here, im_s.at[n], im_r.at[n], {"x": (at_x + 2) % 4}))
        kepts.append(remote(source.at[high], here, im_s.at[2 + n], im_r.at[2 + n], other))
        passes.append(remote(there, there, im_s.at[4 + n], im_r.at[4 + n], other))
    for copy in firsts + swaps + kepts + laters:
        copy.start()
    for copy in firsts:
        copy.wait_recv()
    for copy in seconds:
        copy.start()
    for swap, onward in zip(swaps, passes):
        swap.wait_recv()
        onward.start()
    for copy in kepts + passes:
        copy.wait()
    x_out[...] = got[0]
    lines = lax.broadcasted_iota(jnp.int32, (ROWS, 1), 0)
    for block in range(2):
        live = lines < lengths[2 * lax.axis_index("zl") + block]
        cot_out[block] = jnp.where(live, got[1, block].astype(f32), 0.0).astype(bf16)
    for copy in seconds + laters:
        copy.wait()
    for copy in firsts + swaps:
        copy.wait_send()
    own.wait()


def start_exchange(lengths, images, routes, urgent, later):
    shapes = [images.shape, images.shape, (2,) + routes.shape]
    slabs = [(4, 4) + urgent.shape, (4, 4) + later.shape]
    return pl.pallas_call(
        start_kernel,
        out_shape=[jax.ShapeDtypeStruct(s, bf16) for s in shapes]
        + [jax.ShapeDtypeStruct((1, KEYS), f32)]
        + [jax.ShapeDtypeStruct(s, bf16) for s in slabs],
        in_specs=[SMEM] + [VMEM] * 4,
        out_specs=[VMEM] * 5 + [ANY],
        scratch_shapes=[pltpu.VMEM((2,) + images.shape, bf16), pltpu.SemaphoreType.DMA] + dma_sems(6, 6, 6, 6),
        compiler_params=params(1, 56),
        name="start_exchange",
    )(lengths, images, routes, urgent, later)


def spread_near(whole, send, recv):
    copies = []
    for route in range(2):
        slabs = line(whole, route, places()[1 - route], half(whole.shape[2], route))
        for n, k in enumerate((1, 3)):
            at, peer = 2 * route + n, axis_peer(route == 1, k)[0]
            copies.append(remote(slabs, slabs, send.at[at], recv.at[at], peer))
    return copies


def spread_far(whole, send, recv):
    copies = []
    size = whole.shape[2] // 2
    cut = size // 32 * 16 + size % 32
    for route in range(2):
        b = places()[1 - route]
        for n, k in enumerate((1, 3)):
            rows = pl.ds(route * size + n * cut, size - cut if n else cut)
            slabs = line(whole, route, (b + 4 - k) % 4, rows)
            at, peer = 4 + 2 * route + n, axis_peer(route == 1, k)[0]
            copies.append(remote(slabs, slabs, send.at[at], recv.at[at], peer))
    return copies


def part_rows(rows, route, n):
    size = rows // 2
    cut = size // 32 * 16 + size % 32
    return pl.ds(route * size + n * cut, size - cut if n else cut)


def toward_far(whole, passing, route, send, recv):
    copies, b = [], places()[1 - route]
    for n, k in enumerate((1, 3)):
        rows = part_rows(whole.shape[2], route, n)
        target = passing.at[route, n, :, 0 : rows.size]
        at, peer = 2 * route + n, axis_peer(route == 1, k)[0]
        copies.append(remote(line(whole, route, (b + 2) % 4, rows), target, send.at[at], recv.at[at], peer))
    return copies


def toward_near(whole, passing, landed, route, send, recv):
    copies, b = [], places()[1 - route]
    for n, k in enumerate((1, 3)):
        rows, others = (part_rows(whole.shape[2], route, m) for m in (n, 1 - n))
        at, peer = 4 * route + 2 * n, axis_peer(route == 1, k)[0]
        copies += [
            remote(passing.at[route, n, :, 0 : rows.size], landed.at[n, :, rows], send.at[at], recv.at[at], peer),
            remote(
                line(whole, route, (b + k) % 4, others), landed.at[n, :, others],
                send.at[at + 1], recv.at[at + 1], peer,
            ),
        ]
    return copies


def add_passing(whole, passing, route):
    x, z = places()
    b = (z, x)[route]
    for n, k in enumerate((1, 3)):
        rows, to = part_rows(whole.shape[2], route, n), (b + k) % 4

        def add(j, carry, n=n, rows=rows, to=to):
            own = whole[j, to, rows] if route == 0 else whole[to, j, rows]
            total = passing[route, n, j, 0 : rows.size].astype(f32) + own.astype(f32)
            passing[route, n, j, 0 : rows.size] = total.astype(bf16)
            return carry

        lax.fori_loop(0, 4, add, 0)


def last_copies(some, slabs, send, recv):
    copies = []
    for route in range(2):
        rows = half(some.shape[1], route)
        for k in range(1, 4):
            peer, at = axis_peer(route == 0, k)
            n = 3 * route + k - 1
            copies.append(remote(some.at[at, rows], slabs.at[k - 1, rows], send.at[n], recv.at[n], peer))
    return copies


def add_slabs(some, slabs, out):
    x, z = places()
    steps = some.shape[1] // 48

    def add(i, carry):
        rows, route = pl.ds(pl.multiple_of(i * 48, 48), 48), i // (steps // 2)
        total = some[x * (1 - route) + z * route, rows].astype(f32)
        for k in range(3):
            total = total + slabs[k, rows].astype(f32)
        out[rows] = total.astype(bf16)
        return carry

    lax.fori_loop(0, steps, add, 0)


def end_kernel(
    part, image, half_sum, some, some_attn, tiny, out_image, grad_in, grad_out, grad_attn,
    out, out_half, own_sum, other_sum, landed, sums, pieces, mids, lands, slabs, attn_slabs, cx_s, cx_r, sl_s, sl_r, at_s, at_r, p1_s, p1_r, p2_s, p2_r,
):
    def own_lines(rows):
        rows = rows.astype(f32)
        return jnp.where(core == 0, rows[0:24], rows[24:48])

    def put_experts(layer, own, got):
        for at in range(2 * EXPERTS):
            rows = slice(48 * at, 48 * at + 48)
            mine, others = own_lines(own[rows]), own_lines(got[rows])
            ref = grad_out if at % 2 else grad_in
            ref[layer, at // 2, :, 0:FE] = jnp.where(core == 0, mine, others)
            ref[layer, at // 2, :, FE:] = jnp.where(core == 0, others, mine)

    core, x = lax.axis_index("core"), lax.axis_index("x")
    other = {"core": 1 - core}
    arrive(axis_peers(1, 2, 3) + [other])
    all_here(7)
    crossing = remote(part.at[1 - core], landed, cx_s.at[0], cx_r.at[0], other)
    crossing.start()
    lasts = last_copies(some, slabs, sl_s, sl_r)
    firsts, seconds = [], []
    for route in range(2):
        rows = uneven(64, route)
        for k in range(1, 4):
            peer, at = axis_peer(route == 0, k)
            n = 3 * route + k - 1
            lasts.append(
                remote(some_attn.at[route, at], attn_slabs.at[route, k - 1], at_s.at[n], at_r.at[n], peer)
            )
            seconds.append(remote(mids.at[at, rows], lands.at[k - 1, rows], p2_s.at[n], p2_r.at[n], peer))
            peer, at = axis_peer(route == 1, k)
            firsts.append(
                remote(line(sums, route, at, rows), pieces.at[k - 1, :, rows], p1_s.at[n], p1_r.at[n], peer)
            )
    swap = remote(image, out_image, cx_s.at[1], cx_r.at[1], {"x": (x + 2) % 4})
    halves = remote(half_sum, out_half, cx_s.at[2], cx_r.at[2], other)
    for copy in lasts + [halves]:
        copy.start()
    crossing.wait()

    def add(i, carry):
        total = part[core, i // 4, i % 4].astype(f32) + landed[i // 4, i % 4].astype(f32)
        sums[i // 4, i % 4] = total.astype(bf16)
        return carry

    lax.fori_loop(0, 16, add, 0)
    for copy in firsts + [swap]:
        copy.start()
    halves.wait_recv()
    put_experts(1, half_sum, out_half)
    for copy in firsts:
        copy.wait_recv()
    at_x, at_z = places()
    for route in range(2):
        rows = uneven(64, route)

        def gather(j, carry, route=route, rows=rows):
            total = (sums[j, at_z, rows] if route == 0 else sums[at_x, j, rows]).astype(f32)
            for k in range(3):
                total = total + pieces[k, j, rows].astype(f32)
            mids[j, rows] = total.astype(bf16)
            return carry

        lax.fori_loop(0, 4, gather, 0)
    for copy in seconds:
        copy.start()
    for copy in lasts:
        copy.wait()
    add_slabs(some, slabs, own_sum)
    for route in range(2):
        attn = some_attn[route, places()[route]].astype(f32)
        for k in range(3):
            attn = attn + attn_slabs[route, k].astype(f32)
        first = 384 + 48 * route
        own_sum[first : first + 48] = attn.astype(bf16)
    final = remote(own_sum, other_sum, cx_s.at[3], cx_r.at[3], other)
    final.start()
    for copy in seconds:
        copy.wait()
    for route in range(2):
        rows = uneven(64, route)
        total = mids[places()[route], rows].astype(f32)
        for k in range(3):
            total = total + lands[k, rows].astype(f32)
        out[core, rows] = total
    given = remote(out.at[core], out.at[core], cx_s.at[4], cx_r.at[4], other)
    given.start()
    final.wait()
    put_experts(0, own_sum, other_sum)
    given.wait()
    for route in range(2):
        first = 384 + 48 * route
        rows = slice(first, first + 48)
        grad_attn[0, route] = own_lines(out[route, 0:48])
        grad_attn[1, route] = own_lines(own_sum[rows]) + own_lines(other_sum[rows])
        tiny[route] = jnp.where(core == 0, out[route, 48:56], out[route, 56:64])
    for copy in firsts + [halves]:
        copy.wait_send()
    swap.wait()


def end_exchange(part, image, half_sum, some, some_attn):
    slab = (480, FE)
    scratch = [half_sum.shape, slab, slab] + [(4, 4, 64, FE)] * 2 + [(3, 4, 64, FE), (4, 64, FE), (3, 64, FE)]
    scratch += [(3,) + some.shape[1:], (2, 3, 48, FE)]
    return pl.pallas_call(
        end_kernel,
        out_shape=[
            jax.ShapeDtypeStruct((2, 8, FE), f32),
            jax.ShapeDtypeStruct(image.shape, bf16),
            jax.ShapeDtypeStruct((2, EXPERTS, 24, D), f32),
            jax.ShapeDtypeStruct((2, EXPERTS, 24, D), f32),
            jax.ShapeDtypeStruct((2, 2, 24, FE), f32),
        ],
        in_specs=[VMEM] * 5,
        out_specs=[VMEM] * 5,
        scratch_shapes=[pltpu.VMEM((2, 64, FE), f32)]
        + [pltpu.VMEM(s, bf16) for s in scratch]
        + dma_sems(5, 6, 6, 6, 6),
        compiler_params=params(2, 56),
        name="end_exchange",
    )(part, image, half_sum, some, some_attn)


def block_rows(ref, block):
    top = jnp.concatenate([ref[block, 0, 0:80], ref[block, 1, 0:80]], axis=1)
    low = jnp.concatenate([ref[block, 2, 0:80], ref[block, 3, 0:80]], axis=1)
    return jnp.concatenate([top, low], axis=0).astype(f32)


def pair_rows(ref):
    return jnp.concatenate([block_rows(ref, 0), block_rows(ref, 1)], axis=0)


def put_chunks(ref, block, value, first=0):
    for j in range(4):
        r, c = 80 * (j // 2), 384 * (j % 2)
        ref[block, j, first : first + 80] = value[r : r + 80, c : c + 384]


def norm_parts(rows):
    centered = rows - jnp.mean(rows, axis=-1, keepdims=True)
    scale = lax.rsqrt(jnp.mean(centered * centered, axis=-1, keepdims=True) + EPS)
    return centered * scale, scale


def norm_back(grad, unit, scale, gain):
    inner = grad * gain
    return scale * (
        inner
        - jnp.mean(inner, axis=-1, keepdims=True)
        - unit * jnp.mean(inner * unit, axis=-1, keepdims=True)
    )


def softmax(logits, axis):
    top = jnp.max(logits, axis=axis, keepdims=True)
    powers = jnp.exp(logits - top)
    return powers / jnp.sum(powers, axis=axis, keepdims=True)


def own_rows(core):
    return pl.ds(pl.multiple_of(core * ROWS, ROWS), ROWS)


def head(value, h):
    return value[:, HD * h : HD * h + HD]


def gelu_parts(u):
    c = 0.7978845608028654
    t = jnp.tanh(c * (u + 0.044715 * u * u * u))
    return 0.5 * u * (1.0 + t), t


def gelu_slope(u, t):
    c = 0.7978845608028654
    return 0.5 * (1.0 + t) + 0.5 * u * (1.0 - t * t) * (c * (1.0 + 3 * 0.044715 * u * u))


def attn_weights(weights):
    chips = (slice(None),) * (len(weights.shape) - 2)
    w_kv = weights[(*chips, slice(0, 48))].reshape(D, 2 * WIDTH)
    w_q = weights[(*chips, slice(48, 96), slice(0, WIDTH))].reshape(D, WIDTH)
    return w_kv, w_q, weights[(*chips, slice(48, 96), slice(WIDTH, None))].reshape(D, WIDTH)


def attend_forward_kernel(follows, *refs):
    if follows:
        x, att_before, moe_before, small, weights, dead, q, kv, mixed, att, x_next, *scratch = refs
    else:
        x, small, weights, dead, ahead, _, q, kv, mixed, att, whole, all_ahead, *scratch = refs
        *scratch, sp_send, sp_recv, ah_send, ah_recv, own_sem = scratch
    part, landed, *sems, kv_send, kv_recv = scratch
    sums = (False, att, part, landed, *sems)
    core = lax.axis_index("core")
    other, across, me = chip_peers()
    arrive([other, across] + tp_peers())
    if not follows:
        arrive(axis_peers(1, 2, 3))
    if follows:
        x_next[...] = (x[...].astype(f32) + pair_rows(att_before) + pair_rows(moe_before)).astype(bf16)
        x = x_next
    unit, _ = norm_parts(x[own_rows(core)].astype(f32))
    normed = (unit * small[0:1] + small[2:3]).astype(bf16)
    w_kv, w_q, w_out_t = attn_weights(weights)
    kv[me] = dot(normed, w_kv, NN).astype(bf16)
    all_here(5 if follows else 11)
    far = (me + 2) % 4
    copies = [
        remote(kv.at[at], kv.at[at], kv_send.at[k], kv_recv.at[k], peer)
        for k, (at, peer) in enumerate(((me, across), (me, other), (far, other)))
    ]
    copies[0].start()
    copies[1].start()
    if not follows:
        nears = spread_near(whole, sp_send, sp_recv)
        fars = spread_far(whole, sp_send, sp_recv)
        at_x, at_z = places()
        aheads = [pltpu.make_async_copy(ahead, all_ahead.at[at_x, at_z], own_sem)]
        for route in range(2):
            rows = half(ahead.shape[0], route)
            for k in range(1, 4):
                n, peer = 3 * route + k - 1, axis_peer(route == 0, k)[0]
                aheads.append(
                    remote(ahead.at[rows], all_ahead.at[at_x, at_z, rows], ah_send.at[n], ah_recv.at[n], peer)
                )
        for copy in nears + aheads:
            copy.start()
    queries = dot(normed, w_q, NN).astype(bf16)
    q[...] = queries
    copies[0].wait_recv()
    copies[2].start()
    copies[1].wait_recv()
    copies[2].wait_recv()
    keys = kv[...].reshape(KEYS, 2 * WIDTH)
    outs = []
    for h in range(HEADS):
        scores = HD**-0.5 * dot(head(queries, h), head(keys, h), NT) + dead[...]
        probs = softmax(scores, -1).astype(bf16)
        outs.append(dot(probs, head(keys, HEADS + h), NN))
    heads = jnp.concatenate(outs, axis=1).astype(bf16)
    mixed[...] = heads
    put_chunks(part, 0, dot(heads, w_out_t, NT).astype(bf16))
    sum_start(*sums)
    sum_middle(*sums)
    if not follows:
        for copy in nears:
            copy.wait_recv()
        for copy in fars:
            copy.start()
    sum_end(*sums)
    for copy in copies:
        copy.wait_send()
    if not follows:
        for copy in fars + aheads:
            copy.wait()
        for copy in nears:
            copy.wait_send()


def attend_forward(x, before, small, weights, dead, some, ahead, cid):
    args = (x, *before, small, weights, dead)
    shapes = [(ROWS, WIDTH), (4, ROWS, 2 * WIDTH), (ROWS, WIDTH), (2, 4, 80, 384)]
    in_specs, out_specs = [VMEM] * len(args), [VMEM] * 5
    scratch = sum_scratch(False, 80) + dma_sems(3)
    if before:
        shapes.append((PAIR, D))
    else:
        args += (ahead, some)
        shapes += [some.shape, (4, 4) + ahead.shape]
        in_specs += [VMEM, ANY]
        out_specs[4:] = [ANY, ANY]
        scratch += dma_sems(8, 6) + [pltpu.SemaphoreType.DMA]
    return pl.pallas_call(
        functools.partial(attend_forward_kernel, bool(before)),
        out_shape=[jax.ShapeDtypeStruct(s, bf16) for s in shapes],
        in_specs=in_specs,
        out_specs=out_specs,
        scratch_shapes=scratch,
        input_output_aliases={} if before else {len(args) - 1: 4},
        compiler_params=params(cid, 56),
        name="attend_forward",
    )(*args)


def expert_weights(weights):
    block = weights[...]
    return block[:, 0:48].reshape(D, FE), block[:, 48:96].reshape(D, FE)


def experts_setup(x, att, small, routes, b, gates):
    unit, _ = norm_parts(x[...].astype(f32) + pair_rows(att))
    b[...] = (unit * small[1:2] + small[3:4]).astype(bf16)
    put_gates(b, small, routes, gates)


def put_gates(b, small, routes, gates):
    probs = softmax(dot(b[...], small[4:8].astype(bf16), NT), -1)
    ids = lax.broadcasted_iota(jnp.int32, (PAIR, EXPERTS), 1).astype(f32)
    ones = lax.broadcasted_iota(jnp.int32, (16, 16), 0) == lax.broadcasted_iota(jnp.int32, (16, 16), 1)
    lines = dot(routes[...], ones.astype(f32).astype(bf16), TN)
    named = (lines[:, 0:1] == ids) | (lines[:, 1:2] == ids)
    gates[...] = jnp.where(named, probs, 0.0)


def gate_of(gates, expert):
    ids = lax.broadcasted_iota(jnp.int32, (PAIR, EXPERTS), 1)
    return jnp.sum(jnp.where(ids == expert, gates[...], 0.0), axis=1, keepdims=True)


def fixed(shape):
    return pl.BlockSpec(shape, lambda e: (0,) * len(shape))


def middle_kernel(
    x, att, small, routes, small_next, dead, ahead, later, weights,
    q, kv_result, mixed, att_result, x_next, attn_result, whole,
    b, gates, total, moe, attn_w, kv, att_next,
    ah_send, ah_recv, l_send, l_recv, sp_send, sp_recv, kv_send, kv_recv, own_sem, *sems,
):
    expert = pl.program_id(0)
    sums, sums_next = (True, moe, *sems[:11]), (False, att_next, *sems[11:])
    part, part_next = sums[2], sums_next[2]
    core = lax.axis_index("core")
    at_x, at_z = places()
    other, across, me = chip_peers()
    far = (me + 2) % 4
    aheads, laters = [], []
    for route in range(2):
        second, rows, late = (at_z, at_x)[route], half(ahead.shape[2], route), half(later.shape[0], route)
        for k in range(1, 4):
            n = 3 * route + k - 1
            aheads.append(
                remote(
                    line(ahead, route, second, rows), line(attn_w, route, second, rows),
                    ah_send.at[n], ah_recv.at[n], axis_peer(route == 1, k)[0],
                )
            )
            laters.append(
                remote(
                    later.at[late], whole.at[at_x, at_z, late],
                    l_send.at[n], l_recv.at[n], axis_peer(route == 0, k)[0],
                )
            )
    own = pltpu.make_async_copy(later, whole.at[at_x, at_z], own_sem)
    nears, fars = spread_near(whole, sp_send, sp_recv), spread_far(whole, sp_send, sp_recv)

    @pl.when(expert == 0)
    def _():
        arrive([other, across] + tp_peers() + axis_peers(1, 2, 3))
        experts_setup(x, att, small, routes, b, gates)
        total[...] = jnp.zeros_like(total)
        for j in range(4):
            rows = half(ahead.shape[2], 0)
            attn_w[j, at_z, rows] = ahead[j, at_z, rows]
            rows = half(ahead.shape[2], 1)
            attn_w[at_x, j, rows] = ahead[at_x, j, rows]
        all_here(11)
        for copy in aheads + laters + [own]:
            copy.start()

    w_in, w_out_t = expert_weights(weights)
    u = dot(b[...], w_in, NN)
    active = gelu_parts(u)[0].astype(bf16).astype(f32)
    gated = (gate_of(gates, expert) * active).astype(bf16)
    total[...] += dot(gated, w_out_t, NT)

    @pl.when(expert == EXPERTS - 1)
    def _():
        for block in range(2):
            put_chunks(part, block, total[ROWS * block : ROWS * block + ROWS].astype(bf16))
        sum_start(*sums)
        for copy in laters:
            copy.wait_recv()
        own.wait()
        for copy in nears:
            copy.start()
        sum_middle(*sums)
        sum_end(*sums)
        x_next[...] = (x[...].astype(f32) + pair_rows(att) + pair_rows(moe)).astype(bf16)
        unit, _ = norm_parts(x_next[own_rows(core)].astype(f32))
        normed = (unit * small_next[0:1] + small_next[2:3]).astype(bf16)
        for copy in aheads:
            copy.wait_recv()
        w_kv, w_q, w_out = attn_weights(attn_w)
        kv[me] = dot(normed, w_kv, NN).astype(bf16)
        copies = [
            remote(kv.at[at], kv.at[at], kv_send.at[k], kv_recv.at[k], peer)
            for k, (at, peer) in enumerate(((me, across), (me, other), (far, other)))
        ]
        copies[0].start()
        copies[1].start()
        queries = dot(normed, w_q, NN).astype(bf16)
        q[...] = queries
        attn_result[...] = attn_w[...]
        copies[0].wait_recv()
        copies[2].start()
        copies[1].wait_recv()
        copies[2].wait_recv()
        keys = kv[...].reshape(KEYS, 2 * WIDTH)
        outs = []
        for h in range(HEADS):
            scores = HD**-0.5 * dot(head(queries, h), head(keys, h), NT) + dead[...]
            probs = softmax(scores, -1).astype(bf16)
            outs.append(dot(probs, head(keys, HEADS + h), NN))
        heads = jnp.concatenate(outs, axis=1).astype(bf16)
        mixed[...] = heads
        put_chunks(part_next, 0, dot(heads, w_out, NT).astype(bf16))
        sum_start(*sums_next)
        for copy in nears:
            copy.wait_recv()
        for copy in fars:
            copy.start()
        kv_result[...] = kv[...]
        sum_middle(*sums_next)
        sum_end(*sums_next)
        att_result[...] = att_next[...]
        for copy in copies + nears + laters + aheads:
            copy.wait_send()
        for copy in fars:
            copy.wait()


def middle(x, att, small, routes, small_next, dead, ahead, later, weights, cid):
    args = (x, att, small, routes, small_next, dead, ahead, later)
    shapes = [(ROWS, WIDTH), (4, ROWS, 2 * WIDTH), (ROWS, WIDTH), (2, 4, 80, 384), (PAIR, D), ahead.shape]
    return pl.pallas_call(
        middle_kernel,
        grid=(EXPERTS,),
        out_shape=[jax.ShapeDtypeStruct(s, bf16) for s in shapes + [(4, 4) + later.shape]],
        in_specs=[fixed(a.shape) for a in args] + [pl.BlockSpec((16, 96, FE), lambda e: (0, e, 0))],
        out_specs=[fixed(s) for s in shapes] + [ANY],
        scratch_shapes=[
            pltpu.VMEM((PAIR, D), bf16),
            pltpu.VMEM((PAIR, EXPERTS), f32),
            pltpu.VMEM((PAIR, D), f32),
            pltpu.VMEM((2, 4, 80, 384), bf16),
            pltpu.VMEM(ahead.shape, bf16),
            pltpu.VMEM((4, ROWS, 2 * WIDTH), bf16),
            pltpu.VMEM((2, 4, 80, 384), bf16),
        ]
        + dma_sems(6, 6, 8, 3)
        + [pltpu.SemaphoreType.DMA]
        + sum_scratch(True, 80)
        + sum_scratch(False, 80),
        compiler_params=params(cid, 56),
        name="middle",
    )(*args, weights)


def layer_backward_kernel(with_moe, *refs):
    x, att, small, routes, grad, q, kv, mixed, dead, attn_w, *refs = refs
    if not with_moe:
        extra, some_before, *refs = refs
    weights, grad_x, grad_small, grad_w, some, *refs = refs
    if with_moe:
        moe_result, *refs = refs
    else:
        own_sum, some_attn, *refs = refs
    b, gates, unit_two, scale_two, total, gate_grads, gated_all, grad_u_all, *refs = refs
    whole, slabs, passing, all_probs, grad_h, unit_one, parts, kv_landed, kv_out, back, back_one, *refs = refs
    fs, fr, ns, nr, kv_send, kv_recv, *refs = refs
    sums_two, sums_one, refs = (True, back, *refs[:11]), (False, back_one, *refs[11:19]), refs[19:]
    part_two, part_one = sums_two[2], sums_one[2]
    if with_moe:
        moe, moe_part, moe_out, moe_landed, ms, mr, mg, mh, moe_crossed, ps, pr = refs
        moe_sums = (moe_part, moe_crossed, ps, pr)
    else:
        last_slabs, ls, lr, attn_slabs, as_, ar = refs
        lasts = last_copies(some_before, last_slabs, ls, lr)
        for route in range(2):
            for k in range(1, 4):
                n, (peer, to) = 3 * route + k - 1, axis_peer(route == 1, k)
                slab = extra.at[0, :, to] if route == 0 else extra.at[1, to]
                lasts.append(remote(slab, attn_slabs.at[route, k - 1], as_.at[n], ar.at[n], peer))
    fars = [toward_far(whole, passing, route, fs, fr) for route in range(2)]
    nears = [toward_near(whole, passing, slabs, route, ns, nr) for route in range(2)]
    core, tp = lax.axis_index("core"), lax.axis_index("tp")
    at_x, at_z = places()
    other, across, me = chip_peers()
    far = (me + 2) % 4
    step = pl.program_id(0)

    @pl.when(step == 0)
    def _():
        arrive([other, across] + tp_peers() + axis_peers(1, 2, 3))
        unit, scale = norm_parts(x[...].astype(f32) + pair_rows(att))
        unit_two[...] = unit
        scale_two[...] = scale
        b[...] = (unit * small[1:2] + small[3:4]).astype(bf16)
        put_gates(b, small, routes, gates)
        total[...] = jnp.zeros_like(total)
        gate_grads[...] = jnp.zeros_like(gate_grads)
        if with_moe:
            moe[...] = jnp.zeros_like(moe)
        all_here(11)
        if not with_moe:
            for copy in lasts:
                copy.start()

    @pl.when(step < EXPERTS)
    def _():
        w_in, w_out_t = expert_weights(weights)
        u = dot(b[...], w_in, NN)
        act, t = gelu_parts(u)
        active = act.astype(bf16).astype(f32)
        gate = gate_of(gates, step)
        gated = (gate * active).astype(bf16)
        gated_all[step] = gated
        if with_moe:
            moe[...] += dot(gated, w_out_t, NT)
        grad_active = dot(grad[...], w_out_t, NN)
        ids = lax.broadcasted_iota(jnp.int32, (PAIR, 128), 1)
        gate_grad = jnp.sum(grad_active * active, axis=1, keepdims=True)
        gate_grads[...] = jnp.where(ids == step, gate_grad, gate_grads[...])
        grad_u = (gate * grad_active * gelu_slope(u, t)).astype(bf16)
        grad_u_all[step] = grad_u
        total[...] += dot(grad_u, w_in, NT)

    @pl.when(step == EXPERTS - 1)
    def _():
        part_two[...] = jnp.zeros_like(part_two)
        lines, lanes = (lax.broadcasted_iota(jnp.int32, (16, 128), axis) for axis in range(2))
        ones = ((lines == lanes) & (lines < EXPERTS)).astype(f32).astype(bf16)
        for block in range(2):
            rows = slice(ROWS * block, ROWS * block + ROWS)
            put_chunks(part_two, block, total[rows].astype(bf16))
            part_two[block, 0, 80:96, 0:ROWS] = dot(ones, gate_grads[rows].astype(bf16), NT).astype(bf16)
            if with_moe:
                put_chunks(moe_part, block, moe[rows].astype(bf16))
        sum_start(*sums_two)

    @pl.when(step >= EXPERTS)
    def _():
        at = step - EXPERTS
        first = pl.multiple_of(96 * at, 96)
        grad_in = dot(b[...], grad_u_all[at], TN).astype(bf16)
        whole[:, :, pl.ds(first, 48)] = grad_in.reshape(4, 4, 48, FE)
        grad_out = dot(grad[...], gated_all[at], TN).astype(bf16)
        whole[:, :, pl.ds(first + 48, 48)] = grad_out.reshape(4, 4, 48, FE)

    @pl.when(step == EXPERTS + 1)
    def _():
        sum_middle(*sums_two)

    @pl.when(step == 2 * EXPERTS - 2)
    def _():
        keys = kv[...].reshape(KEYS, 2 * WIDTH)
        for h in range(HEADS):
            all_probs[h] = softmax(HD**-0.5 * dot(head(q[...], h), head(keys, h), NT) + dead[...], -1)
        if not with_moe:
            for copy in lasts:
                copy.wait()
            add_slabs(some_before, last_slabs, own_sum)
            for route in range(2):

                def add(j, carry, route=route):
                    attn = (extra[0, j, at_z] if route == 0 else extra[1, at_x, j]).astype(f32)
                    for k in range(3):
                        attn = attn + attn_slabs[route, k, j].astype(f32)
                    some_attn[route, j] = attn.astype(bf16)
                    return carry

                lax.fori_loop(0, 4, add, 0)

    @pl.when(step == 2 * EXPERTS - 1)
    def _():
        for copy in fars[1] + fars[0]:
            copy.start()
        sum_end(*sums_two)
        router = small[4:8]
        chances = softmax(dot(router.astype(bf16), b[...], NT), 0)
        ids = lax.broadcasted_iota(jnp.int32, (EXPERTS, PAIR), 0).astype(f32)
        lines = routes[...].astype(f32)
        named = (lines[0:1] == ids) | (lines[1:2] == ids)
        tables = [back[block, 0, 80:96, 0:ROWS].astype(f32)[0:EXPERTS] for block in range(2)]
        gate_rows = jnp.where(named, jnp.concatenate(tables, axis=1), 0.0)
        grad_logits = chances * (gate_rows - jnp.sum(chances * gate_rows, axis=0, keepdims=True))
        grad_b = pair_rows(back) + dot_split(grad_logits, router.astype(bf16), TN)
        grad_h[...] = grad[...].astype(f32) + norm_back(grad_b, unit_two[...], scale_two[...], small[1:2])
        grad_att = grad_h[own_rows(core)].astype(bf16)
        w_kv, w_q, w_out_t = attn_weights(attn_w)
        grad_mixed = dot(grad_att, w_out_t, NN).astype(bf16)
        keys = kv[...].reshape(KEYS, 2 * WIDTH)
        queries = q[...]
        q_parts, k_parts, v_parts = [], [], []
        for h in range(HEADS):
            q_h, g_h = head(queries, h), head(grad_mixed, h)
            k_h, v_h = head(keys, h), head(keys, HEADS + h)
            probs = all_probs[h]
            v_parts.append(dot(probs.astype(bf16), g_h, TN))
            grad_weights = dot(g_h, v_h, NT)
            grad_scores = probs * (grad_weights - jnp.sum(probs * grad_weights, axis=-1, keepdims=True))
            grad_scores = grad_scores.astype(bf16)
            q_parts.append(HD**-0.5 * dot(grad_scores, k_h, NN))
            k_parts.append(HD**-0.5 * dot(grad_scores, q_h, TN))
        grad_keys = jnp.concatenate(k_parts + v_parts, axis=1).astype(bf16)
        parts[...] = grad_keys.reshape(4, ROWS, 2 * WIDTH)
        crosses = [
            remote(parts.at[(at + 1 - 2 * core) % 4], kv_landed.at[k], kv_send.at[k], kv_recv.at[k], other)
            for k, at in enumerate((me, far))
        ]
        onward = remote(kv_out, kv_landed.at[2], kv_send.at[2], kv_recv.at[2], across)
        crosses[1].start()
        crosses[0].start()
        if with_moe:
            pres = sum_cores(*moe_sums)
            for copy in pres:
                copy.start()
        crosses[1].wait_recv()
        kv_out[...] = (parts[far].astype(f32) + kv_landed[1].astype(f32)).astype(bf16)
        onward.start()
        if with_moe:
            for copy in pres:
                copy.wait_recv()
            for j in range(4):
                moe_sum = moe_part[core, j].astype(f32) + moe_crossed[j].astype(f32)
                moe_crossed[j] = moe_sum.astype(bf16)
            moe_terms = [
                remote(moe_crossed.at[peer["tp"]], moe_landed.at[k], ms.at[k], mr.at[k], peer)
                for k, peer in enumerate(tp_peers())
            ]
            for copy in moe_terms:
                copy.start()
        for route in (1, 0):
            for copy in fars[route]:
                copy.wait_recv()
            add_passing(whole, passing, route)
            for copy in nears[route]:
                copy.start()
        grad_q = jnp.concatenate(q_parts, axis=1).astype(bf16)
        grad_w[1, :, WIDTH:] = dot(grad_att, mixed[...], TN).astype(bf16)
        lanes = lax.broadcasted_iota(jnp.int32, (EXPERTS, PAIR), 1)
        own_lanes = (lanes < ROWS) == (core == 0)
        own = (lax.broadcasted_iota(jnp.int32, (PAIR, 1), 0) < ROWS) == (core == 0)
        kept = jnp.where(own, grad_b, 0.0)
        grad_small[1:2] = jnp.sum(kept * unit_two[...], axis=0, keepdims=True)
        grad_small[3:4] = jnp.sum(kept, axis=0, keepdims=True)
        grad_small[4:8] = dot_split(jnp.where(own_lanes, grad_logits, 0.0), b[...], NN)
        unit, scale_one = norm_parts(x[...].astype(f32))
        unit_one[...] = unit
        normed = (unit_one[own_rows(core)] * small[0:1] + small[2:3]).astype(bf16)
        crosses[0].wait_recv()
        onward.wait_recv()
        grad_kv = parts[me].astype(f32) + kv_landed[0].astype(f32) + kv_landed[2].astype(f32)
        grad_kv = grad_kv.astype(bf16)
        value = dot(grad_kv, w_kv, NT) + dot(grad_q, w_q, NT)
        put_chunks(part_one, 0, value.astype(bf16))
        sum_start(*sums_one)
        grad_w[0] = dot(normed, grad_kv, TN).astype(bf16)
        grad_w[1, :, :WIDTH] = dot(normed, grad_q, TN).astype(bf16)
        sum_middle(*sums_one)
        if with_moe:
            moe_total = moe_crossed[tp].astype(f32)
            for k, copy in enumerate(moe_terms):
                copy.wait_recv()
                moe_total = moe_total + moe_landed[k].astype(f32)
            moe_out[tp] = moe_total.astype(bf16)
            moe_results = [
                remote(moe_out.at[tp], moe_out.at[tp], mg.at[k], mh.at[k], peer)
                for k, peer in enumerate(tp_peers())
            ]
            for copy in moe_results:
                copy.start()
        for route in range(2):
            for copy in fars[route]:
                copy.wait_send()
            for copy in nears[route]:
                copy.wait()
        steps = some.shape[1] // 48

        def add(i, carry):
            j, at = i % 4, i // 4
            rows, route = pl.ds(pl.multiple_of(at * 48, 48), 48), at // (steps // 2)
            mine = whole[j * (1 - route) + at_x * route, at_z * (1 - route) + j * route, rows]
            total = mine.astype(f32) + slabs[0, j, rows].astype(f32) + slabs[1, j, rows].astype(f32)
            some[j, rows] = total.astype(bf16)
            return carry

        lax.fori_loop(0, 4 * steps, add, 0)
        sum_end(*sums_one)
        grad_a = pair_rows(back_one)
        grad_x[...] = (grad_h[...] + norm_back(grad_a, unit_one[...], scale_one, small[0:1])).astype(bf16)
        kept = jnp.where(own, grad_a, 0.0)
        grad_small[0:1] = jnp.sum(kept * unit_one[...], axis=0, keepdims=True)
        grad_small[2:3] = jnp.sum(kept, axis=0, keepdims=True)
        for copy in crosses + [onward]:
            copy.wait_send()
        if with_moe:
            for copy in pres + moe_terms:
                copy.wait_send()
            for copy in moe_results:
                copy.wait()
            moe_result[...] = moe_out[...]


def layer_backward(args, others, weights, cid):
    with_moe = not others
    slab = (384, FE)
    shapes = [((PAIR, D), bf16), ((8, D), f32), ((2, D, 2 * WIDTH), bf16), ((4,) + slab, bf16)]
    scratch = [
        ((PAIR, D), bf16),
        ((PAIR, EXPERTS), f32),
        ((PAIR, D), f32),
        ((PAIR, 1), f32),
        ((PAIR, D), f32),
        ((PAIR, 128), f32),
        ((EXPERTS, PAIR, FE), bf16),
        ((EXPERTS, PAIR, FE), bf16),
        ((4, 4) + slab, bf16),
        ((2, 4) + slab, bf16),
        ((2, 2, 4, 96, FE), bf16),
        ((HEADS, ROWS, KEYS), f32),
        ((PAIR, D), f32),
        ((PAIR, D), f32),
        ((4, ROWS, 2 * WIDTH), bf16),
        ((3, ROWS, 2 * WIDTH), bf16),
        ((ROWS, 2 * WIDTH), bf16),
        ((2, 4, 96, 384), bf16),
        ((2, 4, 80, 384), bf16),
    ]
    scratch = [pltpu.VMEM(*s) for s in scratch] + dma_sems(4, 8, 3)
    scratch += sum_scratch(True, 96) + sum_scratch(False, 80)
    if with_moe:
        shapes.append(((4, 80, 384), bf16))
        scratch += [pltpu.VMEM((PAIR, D), f32), pltpu.VMEM((2, 4, 80, 384), bf16)]
        scratch += [pltpu.VMEM((4, 80, 384), bf16), pltpu.VMEM((3, 80, 384), bf16)] + dma_sems(3, 3)
        scratch += [pltpu.VMEM((4, 80, 384), bf16)] + dma_sems(2)
    else:
        shapes += [(slab, bf16), ((2, 4, 48, FE), bf16)]
        scratch += [pltpu.VMEM((3,) + slab, bf16)] + dma_sems(6)
        scratch += [pltpu.VMEM((2, 3, 4, 48, FE), bf16)] + dma_sems(6)
    args = args + others
    return pl.pallas_call(
        functools.partial(layer_backward_kernel, with_moe),
        grid=(2 * EXPERTS,),
        out_shape=[jax.ShapeDtypeStruct(*s) for s in shapes],
        in_specs=[fixed(a.shape) for a in args]
        + [pl.BlockSpec((16, 96, FE), lambda s: (0, jnp.minimum(s, EXPERTS - 1), 0))],
        out_specs=[fixed(s) for s, _ in shapes],
        scratch_shapes=scratch,
        compiler_params=params(cid, 60),
        name="layer_backward",
    )(*args, weights)


def shards(boundary, routes, lengths, ln_gains, ln_biases, w_qkv, w_out, w_router, w_in, w_exp_out):
    core = lax.axis_index("core")
    high = lax.axis_index("x") // 2

    def pick(value, at, axis):
        return lax.dynamic_index_in_dim(value, at, axis, keepdims=False)

    halves = jnp.stack(
        [
            w_qkv[:, :, 1:].reshape(2, 24, 384),
            jnp.concatenate([w_qkv[:, :, 0], w_out.transpose(0, 2, 1)], axis=2),
        ],
        axis=1,
    )

    stacked = jnp.stack([w_in, w_exp_out.transpose(0, 1, 3, 2)], axis=2).reshape(384, 2, FE)
    tiny = jnp.concatenate([ln_gains, ln_biases, w_router.transpose(0, 2, 1)], axis=1)
    tiny = jnp.pad(tiny.transpose(1, 0, 2).reshape(8, 48), ((0, 8), (0, 384 - 48)))
    attn_one, attn_zero = halves[1].reshape(48, 384), halves[0].reshape(48, 384)
    own_half = jnp.concatenate([pick(stacked, core, 1), attn_one, attn_zero, tiny])
    got_half = cross(jnp.concatenate([pick(stacked, 1 - core, 1), attn_one, attn_zero, tiny]), 0)
    low_half = jnp.where(core == 0, own_half, got_half)
    high_half = jnp.where(core == 0, got_half, own_half)
    chip = jnp.concatenate(
        [low_half[:480].reshape(20, 24, FE), high_half[:480].reshape(20, 24, FE)], axis=1
    )
    later, ahead = chip[0:8].reshape(384, FE), chip[16:18].reshape(96, FE)
    urgent = jnp.concatenate([chip[18:20].reshape(96, FE), low_half[480:496], high_half[480:496]])

    turned = jnp.pad(routes[0].astype(bf16).transpose(0, 2, 1), ((0, 0), (0, 14), (0, 256 - ROWS)))
    x0, cotangent, got_routes, dead, packs, some = start_exchange(lengths, boundary[0], turned, urgent, later)
    x0, cotangent = x0.reshape(PAIR, D), cotangent.reshape(PAIR, D)
    packs = packs.reshape(16, 128, 384)
    tiny = packs[:, 96:128].reshape(32, 16, 384)[:, 0:8, 0:48].reshape(32, 8, 2, 24).transpose(2, 1, 0, 3).reshape(2, 8, D)
    smalls = [tiny[0].astype(f32), tiny[1].astype(f32)]

    own_length = pick(lengths, 2 * lax.axis_index("zl") + core, 0)
    own_live = jnp.arange(ROWS, dtype=jnp.int32) < own_length
    route_rows = [kind[:, :, 0:ROWS].transpose(1, 0, 2).reshape(16, PAIR) for kind in got_routes]
    q0, kv0, mixed0, att0, experts_zero, ahead = attend_forward(x0, (), smalls[0], packs, dead, some, ahead, 3)
    experts_zero = experts_zero.reshape(16, 384, FE)
    q1, kv1, mixed1, att1, x1, attn_w1, experts_one = middle(
        x0, att0, smalls[0], route_rows[0], smalls[1], dead, ahead, chip[8:16].reshape(384, FE), experts_zero, 4
    )
    experts_one = experts_one.reshape(16, 384, FE)
    grad_x1, grad_small1, grad_attn1, some, moe1 = layer_backward(
        (x1, att1, smalls[1], route_rows[1], cotangent, q1, kv1, mixed1, dead, attn_w1), (), experts_one, 6
    )
    grad_x0, grad_small0, grad_attn0, some, sums1, some_attn = layer_backward(
        (x0, att0, smalls[0], route_rows[0], grad_x1, q0, kv0, mixed0, dead, packs),
        (grad_attn1.reshape(2, 4, 4, 48, FE), some),
        experts_zero,
        7,
    )

    def own_block(value):
        return pick(value, core, 0)

    def unchunk(value):
        return value.reshape(2, 2, 80, 384).transpose(0, 2, 1, 3).reshape(ROWS, D).astype(f32)

    y1 = own_block(x1.reshape(2, ROWS, D)).astype(f32) + unchunk(own_block(att1)) + unchunk(moe1)
    mine = jnp.stack([own_block(grad_x0.reshape(2, ROWS, D)).astype(f32), y1])
    mine = jnp.where(own_live[None, :, None], mine, 0.0)
    kept, sent = pick(mine, high, 0), pick(mine, 1 - high, 0).astype(bf16)

    tiny = jnp.stack([grad_small0, grad_small1]).astype(bf16).reshape(2, 8, 16, 2, 24)
    tiny = tiny.transpose(0, 2, 3, 1, 4).reshape(2, 16, 16, 24)
    tiny = jnp.pad(tiny, ((0, 0), (0, 0), (0, 0), (0, 384 - 24)))
    packs = jnp.concatenate([grad_attn0.reshape(2, 16, 48, 384), tiny], axis=2).reshape(2, 4, 4, 64, FE)
    tiny, landed, grad_w_in, grad_w_exp_out, attn = end_exchange(packs, sent, sums1, some, some_attn)
    landed = landed.astype(f32)
    ends = jnp.where(high == 0, jnp.stack([kept, landed]), jnp.stack([landed, kept]))
    grad_w_qkv = jnp.concatenate([attn[:, 1, :, None, :WIDTH], attn[:, 0].reshape(2, 24, 2, WIDTH)], axis=2)
    grad_w_out = attn[:, 1, :, WIDTH:].transpose(0, 2, 1)
    tiny = tiny[:, :, 0:24]
    return (
        ends[None],
        tiny[:, 0:2],
        tiny[:, 2:4],
        grad_w_qkv,
        grad_w_out,
        tiny[:, 4:8].transpose(0, 2, 1),
        grad_w_in,
        grad_w_exp_out.transpose(0, 1, 3, 2),
    )


def solution(mesh):
    fine = Mesh(mesh.devices.reshape(4, 2, 2, 2, 4), CHIPS + ("core", "tp"))
    section, ctx = ("x", "zh"), ("zl", "core")
    every = section + ctx
    return jax.shard_map(
        shards,
        mesh=fine,
        in_specs=(
            P(ctx, section, None, None),
            P(ctx, section, None, None),
            P(),
            P(None, None, every),
            P(None, None, every),
            P(None, every, None, "tp"),
            P(None, "tp", every),
            P(None, every, None),
            P(None, None, every, "tp"),
            P(None, None, "tp", every),
        ),
        out_specs=(
            P(ctx, section, None, None),
            P(None, None, every),
            P(None, None, every),
            P(None, every, None, "tp"),
            P(None, "tp", every),
            P(None, every, None),
            P(None, None, every, "tp"),
            P(None, None, "tp", every),
        ),
        check_vma=False,
    )
```

```python
import functools

import jax
import jax.numpy as jnp
from jax import lax
from jax.experimental import pallas as pl
from jax.experimental.pallas import tpu as pltpu
from jax.sharding import Mesh
from jax.sharding import PartitionSpec as P

D = 768
HD = 64
HEADS = 3
ROWS = 160
PAIR = 320
KEYS = 640
FE = 384
EXPERTS = 4
EPS = 1e-06
WIDTH = HEADS * HD
MESH = pl.DeviceIdType.MESH
CHIPS = ("x", "zh", "zl")
f32, bf16 = jnp.float32, jnp.bfloat16
VMEM = pl.BlockSpec(memory_space=pltpu.VMEM)
SMEM = pl.BlockSpec(memory_space=pltpu.SMEM)
NN = (((1,), (0,)), ((), ()))
NT = (((1,), (1,)), ((), ()))
TN = (((0,), (0,)), ((), ()))


def dot(a, b, dims):
    return lax.dot_general(a, b, dims, preferred_element_type=f32)


def dot_split(a, b, dims):
    high = a.astype(bf16)
    return dot(high, b, dims) + dot((a - high.astype(f32)).astype(bf16), b, dims)


def params(cid, mib):
    return pltpu.CompilerParams(
        collective_id=cid, has_side_effects=True, vmem_limit_bytes=mib * 2**20
    )


ANY = pl.BlockSpec(memory_space=pl.ANY)


def arrive(peers):
    barrier = pltpu.get_barrier_semaphore()
    for peer in peers:
        pl.semaphore_signal(barrier, inc=1, device_id=peer, device_id_type=MESH)


def all_here(count):
    pl.semaphore_wait(pltpu.get_barrier_semaphore(), count)


def dma_sems(*counts):
    return [pltpu.SemaphoreType.DMA((count,)) for count in counts for _ in range(2)]


def remote(src, dst, send, recv, peer):
    return pltpu.make_async_remote_copy(
        src_ref=src, dst_ref=dst, send_sem=send, recv_sem=recv, device_id=peer, device_id_type=MESH
    )


def tp_peers():
    return [{"tp": (lax.axis_index("tp") + k) % 4} for k in (1, 2, 3)]


def pieces_of(rows):
    return (pl.ds(0, 48), pl.ds(48, rows - 48))


def sum_cores(part, crossed, send, recv):
    core = lax.axis_index("core")
    return [
        remote(part.at[1 - core, :, rows], crossed.at[:, rows], send.at[p], recv.at[p], {"core": 1 - core})
        for p, rows in enumerate(pieces_of(part.shape[2]))
    ]


def sum_terms(both, part, landed, send, recv):
    block = lax.axis_index("core") if both else 0
    return [
        [
            remote(
                part.at[block, peer["tp"], rows], landed.at[k, rows],
                send.at[3 * p + k], recv.at[3 * p + k], peer,
            )
            for k, peer in enumerate(tp_peers())
        ]
        for p, rows in enumerate(pieces_of(part.shape[2]))
    ]


def sum_results(out, send, recv):
    core, tp = lax.axis_index("core"), lax.axis_index("tp")
    return [
        [
            remote(out.at[core, tp, rows], out.at[core, tp, rows], send.at[3 * p + k], recv.at[3 * p + k], peer)
            for k, peer in enumerate(tp_peers())
        ]
        for p, rows in enumerate(pieces_of(out.shape[2]))
    ]


def sum_cross(out, send, recv):
    core, tp = lax.axis_index("core"), lax.axis_index("tp")
    return [
        [
            remote(
                out.at[core, at, rows], out.at[core, at, rows],
                send.at[4 * p + k], recv.at[4 * p + k], {"core": 1 - core},
            )
            for k, at in enumerate([(tp + 4 - k) % 4 for k in range(4)])
        ]
        for p, rows in enumerate(pieces_of(out.shape[2]))
    ]


def sum_start(both, out, part, landed, rs, rr, gs, gr, cs, cr, crossed=None, ps=None, pr=None):
    terms = sum_terms(both, part, landed, rs, rr)
    if both:
        core = lax.axis_index("core")
        pres = sum_cores(part, crossed, ps, pr)
        for pre in pres:
            pre.start()
    for p, rows in enumerate(pieces_of(part.shape[2])):
        if both:
            pres[p].wait_recv()
            for j in range(4):
                total = part[core, j, rows].astype(f32) + crossed[j, rows].astype(f32)
                part[core, j, rows] = total.astype(bf16)
        for copy in terms[p]:
            copy.start()


def sum_middle(both, out, part, landed, rs, rr, gs, gr, cs, cr, *pre):
    core, tp = lax.axis_index("core"), lax.axis_index("tp")
    terms, results, crosses = sum_terms(both, part, landed, rs, rr), sum_results(out, gs, gr), sum_cross(out, cs, cr)
    for p, rows in enumerate(pieces_of(part.shape[2])):
        total = part[core if both else 0, tp, rows].astype(f32)
        for k, copy in enumerate(terms[p]):
            copy.wait_recv()
            total = total + landed[k, rows].astype(f32)
        out[core, tp, rows] = total.astype(bf16)
        for copy in results[p]:
            copy.start()
        crosses[p][0].start()


def sum_end(both, out, part, landed, rs, rr, gs, gr, cs, cr, *pre):
    terms, results, crosses = sum_terms(both, part, landed, rs, rr), sum_results(out, gs, gr), sum_cross(out, cs, cr)
    for p in range(2):
        for k in range(3):
            results[p][k].wait_recv()
            crosses[p][k + 1].start()
    for p in range(2):
        for copy in crosses[p]:
            copy.wait()
        for copy in terms[p] + results[p]:
            copy.wait_send()
    if both:
        for copy in sum_cores(part, *pre):
            copy.wait_send()


def sum_scratch(both, rows):
    scratch = [
        pltpu.VMEM((2 if both else 1, 4, rows, 384), bf16),
        pltpu.VMEM((3, rows, 384), bf16),
    ] + dma_sems(6, 6, 8)
    if both:
        scratch += [pltpu.VMEM((4, rows, 384), bf16)] + dma_sems(2)
    return scratch


def chip_peers():
    core, zl = lax.axis_index("core"), lax.axis_index("zl")
    return {"core": 1 - core}, {"zl": 1 - zl}, zl * 2 + core


def cross_kernel(own, out, send, recv):
    other = {"core": 1 - lax.axis_index("core")}
    arrive([other])
    all_here(1)
    copy = remote(own, out, send.at[0], recv.at[0], other)
    copy.start()
    copy.wait()


def cross(own, cid):
    return pl.pallas_call(
        cross_kernel,
        out_shape=jax.ShapeDtypeStruct(own.shape, own.dtype),
        in_specs=[VMEM],
        out_specs=VMEM,
        scratch_shapes=dma_sems(1),
        compiler_params=params(cid, 8),
        name="cross",
    )(own)


def places():
    return lax.axis_index("x"), lax.axis_index("zh") * 2 + lax.axis_index("zl")


def axis_peer(along_x, k):
    x, z = places()
    if along_x:
        return {"x": (x + k) % 4}, (x + k) % 4
    to = (z + k) % 4
    return {"zh": to // 2, "zl": to % 2}, to


def half(rows, route):
    return pl.ds(route * (rows // 2), rows // 2)


def uneven(rows, route):
    first = {128: 80, 64: 48}[rows]
    return pl.ds(first, rows - first) if route else pl.ds(0, first)


def line(whole, route, second, rows):
    return whole.at[:, second, rows] if route == 0 else whole.at[second, :, rows]


def axis_peers(*ks):
    return [axis_peer(along_x, k)[0] for along_x in (True, False) for k in ks]


def start_kernel(
    lengths, images, routes, urgent, later, x_out, cot_out, out_routes, dead, all_urgent, all_later,
    got, own_sem, im_s, im_r, u1_s, u1_r, u2_s, u2_r, l_s, l_r,
):
    core = lax.axis_index("core")
    at_x, at_z = places()
    high = at_x // 2
    other = {"core": 1 - core}
    arrive(axis_peers(1, 2, 3) + [other])
    all_urgent[at_x, at_z] = urgent[...]
    got[high, core] = images[high]
    out_routes[high, core] = routes[high]
    lanes = lax.broadcasted_iota(jnp.int32, (1, KEYS), 1)
    live = lanes < lengths[0]
    for block in range(1, 4):
        live = live | ((lanes >= ROWS * block) & (lanes < ROWS * block + lengths[block]))
    dead[...] = jnp.where(live, 0.0, -1e30)
    own = pltpu.make_async_copy(later, all_later.at[at_x, at_z], own_sem)
    own.start()
    all_here(7)
    firsts, seconds, laters = [], [], []
    for route in range(2):
        b = (at_z, at_x)[route]
        rows, late = uneven(urgent.shape[0], route), half(later.shape[0], route)
        for k in range(1, 4):
            peer, _ = axis_peer(route == 0, k)
            n = 3 * route + k - 1
            firsts.append(
                remote(urgent.at[rows], all_urgent.at[at_x, at_z, rows], u1_s.at[n], u1_r.at[n], peer)
            )
            laters.append(
                remote(later.at[late], all_later.at[at_x, at_z, late], l_s.at[n], l_r.at[n], peer)
            )
            slabs = line(all_urgent, route, b, rows)
            seconds.append(remote(slabs, slabs, u2_s.at[n], u2_r.at[n], axis_peer(route == 1, k)[0]))
    swaps, kepts, passes = [], [], []
    for n, (source, target) in enumerate(((images, got), (routes, out_routes))):
        here, there = target.at[high, core], target.at[1 - high, core]
        swaps.append(remote(source.at[1 - high], here, im_s.at[n], im_r.at[n], {"x": (at_x + 2) % 4}))
        kepts.append(remote(source.at[high], here, im_s.at[2 + n], im_r.at[2 + n], other))
        passes.append(remote(there, there, im_s.at[4 + n], im_r.at[4 + n], other))
    for copy in firsts + swaps + kepts + laters:
        copy.start()
    for copy in firsts:
        copy.wait_recv()
    for copy in seconds:
        copy.start()
    for swap, onward in zip(swaps, passes):
        swap.wait_recv()
        onward.start()
    for copy in kepts + passes:
        copy.wait()
    x_out[...] = got[0]
    lines = lax.broadcasted_iota(jnp.int32, (ROWS, 1), 0)
    for block in range(2):
        live = lines < lengths[2 * lax.axis_index("zl") + block]
        cot_out[block] = jnp.where(live, got[1, block].astype(f32), 0.0).astype(bf16)
    for copy in seconds + laters:
        copy.wait()
    for copy in firsts + swaps:
        copy.wait_send()
    own.wait()


def start_exchange(lengths, images, routes, urgent, later):
    shapes = [images.shape, images.shape, (2,) + routes.shape]
    slabs = [(4, 4) + urgent.shape, (4, 4) + later.shape]
    return pl.pallas_call(
        start_kernel,
        out_shape=[jax.ShapeDtypeStruct(s, bf16) for s in shapes]
        + [jax.ShapeDtypeStruct((1, KEYS), f32)]
        + [jax.ShapeDtypeStruct(s, bf16) for s in slabs],
        in_specs=[SMEM] + [VMEM] * 4,
        out_specs=[VMEM] * 5 + [ANY],
        scratch_shapes=[pltpu.VMEM((2,) + images.shape, bf16), pltpu.SemaphoreType.DMA] + dma_sems(6, 6, 6, 6),
        compiler_params=params(1, 56),
        name="start_exchange",
    )(lengths, images, routes, urgent, later)


def spread_near(whole, send, recv):
    copies = []
    for route in range(2):
        slabs = line(whole, route, places()[1 - route], half(whole.shape[2], route))
        for n, k in enumerate((1, 3)):
            at, peer = 2 * route + n, axis_peer(route == 1, k)[0]
            copies.append(remote(slabs, slabs, send.at[at], recv.at[at], peer))
    return copies


def spread_far(whole, send, recv):
    copies = []
    size = whole.shape[2] // 2
    cut = size // 32 * 16 + size % 32
    for route in range(2):
        b = places()[1 - route]
        for n, k in enumerate((1, 3)):
            rows = pl.ds(route * size + n * cut, size - cut if n else cut)
            slabs = line(whole, route, (b + 4 - k) % 4, rows)
            at, peer = 4 + 2 * route + n, axis_peer(route == 1, k)[0]
            copies.append(remote(slabs, slabs, send.at[at], recv.at[at], peer))
    return copies


def part_rows(rows, route, n):
    size = rows // 2
    cut = size // 32 * 16 + size % 32
    return pl.ds(route * size + n * cut, size - cut if n else cut)


def toward_far(whole, passing, route, send, recv):
    copies, b = [], places()[1 - route]
    for n, k in enumerate((1, 3)):
        rows = part_rows(whole.shape[2], route, n)
        target = passing.at[route, n, :, 0 : rows.size]
        at, peer = 2 * route + n, axis_peer(route == 1, k)[0]
        copies.append(remote(line(whole, route, (b + 2) % 4, rows), target, send.at[at], recv.at[at], peer))
    return copies


def toward_near(whole, passing, landed, route, send, recv):
    copies, b = [], places()[1 - route]
    for n, k in enumerate((1, 3)):
        rows, others = (part_rows(whole.shape[2], route, m) for m in (n, 1 - n))
        at, peer = 4 * route + 2 * n, axis_peer(route == 1, k)[0]
        copies += [
            remote(passing.at[route, n, :, 0 : rows.size], landed.at[n, :, rows], send.at[at], recv.at[at], peer),
            remote(
                line(whole, route, (b + k) % 4, others), landed.at[n, :, others],
                send.at[at + 1], recv.at[at + 1], peer,
            ),
        ]
    return copies


def add_passing(whole, passing, route):
    x, z = places()
    b = (z, x)[route]
    for n, k in enumerate((1, 3)):
        rows, to = part_rows(whole.shape[2], route, n), (b + k) % 4

        def add(j, carry, n=n, rows=rows, to=to):
            own = whole[j, to, rows] if route == 0 else whole[to, j, rows]
            total = passing[route, n, j, 0 : rows.size].astype(f32) + own.astype(f32)
            passing[route, n, j, 0 : rows.size] = total.astype(bf16)
            return carry

        lax.fori_loop(0, 4, add, 0)


def last_copies(some, slabs, send, recv):
    copies = []
    for route in range(2):
        rows = half(some.shape[1], route)
        for k in range(1, 4):
            peer, at = axis_peer(route == 0, k)
            n = 3 * route + k - 1
            copies.append(remote(some.at[at, rows], slabs.at[k - 1, rows], send.at[n], recv.at[n], peer))
    return copies


def add_slabs(some, slabs, out):
    x, z = places()
    steps = some.shape[1] // 48

    def add(i, carry):
        rows, route = pl.ds(pl.multiple_of(i * 48, 48), 48), i // (steps // 2)
        total = some[x * (1 - route) + z * route, rows].astype(f32)
        for k in range(3):
            total = total + slabs[k, rows].astype(f32)
        out[rows] = total.astype(bf16)
        return carry

    lax.fori_loop(0, steps, add, 0)


def end_kernel(
    part, image, kept, half_sum, some, some_attn, tiny, ends, grad_in, grad_out, grad_attn,
    out, out_image, out_half, own_sum, other_sum, landed, sums, pieces, mids, lands, slabs, attn_slabs, cx_s, cx_r, sl_s, sl_r, at_s, at_r, p1_s, p1_r, p2_s, p2_r,
):
    def own_lines(rows):
        rows = rows.astype(f32)
        return jnp.where(core == 0, rows[0:24], rows[24:48])

    def put_experts(layer, own, got):
        for at in range(2 * EXPERTS):
            rows = slice(48 * at, 48 * at + 48)
            mine, others = own_lines(own[rows]), own_lines(got[rows])
            ref = grad_out if at % 2 else grad_in
            ref[layer, at // 2, :, 0:FE] = jnp.where(core == 0, mine, others)
            ref[layer, at // 2, :, FE:] = jnp.where(core == 0, others, mine)

    core, x = lax.axis_index("core"), lax.axis_index("x")
    other = {"core": 1 - core}
    arrive(axis_peers(1, 2, 3) + [other])
    all_here(7)
    crossing = remote(part.at[1 - core], landed, cx_s.at[0], cx_r.at[0], other)
    crossing.start()
    lasts = last_copies(some, slabs, sl_s, sl_r)
    firsts, seconds = [], []
    for route in range(2):
        rows = uneven(64, route)
        for k in range(1, 4):
            peer, at = axis_peer(route == 0, k)
            n = 3 * route + k - 1
            lasts.append(
                remote(some_attn.at[route, at], attn_slabs.at[route, k - 1], at_s.at[n], at_r.at[n], peer)
            )
            seconds.append(remote(mids.at[at, rows], lands.at[k - 1, rows], p2_s.at[n], p2_r.at[n], peer))
            peer, at = axis_peer(route == 1, k)
            firsts.append(
                remote(line(sums, route, at, rows), pieces.at[k - 1, :, rows], p1_s.at[n], p1_r.at[n], peer)
            )
    swap = remote(image, out_image, cx_s.at[1], cx_r.at[1], {"x": (x + 2) % 4})
    halves = remote(half_sum, out_half, cx_s.at[2], cx_r.at[2], other)
    for copy in lasts + [halves]:
        copy.start()
    crossing.wait()

    def add(i, carry):
        total = part[core, i // 4, i % 4].astype(f32) + landed[i // 4, i % 4].astype(f32)
        sums[i // 4, i % 4] = total.astype(bf16)
        return carry

    lax.fori_loop(0, 16, add, 0)
    for copy in firsts + [swap]:
        copy.start()
    halves.wait_recv()
    put_experts(1, half_sum, out_half)
    for copy in firsts:
        copy.wait_recv()
    at_x, at_z = places()
    for route in range(2):
        rows = uneven(64, route)

        def gather(j, carry, route=route, rows=rows):
            total = (sums[j, at_z, rows] if route == 0 else sums[at_x, j, rows]).astype(f32)
            for k in range(3):
                total = total + pieces[k, j, rows].astype(f32)
            mids[j, rows] = total.astype(bf16)
            return carry

        lax.fori_loop(0, 4, gather, 0)
    for copy in seconds:
        copy.start()
    for copy in lasts:
        copy.wait()
    add_slabs(some, slabs, own_sum)
    for route in range(2):
        attn = some_attn[route, places()[route]].astype(f32)
        for k in range(3):
            attn = attn + attn_slabs[route, k].astype(f32)
        first = 384 + 48 * route
        own_sum[first : first + 48] = attn.astype(bf16)
    final = remote(own_sum, other_sum, cx_s.at[3], cx_r.at[3], other)
    final.start()
    for copy in seconds:
        copy.wait()
    for route in range(2):
        rows = uneven(64, route)
        total = mids[places()[route], rows].astype(f32)
        for k in range(3):
            total = total + lands[k, rows].astype(f32)
        out[core, rows] = total
    given = remote(out.at[core], out.at[core], cx_s.at[4], cx_r.at[4], other)
    given.start()
    final.wait()
    put_experts(0, own_sum, other_sum)
    given.wait()
    for route in range(2):
        first = 384 + 48 * route
        rows = slice(first, first + 48)
        grad_attn[0, route] = own_lines(out[route, 0:48])
        grad_attn[1, route] = own_lines(own_sum[rows]) + own_lines(other_sum[rows])
        tiny[route] = jnp.where(core == 0, out[route, 48:56], out[route, 56:64])
    for copy in firsts + [halves]:
        copy.wait_send()
    swap.wait()
    ends[x // 2] = kept[...]
    ends[1 - x // 2] = out_image[...].astype(f32)


def end_exchange(part, image, kept, half_sum, some, some_attn):
    slab = (480, FE)
    scratch = [image.shape, half_sum.shape, slab, slab] + [(4, 4, 64, FE)] * 2 + [(3, 4, 64, FE), (4, 64, FE), (3, 64, FE)]
    scratch += [(3,) + some.shape[1:], (2, 3, 48, FE)]
    return pl.pallas_call(
        end_kernel,
        out_shape=[
            jax.ShapeDtypeStruct((2, 8, FE), f32),
            jax.ShapeDtypeStruct((2,) + image.shape, f32),
            jax.ShapeDtypeStruct((2, EXPERTS, 24, D), f32),
            jax.ShapeDtypeStruct((2, EXPERTS, 24, D), f32),
            jax.ShapeDtypeStruct((2, 2, 24, FE), f32),
        ],
        in_specs=[VMEM] * 6,
        out_specs=[VMEM] * 5,
        scratch_shapes=[pltpu.VMEM((2, 64, FE), f32)]
        + [pltpu.VMEM(s, bf16) for s in scratch]
        + dma_sems(5, 6, 6, 6, 6),
        compiler_params=params(2, 56),
        name="end_exchange",
    )(part, image, kept, half_sum, some, some_attn)


def block_rows(ref, block):
    top = jnp.concatenate([ref[block, 0, 0:80], ref[block, 1, 0:80]], axis=1)
    low = jnp.concatenate([ref[block, 2, 0:80], ref[block, 3, 0:80]], axis=1)
    return jnp.concatenate([top, low], axis=0).astype(f32)


def pair_rows(ref):
    return jnp.concatenate([block_rows(ref, 0), block_rows(ref, 1)], axis=0)


def put_chunks(ref, block, value, first=0):
    for j in range(4):
        r, c = 80 * (j // 2), 384 * (j % 2)
        ref[block, j, first : first + 80] = value[r : r + 80, c : c + 384]


def norm_parts(rows):
    centered = rows - jnp.mean(rows, axis=-1, keepdims=True)
    scale = lax.rsqrt(jnp.mean(centered * centered, axis=-1, keepdims=True) + EPS)
    return centered * scale, scale


def norm_back(grad, unit, scale, gain):
    inner = grad * gain
    return scale * (
        inner
        - jnp.mean(inner, axis=-1, keepdims=True)
        - unit * jnp.mean(inner * unit, axis=-1, keepdims=True)
    )


def softmax(logits, axis):
    top = jnp.max(logits, axis=axis, keepdims=True)
    powers = jnp.exp(logits - top)
    return powers / jnp.sum(powers, axis=axis, keepdims=True)


def own_rows(core):
    return pl.ds(pl.multiple_of(core * ROWS, ROWS), ROWS)


def head(value, h):
    return value[:, HD * h : HD * h + HD]


def gelu_parts(u):
    c = 0.7978845608028654
    t = jnp.tanh(c * (u + 0.044715 * u * u * u))
    return 0.5 * u * (1.0 + t), t


def gelu_slope(u, t):
    c = 0.7978845608028654
    return 0.5 * (1.0 + t) + 0.5 * u * (1.0 - t * t) * (c * (1.0 + 3 * 0.044715 * u * u))


def attn_weights(weights):
    chips = (slice(None),) * (len(weights.shape) - 2)
    w_kv = weights[(*chips, slice(0, 48))].reshape(D, 2 * WIDTH)
    w_q = weights[(*chips, slice(48, 96), slice(0, WIDTH))].reshape(D, WIDTH)
    return w_kv, w_q, weights[(*chips, slice(48, 96), slice(WIDTH, None))].reshape(D, WIDTH)


def attend_forward_kernel(follows, *refs):
    if follows:
        x, att_before, moe_before, small, weights, dead, q, kv, mixed, att, x_next, *scratch = refs
    else:
        x, small, weights, dead, ahead, _, q, kv, mixed, att, whole, all_ahead, *scratch = refs
        *scratch, sp_send, sp_recv, ah_send, ah_recv, own_sem = scratch
    part, landed, *sems, kv_send, kv_recv = scratch
    sums = (False, att, part, landed, *sems)
    core = lax.axis_index("core")
    other, across, me = chip_peers()
    arrive([other, across] + tp_peers())
    if not follows:
        arrive(axis_peers(1, 2, 3))
    if follows:
        x_next[...] = (x[...].astype(f32) + pair_rows(att_before) + pair_rows(moe_before)).astype(bf16)
        x = x_next
    unit, _ = norm_parts(x[own_rows(core)].astype(f32))
    normed = (unit * small[0:1] + small[2:3]).astype(bf16)
    w_kv, w_q, w_out_t = attn_weights(weights)
    kv[me] = dot(normed, w_kv, NN).astype(bf16)
    all_here(5 if follows else 11)
    far = (me + 2) % 4
    copies = [
        remote(kv.at[at], kv.at[at], kv_send.at[k], kv_recv.at[k], peer)
        for k, (at, peer) in enumerate(((me, across), (me, other), (far, other)))
    ]
    copies[0].start()
    copies[1].start()
    if not follows:
        nears = spread_near(whole, sp_send, sp_recv)
        fars = spread_far(whole, sp_send, sp_recv)
        at_x, at_z = places()
        aheads = [pltpu.make_async_copy(ahead, all_ahead.at[at_x, at_z], own_sem)]
        for route in range(2):
            rows = half(ahead.shape[0], route)
            for k in range(1, 4):
                n, peer = 3 * route + k - 1, axis_peer(route == 0, k)[0]
                aheads.append(
                    remote(ahead.at[rows], all_ahead.at[at_x, at_z, rows], ah_send.at[n], ah_recv.at[n], peer)
                )
        for copy in nears + aheads:
            copy.start()
    queries = dot(normed, w_q, NN).astype(bf16)
    q[...] = queries
    copies[0].wait_recv()
    copies[2].start()
    copies[1].wait_recv()
    copies[2].wait_recv()
    keys = kv[...].reshape(KEYS, 2 * WIDTH)
    outs = []
    for h in range(HEADS):
        scores = HD**-0.5 * dot(head(queries, h), head(keys, h), NT) + dead[...]
        probs = softmax(scores, -1).astype(bf16)
        outs.append(dot(probs, head(keys, HEADS + h), NN))
    heads = jnp.concatenate(outs, axis=1).astype(bf16)
    mixed[...] = heads
    put_chunks(part, 0, dot(heads, w_out_t, NT).astype(bf16))
    sum_start(*sums)
    sum_middle(*sums)
    if not follows:
        for copy in nears:
            copy.wait_recv()
        for copy in fars:
            copy.start()
    sum_end(*sums)
    for copy in copies:
        copy.wait_send()
    if not follows:
        for copy in fars + aheads:
            copy.wait()
        for copy in nears:
            copy.wait_send()


def attend_forward(x, before, small, weights, dead, some, ahead, cid):
    args = (x, *before, small, weights, dead)
    shapes = [(ROWS, WIDTH), (4, ROWS, 2 * WIDTH), (ROWS, WIDTH), (2, 4, 80, 384)]
    in_specs, out_specs = [VMEM] * len(args), [VMEM] * 5
    scratch = sum_scratch(False, 80) + dma_sems(3)
    if before:
        shapes.append((PAIR, D))
    else:
        args += (ahead, some)
        shapes += [some.shape, (4, 4) + ahead.shape]
        in_specs += [VMEM, ANY]
        out_specs[4:] = [ANY, ANY]
        scratch += dma_sems(8, 6) + [pltpu.SemaphoreType.DMA]
    return pl.pallas_call(
        functools.partial(attend_forward_kernel, bool(before)),
        out_shape=[jax.ShapeDtypeStruct(s, bf16) for s in shapes],
        in_specs=in_specs,
        out_specs=out_specs,
        scratch_shapes=scratch,
        input_output_aliases={} if before else {len(args) - 1: 4},
        compiler_params=params(cid, 56),
        name="attend_forward",
    )(*args)


def expert_weights(weights):
    block = weights[...]
    return block[:, 0:48].reshape(D, FE), block[:, 48:96].reshape(D, FE)


def experts_setup(x, att, small, routes, b, gates):
    unit, _ = norm_parts(x[...].astype(f32) + pair_rows(att))
    b[...] = (unit * small[1:2] + small[3:4]).astype(bf16)
    put_gates(b, small, routes, gates)


def put_gates(b, small, routes, gates):
    probs = softmax(dot(b[...], small[4:8].astype(bf16), NT), -1)
    ids = lax.broadcasted_iota(jnp.int32, (PAIR, EXPERTS), 1).astype(f32)
    ones = lax.broadcasted_iota(jnp.int32, (16, 16), 0) == lax.broadcasted_iota(jnp.int32, (16, 16), 1)
    lines = dot(routes[...], ones.astype(f32).astype(bf16), TN)
    named = (lines[:, 0:1] == ids) | (lines[:, 1:2] == ids)
    gates[...] = jnp.where(named, probs, 0.0)


def gate_of(gates, expert):
    ids = lax.broadcasted_iota(jnp.int32, (PAIR, EXPERTS), 1)
    return jnp.sum(jnp.where(ids == expert, gates[...], 0.0), axis=1, keepdims=True)


def fixed(shape):
    return pl.BlockSpec(shape, lambda e: (0,) * len(shape))


def middle_kernel(
    x, att, small, routes, small_next, dead, ahead, later, weights,
    q, kv_result, mixed, att_result, x_next, attn_result, whole,
    b, gates, total, moe, attn_w, kv, att_next,
    ah_send, ah_recv, l_send, l_recv, sp_send, sp_recv, kv_send, kv_recv, own_sem, *sems,
):
    expert = pl.program_id(0)
    sums, sums_next = (True, moe, *sems[:11]), (False, att_next, *sems[11:])
    part, part_next = sums[2], sums_next[2]
    core = lax.axis_index("core")
    at_x, at_z = places()
    other, across, me = chip_peers()
    far = (me + 2) % 4
    aheads, laters = [], []
    for route in range(2):
        second, rows, late = (at_z, at_x)[route], half(ahead.shape[2], route), half(later.shape[0], route)
        for k in range(1, 4):
            n = 3 * route + k - 1
            aheads.append(
                remote(
                    line(ahead, route, second, rows), line(attn_w, route, second, rows),
                    ah_send.at[n], ah_recv.at[n], axis_peer(route == 1, k)[0],
                )
            )
            laters.append(
                remote(
                    later.at[late], whole.at[at_x, at_z, late],
                    l_send.at[n], l_recv.at[n], axis_peer(route == 0, k)[0],
                )
            )
    own = pltpu.make_async_copy(later, whole.at[at_x, at_z], own_sem)
    nears, fars = spread_near(whole, sp_send, sp_recv), spread_far(whole, sp_send, sp_recv)

    @pl.when(expert == 0)
    def _():
        arrive([other, across] + tp_peers() + axis_peers(1, 2, 3))
        experts_setup(x, att, small, routes, b, gates)
        total[...] = jnp.zeros_like(total)
        for j in range(4):
            rows = half(ahead.shape[2], 0)
            attn_w[j, at_z, rows] = ahead[j, at_z, rows]
            rows = half(ahead.shape[2], 1)
            attn_w[at_x, j, rows] = ahead[at_x, j, rows]
        all_here(11)
        for copy in laters + [own] + aheads:
            copy.start()

    w_in, w_out_t = expert_weights(weights)
    u = dot(b[...], w_in, NN)
    active = gelu_parts(u)[0].astype(bf16).astype(f32)
    gated = (gate_of(gates, expert) * active).astype(bf16)
    total[...] += dot(gated, w_out_t, NT)

    @pl.when(expert == EXPERTS - 1)
    def _():
        for block in range(2):
            put_chunks(part, block, total[ROWS * block : ROWS * block + ROWS].astype(bf16))
        sum_start(*sums)
        for copy in laters:
            copy.wait_recv()
        own.wait()
        for copy in nears[2:]:
            copy.start()
        sum_middle(*sums)
        sum_end(*sums)
        x_next[...] = (x[...].astype(f32) + pair_rows(att) + pair_rows(moe)).astype(bf16)
        unit, _ = norm_parts(x_next[own_rows(core)].astype(f32))
        normed = (unit * small_next[0:1] + small_next[2:3]).astype(bf16)
        for copy in aheads:
            copy.wait_recv()
        w_kv, w_q, w_out = attn_weights(attn_w)
        kv[me] = dot(normed, w_kv, NN).astype(bf16)
        copies = [
            remote(kv.at[at], kv.at[at], kv_send.at[k], kv_recv.at[k], peer)
            for k, (at, peer) in enumerate(((me, across), (me, other), (far, other)))
        ]
        copies[0].start()
        copies[1].start()
        for copy in nears[:2]:
            copy.start()
        queries = dot(normed, w_q, NN).astype(bf16)
        q[...] = queries
        attn_result[...] = attn_w[...]
        copies[0].wait_recv()
        copies[2].start()
        copies[1].wait_recv()
        copies[2].wait_recv()
        keys = kv[...].reshape(KEYS, 2 * WIDTH)
        outs = []
        for h in range(HEADS):
            scores = HD**-0.5 * dot(head(queries, h), head(keys, h), NT) + dead[...]
            probs = softmax(scores, -1).astype(bf16)
            outs.append(dot(probs, head(keys, HEADS + h), NN))
        heads = jnp.concatenate(outs, axis=1).astype(bf16)
        mixed[...] = heads
        put_chunks(part_next, 0, dot(heads, w_out, NT).astype(bf16))
        sum_start(*sums_next)
        for copy in nears:
            copy.wait_recv()
        for copy in fars:
            copy.start()
        kv_result[...] = kv[...]
        sum_middle(*sums_next)
        sum_end(*sums_next)
        att_result[...] = att_next[...]
        for copy in copies + nears + laters + aheads:
            copy.wait_send()
        for copy in fars:
            copy.wait()


def middle(x, att, small, routes, small_next, dead, ahead, later, weights, cid):
    args = (x, att, small, routes, small_next, dead, ahead, later)
    shapes = [(ROWS, WIDTH), (4, ROWS, 2 * WIDTH), (ROWS, WIDTH), (2, 4, 80, 384), (PAIR, D), ahead.shape]
    return pl.pallas_call(
        middle_kernel,
        grid=(EXPERTS,),
        out_shape=[jax.ShapeDtypeStruct(s, bf16) for s in shapes + [(4, 4) + later.shape]],
        in_specs=[fixed(a.shape) for a in args] + [pl.BlockSpec((16, 96, FE), lambda e: (0, e, 0))],
        out_specs=[fixed(s) for s in shapes] + [ANY],
        scratch_shapes=[
            pltpu.VMEM((PAIR, D), bf16),
            pltpu.VMEM((PAIR, EXPERTS), f32),
            pltpu.VMEM((PAIR, D), f32),
            pltpu.VMEM((2, 4, 80, 384), bf16),
            pltpu.VMEM(ahead.shape, bf16),
            pltpu.VMEM((4, ROWS, 2 * WIDTH), bf16),
            pltpu.VMEM((2, 4, 80, 384), bf16),
        ]
        + dma_sems(6, 6, 8, 3)
        + [pltpu.SemaphoreType.DMA]
        + sum_scratch(True, 80)
        + sum_scratch(False, 80),
        compiler_params=params(cid, 56),
        name="middle",
    )(*args, weights)


def layer_backward_kernel(with_moe, *refs):
    x, att, small, routes, grad, q, kv, mixed, dead, attn_w, *refs = refs
    if not with_moe:
        extra, some_before, *refs = refs
    weights, grad_x, grad_small, grad_w, some, *refs = refs
    if with_moe:
        moe_result, *refs = refs
    else:
        own_sum, some_attn, *refs = refs
    b, gates, unit_two, scale_two, total, gate_grads, gated_all, grad_u_all, *refs = refs
    whole, slabs, passing, all_probs, grad_h, unit_one, parts, kv_landed, kv_out, back, back_one, *refs = refs
    fs, fr, ns, nr, kv_send, kv_recv, *refs = refs
    sums_two, sums_one, refs = (True, back, *refs[:11]), (False, back_one, *refs[11:19]), refs[19:]
    part_two, part_one = sums_two[2], sums_one[2]
    if with_moe:
        moe, moe_part, moe_out, moe_landed, ms, mr, mg, mh, moe_crossed, ps, pr = refs
        moe_sums = (moe_part, moe_crossed, ps, pr)
    else:
        last_slabs, ls, lr, attn_slabs, as_, ar = refs
        lasts = last_copies(some_before, last_slabs, ls, lr)
        for route in range(2):
            for k in range(1, 4):
                n, (peer, to) = 3 * route + k - 1, axis_peer(route == 1, k)
                slab = extra.at[0, :, to] if route == 0 else extra.at[1, to]
                lasts.append(remote(slab, attn_slabs.at[route, k - 1], as_.at[n], ar.at[n], peer))
    fars = [toward_far(whole, passing, route, fs, fr) for route in range(2)]
    nears = [toward_near(whole, passing, slabs, route, ns, nr) for route in range(2)]
    core, tp = lax.axis_index("core"), lax.axis_index("tp")
    at_x, at_z = places()
    other, across, me = chip_peers()
    far = (me + 2) % 4
    step = pl.program_id(0)

    @pl.when(step == 0)
    def _():
        arrive([other, across] + tp_peers() + axis_peers(1, 2, 3))
        unit, scale = norm_parts(x[...].astype(f32) + pair_rows(att))
        unit_two[...] = unit
        scale_two[...] = scale
        b[...] = (unit * small[1:2] + small[3:4]).astype(bf16)
        put_gates(b, small, routes, gates)
        total[...] = jnp.zeros_like(total)
        gate_grads[...] = jnp.zeros_like(gate_grads)
        if with_moe:
            moe[...] = jnp.zeros_like(moe)
        all_here(11)
        if not with_moe:
            for copy in lasts:
                copy.start()

    @pl.when(step < EXPERTS)
    def _():
        w_in, w_out_t = expert_weights(weights)
        u = dot(b[...], w_in, NN)
        act, t = gelu_parts(u)
        active = act.astype(bf16).astype(f32)
        gate = gate_of(gates, step)
        gated = (gate * active).astype(bf16)
        gated_all[step] = gated
        if with_moe:
            moe[...] += dot(gated, w_out_t, NT)
        grad_active = dot(grad[...], w_out_t, NN)
        ids = lax.broadcasted_iota(jnp.int32, (PAIR, 128), 1)
        gate_grad = jnp.sum(grad_active * active, axis=1, keepdims=True)
        gate_grads[...] = jnp.where(ids == step, gate_grad, gate_grads[...])
        grad_u = (gate * grad_active * gelu_slope(u, t)).astype(bf16)
        grad_u_all[step] = grad_u
        total[...] += dot(grad_u, w_in, NT)

    @pl.when(step == EXPERTS - 1)
    def _():
        part_two[...] = jnp.zeros_like(part_two)
        lines, lanes = (lax.broadcasted_iota(jnp.int32, (16, 128), axis) for axis in range(2))
        ones = ((lines == lanes) & (lines < EXPERTS)).astype(f32).astype(bf16)
        for block in range(2):
            rows = slice(ROWS * block, ROWS * block + ROWS)
            put_chunks(part_two, block, total[rows].astype(bf16))
            part_two[block, 0, 80:96, 0:ROWS] = dot(ones, gate_grads[rows].astype(bf16), NT).astype(bf16)
            if with_moe:
                put_chunks(moe_part, block, moe[rows].astype(bf16))
        sum_start(*sums_two)

    @pl.when(step >= EXPERTS)
    def _():
        at = step - EXPERTS
        first = pl.multiple_of(96 * at, 96)
        grad_in = dot(b[...], grad_u_all[at], TN).astype(bf16)
        whole[:, :, pl.ds(first, 48)] = grad_in.reshape(4, 4, 48, FE)
        grad_out = dot(grad[...], gated_all[at], TN).astype(bf16)
        whole[:, :, pl.ds(first + 48, 48)] = grad_out.reshape(4, 4, 48, FE)

    @pl.when(step == EXPERTS + 1)
    def _():
        sum_middle(*sums_two)

    @pl.when(step == 2 * EXPERTS - 2)
    def _():
        keys = kv[...].reshape(KEYS, 2 * WIDTH)
        for h in range(HEADS):
            all_probs[h] = softmax(HD**-0.5 * dot(head(q[...], h), head(keys, h), NT) + dead[...], -1)
        if not with_moe:
            for copy in lasts:
                copy.wait()
            add_slabs(some_before, last_slabs, own_sum)
            for route in range(2):

                def add(j, carry, route=route):
                    attn = (extra[0, j, at_z] if route == 0 else extra[1, at_x, j]).astype(f32)
                    for k in range(3):
                        attn = attn + attn_slabs[route, k, j].astype(f32)
                    some_attn[route, j] = attn.astype(bf16)
                    return carry

                lax.fori_loop(0, 4, add, 0)

    @pl.when(step == 2 * EXPERTS - 1)
    def _():
        for copy in fars[1] + fars[0]:
            copy.start()
        sum_end(*sums_two)
        router = small[4:8]
        chances = softmax(dot(router.astype(bf16), b[...], NT), 0)
        ids = lax.broadcasted_iota(jnp.int32, (EXPERTS, PAIR), 0).astype(f32)
        lines = routes[...].astype(f32)
        named = (lines[0:1] == ids) | (lines[1:2] == ids)
        tables = [back[block, 0, 80:96, 0:ROWS].astype(f32)[0:EXPERTS] for block in range(2)]
        gate_rows = jnp.where(named, jnp.concatenate(tables, axis=1), 0.0)
        grad_logits = chances * (gate_rows - jnp.sum(chances * gate_rows, axis=0, keepdims=True))
        grad_b = pair_rows(back) + dot_split(grad_logits, router.astype(bf16), TN)
        grad_h[...] = grad[...].astype(f32) + norm_back(grad_b, unit_two[...], scale_two[...], small[1:2])
        grad_att = grad_h[own_rows(core)].astype(bf16)
        w_kv, w_q, w_out_t = attn_weights(attn_w)
        grad_mixed = dot(grad_att, w_out_t, NN).astype(bf16)
        keys = kv[...].reshape(KEYS, 2 * WIDTH)
        queries = q[...]
        q_parts, k_parts, v_parts = [], [], []
        for h in range(HEADS):
            q_h, g_h = head(queries, h), head(grad_mixed, h)
            k_h, v_h = head(keys, h), head(keys, HEADS + h)
            probs = all_probs[h]
            v_parts.append(dot(probs.astype(bf16), g_h, TN))
            grad_weights = dot(g_h, v_h, NT)
            grad_scores = probs * (grad_weights - jnp.sum(probs * grad_weights, axis=-1, keepdims=True))
            grad_scores = grad_scores.astype(bf16)
            q_parts.append(HD**-0.5 * dot(grad_scores, k_h, NN))
            k_parts.append(HD**-0.5 * dot(grad_scores, q_h, TN))
        grad_keys = jnp.concatenate(k_parts + v_parts, axis=1).astype(bf16)
        parts[...] = grad_keys.reshape(4, ROWS, 2 * WIDTH)
        crosses = [
            remote(parts.at[(at + 1 - 2 * core) % 4], kv_landed.at[k], kv_send.at[k], kv_recv.at[k], other)
            for k, at in enumerate((me, far))
        ]
        onward = remote(kv_out, kv_landed.at[2], kv_send.at[2], kv_recv.at[2], across)
        crosses[1].start()
        crosses[0].start()
        if with_moe:
            pres = sum_cores(*moe_sums)
            for copy in pres:
                copy.start()
        crosses[1].wait_recv()
        kv_out[...] = (parts[far].astype(f32) + kv_landed[1].astype(f32)).astype(bf16)
        onward.start()
        if with_moe:
            for copy in pres:
                copy.wait_recv()
            for j in range(4):
                moe_sum = moe_part[core, j].astype(f32) + moe_crossed[j].astype(f32)
                moe_crossed[j] = moe_sum.astype(bf16)
            moe_terms = [
                remote(moe_crossed.at[peer["tp"]], moe_landed.at[k], ms.at[k], mr.at[k], peer)
                for k, peer in enumerate(tp_peers())
            ]
            for copy in moe_terms:
                copy.start()
        for route in (1, 0):
            for copy in fars[route]:
                copy.wait_recv()
            add_passing(whole, passing, route)
            for copy in nears[route]:
                copy.start()
        grad_q = jnp.concatenate(q_parts, axis=1).astype(bf16)
        grad_w[1, :, WIDTH:] = dot(grad_att, mixed[...], TN).astype(bf16)
        lanes = lax.broadcasted_iota(jnp.int32, (EXPERTS, PAIR), 1)
        own_lanes = (lanes < ROWS) == (core == 0)
        own = (lax.broadcasted_iota(jnp.int32, (PAIR, 1), 0) < ROWS) == (core == 0)
        kept = jnp.where(own, grad_b, 0.0)
        grad_small[1:2] = jnp.sum(kept * unit_two[...], axis=0, keepdims=True)
        grad_small[3:4] = jnp.sum(kept, axis=0, keepdims=True)
        grad_small[4:8] = dot_split(jnp.where(own_lanes, grad_logits, 0.0), b[...], NN)
        unit, scale_one = norm_parts(x[...].astype(f32))
        unit_one[...] = unit
        normed = (unit_one[own_rows(core)] * small[0:1] + small[2:3]).astype(bf16)
        crosses[0].wait_recv()
        onward.wait_recv()
        grad_kv = parts[me].astype(f32) + kv_landed[0].astype(f32) + kv_landed[2].astype(f32)
        grad_kv = grad_kv.astype(bf16)
        value = dot(grad_kv, w_kv, NT) + dot(grad_q, w_q, NT)
        put_chunks(part_one, 0, value.astype(bf16))
        sum_start(*sums_one)
        grad_w[0] = dot(normed, grad_kv, TN).astype(bf16)
        grad_w[1, :, :WIDTH] = dot(normed, grad_q, TN).astype(bf16)
        sum_middle(*sums_one)
        if with_moe:
            moe_total = moe_crossed[tp].astype(f32)
            for k, copy in enumerate(moe_terms):
                copy.wait_recv()
                moe_total = moe_total + moe_landed[k].astype(f32)
            moe_out[tp] = moe_total.astype(bf16)
            moe_results = [
                remote(moe_out.at[tp], moe_out.at[tp], mg.at[k], mh.at[k], peer)
                for k, peer in enumerate(tp_peers())
            ]
            for copy in moe_results:
                copy.start()
        for route in range(2):
            for copy in fars[route]:
                copy.wait_send()
            for copy in nears[route]:
                copy.wait()
        steps = some.shape[1] // 48

        def add(i, carry):
            j, at = i % 4, i // 4
            rows, route = pl.ds(pl.multiple_of(at * 48, 48), 48), at // (steps // 2)
            mine = whole[j * (1 - route) + at_x * route, at_z * (1 - route) + j * route, rows]
            total = mine.astype(f32) + slabs[0, j, rows].astype(f32) + slabs[1, j, rows].astype(f32)
            some[j, rows] = total.astype(bf16)
            return carry

        lax.fori_loop(0, 4 * steps, add, 0)
        sum_end(*sums_one)
        grad_a = pair_rows(back_one)
        grad_x[...] = (grad_h[...] + norm_back(grad_a, unit_one[...], scale_one, small[0:1])).astype(bf16)
        kept = jnp.where(own, grad_a, 0.0)
        grad_small[0:1] = jnp.sum(kept * unit_one[...], axis=0, keepdims=True)
        grad_small[2:3] = jnp.sum(kept, axis=0, keepdims=True)
        for copy in crosses + [onward]:
            copy.wait_send()
        if with_moe:
            for copy in pres + moe_terms:
                copy.wait_send()
            for copy in moe_results:
                copy.wait()
            moe_result[...] = moe_out[...]


def layer_backward(args, others, weights, cid):
    with_moe = not others
    slab = (384, FE)
    shapes = [((PAIR, D), bf16), ((8, D), f32), ((2, D, 2 * WIDTH), bf16), ((4,) + slab, bf16)]
    scratch = [
        ((PAIR, D), bf16),
        ((PAIR, EXPERTS), f32),
        ((PAIR, D), f32),
        ((PAIR, 1), f32),
        ((PAIR, D), f32),
        ((PAIR, 128), f32),
        ((EXPERTS, PAIR, FE), bf16),
        ((EXPERTS, PAIR, FE), bf16),
        ((4, 4) + slab, bf16),
        ((2, 4) + slab, bf16),
        ((2, 2, 4, 96, FE), bf16),
        ((HEADS, ROWS, KEYS), f32),
        ((PAIR, D), f32),
        ((PAIR, D), f32),
        ((4, ROWS, 2 * WIDTH), bf16),
        ((3, ROWS, 2 * WIDTH), bf16),
        ((ROWS, 2 * WIDTH), bf16),
        ((2, 4, 96, 384), bf16),
        ((2, 4, 80, 384), bf16),
    ]
    scratch = [pltpu.VMEM(*s) for s in scratch] + dma_sems(4, 8, 3)
    scratch += sum_scratch(True, 96) + sum_scratch(False, 80)
    if with_moe:
        shapes.append(((4, 80, 384), bf16))
        scratch += [pltpu.VMEM((PAIR, D), f32), pltpu.VMEM((2, 4, 80, 384), bf16)]
        scratch += [pltpu.VMEM((4, 80, 384), bf16), pltpu.VMEM((3, 80, 384), bf16)] + dma_sems(3, 3)
        scratch += [pltpu.VMEM((4, 80, 384), bf16)] + dma_sems(2)
    else:
        shapes += [(slab, bf16), ((2, 4, 48, FE), bf16)]
        scratch += [pltpu.VMEM((3,) + slab, bf16)] + dma_sems(6)
        scratch += [pltpu.VMEM((2, 3, 4, 48, FE), bf16)] + dma_sems(6)
    args = args + others
    return pl.pallas_call(
        functools.partial(layer_backward_kernel, with_moe),
        grid=(2 * EXPERTS,),
        out_shape=[jax.ShapeDtypeStruct(*s) for s in shapes],
        in_specs=[fixed(a.shape) for a in args]
        + [pl.BlockSpec((16, 96, FE), lambda s: (0, jnp.minimum(s, EXPERTS - 1), 0))],
        out_specs=[fixed(s) for s, _ in shapes],
        scratch_shapes=scratch,
        compiler_params=params(cid, 60),
        name="layer_backward",
    )(*args, weights)


def shards(boundary, routes, lengths, ln_gains, ln_biases, w_qkv, w_out, w_router, w_in, w_exp_out):
    core = lax.axis_index("core")
    high = lax.axis_index("x") // 2

    def pick(value, at, axis):
        return lax.dynamic_index_in_dim(value, at, axis, keepdims=False)

    halves = jnp.stack(
        [
            w_qkv[:, :, 1:].reshape(2, 24, 384),
            jnp.concatenate([w_qkv[:, :, 0], w_out.transpose(0, 2, 1)], axis=2),
        ],
        axis=1,
    )

    stacked = jnp.stack([w_in, w_exp_out.transpose(0, 1, 3, 2)], axis=2).reshape(384, 2, FE)
    tiny = jnp.concatenate([ln_gains, ln_biases, w_router.transpose(0, 2, 1)], axis=1)
    tiny = jnp.pad(tiny.transpose(1, 0, 2).reshape(8, 48), ((0, 8), (0, 384 - 48)))
    attn_one, attn_zero = halves[1].reshape(48, 384), halves[0].reshape(48, 384)
    own_half = jnp.concatenate([pick(stacked, core, 1), attn_one, attn_zero, tiny])
    got_half = cross(jnp.concatenate([pick(stacked, 1 - core, 1), attn_one, attn_zero, tiny]), 0)
    low_half = jnp.where(core == 0, own_half, got_half)
    high_half = jnp.where(core == 0, got_half, own_half)
    chip = jnp.concatenate(
        [low_half[:480].reshape(20, 24, FE), high_half[:480].reshape(20, 24, FE)], axis=1
    )
    later, ahead = chip[0:8].reshape(384, FE), chip[16:18].reshape(96, FE)
    urgent = jnp.concatenate([chip[18:20].reshape(96, FE), low_half[480:496], high_half[480:496]])

    turned = jnp.pad(routes[0].astype(bf16).transpose(0, 2, 1), ((0, 0), (0, 14), (0, 256 - ROWS)))
    x0, cotangent, got_routes, dead, packs, some = start_exchange(lengths, boundary[0], turned, urgent, later)
    x0, cotangent = x0.reshape(PAIR, D), cotangent.reshape(PAIR, D)
    packs = packs.reshape(16, 128, 384)
    tiny = packs[:, 96:128].reshape(32, 16, 384)[:, 0:8, 0:48].reshape(32, 8, 2, 24).transpose(2, 1, 0, 3).reshape(2, 8, D)
    smalls = [tiny[0].astype(f32), tiny[1].astype(f32)]

    own_length = pick(lengths, 2 * lax.axis_index("zl") + core, 0)
    own_live = jnp.arange(ROWS, dtype=jnp.int32) < own_length
    route_rows = [kind[:, :, 0:ROWS].transpose(1, 0, 2).reshape(16, PAIR) for kind in got_routes]
    q0, kv0, mixed0, att0, experts_zero, ahead = attend_forward(x0, (), smalls[0], packs, dead, some, ahead, 3)
    experts_zero = experts_zero.reshape(16, 384, FE)
    q1, kv1, mixed1, att1, x1, attn_w1, experts_one = middle(
        x0, att0, smalls[0], route_rows[0], smalls[1], dead, ahead, chip[8:16].reshape(384, FE), experts_zero, 4
    )
    experts_one = experts_one.reshape(16, 384, FE)
    grad_x1, grad_small1, grad_attn1, some, moe1 = layer_backward(
        (x1, att1, smalls[1], route_rows[1], cotangent, q1, kv1, mixed1, dead, attn_w1), (), experts_one, 6
    )
    grad_x0, grad_small0, grad_attn0, some, sums1, some_attn = layer_backward(
        (x0, att0, smalls[0], route_rows[0], grad_x1, q0, kv0, mixed0, dead, packs),
        (grad_attn1.reshape(2, 4, 4, 48, FE), some),
        experts_zero,
        7,
    )

    def own_block(value):
        return pick(value, core, 0)

    def unchunk(value):
        return value.reshape(2, 2, 80, 384).transpose(0, 2, 1, 3).reshape(ROWS, D).astype(f32)

    y1 = own_block(x1.reshape(2, ROWS, D)).astype(f32) + unchunk(own_block(att1)) + unchunk(moe1)
    mine = jnp.stack([own_block(grad_x0.reshape(2, ROWS, D)).astype(f32), y1])
    mine = jnp.where(own_live[None, :, None], mine, 0.0)
    kept, sent = pick(mine, high, 0), pick(mine, 1 - high, 0).astype(bf16)

    tiny = jnp.stack([grad_small0, grad_small1]).astype(bf16).reshape(2, 8, 16, 2, 24)
    tiny = tiny.transpose(0, 2, 3, 1, 4).reshape(2, 16, 16, 24)
    tiny = jnp.pad(tiny, ((0, 0), (0, 0), (0, 0), (0, 384 - 24)))
    packs = jnp.concatenate([grad_attn0.reshape(2, 16, 48, 384), tiny], axis=2).reshape(2, 4, 4, 64, FE)
    tiny, ends, grad_w_in, grad_w_exp_out, attn = end_exchange(packs, sent, kept, sums1, some, some_attn)
    grad_w_qkv = jnp.concatenate([attn[:, 1, :, None, :WIDTH], attn[:, 0].reshape(2, 24, 2, WIDTH)], axis=2)
    grad_w_out = attn[:, 1, :, WIDTH:].transpose(0, 2, 1)
    tiny = tiny[:, :, 0:24]
    return (
        ends[None],
        tiny[:, 0:2],
        tiny[:, 2:4],
        grad_w_qkv,
        grad_w_out,
        tiny[:, 4:8].transpose(0, 2, 1),
        grad_w_in,
        grad_w_exp_out.transpose(0, 1, 3, 2),
    )


def solution(mesh):
    fine = Mesh(mesh.devices.reshape(4, 2, 2, 2, 4), CHIPS + ("core", "tp"))
    section, ctx = ("x", "zh"), ("zl", "core")
    every = section + ctx
    return jax.shard_map(
        shards,
        mesh=fine,
        in_specs=(
            P(ctx, section, None, None),
            P(ctx, section, None, None),
            P(),
            P(None, None, every),
            P(None, None, every),
            P(None, every, None, "tp"),
            P(None, "tp", every),
            P(None, every, None),
            P(None, None, every, "tp"),
            P(None, None, "tp", every),
        ),
        out_specs=(
            P(ctx, section, None, None),
            P(None, None, every),
            P(None, None, every),
            P(None, every, None, "tp"),
            P(None, "tp", every),
            P(None, every, None),
            P(None, None, every, "tp"),
            P(None, None, "tp", every),
        ),
        check_vma=False,
    )
```
